32 devices in a mesh: seq: 16 (over z, x, core), head: 2 (over y).
Axes of the slice: x: 2, y: 2, z: 4, core: 2. Of those that a mesh axis runs over, the one named last changes fastest.
Arguments:
- attention: bfloat16 [4, 1024, 1536], P(None, 'seq', 'head'), may hold values from -6 to 6
- encoder_skip: bfloat16 [4, 2048, 1536], P('head', 'seq'), may hold values from -6 to 6
- depth_filter: float32 [3, 1536], replicated, may hold values from -3 to 3
- point_weight: bfloat16 [1536, 1536], P('head'), may hold values from -0.15625 to 0.15625
- crop_offset: int32 [4], P('head'), may hold values from 0 to 128
- target_bins: int32 [4, 32], P('head'), may hold values from 0 to 127
- cotangent: bfloat16 [4, 2048, 1536], P('head', 'seq'), may hold values from -6 to 6
Outputs:
- target_rows: bfloat16 [4, 32, 1536], P('head', 'seq')
- attention_grad: bfloat16 [4, 1024, 1536], P('head', 'seq')
- skip_grad: bfloat16 [4, 2048, 1536], P('head', 'seq')
- filter_grad: float32 [3, 1536], replicated
The draws below stay inside these ranges and needn't reach their ends.
Inputs may be any that keep to these rules, and one draw needn't show every extreme that they name: The cropped window of sequence b starts at bin crop_offset[b]; bins of it past the end of the sequence are empty. Target j of sequence b reads bin 128 * (j // 2) + target_bins[b, j] of the cropped window.
All inputs are finite; a program needn't handle non-finite values.
Results may differ from the reference program's by a relative error of at most 0.007.
Values may be sent and summed in bfloat16 or wider, within the bound.
No kernel may reach another device: no remote copies, remote signals or barrier semaphores. Data moves between devices by JAX's collectives and lax.ppermute only.
A program may use at most 64 MiB of HBM per device.

```python
import math
import jax
import jax.numpy as jnp
from jax import lax

D = 1536
NTD = 2
R1 = 128
L0 = 1024
L1 = 2048
B = 4
NT = 32


def place_ends(drawn, stream_key, low, high):
    extent = drawn.shape
    spot = [jax.random.randint(jax.random.fold_in(stream_key, axis), (), 0, extent[axis]) for axis in range(len(extent))]
    drawn = drawn.at[tuple(spot)].set(low)
    longest = extent.index(max(extent))
    spot[longest] = (spot[longest] + 1) % extent[longest]
    return drawn.at[tuple(spot)].set(high)


def level_of(stream_key, dims, split, least, top_value):
    def one(axis_at, shards_of):
        draws = jax.random.uniform(jax.random.fold_in(jax.random.fold_in(stream_key, 6), axis_at), (shards_of,), jnp.float32, least / len(split), top_value / len(split))
        return jnp.repeat(jnp.exp(draws), dims[axis_at] // shards_of).reshape((-1,) + (1,) * (len(dims) - axis_at - 1))

    loudness = one(*split[0])
    for cut in split[1:]:
        loudness = loudness * one(*cut)
    return loudness


def normal_values(stream_key, extent, deviation, most, cuts=(), kind=jnp.bfloat16):
    drawn = deviation * jax.random.normal(stream_key, extent, jnp.float32)
    if cuts:
        drawn = drawn * level_of(stream_key, extent, cuts, -0.22, 0.18)
    return jnp.clip(drawn, -most, most).astype(kind)


def setup_inputs(seed: int = 0) -> dict:
    arg_keys = jax.random.split(jax.random.key(seed), 8)
    return {
        "attention": normal_values(arg_keys[0], (B, L0, D), 1.0, 6.0, ((1, 16), (2, 2))),
        "encoder_skip": normal_values(arg_keys[1], (B, L1, D), 1.0, 6.0, ((0, 2), (1, 16))),
        "depth_filter": normal_values(arg_keys[2], (3, D), 0.6, 3.0, (), jnp.float32),
        "point_weight": normal_values(arg_keys[3], (D, D), D ** -0.5, 0.15625, ((0, 2),)),
        "crop_offset": place_ends(jax.random.randint(arg_keys[4], (B,), 0, R1 + 1), jax.random.fold_in(arg_keys[4], 1), 0, R1).astype(jnp.int32),
        "target_bins": place_ends(jax.random.randint(arg_keys[5], (B, NT), 0, R1), jax.random.fold_in(arg_keys[5], 1), 0, R1 - 1).astype(jnp.int32),
        "cotangent": normal_values(arg_keys[6], (B, L1, D), 1.0, 6.0, ((0, 2), (1, 16))),
    }


def gelu_slope(values):
    return 0.5 * (1.0 + lax.erf(values * 0.7071067811865476)) + values * jnp.exp(-0.5 * values * values) * 0.3989422804014327

def one_sequence(attention_row, skip_row, depth_filter, point_weight, offset, targets, cot_row):
    summed = (jnp.repeat(attention_row.astype(jnp.float32), 2, axis=0) + skip_row.astype(jnp.float32)).astype(jnp.bfloat16)
    padded = jnp.pad(summed, ((1, 1), (0, 0)))
    filtered = depth_filter[0] * padded[:-2] + depth_filter[1] * padded[1:-1] + depth_filter[2] * padded[2:]
    activated = jax.nn.gelu(filtered, approximate=False).astype(jnp.bfloat16)
    mixed_rows = jnp.dot(activated, point_weight, preferred_element_type=jnp.float32)
    block_out = (summed.astype(jnp.float32) + mixed_rows).astype(jnp.bfloat16)
    places = jnp.arange(NT, dtype=jnp.int32) // NTD * R1 + targets.astype(jnp.int32) + offset.astype(jnp.int32)
    inside = places < L1
    chosen = block_out[jnp.minimum(places, L1 - 1)]
    target_rows = jnp.where(inside[:, None], chosen, jnp.zeros_like(chosen)).astype(jnp.bfloat16)
    sources = jnp.arange(L1, dtype=jnp.int32) - offset.astype(jnp.int32)
    taken = cot_row[jnp.maximum(sources, 0)]
    grad_out = jnp.where((sources >= 0)[:, None], taken, jnp.zeros_like(taken)).astype(jnp.bfloat16)
    grad_act = jnp.dot(grad_out, point_weight.T, preferred_element_type=jnp.float32)
    grad_conv = (grad_act * gelu_slope(filtered)).astype(jnp.bfloat16)
    grad_padded = jnp.pad(grad_conv, ((1, 1), (0, 0)))
    grad_sum = grad_out.astype(jnp.float32) + depth_filter[0] * grad_padded[2:] + depth_filter[1] * grad_padded[1:-1] + depth_filter[2] * grad_padded[:-2]
    skip_grad = grad_sum.astype(jnp.bfloat16)
    attention_grad = grad_sum.reshape(L1 // 2, 2, D).sum(axis=1).astype(jnp.bfloat16)
    conv_wide = grad_conv.astype(jnp.float32)
    filter_terms = jnp.stack([lax.optimization_barrier(jnp.sum(conv_wide * padded[:-2].astype(jnp.float32), axis=0)), lax.optimization_barrier(jnp.sum(conv_wide * padded[1:-1].astype(jnp.float32), axis=0)), lax.optimization_barrier(jnp.sum(conv_wide * padded[2:].astype(jnp.float32), axis=0))])
    return (target_rows, attention_grad, skip_grad, filter_terms)

def reference(attention, encoder_skip, depth_filter, point_weight, crop_offset, target_bins, cotangent):

    def per_sequence(members):
        return one_sequence(members[0], members[1], depth_filter, point_weight, members[2], members[3], members[4])
    target_rows, attention_grad, skip_grad, filter_terms = lax.map(per_sequence, (attention, encoder_skip, crop_offset, target_bins, cotangent))
    filter_grad = lax.optimization_barrier(jnp.sum(filter_terms, axis=0)) * (1.0 / math.sqrt(B * L1))
    return (target_rows, attention_grad, skip_grad, filter_grad)
```

```python
import math

import jax
import jax.numpy as jnp
from jax import lax
from jax.sharding import PartitionSpec as P

NTD = 2


def extended(shard, sides, width):
    for axis, dim in sides:
        count, length = (lax.axis_size(axis), shard.shape[dim])
        up = [(i, (i + 1) % count) for i in range(count - 1)]
        down = [(j, i) for i, j in up]
        last = lax.slice_in_dim(shard, length - width, length, axis=dim)
        initial = lax.slice_in_dim(shard, 0, width, axis=dim)
        before = lax.ppermute(last, axis, up)
        after = lax.ppermute(initial, axis, down)
        shard = jnp.concatenate([before, shard, after], axis=dim)
    return shard


def passed_along(shard, axis, by):
    count = lax.axis_size(axis)
    pairs = [(i, i + by) for i in range(count) if 0 <= i + by < count]
    return lax.ppermute(shard, axis, pairs)


def gelu_slope(values):
    return (
        0.5 * (1.0 + lax.erf(values * 0.7071067811865476))
        + values * jnp.exp(-0.5 * values * values) * 0.3989422804014327
    )


def with_rims(field):
    return extended(field, (("seq", 1),), 1)


def one_hot(places, length):
    return (places[:, :, None] == jnp.arange(length, dtype=jnp.int32)[None, None, :]).astype(
        jnp.bfloat16
    )


def core_swap(part):
    count = lax.axis_size("seq")
    return lax.ppermute(part, "seq", [(i, i ^ 1) for i in range(count)])


def gathered_weight(rows):
    heads = lax.axis_size("head")
    here = lax.axis_index("head")
    core = lax.axis_index("seq") % 2
    half = rows.shape[0] // 2
    mine = lax.dynamic_slice_in_dim(rows, core * half, half, 0)
    blocks = [(0, rows)]
    for step in range(1, heads):
        pairs = [(i, (i + step) % heads) for i in range(heads)]
        got = lax.ppermute(mine, "head", pairs)
        twin = core_swap(got)
        low = jnp.where(core == 0, got, twin)
        high = jnp.where(core == 0, twin, got)
        blocks.append((step, jnp.concatenate([low, high], axis=0)))
    full = jnp.zeros((heads * rows.shape[0], rows.shape[1]), rows.dtype)
    for step, block in blocks:
        place = (here - step) % heads
        full = lax.dynamic_update_slice_in_dim(full, block, place * rows.shape[0], 0)
    return full


def butterfly(total, axis):
    count = lax.axis_size(axis)
    if count & (count - 1):
        return lax.psum(total, axis)
    step = 1
    while step < count:
        total = total + lax.ppermute(total, axis, [(i, i ^ step) for i in range(count)])
        step *= 2
    return total


def shards(
    attention, encoder_skip, depth_filter, point_weight, crop_offset, target_bins, cotangent
):
    slab_input = lax.all_to_all(attention, "head", split_axis=0, concat_axis=2, tiled=True)
    local_seqs = encoder_skip.shape[0]
    slab_rows = encoder_skip.shape[1]
    channels = encoder_skip.shape[2]
    summed = (
        jnp.repeat(slab_input, 2, axis=1).astype(jnp.float32) + encoder_skip.astype(jnp.float32)
    ).astype(jnp.bfloat16)
    padded = with_rims(summed)
    filtered = (
        depth_filter[0] * padded[:, :-2]
        + depth_filter[1] * padded[:, 1:-1]
        + depth_filter[2] * padded[:, 2:]
    )
    activated = jax.nn.gelu(filtered, approximate=False).astype(jnp.bfloat16)
    flat_act = activated.reshape(local_seqs * slab_rows, channels)
    full_weight = gathered_weight(point_weight)
    mixed_rows = jnp.dot(flat_act, full_weight, preferred_element_type=jnp.float32)
    block_out = (
        summed.astype(jnp.float32) + mixed_rows.reshape(local_seqs, slab_rows, channels)
    ).astype(jnp.bfloat16)
    slab_index = lax.axis_index("seq")
    bins = jnp.concatenate(
        [jnp.zeros_like(target_bins[:, :NTD]), target_bins], axis=1
    )
    asked = lax.dynamic_slice_in_dim(bins, slab_index * NTD, 2 * NTD, 1) + crop_offset[:, None]
    back = jnp.where(jnp.arange(2 * NTD, dtype=jnp.int32) < NTD, slab_rows, 0)
    asked = asked - back[None, :]
    picked = jnp.einsum(
        "sjr,srd->sjd",
        one_hot(asked, slab_rows),
        block_out,
        preferred_element_type=jnp.float32,
    ).astype(jnp.bfloat16)
    from_next = passed_along(picked[:, :NTD], "seq", -1)
    target_rows = picked[:, NTD:] + from_next
    prev_cot = passed_along(cotangent, "seq", 1)
    cot_pair = jnp.concatenate([prev_cot, cotangent], axis=1)

    def crop_back(cot_block, shift_by):
        return lax.dynamic_slice_in_dim(cot_block, slab_rows - shift_by, slab_rows, 0)

    grad_out = jax.vmap(crop_back)(cot_pair, crop_offset)
    flat_grad = grad_out.reshape(local_seqs * slab_rows, channels)
    grad_act = lax.dot_general(
        flat_grad, full_weight, (((1,), (1,)), ((), ())), preferred_element_type=jnp.float32
    )
    grad_conv = (grad_act.reshape(local_seqs, slab_rows, channels) * gelu_slope(filtered)).astype(
        jnp.bfloat16
    )
    grad_padded = with_rims(grad_conv)
    grad_sum = (
        grad_out.astype(jnp.float32)
        + depth_filter[0] * grad_padded[:, 2:]
        + depth_filter[1] * grad_padded[:, 1:-1]
        + depth_filter[2] * grad_padded[:, :-2]
    )
    skip_grad = grad_sum.astype(jnp.bfloat16)
    attention_grad = (
        grad_sum.reshape(local_seqs, slab_rows // 2, 2, channels).sum(axis=2).astype(jnp.bfloat16)
    )
    filter_terms = jnp.stack(
        [
            jnp.einsum(
                "srd,srd->d", grad_conv, padded[:, 0:slab_rows], preferred_element_type=jnp.float32
            ),
            jnp.einsum(
                "srd,srd->d",
                grad_conv,
                padded[:, 1 : slab_rows + 1],
                preferred_element_type=jnp.float32,
            ),
            jnp.einsum(
                "srd,srd->d",
                grad_conv,
                padded[:, 2 : slab_rows + 2],
                preferred_element_type=jnp.float32,
            ),
        ]
    )
    filter_sum = butterfly(butterfly(filter_terms, "seq"), "head")
    row_count = local_seqs * lax.axis_size("head") * slab_rows * lax.axis_size("seq")
    filter_grad = filter_sum * (1.0 / math.sqrt(row_count))
    return (target_rows, attention_grad, skip_grad, filter_grad)


def solution(mesh):
    in_specs = (
        P(None, "seq", "head"),
        P("head", "seq", None),
        P(),
        P("head", None),
        P("head"),
        P("head", None),
        P("head", "seq", None),
    )
    out_specs = (P("head", "seq", None), P("head", "seq", None), P("head", "seq", None), P())
    return jax.shard_map(shards, mesh=mesh, in_specs=in_specs, out_specs=out_specs, check_vma=False)
```

```python
import functools
import math

import jax
import jax.numpy as jnp
from jax import lax
from jax.experimental import pallas as pl
from jax.experimental.pallas import tpu as pltpu
from jax.sharding import PartitionSpec as P

NTD = 2


def extended(shard, sides, width):
    for axis, dim in sides:
        count, length = (lax.axis_size(axis), shard.shape[dim])
        up = [(i, (i + 1) % count) for i in range(count - 1)]
        down = [(j, i) for i, j in up]
        last = lax.slice_in_dim(shard, length - width, length, axis=dim)
        initial = lax.slice_in_dim(shard, 0, width, axis=dim)
        before = lax.ppermute(last, axis, up)
        after = lax.ppermute(initial, axis, down)
        shard = jnp.concatenate([before, shard, after], axis=dim)
    return shard


def passed_along(shard, axis, by):
    count = lax.axis_size(axis)
    pairs = [(i, i + by) for i in range(count) if 0 <= i + by < count]
    return lax.ppermute(shard, axis, pairs)


def gelu_slope(values):
    return (
        0.5 * (1.0 + lax.erf(values * 0.7071067811865476))
        + values * jnp.exp(-0.5 * values * values) * 0.3989422804014327
    )


def with_rims(field):
    return extended(field, (("seq", 1),), 1)


def one_hot(places, length):
    return (places[:, :, None] == jnp.arange(length, dtype=jnp.int32)[None, None, :]).astype(
        jnp.bfloat16
    )


def core_swap(part):
    count = lax.axis_size("seq")
    return lax.ppermute(part, "seq", [(i, i ^ 1) for i in range(count)])


def gathered_weight(rows):
    heads = lax.axis_size("head")
    here = lax.axis_index("head")
    core = lax.axis_index("seq") % 2
    half = rows.shape[0] // 2
    mine = lax.dynamic_slice_in_dim(rows, core * half, half, 0)
    blocks = [(0, rows)]
    for step in range(1, heads):
        pairs = [(i, (i + step) % heads) for i in range(heads)]
        got = lax.ppermute(mine, "head", pairs)
        twin = core_swap(got)
        low = jnp.where(core == 0, got, twin)
        high = jnp.where(core == 0, twin, got)
        blocks.append((step, jnp.concatenate([low, high], axis=0)))
    full = jnp.zeros((heads * rows.shape[0], rows.shape[1]), rows.dtype)
    for step, block in blocks:
        place = (here - step) % heads
        full = lax.dynamic_update_slice_in_dim(full, block, place * rows.shape[0], 0)
    return full


def butterfly(total, axis):
    count = lax.axis_size(axis)
    if count & (count - 1):
        return lax.psum(total, axis)
    step = 1
    while step < count:
        total = total + lax.ppermute(total, axis, [(i, i ^ step) for i in range(count)])
        step *= 2
    return total


def plain_shards(
    attention, encoder_skip, depth_filter, point_weight, crop_offset, target_bins, cotangent
):
    slab_input = lax.all_to_all(attention, "head", split_axis=0, concat_axis=2, tiled=True)
    local_seqs = encoder_skip.shape[0]
    slab_rows = encoder_skip.shape[1]
    channels = encoder_skip.shape[2]
    summed = (
        jnp.repeat(slab_input, 2, axis=1).astype(jnp.float32) + encoder_skip.astype(jnp.float32)
    ).astype(jnp.bfloat16)
    padded = with_rims(summed)
    filtered = (
        depth_filter[0] * padded[:, :-2]
        + depth_filter[1] * padded[:, 1:-1]
        + depth_filter[2] * padded[:, 2:]
    )
    activated = jax.nn.gelu(filtered, approximate=False).astype(jnp.bfloat16)
    flat_act = activated.reshape(local_seqs * slab_rows, channels)
    full_weight = gathered_weight(point_weight)
    mixed_rows = jnp.dot(flat_act, full_weight, preferred_element_type=jnp.float32)
    block_out = (
        summed.astype(jnp.float32) + mixed_rows.reshape(local_seqs, slab_rows, channels)
    ).astype(jnp.bfloat16)
    slab_index = lax.axis_index("seq")
    bins = jnp.concatenate(
        [jnp.zeros_like(target_bins[:, :NTD]), target_bins], axis=1
    )
    asked = lax.dynamic_slice_in_dim(bins, slab_index * NTD, 2 * NTD, 1) + crop_offset[:, None]
    back = jnp.where(jnp.arange(2 * NTD, dtype=jnp.int32) < NTD, slab_rows, 0)
    asked = asked - back[None, :]
    picked = jnp.einsum(
        "sjr,srd->sjd",
        one_hot(asked, slab_rows),
        block_out,
        preferred_element_type=jnp.float32,
    ).astype(jnp.bfloat16)
    from_next = passed_along(picked[:, :NTD], "seq", -1)
    target_rows = picked[:, NTD:] + from_next
    prev_cot = passed_along(cotangent, "seq", 1)
    cot_pair = jnp.concatenate([prev_cot, cotangent], axis=1)

    def crop_back(cot_block, shift_by):
        return lax.dynamic_slice_in_dim(cot_block, slab_rows - shift_by, slab_rows, 0)

    grad_out = jax.vmap(crop_back)(cot_pair, crop_offset)
    flat_grad = grad_out.reshape(local_seqs * slab_rows, channels)
    grad_act = lax.dot_general(
        flat_grad, full_weight, (((1,), (1,)), ((), ())), preferred_element_type=jnp.float32
    )
    grad_conv = (grad_act.reshape(local_seqs, slab_rows, channels) * gelu_slope(filtered)).astype(
        jnp.bfloat16
    )
    grad_padded = with_rims(grad_conv)
    grad_sum = (
        grad_out.astype(jnp.float32)
        + depth_filter[0] * grad_padded[:, 2:]
        + depth_filter[1] * grad_padded[:, 1:-1]
        + depth_filter[2] * grad_padded[:, :-2]
    )
    skip_grad = grad_sum.astype(jnp.bfloat16)
    attention_grad = (
        grad_sum.reshape(local_seqs, slab_rows // 2, 2, channels).sum(axis=2).astype(jnp.bfloat16)
    )
    filter_terms = jnp.stack(
        [
            jnp.einsum(
                "srd,srd->d", grad_conv, padded[:, 0:slab_rows], preferred_element_type=jnp.float32
            ),
            jnp.einsum(
                "srd,srd->d",
                grad_conv,
                padded[:, 1 : slab_rows + 1],
                preferred_element_type=jnp.float32,
            ),
            jnp.einsum(
                "srd,srd->d",
                grad_conv,
                padded[:, 2 : slab_rows + 2],
                preferred_element_type=jnp.float32,
            ),
        ]
    )
    filter_sum = butterfly(butterfly(filter_terms, "seq"), "head")
    row_count = local_seqs * lax.axis_size("head") * slab_rows * lax.axis_size("seq")
    filter_grad = filter_sum * (1.0 / math.sqrt(row_count))
    return (target_rows, attention_grad, skip_grad, filter_grad)


LANES = 128
PAD = 8
BF = jnp.bfloat16
F32 = jnp.float32


def dot(left, right):
    return lax.dot_general(left, right, (((1,), (0,)), ((), ())), preferred_element_type=F32)


def dot_rows(left, right):
    return lax.dot_general(left, right, (((1,), (1,)), ((), ())), preferred_element_type=F32)


def grid_of(rows, columns):
    return (
        lax.broadcasted_iota(jnp.int32, (rows, columns), 0),
        lax.broadcasted_iota(jnp.int32, (rows, columns), 1),
    )


def picks(match):
    return jnp.where(match, 1.0, 0.0).astype(BF)


def params():
    return pltpu.CompilerParams(vmem_limit_bytes=40 * 1024 * 1024)


def cost(flops, moved, special=0):
    return pl.CostEstimate(flops=flops, bytes_accessed=moved, transcendentals=special)


def pack_kernel(skip_lo, skip_hi, att_lo, att_hi, cot_lo, cot_hi, up, down, far):
    half = att_lo.shape[2]
    row, col = grid_of(16, 32)
    at, base = row & 7, (row >> 3) * 16
    skips = skip_hi[...].reshape(32, 2 * half)
    out = dot(picks((at >= 6) & (col == base + at + 8)), skips)
    edge = picks((at == 5) & (col == base + 15))
    for group in range(2):
        rows = att_hi[2 * group : 2 * group + 2].reshape(32, half)
        cols = slice(group * half, (group + 1) * half)
        up[:, cols] = (out[:, cols] + dot(edge, rows)).astype(BF)
    skips = skip_lo[...].reshape(32, 2 * half)
    cots = cot_lo[...].reshape(32, 2 * half)
    out = dot(picks((at < 2) & (col == base + at)), skips) + dot(
        picks((at == 3) & (col == base)), cots
    )
    edge = picks((at == 2) & (col == base))
    for group in range(2):
        rows = att_lo[2 * group : 2 * group + 2].reshape(32, half)
        cols = slice(group * half, (group + 1) * half)
        down[:, cols] = (out[:, cols] + dot(edge, rows)).astype(BF)
    cots = cot_hi[...].reshape(32, 2 * half)
    far[...] = dot(picks((at == 7) & (col == base + 15)), cots).astype(BF)


def packed(encoder_skip, attention, cotangent):
    seqs, rows, wide = encoder_skip.shape
    half = attention.shape[2]
    short = attention.shape[1]

    def block(count, width, place):
        return pl.BlockSpec((count, 16, width), lambda i: (0, place, 0))

    out = jax.ShapeDtypeStruct((16, wide), BF)
    return pl.pallas_call(
        pack_kernel,
        grid=(1,),
        in_specs=[
            block(seqs, wide, 0),
            block(seqs, wide, rows // 16 - 1),
            block(2 * seqs, half, 0),
            block(2 * seqs, half, short // 16 - 1),
            block(seqs, wide, 0),
            block(seqs, wide, rows // 16 - 1),
        ],
        out_specs=[pl.BlockSpec((16, wide), lambda i: (0, 0))] * 3,
        out_shape=[out, out, out],
        compiler_params=params(),
        name="pack_edges",
    )(encoder_skip, encoder_skip, attention, attention, cotangent, cotangent)


def ship_kernel(meta, att, up, down, out):
    short = att.shape[1]
    row, col = grid_of(16, 16)
    for s in range(2):
        out[s, 0:short] = att[s]
        edges = dot(picks((row == 0) & (col == s * 8 + 5)), up[...]) + dot(
            picks((row == 1) & (col == s * 8 + 2)), down[...]
        )
        out[s, short : short + 16] = edges.astype(BF)


def shipment(meta, attention, up, down):
    _, short, half = attention.shape
    return pl.pallas_call(
        ship_kernel,
        grid_spec=pltpu.PrefetchScalarGridSpec(
            num_scalar_prefetch=1,
            grid=(1,),
            in_specs=[
                pl.BlockSpec((2, short, half), lambda i, m: (1 - m[0], 0, 0)),
                pl.BlockSpec((16, half), lambda i, m: (0, 1 - m[0])),
                pl.BlockSpec((16, half), lambda i, m: (0, 1 - m[0])),
            ],
            out_specs=pl.BlockSpec((2, short + 16, half), lambda i, m: (0, 0, 0)),
        ),
        out_shape=jax.ShapeDtypeStruct((2, short + 16, half), BF),
        compiler_params=params(),
        name="pack_attention",
    )(meta, attention, up, down)


def slab_sums(att, skip, up, down, ext, cols, from_ship):
    width = cols.size
    short = 64
    row, col = grid_of(2 * short, short)
    spread = picks((row >> 1) == col)
    row, col = grid_of(16, 32 if from_ship else 16)
    at = row & 7
    high, low = up[:, cols], down[:, cols]
    if from_ship:
        edges = jnp.concatenate([att[0, short : short + 16, cols], att[1, short : short + 16, cols]])
        base = (row >> 3) * 16
        above = dot(picks((at >= 6) & (col == base)), edges)
        below = dot(picks((at < 2) & (col == base + 1)), edges)
    else:
        base = row & 8
        above = dot(picks((at >= 6) & (col == base + 5)), high)
        below = dot(picks((at < 2) & (col == base + 2)), low)
    at = lax.broadcasted_iota(jnp.int32, (16, width), 0) & 7
    above = jnp.where(at >= 6, above + high.astype(F32), 0.0).astype(BF).astype(F32)
    below = jnp.where(at < 2, below + low.astype(F32), 0.0).astype(BF).astype(F32)
    for s in range(2):
        body = dot(spread, att[s, 0:short, cols]) + skip[s, :, cols].astype(F32)
        ext[s, 0:PAD] = above[s * 8 : s * 8 + 8]
        ext[s, PAD : PAD + 2 * short] = body.astype(BF).astype(F32)
        ext[s, PAD + 2 * short : 2 * PAD + 2 * short] = below[s * 8 : s * 8 + 8]


def around(field):
    tall = field.shape[0]
    return pltpu.roll(field, 1, 0), pltpu.roll(field, tall - 1, 0)


def phi_of(values):
    return 0.5 * (1.0 + lax.erf(values * 0.7071067811865476))


def slope_of(values):
    return phi_of(values) + values * jnp.exp(-0.5 * values * values) * 0.3989422804014327


def asked_rows(meta, offsets, bins, s, ext, taps, tall):
    row, col = grid_of(16, tall)
    want = row & 3
    at = jnp.full((16, tall), -4096, jnp.int32)
    slab = meta[1]
    for k in range(4):
        mine = k < NTD
        home = slab if mine else jnp.maximum(slab - 1, 0)
        place = bins[s, home * NTD + (k % NTD)] + offsets[s] - (0 if mine else tall - 2 * PAD)
        fits = (place >= 0) & (place < tall - 2 * PAD)
        at = jnp.where((want == k) & (row < 8), jnp.where(fits, place + PAD, -4096), at)
    source = ext.astype(BF)
    before = dot(picks(col == at - 1), source)
    here = dot(picks(col == at), source)
    after = dot(picks(col == at + 1), source)
    value = taps[0] * before + taps[1] * here + taps[2] * after
    act = value * phi_of(value)
    row = lax.broadcasted_iota(jnp.int32, act.shape, 0)
    return jnp.where(row < 4, act, here).astype(BF)


def taps_of(filt, cols):
    return [filt[k : k + 1, cols] for k in range(3)]


def tap_sums(conv, ext, rows):
    before, after = around(ext)
    body = slice(PAD, PAD + rows)
    mine = conv[body]
    return [
        jnp.sum(mine * other[body], axis=0, keepdims=True) for other in (before, ext, after)
    ]


def grads(conv, direct, taps, rows, pair):
    before, after = around(conv)
    body = slice(PAD, PAD + rows)
    total = direct + taps[0] * after[body] + taps[1] * conv[body] + taps[2] * before[body]
    short = rows // 2
    sums = []
    for k in range(total.shape[1] // LANES):
        pair[k] = total[:, k * LANES : (k + 1) * LANES]
        sums.append(pair[k, pl.ds(0, short, 2), :] + pair[k, pl.ds(1, short, 2), :])
    return total, jnp.concatenate(sums, axis=1)


def own_kernel(
    slabs, meta, offsets, bins, att, skip, up, down, down_all, far, prev, cot, weight, filt,
    moved, asked, terms, skip_grad, att_grad, ext, pair,
):
    rows = skip.shape[1]
    tall = rows + 2 * PAD
    wide = cot.shape[2]
    row, col = grid_of(tall, rows)
    last = meta[1] == slabs - 1
    for s in range(2):
        at = row - PAD
        fits = (at >= -1) & (at < jnp.where(last, rows, rows + 1))
        source = jnp.where(fits, at - offsets[s], -4096)
        older = picks(col == source + rows)
        newer = picks(col == source)
        source, narrow = source[:, :16], col[:, :16]
        below = picks((source == rows) & (narrow == s * 8 + 3))
        above = picks((source == -rows - 1) & (narrow == s * 8 + 7))
        for part in range(0, wide, 512):
            cols = slice(part, part + 512)
            moved[s, :, cols] = (
                dot(older, prev[s, :, cols])
                + dot(newer, cot[s, :, cols])
                + dot(below, down_all[:, cols])
                + dot(above, far[:, cols])
            ).astype(BF)
    width = ext.shape[2]
    half = skip.shape[2]
    first = meta[0] * half

    @pl.loop(0, half // width)
    def _(part):
        begin = pl.multiple_of(part * width, width)
        cols = pl.ds(begin, width)
        slab_sums(att, skip, up, down, ext, cols, False)
        taps = taps_of(filt, cols)
        piece = weight[pl.ds(begin, width), :]
        sums = [0.0, 0.0, 0.0]
        there = pl.ds(pl.multiple_of(first + begin, width), width)
        for s in range(2):
            field = ext[s]
            before, after = around(field)
            slope = slope_of(taps[0] * before + taps[1] * field + taps[2] * after)
            asked[s * 16 : s * 16 + 16, cols] = asked_rows(
                meta, offsets, bins, s, field, taps, tall
            )
            conv = (dot_rows(moved[s], piece) * slope).astype(BF).astype(F32)
            sums = [a + b for a, b in zip(sums, tap_sums(conv, field, rows))]
            direct = moved[s, :, there].astype(F32)[PAD : PAD + rows]
            total, pairs = grads(conv, direct, taps, rows, pair)
            skip_grad[s, :, cols] = total.astype(BF)
            att_grad[s, :, cols] = pairs.astype(BF)
        for k in range(3):
            terms[k : k + 1, cols] = sums[k]


def own_half(meta, offsets, bins, attention, skip, up, down, far, prev, cot, weight, filt, slabs):
    seqs, rows, wide = skip.shape
    _, short, half = attention.shape
    tall = rows + 2 * PAD

    def whole(*shape):
        return pl.BlockSpec(shape, lambda i, m, o, b: (0,) * len(shape))

    def mine(*shape):
        return pl.BlockSpec(shape, lambda i, m, o, b: (0,) * (len(shape) - 1) + (m[0],))

    return pl.pallas_call(
        functools.partial(own_kernel, slabs),
        grid_spec=pltpu.PrefetchScalarGridSpec(
            num_scalar_prefetch=3,
            grid=(1,),
            in_specs=[
                pl.BlockSpec((2, short, half), lambda i, m, o, b: (m[0], 0, 0)),
                mine(2, rows, half),
                mine(16, half),
                mine(16, half),
                whole(16, wide),
                whole(16, wide),
                whole(2, rows, wide),
                whole(2, rows, wide),
                whole(half, wide),
                mine(3, half),
            ],
            out_specs=[
                whole(2, tall, wide),
                whole(32, half),
                whole(3, half),
                mine(2, rows, half),
                mine(2, short, half),
            ],
            scratch_shapes=[pltpu.VMEM((2, tall, 256), F32), pltpu.VMEM((2, rows, LANES), F32)],
        ),
        out_shape=[
            jax.ShapeDtypeStruct((2, tall, wide), BF),
            jax.ShapeDtypeStruct((32, half), BF),
            jax.ShapeDtypeStruct((3, half), F32),
            jax.ShapeDtypeStruct((2, rows, wide), BF),
            jax.ShapeDtypeStruct((2, short, wide), BF),
        ],
        compiler_params=params(),
        cost_estimate=cost(2 * 2 * tall * half * wide, 8 * 1024 * 1024, 2 * tall * half),
        name="own_half",
    )(meta, offsets, bins, attention, skip, up, down, down, far, prev, cot, weight, filt)


def slope_kernel(
    meta, offsets, bins, att, skip, up, down, filt, asked, sums, slopes, mine, shown, ext
):
    rows = skip.shape[1]
    tall = rows + 2 * PAD
    half = skip.shape[2]
    width = ext.shape[2]
    there = (1 - meta[0]) * half
    row, col = grid_of(16, 32)
    at, base = row & 7, (row >> 3) * 16
    kept = picks((at < 4) & (col == base + at + jnp.where(at < 2, 0, 2)))
    told = picks((at < 4) & (col == base + at + jnp.where(at < 2, 2, 4)))
    here = pl.ds(pl.multiple_of(meta[0] * half, half), half)
    mine[:, here] = dot(kept, asked[...]).astype(BF)
    shown[:, here] = dot(told, asked[...]).astype(BF)

    @pl.loop(0, half // width)
    def _(part):
        begin = pl.multiple_of(part * width, width)
        cols = pl.ds(begin, width)
        slab_sums(att, skip, up, down, ext, cols, True)
        taps = taps_of(filt, cols)
        got = []
        for s in range(2):
            field = ext[s]
            before, after = around(field)
            slopes[s, :, cols] = slope_of(taps[0] * before + taps[1] * field + taps[2] * after)
            sums[s, :, cols] = field.astype(BF)
            got.append(asked_rows(meta, offsets, bins, s, field, taps, tall))
        got = jnp.concatenate(got)
        place = pl.ds(pl.multiple_of(there + begin, width), width)
        mine[:, place] = dot(kept, got).astype(BF)
        shown[:, place] = dot(told, got).astype(BF)


def other_slopes(meta, offsets, bins, shipped, skip, up, down, filt, asked):
    seqs, rows, wide = skip.shape
    _, packed_rows, half = shipped.shape
    tall = rows + 2 * PAD

    def whole(*shape):
        return pl.BlockSpec(shape, lambda i, m, o, b: (0,) * len(shape))

    def other(*shape):
        return pl.BlockSpec(shape, lambda i, m, o, b: (0,) * (len(shape) - 1) + (1 - m[0],))

    return pl.pallas_call(
        slope_kernel,
        grid_spec=pltpu.PrefetchScalarGridSpec(
            num_scalar_prefetch=3,
            grid=(1,),
            in_specs=[
                whole(2, packed_rows, half),
                other(2, rows, half),
                other(16, half),
                other(16, half),
                other(3, half),
                whole(32, half),
            ],
            out_specs=[whole(2, tall, half), whole(2, tall, half), whole(16, wide), whole(16, wide)],
            scratch_shapes=[pltpu.VMEM((2, tall, 256), F32)],
        ),
        out_shape=[
            jax.ShapeDtypeStruct((2, tall, half), BF),
            jax.ShapeDtypeStruct((2, tall, half), F32),
            jax.ShapeDtypeStruct((16, wide), BF),
            jax.ShapeDtypeStruct((16, wide), BF),
        ],
        compiler_params=params(),
        cost_estimate=cost(2 * 2 * tall * half * 64, 4 * 1024 * 1024, 2 * tall * half),
        name="other_slopes",
    )(meta, offsets, bins, shipped, skip, up, down, filt, asked)


def terms_kernel(meta, order, moved, sums, slopes, own_terms, *refs):
    pieces, (convs, terms) = refs[:6], refs[6:]
    half = sums.shape[2]
    tall = sums.shape[1]
    rows = tall - 2 * PAD
    there = (1 - meta[0]) * half
    terms[:, pl.ds(pl.multiple_of(meta[0] * half, half), half)] = own_terms[...]
    for k, piece in enumerate(pieces):
        begin = pl.multiple_of(order[k] * LANES, LANES)
        cols = pl.ds(begin, LANES)
        total = [0.0, 0.0, 0.0]
        for s in range(2):
            grad = dot_rows(moved[s], piece[...])
            conv = (grad * slopes[s, :, cols]).astype(BF)
            convs[s, :, cols] = conv
            got = tap_sums(conv.astype(F32), sums[s, :, cols].astype(F32), rows)
            total = [a + b for a, b in zip(total, got)]
        place = pl.ds(pl.multiple_of(there + begin, LANES), LANES)
        for k in range(3):
            terms[k : k + 1, place] = total[k]


def other_terms(meta, order, moved, sums, slopes, own_terms, pieces):
    _, tall, wide = moved.shape
    half = sums.shape[2]

    def whole(*shape):
        return pl.BlockSpec(shape, lambda i, m, o: (0,) * len(shape))

    return pl.pallas_call(
        terms_kernel,
        grid_spec=pltpu.PrefetchScalarGridSpec(
            num_scalar_prefetch=2,
            grid=(1,),
            in_specs=[
                whole(2, tall, wide),
                whole(2, tall, half),
                whole(2, tall, half),
                whole(3, half),
            ]
            + [whole(LANES, wide)] * 6,
            out_specs=[whole(2, tall, half), whole(3, wide)],
        ),
        out_shape=[
            jax.ShapeDtypeStruct((2, tall, half), BF),
            jax.ShapeDtypeStruct((3, wide), F32),
        ],
        compiler_params=params(),
        cost_estimate=cost(2 * 2 * tall * half * wide, 6 * 1024 * 1024),
        name="other_terms",
    )(meta, order, moved, sums, slopes, own_terms, *pieces)


def out_kernel(meta, order, moved, convs, filt, mine, got, weight, *refs):
    pieces = refs[:6]
    target, skip_grad, att_grad, pair = refs[8:]
    half = convs.shape[2]
    tall = convs.shape[1]
    rows = tall - 2 * PAD
    there = (1 - meta[0]) * half
    width = 2 * LANES

    @pl.loop(0, half // width)
    def _(part):
        begin = pl.multiple_of(part * width, width)
        cols = pl.ds(begin, width)
        taps = taps_of(filt, cols)
        place = pl.ds(pl.multiple_of(there + begin, width), width)
        for s in range(2):
            direct = moved[s, :, place].astype(F32)[PAD : PAD + rows]
            total, pairs = grads(convs[s, :, cols].astype(F32), direct, taps, rows, pair)
            skip_grad[s, :, cols] = total.astype(BF)
            att_grad[s, :, cols] = pairs.astype(BF)

    mine[...] = mine[...] + got[...]
    here = pl.ds(pl.multiple_of(meta[0] * half, half), half)
    mixed = dot(mine[:, here], weight[...])
    for k, piece in enumerate(pieces):
        place = pl.ds(pl.multiple_of(there + order[k] * LANES, LANES), LANES)
        mixed = mixed + dot(mine[:, place], piece[...])
    value = mixed + pltpu.roll(mine[...].astype(F32), 14, 0)
    for s in range(2):
        target[s] = value[s * 8 : s * 8 + 2].astype(BF)


def outputs(meta, order, moved, convs, filt, mine, got, weight, pieces, skip_grad, att_grad):
    _, tall, wide = moved.shape
    half = convs.shape[2]
    rows = tall - 2 * PAD

    def whole(*shape):
        return pl.BlockSpec(shape, lambda i, m, o: (0,) * len(shape))

    def other(*shape):
        return pl.BlockSpec(shape, lambda i, m, o: (0,) * (len(shape) - 1) + (1 - m[0],))

    return pl.pallas_call(
        out_kernel,
        grid_spec=pltpu.PrefetchScalarGridSpec(
            num_scalar_prefetch=2,
            grid=(1,),
            in_specs=[
                whole(2, tall, wide),
                whole(2, tall, half),
                other(3, half),
                whole(16, wide),
                whole(16, wide),
                whole(half, wide),
            ]
            + [whole(LANES, wide)] * 6
            + [pl.BlockSpec(memory_space=pl.ANY)] * 2,
            out_specs=[
                whole(2, NTD, wide),
                other(2, rows, half),
                other(2, rows // 2, half),
            ],
            scratch_shapes=[pltpu.VMEM((2, rows, LANES), F32)],
        ),
        out_shape=[
            jax.ShapeDtypeStruct((2, NTD, wide), BF),
            jax.ShapeDtypeStruct((2, rows, wide), BF),
            jax.ShapeDtypeStruct((2, rows // 2, wide), BF),
        ],
        input_output_aliases={14: 1, 15: 2},
        compiler_params=params(),
        cost_estimate=cost(2 * 16 * wide * wide, 8 * 1024 * 1024),
        name="outputs",
    )(meta, order, moved, convs, filt, mine, got, weight, *pieces, skip_grad, att_grad)


def paired(part, axis, bit):
    count = lax.axis_size(axis)
    return lax.ppermute(part, axis, [(i, i ^ bit) for i in range(count)])


def fast_shards(
    attention, encoder_skip, depth_filter, point_weight, crop_offset, target_bins, cotangent
):
    head = lax.axis_index("head")
    slab = lax.axis_index("seq")
    slabs = lax.axis_size("seq")
    meta = jnp.stack([head, slab]).astype(jnp.int32)
    quarter = slab % 4
    core = slab % 2
    first = lax.dynamic_slice_in_dim(point_weight, quarter * LANES, LANES, 0)
    first = paired(first, "head", 1)
    up, down, far = packed(encoder_skip, attention, cotangent)
    prev = passed_along(cotangent, "seq", 1)
    up = passed_along(up, "seq", 1)
    down = passed_along(down, "seq", -1)
    far = passed_along(far, "seq", 2)
    shipped = paired(shipment(meta, attention, up, down), "head", 1)
    common = lax.dynamic_slice_in_dim(point_weight, (4 + core) * LANES, LANES, 0)
    common = paired(common, "head", 1)
    crossed = paired(first, "seq", 2)
    pieces = [
        first,
        paired(first, "seq", 1),
        crossed,
        paired(crossed, "seq", 1),
        common,
        paired(common, "seq", 1),
    ]
    order = jnp.stack(
        [quarter, quarter ^ 1, quarter ^ 2, quarter ^ 3, 4 + core, 5 - core]
    ).astype(jnp.int32)
    moved, asked, own_terms, skip_grad, att_grad = own_half(
        meta, crop_offset, target_bins, attention, encoder_skip, up, down, far, prev, cotangent,
        point_weight, depth_filter, slabs,
    )
    sums, slopes, mine, shown = other_slopes(
        meta, crop_offset, target_bins, shipped, encoder_skip, up, down, depth_filter, asked
    )
    got = passed_along(shown, "seq", -1)
    convs, terms = other_terms(meta, order, moved, sums, slopes, own_terms, pieces)
    target_rows, skip_grad, attention_grad = outputs(
        meta, order, moved, convs, depth_filter, mine, got, point_weight, pieces, skip_grad,
        att_grad,
    )
    total = butterfly(butterfly(terms, "seq"), "head")
    count = encoder_skip.shape[0] * lax.axis_size("head") * encoder_skip.shape[1] * slabs
    return (target_rows, attention_grad, skip_grad, total * (1.0 / math.sqrt(count)))


def shards(*args):
    attention, encoder_skip, point_weight = args[0], args[1], args[3]
    fits = (
        lax.axis_size("head") == 2
        and lax.axis_size("seq") % 4 == 0
        and encoder_skip.shape[:2] == (2, 128)
        and point_weight.shape[0] == 6 * LANES
        and attention.shape[1] == 64
    )
    return fast_shards(*args) if fits else plain_shards(*args)


def solution(mesh):
    in_specs = (
        P(None, "seq", "head"),
        P("head", "seq", None),
        P(),
        P("head", None),
        P("head"),
        P("head", None),
        P("head", "seq", None),
    )
    out_specs = (P("head", "seq", None), P("head", "seq", None), P("head", "seq", None), P())
    return jax.shard_map(shards, mesh=mesh, in_specs=in_specs, out_specs=out_specs, check_vma=False)
```

```python
import functools
import math

import jax
import jax.numpy as jnp
from jax import lax
from jax.experimental import pallas as pl
from jax.experimental.pallas import tpu as pltpu
from jax.sharding import PartitionSpec as P

NTD = 2


def extended(shard, sides, width):
    for axis, dim in sides:
        count, length = (lax.axis_size(axis), shard.shape[dim])
        up = [(i, (i + 1) % count) for i in range(count - 1)]
        down = [(j, i) for i, j in up]
        last = lax.slice_in_dim(shard, length - width, length, axis=dim)
        initial = lax.slice_in_dim(shard, 0, width, axis=dim)
        before = lax.ppermute(last, axis, up)
        after = lax.ppermute(initial, axis, down)
        shard = jnp.concatenate([before, shard, after], axis=dim)
    return shard


def passed_along(shard, axis, by):
    count = lax.axis_size(axis)
    pairs = [(i, i + by) for i in range(count) if 0 <= i + by < count]
    return lax.ppermute(shard, axis, pairs)


def gelu_slope(values):
    return (
        0.5 * (1.0 + lax.erf(values * 0.7071067811865476))
        + values * jnp.exp(-0.5 * values * values) * 0.3989422804014327
    )


def with_rims(field):
    return extended(field, (("seq", 1),), 1)


def one_hot(places, length):
    return (places[:, :, None] == jnp.arange(length, dtype=jnp.int32)[None, None, :]).astype(
        jnp.bfloat16
    )


def core_swap(part):
    count = lax.axis_size("seq")
    return lax.ppermute(part, "seq", [(i, i ^ 1) for i in range(count)])


def gathered_weight(rows):
    heads = lax.axis_size("head")
    here = lax.axis_index("head")
    core = lax.axis_index("seq") % 2
    half = rows.shape[0] // 2
    mine = lax.dynamic_slice_in_dim(rows, core * half, half, 0)
    blocks = [(0, rows)]
    for step in range(1, heads):
        pairs = [(i, (i + step) % heads) for i in range(heads)]
        got = lax.ppermute(mine, "head", pairs)
        twin = core_swap(got)
        low = jnp.where(core == 0, got, twin)
        high = jnp.where(core == 0, twin, got)
        blocks.append((step, jnp.concatenate([low, high], axis=0)))
    full = jnp.zeros((heads * rows.shape[0], rows.shape[1]), rows.dtype)
    for step, block in blocks:
        place = (here - step) % heads
        full = lax.dynamic_update_slice_in_dim(full, block, place * rows.shape[0], 0)
    return full


def butterfly(total, axis):
    count = lax.axis_size(axis)
    if count & (count - 1):
        return lax.psum(total, axis)
    step = 1
    while step < count:
        total = total + lax.ppermute(total, axis, [(i, i ^ step) for i in range(count)])
        step *= 2
    return total


def plain_shards(
    attention, encoder_skip, depth_filter, point_weight, crop_offset, target_bins, cotangent
):
    slab_input = lax.all_to_all(attention, "head", split_axis=0, concat_axis=2, tiled=True)
    local_seqs = encoder_skip.shape[0]
    slab_rows = encoder_skip.shape[1]
    channels = encoder_skip.shape[2]
    summed = (
        jnp.repeat(slab_input, 2, axis=1).astype(jnp.float32) + encoder_skip.astype(jnp.float32)
    ).astype(jnp.bfloat16)
    padded = with_rims(summed)
    filtered = (
        depth_filter[0] * padded[:, :-2]
        + depth_filter[1] * padded[:, 1:-1]
        + depth_filter[2] * padded[:, 2:]
    )
    activated = jax.nn.gelu(filtered, approximate=False).astype(jnp.bfloat16)
    flat_act = activated.reshape(local_seqs * slab_rows, channels)
    full_weight = gathered_weight(point_weight)
    mixed_rows = jnp.dot(flat_act, full_weight, preferred_element_type=jnp.float32)
    block_out = (
        summed.astype(jnp.float32) + mixed_rows.reshape(local_seqs, slab_rows, channels)
    ).astype(jnp.bfloat16)
    slab_index = lax.axis_index("seq")
    bins = jnp.concatenate(
        [jnp.zeros_like(target_bins[:, :NTD]), target_bins], axis=1
    )
    asked = lax.dynamic_slice_in_dim(bins, slab_index * NTD, 2 * NTD, 1) + crop_offset[:, None]
    back = jnp.where(jnp.arange(2 * NTD, dtype=jnp.int32) < NTD, slab_rows, 0)
    asked = asked - back[None, :]
    picked = jnp.einsum(
        "sjr,srd->sjd",
        one_hot(asked, slab_rows),
        block_out,
        preferred_element_type=jnp.float32,
    ).astype(jnp.bfloat16)
    from_next = passed_along(picked[:, :NTD], "seq", -1)
    target_rows = picked[:, NTD:] + from_next
    prev_cot = passed_along(cotangent, "seq", 1)
    cot_pair = jnp.concatenate([prev_cot, cotangent], axis=1)

    def crop_back(cot_block, shift_by):
        return lax.dynamic_slice_in_dim(cot_block, slab_rows - shift_by, slab_rows, 0)

    grad_out = jax.vmap(crop_back)(cot_pair, crop_offset)
    flat_grad = grad_out.reshape(local_seqs * slab_rows, channels)
    grad_act = lax.dot_general(
        flat_grad, full_weight, (((1,), (1,)), ((), ())), preferred_element_type=jnp.float32
    )
    grad_conv = (grad_act.reshape(local_seqs, slab_rows, channels) * gelu_slope(filtered)).astype(
        jnp.bfloat16
    )
    grad_padded = with_rims(grad_conv)
    grad_sum = (
        grad_out.astype(jnp.float32)
        + depth_filter[0] * grad_padded[:, 2:]
        + depth_filter[1] * grad_padded[:, 1:-1]
        + depth_filter[2] * grad_padded[:, :-2]
    )
    skip_grad = grad_sum.astype(jnp.bfloat16)
    attention_grad = (
        grad_sum.reshape(local_seqs, slab_rows // 2, 2, channels).sum(axis=2).astype(jnp.bfloat16)
    )
    filter_terms = jnp.stack(
        [
            jnp.einsum(
                "srd,srd->d", grad_conv, padded[:, 0:slab_rows], preferred_element_type=jnp.float32
            ),
            jnp.einsum(
                "srd,srd->d",
                grad_conv,
                padded[:, 1 : slab_rows + 1],
                preferred_element_type=jnp.float32,
            ),
            jnp.einsum(
                "srd,srd->d",
                grad_conv,
                padded[:, 2 : slab_rows + 2],
                preferred_element_type=jnp.float32,
            ),
        ]
    )
    filter_sum = butterfly(butterfly(filter_terms, "seq"), "head")
    row_count = local_seqs * lax.axis_size("head") * slab_rows * lax.axis_size("seq")
    filter_grad = filter_sum * (1.0 / math.sqrt(row_count))
    return (target_rows, attention_grad, skip_grad, filter_grad)


LANES = 128
PAD = 8
BF = jnp.bfloat16
F32 = jnp.float32


def dot(left, right):
    return lax.dot_general(left, right, (((1,), (0,)), ((), ())), preferred_element_type=F32)


def dot_rows(left, right):
    return lax.dot_general(left, right, (((1,), (1,)), ((), ())), preferred_element_type=F32)


def grid_of(rows, columns):
    return (
        lax.broadcasted_iota(jnp.int32, (rows, columns), 0),
        lax.broadcasted_iota(jnp.int32, (rows, columns), 1),
    )


def picks(match):
    return jnp.where(match, 1.0, 0.0).astype(BF)


def params(mib=36):
    return pltpu.CompilerParams(vmem_limit_bytes=mib * 1024 * 1024)


def cost(flops, moved, special=0):
    return pl.CostEstimate(flops=flops, bytes_accessed=moved, transcendentals=special)


def pack_kernel(skip_lo, skip_hi, att_lo, att_hi, cot_lo, cot_hi, up, down, far):
    half = att_lo.shape[2]
    row, col = grid_of(16, 32)
    at, base = row & 7, (row >> 3) * 16
    skips = skip_hi[...].reshape(32, 2 * half)
    out = dot(picks((at >= 6) & (col == base + at + 8)), skips)
    edge = picks((at == 5) & (col == base + 15))
    for group in range(2):
        rows = att_hi[2 * group : 2 * group + 2].reshape(32, half)
        cols = slice(group * half, (group + 1) * half)
        up[:, cols] = (out[:, cols] + dot(edge, rows)).astype(BF)
    skips = skip_lo[...].reshape(32, 2 * half)
    cots = cot_lo[...].reshape(32, 2 * half)
    out = dot(picks((at < 2) & (col == base + at)), skips) + dot(
        picks((at == 3) & (col == base)), cots
    )
    edge = picks((at == 2) & (col == base))
    for group in range(2):
        rows = att_lo[2 * group : 2 * group + 2].reshape(32, half)
        cols = slice(group * half, (group + 1) * half)
        down[:, cols] = (out[:, cols] + dot(edge, rows)).astype(BF)
    cots = cot_hi[...].reshape(32, 2 * half)
    far[...] = dot(picks((at == 7) & (col == base + 15)), cots).astype(BF)


def packed(encoder_skip, attention, cotangent):
    seqs, rows, wide = encoder_skip.shape
    half = attention.shape[2]
    short = attention.shape[1]

    def block(count, width, place):
        return pl.BlockSpec((count, 16, width), lambda i: (0, place, 0))

    out = jax.ShapeDtypeStruct((16, wide), BF)
    return pl.pallas_call(
        pack_kernel,
        grid=(1,),
        in_specs=[
            block(seqs, wide, 0),
            block(seqs, wide, rows // 16 - 1),
            block(2 * seqs, half, 0),
            block(2 * seqs, half, short // 16 - 1),
            block(seqs, wide, 0),
            block(seqs, wide, rows // 16 - 1),
        ],
        out_specs=[pl.BlockSpec((16, wide), lambda i: (0, 0))] * 3,
        out_shape=[out, out, out],
        compiler_params=params(60),
        name="pack_edges",
    )(encoder_skip, encoder_skip, attention, attention, cotangent, cotangent)


def ship_kernel(meta, att, up, down, out):
    short = att.shape[1]
    row, col = grid_of(16, 16)
    for s in range(2):
        out[s, 0:short] = att[s]
        edges = dot(picks((row == 0) & (col == s * 8 + 5)), up[...]) + dot(
            picks((row == 1) & (col == s * 8 + 2)), down[...]
        )
        out[s, short : short + 16] = edges.astype(BF)


def shipment(meta, attention, up, down):
    _, short, half = attention.shape
    return pl.pallas_call(
        ship_kernel,
        grid_spec=pltpu.PrefetchScalarGridSpec(
            num_scalar_prefetch=1,
            grid=(1,),
            in_specs=[
                pl.BlockSpec((2, short, half), lambda i, m: (1 - m[0], 0, 0)),
                pl.BlockSpec((16, half), lambda i, m: (0, 1 - m[0])),
                pl.BlockSpec((16, half), lambda i, m: (0, 1 - m[0])),
            ],
            out_specs=pl.BlockSpec((2, short + 16, half), lambda i, m: (0, 0, 0)),
        ),
        out_shape=jax.ShapeDtypeStruct((2, short + 16, half), BF),
        compiler_params=params(),
        name="pack_attention",
    )(meta, attention, up, down)


def slab_sums(att, skip, up, down, ext, cols, from_ship):
    width = cols.size
    short = 64
    row, col = grid_of(2 * short, short)
    spread = picks((row >> 1) == col)
    row, col = grid_of(16, 32 if from_ship else 16)
    at = row & 7
    high, low = up[:, cols], down[:, cols]
    if from_ship:
        edges = jnp.concatenate([att[0, short : short + 16, cols], att[1, short : short + 16, cols]])
        base = (row >> 3) * 16
        above = dot(picks((at >= 6) & (col == base)), edges)
        below = dot(picks((at < 2) & (col == base + 1)), edges)
    else:
        base = row & 8
        above = dot(picks((at >= 6) & (col == base + 5)), high)
        below = dot(picks((at < 2) & (col == base + 2)), low)
    at = lax.broadcasted_iota(jnp.int32, (16, width), 0) & 7
    above = jnp.where(at >= 6, above + high.astype(F32), 0.0).astype(BF).astype(F32)
    below = jnp.where(at < 2, below + low.astype(F32), 0.0).astype(BF).astype(F32)
    for s in range(2):
        body = dot(spread, att[s, 0:short, cols]) + skip[s, :, cols].astype(F32)
        ext[s, 0:PAD] = above[s * 8 : s * 8 + 8]
        ext[s, PAD : PAD + 2 * short] = body.astype(BF).astype(F32)
        ext[s, PAD + 2 * short : 2 * PAD + 2 * short] = below[s * 8 : s * 8 + 8]


def around(field):
    tall = field.shape[0]
    return pltpu.roll(field, 1, 0), pltpu.roll(field, tall - 1, 0)


def phi_of(values):
    return 0.5 * (1.0 + lax.erf(values * 0.7071067811865476))


def slope_of(values):
    return phi_of(values) + values * jnp.exp(-0.5 * values * values) * 0.3989422804014327


def asked_rows(meta, offsets, bins, s, ext, taps, tall):
    row, col = grid_of(48, tall)
    want = row & 3
    shift = (row >> 4) - 1
    at = jnp.full((48, tall), -4096, jnp.int32)
    slab = meta[1]
    for k in range(4):
        mine = k < NTD
        home = slab if mine else jnp.maximum(slab - 1, 0)
        place = bins[s, home * NTD + (k % NTD)] + offsets[s] - (0 if mine else tall - 2 * PAD)
        fits = (place >= 0) & (place < tall - 2 * PAD)
        at = jnp.where(want == k, jnp.where(fits, place + PAD, -4096), at)
    found = dot(picks((col == at + shift) & ((row & 15) < 8)), ext.astype(BF))
    here = found[16:32]
    value = taps[0] * found[0:16] + taps[1] * here + taps[2] * found[32:48]
    act = value * phi_of(value)
    row = lax.broadcasted_iota(jnp.int32, act.shape, 0)
    return jnp.where(row < 4, act, here).astype(BF)


def taps_of(filt, cols):
    return [filt[k : k + 1, cols] for k in range(3)]


def tap_sums(conv, ext, rows):
    before, after = around(ext)
    body = slice(PAD, PAD + rows)
    mine = conv[body]
    return [
        jnp.sum(mine * other[body], axis=0, keepdims=True) for other in (before, ext, after)
    ]


def grads(conv, direct, taps, rows, pair):
    before, after = around(conv)
    body = slice(PAD, PAD + rows)
    total = direct + taps[0] * after[body] + taps[1] * conv[body] + taps[2] * before[body]
    short = rows // 2
    sums = []
    for k in range(total.shape[1] // LANES):
        pair[k] = total[:, k * LANES : (k + 1) * LANES]
        sums.append(pair[k, pl.ds(0, short, 2), :] + pair[k, pl.ds(1, short, 2), :])
    return total, jnp.concatenate(sums, axis=1)


def own_kernel(
    slabs, meta, offsets, bins, att, skip, up, down, down_all, far, prev, cot, weight, filt,
    moved, asked, terms, skip_grad, att_grad, ext, pair,
):
    rows = skip.shape[1]
    tall = rows + 2 * PAD
    wide = cot.shape[2]
    row, col = grid_of(tall, rows)
    last = meta[1] == slabs - 1
    for s in range(2):
        at = row - PAD
        fits = (at >= -1) & (at < jnp.where(last, rows, rows + 1))
        source = jnp.where(fits, at - offsets[s], -4096)
        older = picks(col == source + rows)
        newer = picks(col == source)
        edge = lax.broadcasted_iota(jnp.int32, (PAD, 512), 0)
        top = (edge == PAD - 1) & (offsets[s] == rows)
        bottom = (edge == 0) & (offsets[s] == 0) & jnp.logical_not(last)
        for part in range(0, wide, 512):
            cols = slice(part, part + 512)
            found = dot(older, prev[s, :, cols]) + dot(newer, cot[s, :, cols])
            above = far[:, cols].astype(F32)[s * 8 + 7 : s * 8 + 8]
            below = down_all[:, cols].astype(F32)[s * 8 + 3 : s * 8 + 4]
            found = jnp.concatenate(
                [
                    found[:PAD] + jnp.where(top, above, 0.0),
                    found[PAD : PAD + rows],
                    found[PAD + rows :] + jnp.where(bottom, below, 0.0),
                ]
            )
            moved[s, :, cols] = found.astype(BF)
    width = ext.shape[2]
    half = skip.shape[2]
    first = meta[0] * half

    @pl.loop(0, half // width)
    def _(part):
        begin = pl.multiple_of(part * width, width)
        cols = pl.ds(begin, width)
        slab_sums(att, skip, up, down, ext, cols, False)
        taps = taps_of(filt, cols)
        piece = weight[pl.ds(begin, width), :]
        sums = [0.0, 0.0, 0.0]
        there = pl.ds(pl.multiple_of(first + begin, width), width)
        for s in range(2):
            field = ext[s]
            before, after = around(field)
            slope = slope_of(taps[0] * before + taps[1] * field + taps[2] * after)
            asked[s * 16 : s * 16 + 16, cols] = asked_rows(
                meta, offsets, bins, s, field, taps, tall
            )
            conv = (dot_rows(moved[s], piece) * slope).astype(BF).astype(F32)
            sums = [a + b for a, b in zip(sums, tap_sums(conv, field, rows))]
            direct = moved[s, :, there].astype(F32)[PAD : PAD + rows]
            total, pairs = grads(conv, direct, taps, rows, pair)
            skip_grad[s, :, cols] = total.astype(BF)
            att_grad[s, :, cols] = pairs.astype(BF)
        for k in range(3):
            terms[k : k + 1, cols] = sums[k]


def own_half(meta, offsets, bins, attention, skip, up, down, far, prev, cot, weight, filt, slabs):
    seqs, rows, wide = skip.shape
    _, short, half = attention.shape
    tall = rows + 2 * PAD

    def whole(*shape):
        return pl.BlockSpec(shape, lambda i, m, o, b: (0,) * len(shape))

    def mine(*shape):
        return pl.BlockSpec(shape, lambda i, m, o, b: (0,) * (len(shape) - 1) + (m[0],))

    return pl.pallas_call(
        functools.partial(own_kernel, slabs),
        grid_spec=pltpu.PrefetchScalarGridSpec(
            num_scalar_prefetch=3,
            grid=(1,),
            in_specs=[
                pl.BlockSpec((2, short, half), lambda i, m, o, b: (m[0], 0, 0)),
                mine(2, rows, half),
                mine(16, half),
                mine(16, half),
                whole(16, wide),
                whole(16, wide),
                whole(2, rows, wide),
                whole(2, rows, wide),
                whole(half, wide),
                mine(3, half),
            ],
            out_specs=[
                whole(2, tall, wide),
                whole(32, half),
                whole(3, half),
                mine(2, rows, half),
                mine(2, short, half),
            ],
            scratch_shapes=[pltpu.VMEM((2, tall, 256), F32), pltpu.VMEM((2, rows, LANES), F32)],
        ),
        out_shape=[
            jax.ShapeDtypeStruct((2, tall, wide), BF),
            jax.ShapeDtypeStruct((32, half), BF),
            jax.ShapeDtypeStruct((3, half), F32),
            jax.ShapeDtypeStruct((2, rows, wide), BF),
            jax.ShapeDtypeStruct((2, short, wide), BF),
        ],
        compiler_params=params(),
        cost_estimate=cost(2 * 2 * tall * half * wide, 8 * 1024 * 1024, 2 * tall * half),
        name="own_half",
    )(meta, offsets, bins, attention, skip, up, down, down, far, prev, cot, weight, filt)


def slope_kernel(
    meta, offsets, bins, att, skip, up, down, filt, asked, sums, slopes, mine, shown, ext
):
    rows = skip.shape[1]
    tall = rows + 2 * PAD
    half = skip.shape[2]
    width = ext.shape[2]
    there = (1 - meta[0]) * half
    row, col = grid_of(16, 32)
    at, base = row & 7, (row >> 3) * 16
    kept = picks((at < 4) & (col == base + at + jnp.where(at < 2, 0, 2)))
    told = picks((at < 4) & (col == base + at + jnp.where(at < 2, 2, 4)))
    here = pl.ds(pl.multiple_of(meta[0] * half, half), half)
    mine[:, here] = dot(kept, asked[...]).astype(BF)
    shown[:, here] = dot(told, asked[...]).astype(BF)

    @pl.loop(0, half // width)
    def _(part):
        begin = pl.multiple_of(part * width, width)
        cols = pl.ds(begin, width)
        slab_sums(att, skip, up, down, ext, cols, True)
        taps = taps_of(filt, cols)
        got = []
        for s in range(2):
            field = ext[s]
            before, after = around(field)
            slopes[s, :, cols] = slope_of(taps[0] * before + taps[1] * field + taps[2] * after)
            sums[s, :, cols] = field.astype(BF)
            got.append(asked_rows(meta, offsets, bins, s, field, taps, tall))
        got = jnp.concatenate(got)
        place = pl.ds(pl.multiple_of(there + begin, width), width)
        mine[:, place] = dot(kept, got).astype(BF)
        shown[:, place] = dot(told, got).astype(BF)


def other_slopes(meta, offsets, bins, shipped, skip, up, down, filt, asked):
    seqs, rows, wide = skip.shape
    _, packed_rows, half = shipped.shape
    tall = rows + 2 * PAD

    def whole(*shape):
        return pl.BlockSpec(shape, lambda i, m, o, b: (0,) * len(shape))

    def other(*shape):
        return pl.BlockSpec(shape, lambda i, m, o, b: (0,) * (len(shape) - 1) + (1 - m[0],))

    return pl.pallas_call(
        slope_kernel,
        grid_spec=pltpu.PrefetchScalarGridSpec(
            num_scalar_prefetch=3,
            grid=(1,),
            in_specs=[
                whole(2, packed_rows, half),
                other(2, rows, half),
                other(16, half),
                other(16, half),
                other(3, half),
                whole(32, half),
            ],
            out_specs=[whole(2, tall, half), whole(2, tall, half), whole(16, wide), whole(16, wide)],
            scratch_shapes=[pltpu.VMEM((2, tall, 256), F32)],
        ),
        out_shape=[
            jax.ShapeDtypeStruct((2, tall, half), BF),
            jax.ShapeDtypeStruct((2, tall, half), F32),
            jax.ShapeDtypeStruct((16, wide), BF),
            jax.ShapeDtypeStruct((16, wide), BF),
        ],
        compiler_params=params(),
        cost_estimate=cost(10**11, 4 * 1024 * 1024, 2 * tall * half),
        name="other_slopes",
    )(meta, offsets, bins, shipped, skip, up, down, filt, asked)


def terms_kernel(meta, order, moved, sums, slopes, own_terms, *refs):
    pieces, (convs, terms, full, sems) = refs[:8], refs[8:]
    half = sums.shape[2]
    tall = sums.shape[1]
    rows = tall - 2 * PAD
    there = (1 - meta[0]) * half
    tile = pieces[0].shape[0]
    copies = []
    for k, piece in enumerate(pieces):
        down = pl.multiple_of(order[4 + k // 4] * tile, tile)
        over = pl.multiple_of(order[k % 4] * tile, tile)
        copies.append(
            pltpu.make_async_copy(
                piece, full.at[pl.ds(down, tile), pl.ds(over, tile)], sems.at[k]
            )
        )
        copies[-1].start()
    terms[:, pl.ds(pl.multiple_of(meta[0] * half, half), half)] = own_terms[...]
    for copy in copies:
        copy.wait()
    width = 2 * LANES
    for begin in range(0, half, width):
        cols = slice(begin, begin + width)
        total = [0.0, 0.0, 0.0]
        for s in range(2):
            grad = dot_rows(moved[s], full[cols, :])
            conv = (grad * slopes[s, :, cols]).astype(BF)
            convs[s, :, cols] = conv
            got = tap_sums(conv.astype(F32), sums[s, :, cols].astype(F32), rows)
            total = [a + b for a, b in zip(total, got)]
        place = pl.ds(pl.multiple_of(there + begin, width), width)
        for k in range(3):
            terms[k : k + 1, place] = total[k]


def other_terms(meta, order, moved, sums, slopes, own_terms, pieces):
    _, tall, wide = moved.shape
    half = sums.shape[2]

    def whole(*shape):
        return pl.BlockSpec(shape, lambda i, m, o: (0,) * len(shape))

    return pl.pallas_call(
        terms_kernel,
        grid_spec=pltpu.PrefetchScalarGridSpec(
            num_scalar_prefetch=2,
            grid=(1,),
            in_specs=[
                whole(2, tall, wide),
                whole(2, tall, half),
                whole(2, tall, half),
                whole(3, half),
            ]
            + [pl.BlockSpec(memory_space=pl.ANY)] * 8,
            out_specs=[whole(2, tall, half), whole(3, wide)],
            scratch_shapes=[pltpu.VMEM((half, wide), BF), pltpu.SemaphoreType.DMA((8,))],
        ),
        out_shape=[
            jax.ShapeDtypeStruct((2, tall, half), BF),
            jax.ShapeDtypeStruct((3, wide), F32),
        ],
        compiler_params=params(),
        cost_estimate=cost(2 * 2 * tall * half * wide, 6 * 1024 * 1024),
        name="other_terms",
    )(meta, order, moved, sums, slopes, own_terms, *pieces)


def grads_kernel(meta, moved, convs, filt, old_skip, old_att, skip_grad, att_grad, pair):
    half = convs.shape[2]
    rows = convs.shape[1] - 2 * PAD
    width = 2 * LANES

    @pl.loop(0, half // width)
    def _(part):
        cols = pl.ds(pl.multiple_of(part * width, width), width)
        taps = taps_of(filt, cols)
        for s in range(2):
            direct = moved[s, :, cols].astype(F32)[PAD : PAD + rows]
            total, pairs = grads(convs[s, :, cols].astype(F32), direct, taps, rows, pair)
            skip_grad[s, :, cols] = total.astype(BF)
            att_grad[s, :, cols] = pairs.astype(BF)


def other_grads(meta, moved, convs, filt, skip_grad, att_grad):
    _, tall, wide = moved.shape
    half = convs.shape[2]
    rows = tall - 2 * PAD

    def whole(*shape):
        return pl.BlockSpec(shape, lambda i, m: (0,) * len(shape))

    def other(*shape):
        return pl.BlockSpec(shape, lambda i, m: (0,) * (len(shape) - 1) + (1 - m[0],))

    return pl.pallas_call(
        grads_kernel,
        grid_spec=pltpu.PrefetchScalarGridSpec(
            num_scalar_prefetch=1,
            grid=(1,),
            in_specs=[other(2, tall, half), whole(2, tall, half), other(3, half)]
            + [pl.BlockSpec(memory_space=pl.ANY)] * 2,
            out_specs=[other(2, rows, half), other(2, rows // 2, half)],
            scratch_shapes=[pltpu.VMEM((2, rows, LANES), F32)],
        ),
        out_shape=[
            jax.ShapeDtypeStruct((2, rows, wide), BF),
            jax.ShapeDtypeStruct((2, rows // 2, wide), BF),
        ],
        input_output_aliases={4: 0, 5: 1},
        compiler_params=params(),
        cost_estimate=cost(2 * tall * half * 20, 4 * 1024 * 1024),
        name="other_grads",
    )(meta, moved, convs, filt, skip_grad, att_grad)


def target_kernel(meta, order, mine, got, weight, *refs):
    pieces, (target, total) = refs[:8], refs[8:]
    half = weight.shape[0]
    there = (1 - meta[0]) * half
    tile = pieces[0].shape[0]
    mine[...] = mine[...] + got[...]
    here = pl.ds(pl.multiple_of(meta[0] * half, half), half)
    total[...] = dot(mine[:, here], weight[...]) + pltpu.roll(mine[...].astype(F32), 12 + 2, 0)
    for k, piece in enumerate(pieces):
        place = pl.ds(pl.multiple_of(there + order[4 + k // 4] * tile, tile), tile)
        over = pl.ds(pl.multiple_of(order[k % 4] * tile, tile), tile)
        total[:, over] += dot(mine[:, place], piece[...])
    for s in range(2):
        target[s] = total[s * 8 : s * 8 + 2].astype(BF)


def targets(meta, order, mine, got, weight, pieces):
    half, wide = weight.shape
    tile = pieces[0].shape[0]

    def whole(*shape):
        return pl.BlockSpec(shape, lambda i, m, o: (0,) * len(shape))

    return pl.pallas_call(
        target_kernel,
        grid_spec=pltpu.PrefetchScalarGridSpec(
            num_scalar_prefetch=2,
            grid=(1,),
            in_specs=[whole(16, wide), whole(16, wide), whole(half, wide)]
            + [whole(tile, tile)] * 8,
            out_specs=whole(2, NTD, wide),
            scratch_shapes=[pltpu.VMEM((16, wide), F32)],
        ),
        out_shape=jax.ShapeDtypeStruct((2, NTD, wide), BF),
        compiler_params=params(),
        cost_estimate=cost(2 * 16 * wide * wide, 6 * 1024 * 1024),
        name="targets",
    )(meta, order, mine, got, weight, *pieces)


def paired(part, axis, bit):
    count = lax.axis_size(axis)
    return lax.ppermute(part, axis, [(i, i ^ bit) for i in range(count)])


def after(value, *others):
    return lax.optimization_barrier((value,) + others)[0]


def crossed(part, seq_bit, head_bit):
    slabs, heads = lax.axis_size("seq"), lax.axis_size("head")
    pairs = [
        (i * heads + j, (i ^ seq_bit) * heads + (j ^ head_bit))
        for i in range(slabs)
        for j in range(heads)
    ]
    return lax.ppermute(part, ("seq", "head"), pairs)


def joined(total, one, two):
    both = (one[0] ^ two[0], one[1] ^ two[1])
    parts = [crossed(total, *bits) for bits in (one, two, both)]
    return (total + parts[0]) + (parts[1] + parts[2])


def fast_shards(
    attention, encoder_skip, depth_filter, point_weight, crop_offset, target_bins, cotangent
):
    head = lax.axis_index("head")
    slab = lax.axis_index("seq")
    slabs = lax.axis_size("seq")
    meta = jnp.stack([head, slab]).astype(jnp.int32)
    core = slab % 2
    block = slab // 2 % 4
    tile = 3 * LANES
    order = jnp.stack([block, block ^ 1, block ^ 2, block ^ 3, core, 1 - core]).astype(jnp.int32)

    def tile_of(weight, which):
        return lax.dynamic_slice(weight, (core * tile, which * tile), (tile, tile))

    first = paired(tile_of(point_weight, block), "head", 1)
    up, down, far = packed(encoder_skip, attention, cotangent)
    prev = passed_along(cotangent, "seq", 1)
    up = passed_along(up, "seq", 1)
    down = passed_along(down, "seq", -1)
    far = passed_along(far, "seq", 2)
    message = shipment(meta, attention, up, down)
    shipped = paired(message, "head", 1)
    first, up, down, far = lax.optimization_barrier((first, up, down, far))
    second = paired(first, "seq", 2)
    third = paired(first, "seq", 4)
    last_tile = tile_of(after(point_weight, message, prev), block ^ 3)
    fourth = paired(last_tile, "head", 1)
    moved, asked, own_terms, skip_grad, att_grad = own_half(
        meta, crop_offset, target_bins, attention, encoder_skip, up, down, far, prev, cotangent,
        after(point_weight, first, message, last_tile), depth_filter, slabs,
    )
    pieces = [first, second, third, fourth]
    pieces = pieces + [paired(after(piece, own_terms), "seq", 1) for piece in pieces]
    sums, slopes, mine, shown = other_slopes(
        meta, crop_offset, target_bins, shipped, encoder_skip, up, down, depth_filter, asked
    )
    got = passed_along(shown, "seq", -1)
    convs, terms = other_terms(meta, order, moved, sums, slopes, own_terms, pieces)
    terms, got = lax.optimization_barrier((terms, got))
    total = terms + crossed(terms, 1, 0)
    total = joined(total, (2, 0), (0, 1))
    skip_grad, attention_grad = other_grads(
        meta, moved, convs, depth_filter, skip_grad, att_grad
    )
    target_rows = targets(meta, order, mine, got, point_weight, pieces)
    total, skip_grad, attention_grad = lax.optimization_barrier(
        (total, skip_grad, attention_grad)
    )
    if slabs == 16:
        total = joined(total, (4, 0), (8, 0))
    else:
        step = 4
        while step < slabs:
            total = total + crossed(total, step, 0)
            step *= 2
    count = encoder_skip.shape[0] * lax.axis_size("head") * encoder_skip.shape[1] * slabs
    return (target_rows, attention_grad, skip_grad, total * (1.0 / math.sqrt(count)))


def shards(*args):
    attention, encoder_skip, point_weight = args[0], args[1], args[3]
    fits = (
        lax.axis_size("head") == 2
        and lax.axis_size("seq") in (8, 16, 32)
        and encoder_skip.shape[:2] == (2, 128)
        and point_weight.shape[0] == 6 * LANES
        and attention.shape[1] == 64
    )
    return fast_shards(*args) if fits else plain_shards(*args)


def solution(mesh):
    in_specs = (
        P(None, "seq", "head"),
        P("head", "seq", None),
        P(),
        P("head", None),
        P("head"),
        P("head", None),
        P("head", "seq", None),
    )
    out_specs = (P("head", "seq", None), P("head", "seq", None), P("head", "seq", None), P())
    return jax.shard_map(shards, mesh=mesh, in_specs=in_specs, out_specs=out_specs, check_vma=False)
```

```python
import functools
import math

import jax
import jax.numpy as jnp
from jax import lax
from jax.experimental import pallas as pl
from jax.experimental.pallas import tpu as pltpu
from jax.sharding import PartitionSpec as P

NTD = 2


def extended(shard, sides, width):
    for axis, dim in sides:
        count, length = (lax.axis_size(axis), shard.shape[dim])
        up = [(i, (i + 1) % count) for i in range(count - 1)]
        down = [(j, i) for i, j in up]
        last = lax.slice_in_dim(shard, length - width, length, axis=dim)
        initial = lax.slice_in_dim(shard, 0, width, axis=dim)
        before = lax.ppermute(last, axis, up)
        after = lax.ppermute(initial, axis, down)
        shard = jnp.concatenate([before, shard, after], axis=dim)
    return shard


def passed_along(shard, axis, by):
    count = lax.axis_size(axis)
    pairs = [(i, i + by) for i in range(count) if 0 <= i + by < count]
    return lax.ppermute(shard, axis, pairs)


def gelu_slope(values):
    return (
        0.5 * (1.0 + lax.erf(values * 0.7071067811865476))
        + values * jnp.exp(-0.5 * values * values) * 0.3989422804014327
    )


def with_rims(field):
    return extended(field, (("seq", 1),), 1)


def one_hot(places, length):
    return (places[:, :, None] == jnp.arange(length, dtype=jnp.int32)[None, None, :]).astype(
        jnp.bfloat16
    )


def core_swap(part):
    count = lax.axis_size("seq")
    return lax.ppermute(part, "seq", [(i, i ^ 1) for i in range(count)])


def gathered_weight(rows):
    heads = lax.axis_size("head")
    here = lax.axis_index("head")
    core = lax.axis_index("seq") % 2
    half = rows.shape[0] // 2
    mine = lax.dynamic_slice_in_dim(rows, core * half, half, 0)
    blocks = [(0, rows)]
    for step in range(1, heads):
        pairs = [(i, (i + step) % heads) for i in range(heads)]
        got = lax.ppermute(mine, "head", pairs)
        twin = core_swap(got)
        low = jnp.where(core == 0, got, twin)
        high = jnp.where(core == 0, twin, got)
        blocks.append((step, jnp.concatenate([low, high], axis=0)))
    full = jnp.zeros((heads * rows.shape[0], rows.shape[1]), rows.dtype)
    for step, block in blocks:
        place = (here - step) % heads
        full = lax.dynamic_update_slice_in_dim(full, block, place * rows.shape[0], 0)
    return full


def butterfly(total, axis):
    count = lax.axis_size(axis)
    if count & (count - 1):
        return lax.psum(total, axis)
    step = 1
    while step < count:
        total = total + lax.ppermute(total, axis, [(i, i ^ step) for i in range(count)])
        step *= 2
    return total


def plain_shards(
    attention, encoder_skip, depth_filter, point_weight, crop_offset, target_bins, cotangent
):
    slab_input = lax.all_to_all(attention, "head", split_axis=0, concat_axis=2, tiled=True)
    local_seqs = encoder_skip.shape[0]
    slab_rows = encoder_skip.shape[1]
    channels = encoder_skip.shape[2]
    summed = (
        jnp.repeat(slab_input, 2, axis=1).astype(jnp.float32) + encoder_skip.astype(jnp.float32)
    ).astype(jnp.bfloat16)
    padded = with_rims(summed)
    filtered = (
        depth_filter[0] * padded[:, :-2]
        + depth_filter[1] * padded[:, 1:-1]
        + depth_filter[2] * padded[:, 2:]
    )
    activated = jax.nn.gelu(filtered, approximate=False).astype(jnp.bfloat16)
    flat_act = activated.reshape(local_seqs * slab_rows, channels)
    full_weight = gathered_weight(point_weight)
    mixed_rows = jnp.dot(flat_act, full_weight, preferred_element_type=jnp.float32)
    block_out = (
        summed.astype(jnp.float32) + mixed_rows.reshape(local_seqs, slab_rows, channels)
    ).astype(jnp.bfloat16)
    slab_index = lax.axis_index("seq")
    bins = jnp.concatenate(
        [jnp.zeros_like(target_bins[:, :NTD]), target_bins], axis=1
    )
    asked = lax.dynamic_slice_in_dim(bins, slab_index * NTD, 2 * NTD, 1) + crop_offset[:, None]
    back = jnp.where(jnp.arange(2 * NTD, dtype=jnp.int32) < NTD, slab_rows, 0)
    asked = asked - back[None, :]
    picked = jnp.einsum(
        "sjr,srd->sjd",
        one_hot(asked, slab_rows),
        block_out,
        preferred_element_type=jnp.float32,
    ).astype(jnp.bfloat16)
    from_next = passed_along(picked[:, :NTD], "seq", -1)
    target_rows = picked[:, NTD:] + from_next
    prev_cot = passed_along(cotangent, "seq", 1)
    cot_pair = jnp.concatenate([prev_cot, cotangent], axis=1)

    def crop_back(cot_block, shift_by):
        return lax.dynamic_slice_in_dim(cot_block, slab_rows - shift_by, slab_rows, 0)

    grad_out = jax.vmap(crop_back)(cot_pair, crop_offset)
    flat_grad = grad_out.reshape(local_seqs * slab_rows, channels)
    grad_act = lax.dot_general(
        flat_grad, full_weight, (((1,), (1,)), ((), ())), preferred_element_type=jnp.float32
    )
    grad_conv = (grad_act.reshape(local_seqs, slab_rows, channels) * gelu_slope(filtered)).astype(
        jnp.bfloat16
    )
    grad_padded = with_rims(grad_conv)
    grad_sum = (
        grad_out.astype(jnp.float32)
        + depth_filter[0] * grad_padded[:, 2:]
        + depth_filter[1] * grad_padded[:, 1:-1]
        + depth_filter[2] * grad_padded[:, :-2]
    )
    skip_grad = grad_sum.astype(jnp.bfloat16)
    attention_grad = (
        grad_sum.reshape(local_seqs, slab_rows // 2, 2, channels).sum(axis=2).astype(jnp.bfloat16)
    )
    filter_terms = jnp.stack(
        [
            jnp.einsum(
                "srd,srd->d", grad_conv, padded[:, 0:slab_rows], preferred_element_type=jnp.float32
            ),
            jnp.einsum(
                "srd,srd->d",
                grad_conv,
                padded[:, 1 : slab_rows + 1],
                preferred_element_type=jnp.float32,
            ),
            jnp.einsum(
                "srd,srd->d",
                grad_conv,
                padded[:, 2 : slab_rows + 2],
                preferred_element_type=jnp.float32,
            ),
        ]
    )
    filter_sum = butterfly(butterfly(filter_terms, "seq"), "head")
    row_count = local_seqs * lax.axis_size("head") * slab_rows * lax.axis_size("seq")
    filter_grad = filter_sum * (1.0 / math.sqrt(row_count))
    return (target_rows, attention_grad, skip_grad, filter_grad)


LANES = 128
PAD = 8
BF = jnp.bfloat16
F32 = jnp.float32


def dot(left, right):
    return lax.dot_general(left, right, (((1,), (0,)), ((), ())), preferred_element_type=F32)


def dot_rows(left, right):
    return lax.dot_general(left, right, (((1,), (1,)), ((), ())), preferred_element_type=F32)


def grid_of(rows, columns):
    return (
        lax.broadcasted_iota(jnp.int32, (rows, columns), 0),
        lax.broadcasted_iota(jnp.int32, (rows, columns), 1),
    )


def picks(match):
    return jnp.where(match, 1.0, 0.0).astype(BF)


def params(mib=36):
    return pltpu.CompilerParams(vmem_limit_bytes=mib * 1024 * 1024)


def cost(flops, moved, special=0):
    return pl.CostEstimate(flops=flops, bytes_accessed=moved, transcendentals=special)


def pack_kernel(
    meta, skip_lo, skip_hi, att_lo, att_hi, cot_lo, cot_hi, near, distant,
    edge_a, edge_b, far, tile_a, tile_b,
):
    half = att_lo.shape[2]
    tile_a[...] = near[...]
    tile_b[...] = distant[...]
    row, col = grid_of(16, 32)
    at, base = row & 7, (row >> 3) * 16
    even = (meta[1] & 1) == 0

    def edges(body, others, edge):
        parts = []
        for group in range(2):
            rows = others[2 * group : 2 * group + 2].reshape(32, half)
            parts.append(body[:, group * half : (group + 1) * half] + dot(edge, rows))
        return jnp.concatenate(parts, axis=1)

    skips = skip_hi[...].reshape(32, 2 * half)
    up = dot(picks((at >= 6) & (col == base + at + 8)), skips)
    up = edges(up, att_hi, picks((at == 5) & (col == base + 15)))
    skips = skip_lo[...].reshape(32, 2 * half)
    cots = cot_lo[...].reshape(32, 2 * half)
    down = dot(picks((at < 2) & (col == base + at)), skips)
    down = down + dot(picks((at == 3) & (col == base)), cots)
    down = edges(down, att_lo, picks((at == 2) & (col == base)))
    edge_a[...] = jnp.where(even, up, down).astype(BF)
    edge_b[...] = jnp.where(even, down, up).astype(BF)
    cots = cot_hi[...].reshape(32, 2 * half)
    far[...] = dot(picks((at == 7) & (col == base + 15)), cots).astype(BF)


def packed(meta, encoder_skip, attention, cotangent, weight, tile):
    seqs, rows, wide = encoder_skip.shape
    half = attention.shape[2]
    short = attention.shape[1]

    def block(count, width, place):
        return pl.BlockSpec((count, 16, width), lambda i, m: (0, place, 0))

    out = jax.ShapeDtypeStruct((16, wide), BF)
    square = jax.ShapeDtypeStruct((tile, tile), BF)
    return pl.pallas_call(
        pack_kernel,
        grid_spec=pltpu.PrefetchScalarGridSpec(
            num_scalar_prefetch=1,
            grid=(1,),
            in_specs=[
                block(seqs, wide, 0),
                block(seqs, wide, rows // 16 - 1),
                block(2 * seqs, half, 0),
                block(2 * seqs, half, short // 16 - 1),
                block(seqs, wide, 0),
                block(seqs, wide, rows // 16 - 1),
                pl.BlockSpec((tile, tile), lambda i, m: (m[1] & 1, (m[1] >> 1) & 3)),
                pl.BlockSpec((tile, tile), lambda i, m: (m[1] & 1, 3 - ((m[1] >> 1) & 3))),
            ],
            out_specs=[pl.BlockSpec((16, wide), lambda i, m: (0, 0))] * 3
            + [pl.BlockSpec((tile, tile), lambda i, m: (0, 0))] * 2,
        ),
        out_shape=[out, out, out, square, square],
        compiler_params=params(60),
        name="pack_edges",
    )(
        meta, encoder_skip, encoder_skip, attention, attention, cotangent, cotangent, weight,
        weight,
    )


def ship_kernel(meta, att, edge, out):
    short = att.shape[1]
    row, col = grid_of(16, 16)
    for s in range(2):
        out[s, 0:short] = att[s]
        wanted = ((row == 0) & (col == s * 8 + 5)) | ((row == 1) & (col == s * 8 + 2))
        out[s, short : short + 16] = dot(picks(wanted), edge[...]).astype(BF)


def shipment(meta, attention, edge):
    _, short, half = attention.shape
    return pl.pallas_call(
        ship_kernel,
        grid_spec=pltpu.PrefetchScalarGridSpec(
            num_scalar_prefetch=1,
            grid=(1,),
            in_specs=[
                pl.BlockSpec((2, short, half), lambda i, m: (1 - m[0], 0, 0)),
                pl.BlockSpec((16, half), lambda i, m: (0, 1 - m[0])),
            ],
            out_specs=pl.BlockSpec((2, short + 16, half), lambda i, m: (0, 0, 0)),
        ),
        out_shape=jax.ShapeDtypeStruct((2, short + 16, half), BF),
        compiler_params=params(),
        name="pack_attention",
    )(meta, attention, edge)


def slab_sums(att, skip, edge, ext, cols, from_ship):
    width = cols.size
    short = 64
    row, col = grid_of(2 * short, short)
    spread = picks((row >> 1) == col)
    row, col = grid_of(16, 32 if from_ship else 16)
    at = row & 7
    rims = edge[:, cols]
    if from_ship:
        edges = jnp.concatenate([att[0, short : short + 16, cols], att[1, short : short + 16, cols]])
        base = (row >> 3) * 16
        wanted = ((at >= 6) & (col == base)) | ((at < 2) & (col == base + 1))
        from_att = dot(picks(wanted), edges)
    else:
        base = row & 8
        wanted = ((at >= 6) & (col == base + 5)) | ((at < 2) & (col == base + 2))
        from_att = dot(picks(wanted), rims)
    at = lax.broadcasted_iota(jnp.int32, (16, width), 0) & 7
    rims = (from_att + rims.astype(F32)).astype(BF).astype(F32)
    above = jnp.where(at >= 6, rims, 0.0)
    below = jnp.where(at < 2, rims, 0.0)
    for s in range(2):
        body = dot(spread, att[s, 0:short, cols]) + skip[s, :, cols].astype(F32)
        ext[s, 0:PAD] = above[s * 8 : s * 8 + 8]
        ext[s, PAD : PAD + 2 * short] = body.astype(BF).astype(F32)
        ext[s, PAD + 2 * short : 2 * PAD + 2 * short] = below[s * 8 : s * 8 + 8]


def around(field):
    tall = field.shape[0]
    return pltpu.roll(field, 1, 0), pltpu.roll(field, tall - 1, 0)


def phi_of(values):
    return 0.5 * (1.0 + lax.erf(values * 0.7071067811865476))


def slope_of(values):
    return phi_of(values) + values * jnp.exp(-0.5 * values * values) * 0.3989422804014327


def asked_rows(meta, offsets, bins, s, ext, taps, tall):
    row, col = grid_of(48, tall)
    want = row & 3
    shift = (row >> 4) - 1
    at = jnp.full((48, tall), -4096, jnp.int32)
    slab = meta[1]
    for k in range(4):
        mine = k < NTD
        home = slab if mine else jnp.maximum(slab - 1, 0)
        place = bins[s, home * NTD + (k % NTD)] + offsets[s] - (0 if mine else tall - 2 * PAD)
        fits = (place >= 0) & (place < tall - 2 * PAD)
        at = jnp.where(want == k, jnp.where(fits, place + PAD, -4096), at)
    found = dot(picks((col == at + shift) & ((row & 15) < 8)), ext.astype(BF))
    here = found[16:32]
    value = taps[0] * found[0:16] + taps[1] * here + taps[2] * found[32:48]
    act = value * phi_of(value)
    row = lax.broadcasted_iota(jnp.int32, act.shape, 0)
    return jnp.where(row < 4, act, here).astype(BF)


def taps_of(filt, cols):
    return [filt[k : k + 1, cols] for k in range(3)]


def tap_sums(conv, ext, rows):
    before, after = around(ext)
    body = slice(PAD, PAD + rows)
    mine = conv[body]
    return [
        jnp.sum(mine * other[body], axis=0, keepdims=True) for other in (before, ext, after)
    ]


def grads(conv, direct, taps, rows, pair):
    before, after = around(conv)
    body = slice(PAD, PAD + rows)
    total = direct + taps[0] * after[body] + taps[1] * conv[body] + taps[2] * before[body]
    short = rows // 2
    sums = []
    for k in range(total.shape[1] // LANES):
        pair[k] = total[:, k * LANES : (k + 1) * LANES]
        sums.append(pair[k, pl.ds(0, short, 2), :] + pair[k, pl.ds(1, short, 2), :])
    return total, jnp.concatenate(sums, axis=1)


def own_kernel(
    slabs, meta, offsets, bins, att, skip, edge, rims, far_a, far_b, prev_a, prev_b, cot, weight,
    filt, moved, asked, terms, skip_grad, att_grad, ext, pair, prev, sem,
):
    from_a = pltpu.make_async_copy(prev_a, prev, sem)
    from_b = pltpu.make_async_copy(prev_b, prev, sem)
    pl.when((meta[1] & 1) == 1)(from_a.start)
    pl.when((meta[1] & 1) == 0)(from_b.start)
    rows = skip.shape[1]
    tall = rows + 2 * PAD
    wide = cot.shape[2]
    row, col = grid_of(tall, rows)
    last = meta[1] == slabs - 1
    from_a.wait()
    for s in range(2):
        at = row - PAD
        fits = (at >= -1) & (at < jnp.where(last, rows, rows + 1))
        source = jnp.where(fits, at - offsets[s], -4096)
        older = picks(col == source + rows)
        newer = picks(col == source)
        place = lax.broadcasted_iota(jnp.int32, (PAD, 512), 0)
        top = (place == PAD - 1) & (offsets[s] == rows)
        bottom = (place == 0) & (offsets[s] == 0) & jnp.logical_not(last)
        for part in range(0, wide, 512):
            cols = slice(part, part + 512)
            found = dot(older, prev[s, :, cols]) + dot(newer, cot[s, :, cols])
            far = far_a[:, cols].astype(F32) + far_b[:, cols].astype(F32)
            above = far[s * 8 + 7 : s * 8 + 8]
            below = rims[:, cols].astype(F32)[s * 8 + 3 : s * 8 + 4]
            found = jnp.concatenate(
                [
                    found[:PAD] + jnp.where(top, above, 0.0),
                    found[PAD : PAD + rows],
                    found[PAD + rows :] + jnp.where(bottom, below, 0.0),
                ]
            )
            moved[s, :, cols] = found.astype(BF)
    width = ext.shape[2]
    half = skip.shape[2]
    first = meta[0] * half

    @pl.loop(0, half // width)
    def _(part):
        begin = pl.multiple_of(part * width, width)
        cols = pl.ds(begin, width)
        slab_sums(att, skip, edge, ext, cols, False)
        taps = taps_of(filt, cols)
        piece = weight[pl.ds(begin, width), :]
        sums = [0.0, 0.0, 0.0]
        there = pl.ds(pl.multiple_of(first + begin, width), width)
        for s in range(2):
            field = ext[s]
            before, after = around(field)
            slope = slope_of(taps[0] * before + taps[1] * field + taps[2] * after)
            asked[s * 16 : s * 16 + 16, cols] = asked_rows(
                meta, offsets, bins, s, field, taps, tall
            )
            conv = (dot_rows(moved[s], piece) * slope).astype(BF).astype(F32)
            sums = [a + b for a, b in zip(sums, tap_sums(conv, field, rows))]
            direct = moved[s, :, there].astype(F32)[PAD : PAD + rows]
            total, pairs = grads(conv, direct, taps, rows, pair)
            skip_grad[s, :, cols] = total.astype(BF)
            att_grad[s, :, cols] = pairs.astype(BF)
        for k in range(3):
            terms[k : k + 1, cols] = sums[k]


def own_half(meta, offsets, bins, attention, skip, edge, far, prev, cot, weight, filt, slabs):
    seqs, rows, wide = skip.shape
    _, short, half = attention.shape
    tall = rows + 2 * PAD

    def whole(*shape):
        return pl.BlockSpec(shape, lambda i, m, o, b: (0,) * len(shape))

    def mine(*shape):
        return pl.BlockSpec(shape, lambda i, m, o, b: (0,) * (len(shape) - 1) + (m[0],))

    return pl.pallas_call(
        functools.partial(own_kernel, slabs),
        grid_spec=pltpu.PrefetchScalarGridSpec(
            num_scalar_prefetch=3,
            grid=(1,),
            in_specs=[
                pl.BlockSpec((2, short, half), lambda i, m, o, b: (m[0], 0, 0)),
                mine(2, rows, half),
                mine(16, half),
                whole(16, wide),
                whole(16, wide),
                whole(16, wide),
                pl.BlockSpec(memory_space=pl.ANY),
                pl.BlockSpec(memory_space=pl.ANY),
                whole(2, rows, wide),
                whole(half, wide),
                mine(3, half),
            ],
            out_specs=[
                whole(2, tall, wide),
                whole(32, half),
                whole(3, half),
                mine(2, rows, half),
                mine(2, short, half),
            ],
            scratch_shapes=[
                pltpu.VMEM((2, tall, 256), F32),
                pltpu.VMEM((2, rows, LANES), F32),
                pltpu.VMEM((2, rows, wide), BF),
                pltpu.SemaphoreType.DMA(()),
            ],
        ),
        out_shape=[
            jax.ShapeDtypeStruct((2, tall, wide), BF),
            jax.ShapeDtypeStruct((32, half), BF),
            jax.ShapeDtypeStruct((3, half), F32),
            jax.ShapeDtypeStruct((2, rows, wide), BF),
            jax.ShapeDtypeStruct((2, short, wide), BF),
        ],
        compiler_params=params(),
        cost_estimate=cost(1, 1),
        name="own_half",
    )(
        meta, offsets, bins, attention, skip, edge, edge, *far, *prev, cot, weight, filt,
    )


def slope_kernel(
    meta, offsets, bins, att, skip, edge, filt, asked, sums, slopes, mine, shown, ext
):
    rows = skip.shape[1]
    tall = rows + 2 * PAD
    half = skip.shape[2]
    width = ext.shape[2]
    there = (1 - meta[0]) * half
    row, col = grid_of(16, 32)
    at, base = row & 7, (row >> 3) * 16
    kept = picks((at < 4) & (col == base + at + jnp.where(at < 2, 0, 2)))
    told = picks((at < 4) & (col == base + at + jnp.where(at < 2, 2, 4)))
    here = pl.ds(pl.multiple_of(meta[0] * half, half), half)
    mine[:, here] = dot(kept, asked[...]).astype(BF)
    shown[:, here] = dot(told, asked[...]).astype(BF)

    @pl.loop(0, half // width)
    def _(part):
        begin = pl.multiple_of(part * width, width)
        cols = pl.ds(begin, width)
        slab_sums(att, skip, edge, ext, cols, True)
        taps = taps_of(filt, cols)
        got = []
        for s in range(2):
            field = ext[s]
            before, after = around(field)
            slopes[s, :, cols] = slope_of(taps[0] * before + taps[1] * field + taps[2] * after)
            sums[s, :, cols] = field.astype(BF)
            got.append(asked_rows(meta, offsets, bins, s, field, taps, tall))
        got = jnp.concatenate(got)
        place = pl.ds(pl.multiple_of(there + begin, width), width)
        mine[:, place] = dot(kept, got).astype(BF)
        shown[:, place] = dot(told, got).astype(BF)


def other_slopes(meta, offsets, bins, shipped, skip, edge, filt, asked):
    seqs, rows, wide = skip.shape
    _, packed_rows, half = shipped.shape
    tall = rows + 2 * PAD

    def whole(*shape):
        return pl.BlockSpec(shape, lambda i, m, o, b: (0,) * len(shape))

    def other(*shape):
        return pl.BlockSpec(shape, lambda i, m, o, b: (0,) * (len(shape) - 1) + (1 - m[0],))

    return pl.pallas_call(
        slope_kernel,
        grid_spec=pltpu.PrefetchScalarGridSpec(
            num_scalar_prefetch=3,
            grid=(1,),
            in_specs=[
                whole(2, packed_rows, half),
                other(2, rows, half),
                other(16, half),
                other(3, half),
                whole(32, half),
            ],
            out_specs=[whole(2, tall, half), whole(2, tall, half), whole(16, wide), whole(16, wide)],
            scratch_shapes=[pltpu.VMEM((2, tall, 256), F32)],
        ),
        out_shape=[
            jax.ShapeDtypeStruct((2, tall, half), BF),
            jax.ShapeDtypeStruct((2, tall, half), F32),
            jax.ShapeDtypeStruct((16, wide), BF),
            jax.ShapeDtypeStruct((16, wide), BF),
        ],
        compiler_params=params(),
        cost_estimate=cost(10**11, 4 * 1024 * 1024, 2 * tall * half),
        name="other_slopes",
    )(meta, offsets, bins, shipped, skip, edge, filt, asked)


def terms_kernel(meta, order, moved, sums, slopes, own_terms, *refs):
    pieces, (convs, terms, full, sems) = refs[:8], refs[8:]
    half = sums.shape[2]
    tall = sums.shape[1]
    rows = tall - 2 * PAD
    there = (1 - meta[0]) * half
    tile = pieces[0].shape[0]
    copies = []
    for k, piece in enumerate(pieces):
        down = pl.multiple_of(order[4 + k // 4] * tile, tile)
        over = pl.multiple_of(order[k % 4] * tile, tile)
        copies.append(
            pltpu.make_async_copy(
                piece, full.at[pl.ds(down, tile), pl.ds(over, tile)], sems.at[k]
            )
        )
        copies[-1].start()
    terms[:, pl.ds(pl.multiple_of(meta[0] * half, half), half)] = own_terms[...]
    for copy in copies:
        copy.wait()
    width = 2 * LANES
    for begin in range(0, half, width):
        cols = slice(begin, begin + width)
        total = [0.0, 0.0, 0.0]
        for s in range(2):
            grad = dot_rows(moved[s], full[cols, :])
            conv = (grad * slopes[s, :, cols]).astype(BF)
            convs[s, :, cols] = conv
            got = tap_sums(conv.astype(F32), sums[s, :, cols].astype(F32), rows)
            total = [a + b for a, b in zip(total, got)]
        place = pl.ds(pl.multiple_of(there + begin, width), width)
        for k in range(3):
            terms[k : k + 1, place] = total[k]


def other_terms(meta, order, moved, sums, slopes, own_terms, pieces):
    _, tall, wide = moved.shape
    half = sums.shape[2]

    def whole(*shape):
        return pl.BlockSpec(shape, lambda i, m, o: (0,) * len(shape))

    return pl.pallas_call(
        terms_kernel,
        grid_spec=pltpu.PrefetchScalarGridSpec(
            num_scalar_prefetch=2,
            grid=(1,),
            in_specs=[
                whole(2, tall, wide),
                whole(2, tall, half),
                whole(2, tall, half),
                whole(3, half),
            ]
            + [pl.BlockSpec(memory_space=pl.ANY)] * 8,
            out_specs=[whole(2, tall, half), whole(3, wide)],
            scratch_shapes=[pltpu.VMEM((half, wide), BF), pltpu.SemaphoreType.DMA((8,))],
        ),
        out_shape=[
            jax.ShapeDtypeStruct((2, tall, half), BF),
            jax.ShapeDtypeStruct((3, wide), F32),
        ],
        compiler_params=params(),
        cost_estimate=cost(2 * 2 * tall * half * wide, 6 * 1024 * 1024),
        name="other_terms",
    )(meta, order, moved, sums, slopes, own_terms, *pieces)


def grads_kernel(meta, moved, convs, filt, old_skip, old_att, skip_grad, att_grad, pair):
    half = convs.shape[2]
    rows = convs.shape[1] - 2 * PAD
    width = 2 * LANES

    @pl.loop(0, half // width)
    def _(part):
        cols = pl.ds(pl.multiple_of(part * width, width), width)
        taps = taps_of(filt, cols)
        for s in range(2):
            direct = moved[s, :, cols].astype(F32)[PAD : PAD + rows]
            total, pairs = grads(convs[s, :, cols].astype(F32), direct, taps, rows, pair)
            skip_grad[s, :, cols] = total.astype(BF)
            att_grad[s, :, cols] = pairs.astype(BF)


def other_grads(meta, moved, convs, filt, skip_grad, att_grad):
    _, tall, wide = moved.shape
    half = convs.shape[2]
    rows = tall - 2 * PAD

    def whole(*shape):
        return pl.BlockSpec(shape, lambda i, m: (0,) * len(shape))

    def other(*shape):
        return pl.BlockSpec(shape, lambda i, m: (0,) * (len(shape) - 1) + (1 - m[0],))

    return pl.pallas_call(
        grads_kernel,
        grid_spec=pltpu.PrefetchScalarGridSpec(
            num_scalar_prefetch=1,
            grid=(1,),
            in_specs=[other(2, tall, half), whole(2, tall, half), other(3, half)]
            + [pl.BlockSpec(memory_space=pl.ANY)] * 2,
            out_specs=[other(2, rows, half), other(2, rows // 2, half)],
            scratch_shapes=[pltpu.VMEM((2, rows, LANES), F32)],
        ),
        out_shape=[
            jax.ShapeDtypeStruct((2, rows, wide), BF),
            jax.ShapeDtypeStruct((2, rows // 2, wide), BF),
        ],
        input_output_aliases={4: 0, 5: 1},
        compiler_params=params(),
        cost_estimate=cost(2 * tall * half * 20, 4 * 1024 * 1024),
        name="other_grads",
    )(meta, moved, convs, filt, skip_grad, att_grad)


def target_kernel(meta, order, mine, got_a, got_b, weight, *refs):
    pieces, (target, total) = refs[:8], refs[8:]
    half = weight.shape[0]
    there = (1 - meta[0]) * half
    tile = pieces[0].shape[0]
    mine[...] = mine[...] + got_a[...] + got_b[...]
    here = pl.ds(pl.multiple_of(meta[0] * half, half), half)
    total[...] = dot(mine[:, here], weight[...]) + pltpu.roll(mine[...].astype(F32), 12 + 2, 0)
    for k, piece in enumerate(pieces):
        place = pl.ds(pl.multiple_of(there + order[4 + k // 4] * tile, tile), tile)
        over = pl.ds(pl.multiple_of(order[k % 4] * tile, tile), tile)
        total[:, over] += dot(mine[:, place], piece[...])
    for s in range(2):
        target[s] = total[s * 8 : s * 8 + 2].astype(BF)


def targets(meta, order, mine, got, weight, pieces):
    half, wide = weight.shape
    tile = pieces[0].shape[0]

    def whole(*shape):
        return pl.BlockSpec(shape, lambda i, m, o: (0,) * len(shape))

    return pl.pallas_call(
        target_kernel,
        grid_spec=pltpu.PrefetchScalarGridSpec(
            num_scalar_prefetch=2,
            grid=(1,),
            in_specs=[whole(16, wide)] * 3 + [whole(half, wide)]
            + [whole(tile, tile)] * 8,
            out_specs=whole(2, NTD, wide),
            scratch_shapes=[pltpu.VMEM((16, wide), F32)],
        ),
        out_shape=jax.ShapeDtypeStruct((2, NTD, wide), BF),
        compiler_params=params(),
        cost_estimate=cost(2 * 16 * wide * wide, 6 * 1024 * 1024),
        name="targets",
    )(meta, order, mine, *got, weight, *pieces)


def paired(part, axis, bit):
    count = lax.axis_size(axis)
    return lax.ppermute(part, axis, [(i, i ^ bit) for i in range(count)])


def sent(part, by, odd):
    count = lax.axis_size("seq")
    pairs = [(i, i + by) for i in range(odd, count, 2) if 0 <= i + by < count]
    return lax.ppermute(part, "seq", pairs)


def after(value, *others):
    return lax.optimization_barrier((value,) + others)[0]


def crossed(part, seq_bit, head_bit):
    slabs, heads = lax.axis_size("seq"), lax.axis_size("head")
    pairs = [
        (i * heads + j, (i ^ seq_bit) * heads + (j ^ head_bit))
        for i in range(slabs)
        for j in range(heads)
    ]
    return lax.ppermute(part, ("seq", "head"), pairs)


def joined(total, one, two):
    both = (one[0] ^ two[0], one[1] ^ two[1])
    parts = [crossed(total, *bits) for bits in (one, two, both)]
    return (total + parts[0]) + (parts[1] + parts[2])


def fast_shards(
    attention, encoder_skip, depth_filter, point_weight, crop_offset, target_bins, cotangent
):
    head = lax.axis_index("head")
    slab = lax.axis_index("seq")
    slabs = lax.axis_size("seq")
    meta = jnp.stack([head, slab]).astype(jnp.int32)
    core = slab % 2
    block = slab // 2 % 4
    tile = 3 * LANES
    order = jnp.stack([block, block ^ 1, block ^ 2, block ^ 3, core, 1 - core]).astype(jnp.int32)

    edge_a, edge_b, far, first, last_tile = packed(
        meta, encoder_skip, attention, cotangent, point_weight, tile
    )
    prev = [sent(cotangent, 1, odd) for odd in (0, 1)]
    first = paired(first, "head", 1)
    edge_a = paired(edge_a, "seq", 1)
    edge_b = lax.ppermute(
        edge_b, "seq", [pair for i in range(1, slabs - 1, 2) for pair in ((i, i + 1), (i + 1, i))]
    )
    far = [
        lax.ppermute(
            far, "seq", [(i, i + 2) for i in range(slabs - 2) if i // 2 % 2 == odd]
        )
        for odd in (0, 1)
    ]
    edge = edge_a + edge_b
    message = shipment(meta, attention, edge)
    shipped = paired(message, "head", 1)
    first, edge, *far = lax.optimization_barrier((first, edge, *far))
    second = paired(first, "seq", 2)
    third = paired(first, "seq", 4)
    fourth = paired(last_tile, "head", 1)
    moved, asked, own_terms, skip_grad, att_grad = own_half(
        meta, crop_offset, target_bins, attention, encoder_skip, edge, far, prev, cotangent,
        after(point_weight, first, message, last_tile), depth_filter, slabs,
    )
    pieces = [first, second, third, fourth]
    pieces = pieces + [paired(after(piece, own_terms), "seq", 1) for piece in pieces]
    sums, slopes, mine, shown = other_slopes(
        meta, crop_offset, target_bins, shipped, encoder_skip, edge, depth_filter, asked
    )
    got = [sent(shown, -1, odd) for odd in (1, 0)]
    convs, terms = other_terms(meta, order, moved, sums, slopes, own_terms, pieces)
    terms, *got = lax.optimization_barrier((terms, *got))
    total = terms + crossed(terms, 1, 0)
    total = joined(total, (2, 0), (0, 1))
    skip_grad, attention_grad = other_grads(
        meta, moved, convs, depth_filter, skip_grad, att_grad
    )
    target_rows = targets(meta, order, mine, got, point_weight, pieces)
    total, skip_grad, attention_grad = lax.optimization_barrier(
        (total, skip_grad, attention_grad)
    )
    if slabs == 16:
        total = joined(total, (4, 0), (8, 0))
    else:
        step = 4
        while step < slabs:
            total = total + crossed(total, step, 0)
            step *= 2
    count = encoder_skip.shape[0] * lax.axis_size("head") * encoder_skip.shape[1] * slabs
    return (target_rows, attention_grad, skip_grad, total * (1.0 / math.sqrt(count)))


def shards(*args):
    attention, encoder_skip, point_weight = args[0], args[1], args[3]
    fits = (
        lax.axis_size("head") == 2
        and lax.axis_size("seq") in (8, 16, 32)
        and encoder_skip.shape[:2] == (2, 128)
        and point_weight.shape[0] == 6 * LANES
        and attention.shape[1] == 64
    )
    return fast_shards(*args) if fits else plain_shards(*args)


def solution(mesh):
    in_specs = (
        P(None, "seq", "head"),
        P("head", "seq", None),
        P(),
        P("head", None),
        P("head"),
        P("head", None),
        P("head", "seq", None),
    )
    out_specs = (P("head", "seq", None), P("head", "seq", None), P("head", "seq", None), P())
    return jax.shard_map(shards, mesh=mesh, in_specs=in_specs, out_specs=out_specs, check_vma=False)
```

```python
import functools
import math

import jax
import jax.numpy as jnp
from jax import lax
from jax.experimental import pallas as pl
from jax.experimental.pallas import tpu as pltpu
from jax.sharding import PartitionSpec as P

NTD = 2


def extended(shard, sides, width):
    for axis, dim in sides:
        count, length = (lax.axis_size(axis), shard.shape[dim])
        up = [(i, (i + 1) % count) for i in range(count - 1)]
        down = [(j, i) for i, j in up]
        last = lax.slice_in_dim(shard, length - width, length, axis=dim)
        initial = lax.slice_in_dim(shard, 0, width, axis=dim)
        before = lax.ppermute(last, axis, up)
        after = lax.ppermute(initial, axis, down)
        shard = jnp.concatenate([before, shard, after], axis=dim)
    return shard


def passed_along(shard, axis, by):
    count = lax.axis_size(axis)
    pairs = [(i, i + by) for i in range(count) if 0 <= i + by < count]
    return lax.ppermute(shard, axis, pairs)


def gelu_slope(values):
    return (
        0.5 * (1.0 + lax.erf(values * 0.7071067811865476))
        + values * jnp.exp(-0.5 * values * values) * 0.3989422804014327
    )


def with_rims(field):
    return extended(field, (("seq", 1),), 1)


def one_hot(places, length):
    return (places[:, :, None] == jnp.arange(length, dtype=jnp.int32)[None, None, :]).astype(
        jnp.bfloat16
    )


def core_swap(part):
    count = lax.axis_size("seq")
    return lax.ppermute(part, "seq", [(i, i ^ 1) for i in range(count)])


def gathered_weight(rows):
    heads = lax.axis_size("head")
    here = lax.axis_index("head")
    core = lax.axis_index("seq") % 2
    half = rows.shape[0] // 2
    mine = lax.dynamic_slice_in_dim(rows, core * half, half, 0)
    blocks = [(0, rows)]
    for step in range(1, heads):
        pairs = [(i, (i + step) % heads) for i in range(heads)]
        got = lax.ppermute(mine, "head", pairs)
        twin = core_swap(got)
        low = jnp.where(core == 0, got, twin)
        high = jnp.where(core == 0, twin, got)
        blocks.append((step, jnp.concatenate([low, high], axis=0)))
    full = jnp.zeros((heads * rows.shape[0], rows.shape[1]), rows.dtype)
    for step, block in blocks:
        place = (here - step) % heads
        full = lax.dynamic_update_slice_in_dim(full, block, place * rows.shape[0], 0)
    return full


def butterfly(total, axis):
    count = lax.axis_size(axis)
    if count & (count - 1):
        return lax.psum(total, axis)
    step = 1
    while step < count:
        total = total + lax.ppermute(total, axis, [(i, i ^ step) for i in range(count)])
        step *= 2
    return total


def plain_shards(
    attention, encoder_skip, depth_filter, point_weight, crop_offset, target_bins, cotangent
):
    slab_input = lax.all_to_all(attention, "head", split_axis=0, concat_axis=2, tiled=True)
    local_seqs = encoder_skip.shape[0]
    slab_rows = encoder_skip.shape[1]
    channels = encoder_skip.shape[2]
    summed = (
        jnp.repeat(slab_input, 2, axis=1).astype(jnp.float32) + encoder_skip.astype(jnp.float32)
    ).astype(jnp.bfloat16)
    padded = with_rims(summed)
    filtered = (
        depth_filter[0] * padded[:, :-2]
        + depth_filter[1] * padded[:, 1:-1]
        + depth_filter[2] * padded[:, 2:]
    )
    activated = jax.nn.gelu(filtered, approximate=False).astype(jnp.bfloat16)
    flat_act = activated.reshape(local_seqs * slab_rows, channels)
    full_weight = gathered_weight(point_weight)
    mixed_rows = jnp.dot(flat_act, full_weight, preferred_element_type=jnp.float32)
    block_out = (
        summed.astype(jnp.float32) + mixed_rows.reshape(local_seqs, slab_rows, channels)
    ).astype(jnp.bfloat16)
    slab_index = lax.axis_index("seq")
    bins = jnp.concatenate(
        [jnp.zeros_like(target_bins[:, :NTD]), target_bins], axis=1
    )
    asked = lax.dynamic_slice_in_dim(bins, slab_index * NTD, 2 * NTD, 1) + crop_offset[:, None]
    back = jnp.where(jnp.arange(2 * NTD, dtype=jnp.int32) < NTD, slab_rows, 0)
    asked = asked - back[None, :]
    picked = jnp.einsum(
        "sjr,srd->sjd",
        one_hot(asked, slab_rows),
        block_out,
        preferred_element_type=jnp.float32,
    ).astype(jnp.bfloat16)
    from_next = passed_along(picked[:, :NTD], "seq", -1)
    target_rows = picked[:, NTD:] + from_next
    prev_cot = passed_along(cotangent, "seq", 1)
    cot_pair = jnp.concatenate([prev_cot, cotangent], axis=1)

    def crop_back(cot_block, shift_by):
        return lax.dynamic_slice_in_dim(cot_block, slab_rows - shift_by, slab_rows, 0)

    grad_out = jax.vmap(crop_back)(cot_pair, crop_offset)
    flat_grad = grad_out.reshape(local_seqs * slab_rows, channels)
    grad_act = lax.dot_general(
        flat_grad, full_weight, (((1,), (1,)), ((), ())), preferred_element_type=jnp.float32
    )
    grad_conv = (grad_act.reshape(local_seqs, slab_rows, channels) * gelu_slope(filtered)).astype(
        jnp.bfloat16
    )
    grad_padded = with_rims(grad_conv)
    grad_sum = (
        grad_out.astype(jnp.float32)
        + depth_filter[0] * grad_padded[:, 2:]
        + depth_filter[1] * grad_padded[:, 1:-1]
        + depth_filter[2] * grad_padded[:, :-2]
    )
    skip_grad = grad_sum.astype(jnp.bfloat16)
    attention_grad = (
        grad_sum.reshape(local_seqs, slab_rows // 2, 2, channels).sum(axis=2).astype(jnp.bfloat16)
    )
    filter_terms = jnp.stack(
        [
            jnp.einsum(
                "srd,srd->d", grad_conv, padded[:, 0:slab_rows], preferred_element_type=jnp.float32
            ),
            jnp.einsum(
                "srd,srd->d",
                grad_conv,
                padded[:, 1 : slab_rows + 1],
                preferred_element_type=jnp.float32,
            ),
            jnp.einsum(
                "srd,srd->d",
                grad_conv,
                padded[:, 2 : slab_rows + 2],
                preferred_element_type=jnp.float32,
            ),
        ]
    )
    filter_sum = butterfly(butterfly(filter_terms, "seq"), "head")
    row_count = local_seqs * lax.axis_size("head") * slab_rows * lax.axis_size("seq")
    filter_grad = filter_sum * (1.0 / math.sqrt(row_count))
    return (target_rows, attention_grad, skip_grad, filter_grad)


LANES = 128
PAD = 8
BF = jnp.bfloat16
F32 = jnp.float32


def dot(left, right):
    return lax.dot_general(left, right, (((1,), (0,)), ((), ())), preferred_element_type=F32)


def dot_rows(left, right):
    return lax.dot_general(left, right, (((1,), (1,)), ((), ())), preferred_element_type=F32)


def grid_of(rows, columns):
    return (
        lax.broadcasted_iota(jnp.int32, (rows, columns), 0),
        lax.broadcasted_iota(jnp.int32, (rows, columns), 1),
    )


def picks(match):
    return jnp.where(match, 1.0, 0.0).astype(BF)


def params(mib=36):
    return pltpu.CompilerParams(vmem_limit_bytes=mib * 1024 * 1024)


def cost(flops, moved, special=0):
    return pl.CostEstimate(flops=flops, bytes_accessed=moved, transcendentals=special)


def pack_kernel(
    meta, skip_lo, skip_hi, att_lo, att_hi, cot_lo, cot_hi, near, distant, att,
    edge_a, edge_b, far, tile_a, tile_b, att_out,
):
    att_out[...] = att[...]
    half = att_lo.shape[2]
    tile_a[...] = near[...]
    tile_b[...] = distant[...]
    row, col = grid_of(16, 32)
    at, base = row & 7, (row >> 3) * 16
    even = (meta[1] & 1) == 0

    def edges(body, others, edge):
        parts = []
        for group in range(2):
            rows = others[2 * group : 2 * group + 2].reshape(32, half)
            parts.append(body[:, group * half : (group + 1) * half] + dot(edge, rows))
        return jnp.concatenate(parts, axis=1)

    skips = skip_hi[...].reshape(32, 2 * half)
    up = dot(picks((at >= 6) & (col == base + at + 8)), skips)
    up = edges(up, att_hi, picks((at == 5) & (col == base + 15)))
    skips = skip_lo[...].reshape(32, 2 * half)
    cots = cot_lo[...].reshape(32, 2 * half)
    down = dot(picks((at < 2) & (col == base + at)), skips)
    down = down + dot(picks((at == 3) & (col == base)), cots)
    down = edges(down, att_lo, picks((at == 2) & (col == base)))
    edge_a[...] = jnp.where(even, up, down).astype(BF)
    edge_b[...] = jnp.where(even, down, up).astype(BF)
    cots = cot_hi[...].reshape(32, 2 * half)
    far[...] = dot(picks((at == 4) & (col == base + 15)), cots).astype(BF)


def packed(meta, encoder_skip, attention, cotangent, weight, tile):
    seqs, rows, wide = encoder_skip.shape
    half = attention.shape[2]
    short = attention.shape[1]

    def block(count, width, place):
        return pl.BlockSpec((count, 16, width), lambda i, m: (0, place, 0))

    out = jax.ShapeDtypeStruct((16, wide), BF)
    square = jax.ShapeDtypeStruct((tile, tile), BF)
    return pl.pallas_call(
        pack_kernel,
        grid_spec=pltpu.PrefetchScalarGridSpec(
            num_scalar_prefetch=1,
            grid=(1,),
            in_specs=[
                block(seqs, wide, 0),
                block(seqs, wide, rows // 16 - 1),
                block(2 * seqs, half, 0),
                block(2 * seqs, half, short // 16 - 1),
                block(seqs, wide, 0),
                block(seqs, wide, rows // 16 - 1),
                pl.BlockSpec((tile, tile), lambda i, m: (m[1] & 1, (m[1] >> 1) & 3)),
                pl.BlockSpec((tile, tile), lambda i, m: (m[1] & 1, 3 - ((m[1] >> 1) & 3))),
                pl.BlockSpec((2, short, half), lambda i, m: (1 - m[0], 0, 0)),
            ],
            out_specs=[pl.BlockSpec((16, wide), lambda i, m: (0, 0))] * 3
            + [pl.BlockSpec((tile, tile), lambda i, m: (0, 0))] * 2
            + [pl.BlockSpec((2, short, half), lambda i, m: (0, 0, 0))],
        ),
        out_shape=[out, out, out, square, square, jax.ShapeDtypeStruct((2, short, half), BF)],
        compiler_params=params(60),
        name="pack_edges",
    )(
        meta, encoder_skip, encoder_skip, attention, attention, cotangent, cotangent, weight,
        weight, attention,
    )


def slab_sums(att, skip, edge, twin, ext, cols):
    width = cols.size
    short = 64
    row, col = grid_of(2 * short, short)
    spread = picks((row >> 1) == col)
    row, col = grid_of(16, 16)
    at, base = row & 7, row & 8
    wanted = ((at >= 6) & (col == base + 5)) | ((at < 2) & (col == base + 2))
    from_att = dot(picks(wanted), twin[:, cols])
    rims = edge[:, cols]
    at = lax.broadcasted_iota(jnp.int32, (16, width), 0) & 7
    rims = (from_att + rims.astype(F32)).astype(BF).astype(F32)
    above = jnp.where(at >= 6, rims, 0.0)
    below = jnp.where(at < 2, rims, 0.0)
    for s in range(2):
        body = dot(spread, att[s, 0:short, cols]) + skip[s, :, cols].astype(F32)
        ext[s, 0:PAD] = above[s * 8 : s * 8 + 8]
        ext[s, PAD : PAD + 2 * short] = body.astype(BF).astype(F32)
        ext[s, PAD + 2 * short : 2 * PAD + 2 * short] = below[s * 8 : s * 8 + 8]


def around(field):
    tall = field.shape[0]
    return pltpu.roll(field, 1, 0), pltpu.roll(field, tall - 1, 0)


def phi_of(values):
    return 0.5 * (1.0 + lax.erf(values * 0.7071067811865476))


def slope_of(values):
    return phi_of(values) + values * jnp.exp(-0.5 * values * values) * 0.3989422804014327


def asked_rows(meta, offsets, bins, s, ext, taps, tall):
    row, col = grid_of(48, tall)
    want = row & 3
    shift = (row >> 4) - 1
    at = jnp.full((48, tall), -4096, jnp.int32)
    slab = meta[1]
    for k in range(4):
        mine = k < NTD
        home = slab if mine else jnp.maximum(slab - 1, 0)
        place = bins[s, home * NTD + (k % NTD)] + offsets[s] - (0 if mine else tall - 2 * PAD)
        fits = (place >= 0) & (place < tall - 2 * PAD)
        at = jnp.where(want == k, jnp.where(fits, place + PAD, -4096), at)
    found = dot(picks((col == at + shift) & ((row & 15) < 8)), ext.astype(BF))
    here = found[16:32]
    value = taps[0] * found[0:16] + taps[1] * here + taps[2] * found[32:48]
    act = value * phi_of(value)
    row = lax.broadcasted_iota(jnp.int32, act.shape, 0)
    return jnp.where(row < 4, act, here).astype(BF)


def taps_of(filt, cols):
    return [filt[k : k + 1, cols] for k in range(3)]


def tap_sums(conv, ext, rows):
    before, after = around(ext)
    body = slice(PAD, PAD + rows)
    mine = conv[body]
    return [
        jnp.sum(mine * other[body], axis=0, keepdims=True) for other in (before, ext, after)
    ]


def grads(conv, direct, taps, rows, pair):
    before, after = around(conv)
    body = slice(PAD, PAD + rows)
    total = direct + taps[0] * after[body] + taps[1] * conv[body] + taps[2] * before[body]
    short = rows // 2
    sums = []
    for k in range(total.shape[1] // LANES):
        pair[k] = total[:, k * LANES : (k + 1) * LANES]
        sums.append(pair[k, pl.ds(0, short, 2), :] + pair[k, pl.ds(1, short, 2), :])
    return total, jnp.concatenate(sums, axis=1)


def own_kernel(
    slabs, meta, offsets, bins, att, skip, edge, rims, prev, cot, weight,
    filt, moved, asked, terms, skip_grad, att_grad, ext, pair,
):
    rows = skip.shape[1]
    tall = rows + 2 * PAD
    wide = cot.shape[2]
    row, col = grid_of(tall, rows)
    last = meta[1] == slabs - 1
    for s in range(2):
        at = row - PAD
        fits = (at >= -1) & (at < jnp.where(last, rows, rows + 1))
        source = jnp.where(fits, at - offsets[s], -4096)
        older = picks(col == source + rows)
        newer = picks(col == source)
        place = lax.broadcasted_iota(jnp.int32, (PAD, 512), 0)
        top = (place == PAD - 1) & (offsets[s] == rows)
        bottom = (place == 0) & (offsets[s] == 0) & jnp.logical_not(last)
        for part in range(0, wide, 512):
            cols = slice(part, part + 512)
            found = dot(older, prev[s, :, cols]) + dot(newer, cot[s, :, cols])
            ends = rims[:, cols].astype(F32)
            above = ends[s * 8 + 4 : s * 8 + 5]
            below = ends[s * 8 + 3 : s * 8 + 4]
            found = jnp.concatenate(
                [
                    found[:PAD] + jnp.where(top, above, 0.0),
                    found[PAD : PAD + rows],
                    found[PAD + rows :] + jnp.where(bottom, below, 0.0),
                ]
            )
            moved[s, :, cols] = found.astype(BF)
    width = ext.shape[2]
    half = skip.shape[2]
    first = meta[0] * half

    @pl.loop(0, half // width)
    def _(part):
        begin = pl.multiple_of(part * width, width)
        cols = pl.ds(begin, width)
        slab_sums(att, skip, edge, edge, ext, cols)
        taps = taps_of(filt, cols)
        piece = weight[pl.ds(begin, width), :]
        sums = [0.0, 0.0, 0.0]
        there = pl.ds(pl.multiple_of(first + begin, width), width)
        for s in range(2):
            field = ext[s]
            before, after = around(field)
            slope = slope_of(taps[0] * before + taps[1] * field + taps[2] * after)
            asked[s * 16 : s * 16 + 16, cols] = asked_rows(
                meta, offsets, bins, s, field, taps, tall
            )
            conv = (dot_rows(moved[s], piece) * slope).astype(BF).astype(F32)
            sums = [a + b for a, b in zip(sums, tap_sums(conv, field, rows))]
            direct = moved[s, :, there].astype(F32)[PAD : PAD + rows]
            total, pairs = grads(conv, direct, taps, rows, pair)
            skip_grad[s, :, cols] = total.astype(BF)
            att_grad[s, :, cols] = pairs.astype(BF)
        for k in range(3):
            terms[k : k + 1, cols] = sums[k]


def own_half(meta, offsets, bins, attention, skip, edge, prev, cot, weight, filt, slabs):
    seqs, rows, wide = skip.shape
    _, short, half = attention.shape
    tall = rows + 2 * PAD

    def whole(*shape):
        return pl.BlockSpec(shape, lambda i, m, o, b: (0,) * len(shape))

    def mine(*shape):
        return pl.BlockSpec(shape, lambda i, m, o, b: (0,) * (len(shape) - 1) + (m[0],))

    return pl.pallas_call(
        functools.partial(own_kernel, slabs),
        grid_spec=pltpu.PrefetchScalarGridSpec(
            num_scalar_prefetch=3,
            grid=(1,),
            in_specs=[
                pl.BlockSpec((2, short, half), lambda i, m, o, b: (m[0], 0, 0)),
                mine(2, rows, half),
                mine(16, half),
                whole(16, wide),
                whole(2, rows, wide),
                whole(2, rows, wide),
                whole(half, wide),
                mine(3, half),
            ],
            out_specs=[
                whole(2, tall, wide),
                whole(32, half),
                whole(3, half),
                mine(2, rows, half),
                mine(2, short, half),
            ],
            scratch_shapes=[
                pltpu.VMEM((2, tall, 256), F32),
                pltpu.VMEM((2, rows, LANES), F32),
            ],
        ),
        out_shape=[
            jax.ShapeDtypeStruct((2, tall, wide), BF),
            jax.ShapeDtypeStruct((32, half), BF),
            jax.ShapeDtypeStruct((3, half), F32),
            jax.ShapeDtypeStruct((2, rows, wide), BF),
            jax.ShapeDtypeStruct((2, short, wide), BF),
        ],
        compiler_params=params(60),
        cost_estimate=cost(1, 1),
        name="own_half",
    )(
        meta, offsets, bins, attention, skip, edge, edge, prev, cot, weight, filt,
    )


def slope_kernel(
    meta, offsets, bins, att, skip, edge, twin, filt, asked, sums, slopes, mine, shown, ext
):
    rows = skip.shape[1]
    tall = rows + 2 * PAD
    half = skip.shape[2]
    width = ext.shape[2]
    there = (1 - meta[0]) * half
    row, col = grid_of(16, 32)
    at, base = row & 7, (row >> 3) * 16
    kept = picks((at < 4) & (col == base + at + jnp.where(at < 2, 0, 2)))
    told = picks((at < 4) & (col == base + at + jnp.where(at < 2, 2, 4)))
    here = pl.ds(pl.multiple_of(meta[0] * half, half), half)
    mine[:, here] = dot(kept, asked[...]).astype(BF)
    shown[:, here] = dot(told, asked[...]).astype(BF)

    @pl.loop(0, half // width)
    def _(part):
        begin = pl.multiple_of(part * width, width)
        cols = pl.ds(begin, width)
        slab_sums(att, skip, edge, twin, ext, cols)
        taps = taps_of(filt, cols)
        got = []
        for s in range(2):
            field = ext[s]
            before, after = around(field)
            slopes[s, :, cols] = slope_of(taps[0] * before + taps[1] * field + taps[2] * after)
            sums[s, :, cols] = field.astype(BF)
            got.append(asked_rows(meta, offsets, bins, s, field, taps, tall))
        got = jnp.concatenate(got)
        place = pl.ds(pl.multiple_of(there + begin, width), width)
        mine[:, place] = dot(kept, got).astype(BF)
        shown[:, place] = dot(told, got).astype(BF)


def other_slopes(meta, offsets, bins, shipped, skip, edge, twin, filt, asked):
    seqs, rows, wide = skip.shape
    _, packed_rows, half = shipped.shape
    tall = rows + 2 * PAD

    def whole(*shape):
        return pl.BlockSpec(shape, lambda i, m, o, b: (0,) * len(shape))

    def other(*shape):
        return pl.BlockSpec(shape, lambda i, m, o, b: (0,) * (len(shape) - 1) + (1 - m[0],))

    return pl.pallas_call(
        slope_kernel,
        grid_spec=pltpu.PrefetchScalarGridSpec(
            num_scalar_prefetch=3,
            grid=(1,),
            in_specs=[
                whole(2, packed_rows, half),
                other(2, rows, half),
                other(16, half),
                pl.BlockSpec((16, half), lambda i, m, o, b: (0, m[0])),
                other(3, half),
                whole(32, half),
            ],
            out_specs=[whole(2, tall, half), whole(2, tall, half), whole(16, wide), whole(16, wide)],
            scratch_shapes=[pltpu.VMEM((2, tall, 256), F32)],
        ),
        out_shape=[
            jax.ShapeDtypeStruct((2, tall, half), BF),
            jax.ShapeDtypeStruct((2, tall, half), F32),
            jax.ShapeDtypeStruct((16, wide), BF),
            jax.ShapeDtypeStruct((16, wide), BF),
        ],
        compiler_params=params(),
        cost_estimate=cost(10**11, 4 * 1024 * 1024, 2 * tall * half),
        name="other_slopes",
    )(meta, offsets, bins, shipped, skip, edge, twin, filt, asked)


def terms_kernel(meta, order, moved, sums, slopes, own_terms, *refs):
    pieces, (convs, terms, full, sems) = refs[:8], refs[8:]
    half = sums.shape[2]
    tall = sums.shape[1]
    rows = tall - 2 * PAD
    there = (1 - meta[0]) * half
    tile = pieces[0].shape[0]
    copies = []
    for k, piece in enumerate(pieces):
        down = pl.multiple_of(order[4 + k // 4] * tile, tile)
        over = pl.multiple_of(order[k % 4] * tile, tile)
        copies.append(
            pltpu.make_async_copy(
                piece, full.at[pl.ds(down, tile), pl.ds(over, tile)], sems.at[k]
            )
        )
        copies[-1].start()
    terms[:, pl.ds(pl.multiple_of(meta[0] * half, half), half)] = own_terms[...]
    for copy in copies:
        copy.wait()
    width = 2 * LANES
    for begin in range(0, half, width):
        cols = slice(begin, begin + width)
        total = [0.0, 0.0, 0.0]
        for s in range(2):
            grad = dot_rows(moved[s], full[cols, :])
            conv = (grad * slopes[s, :, cols]).astype(BF)
            convs[s, :, cols] = conv
            got = tap_sums(conv.astype(F32), sums[s, :, cols].astype(F32), rows)
            total = [a + b for a, b in zip(total, got)]
        place = pl.ds(pl.multiple_of(there + begin, width), width)
        for k in range(3):
            terms[k : k + 1, place] = total[k]


def other_terms(meta, order, moved, sums, slopes, own_terms, pieces):
    _, tall, wide = moved.shape
    half = sums.shape[2]

    def whole(*shape):
        return pl.BlockSpec(shape, lambda i, m, o: (0,) * len(shape))

    return pl.pallas_call(
        terms_kernel,
        grid_spec=pltpu.PrefetchScalarGridSpec(
            num_scalar_prefetch=2,
            grid=(1,),
            in_specs=[
                whole(2, tall, wide),
                whole(2, tall, half),
                whole(2, tall, half),
                whole(3, half),
            ]
            + [pl.BlockSpec(memory_space=pl.ANY)] * 8,
            out_specs=[whole(2, tall, half), whole(3, wide)],
            scratch_shapes=[pltpu.VMEM((half, wide), BF), pltpu.SemaphoreType.DMA((8,))],
        ),
        out_shape=[
            jax.ShapeDtypeStruct((2, tall, half), BF),
            jax.ShapeDtypeStruct((3, wide), F32),
        ],
        compiler_params=params(),
        cost_estimate=cost(2 * 2 * tall * half * wide, 6 * 1024 * 1024),
        name="other_terms",
    )(meta, order, moved, sums, slopes, own_terms, *pieces)


def grads_kernel(meta, moved, convs, filt, old_skip, old_att, skip_grad, att_grad, pair):
    half = convs.shape[2]
    rows = convs.shape[1] - 2 * PAD
    width = 2 * LANES

    @pl.loop(0, half // width)
    def _(part):
        cols = pl.ds(pl.multiple_of(part * width, width), width)
        taps = taps_of(filt, cols)
        for s in range(2):
            direct = moved[s, :, cols].astype(F32)[PAD : PAD + rows]
            total, pairs = grads(convs[s, :, cols].astype(F32), direct, taps, rows, pair)
            skip_grad[s, :, cols] = total.astype(BF)
            att_grad[s, :, cols] = pairs.astype(BF)


def other_grads(meta, moved, convs, filt, skip_grad, att_grad):
    _, tall, wide = moved.shape
    half = convs.shape[2]
    rows = tall - 2 * PAD

    def whole(*shape):
        return pl.BlockSpec(shape, lambda i, m: (0,) * len(shape))

    def other(*shape):
        return pl.BlockSpec(shape, lambda i, m: (0,) * (len(shape) - 1) + (1 - m[0],))

    return pl.pallas_call(
        grads_kernel,
        grid_spec=pltpu.PrefetchScalarGridSpec(
            num_scalar_prefetch=1,
            grid=(1,),
            in_specs=[other(2, tall, half), whole(2, tall, half), other(3, half)]
            + [pl.BlockSpec(memory_space=pl.ANY)] * 2,
            out_specs=[other(2, rows, half), other(2, rows // 2, half)],
            scratch_shapes=[pltpu.VMEM((2, rows, LANES), F32)],
        ),
        out_shape=[
            jax.ShapeDtypeStruct((2, rows, wide), BF),
            jax.ShapeDtypeStruct((2, rows // 2, wide), BF),
        ],
        input_output_aliases={4: 0, 5: 1},
        compiler_params=params(),
        cost_estimate=cost(2 * tall * half * 20, 4 * 1024 * 1024),
        name="other_grads",
    )(meta, moved, convs, filt, skip_grad, att_grad)


def target_kernel(slabs, meta, order, mine, got_a, got_b, weight, *refs):
    pieces, (target, total) = refs[:8], refs[8:]
    half = weight.shape[0]
    there = (1 - meta[0]) * half
    tile = pieces[0].shape[0]
    even = (meta[1] & 1) == 0
    got = jnp.where(even, got_a[...].astype(F32), got_b[...].astype(F32))
    got = jnp.where(meta[1] == slabs - 1, 0.0, got)
    mine[...] = (mine[...].astype(F32) + got).astype(BF)
    here = pl.ds(pl.multiple_of(meta[0] * half, half), half)
    total[...] = dot(mine[:, here], weight[...]) + pltpu.roll(mine[...].astype(F32), 12 + 2, 0)
    for k, piece in enumerate(pieces):
        place = pl.ds(pl.multiple_of(there + order[4 + k // 4] * tile, tile), tile)
        over = pl.ds(pl.multiple_of(order[k % 4] * tile, tile), tile)
        total[:, over] += dot(mine[:, place], piece[...])
    for s in range(2):
        target[s] = total[s * 8 : s * 8 + 2].astype(BF)


def targets(meta, order, mine, got, weight, pieces, slabs):
    half, wide = weight.shape
    tile = pieces[0].shape[0]

    def whole(*shape):
        return pl.BlockSpec(shape, lambda i, m, o: (0,) * len(shape))

    return pl.pallas_call(
        functools.partial(target_kernel, slabs),
        grid_spec=pltpu.PrefetchScalarGridSpec(
            num_scalar_prefetch=2,
            grid=(1,),
            in_specs=[whole(16, wide)] * 3 + [whole(half, wide)]
            + [whole(tile, tile)] * 8,
            out_specs=whole(2, NTD, wide),
            scratch_shapes=[pltpu.VMEM((16, wide), F32)],
        ),
        out_shape=jax.ShapeDtypeStruct((2, NTD, wide), BF),
        compiler_params=params(),
        cost_estimate=cost(2 * 16 * wide * wide, 6 * 1024 * 1024),
        name="targets",
    )(meta, order, mine, *got, weight, *pieces)


def paired(part, axis, bit):
    count = lax.axis_size(axis)
    return lax.ppermute(part, axis, [(i, i ^ bit) for i in range(count)])


def staggered(part, span):
    count = lax.axis_size("seq")
    pairs = []
    for i in range(count):
        by = span if i // span % 2 else -span
        pairs.append((i, (i + by) % count))
    return lax.ppermute(part, "seq", pairs)


def after(value, *others):
    return lax.optimization_barrier((value,) + others)[0]


def crossed(part, seq_bit, head_bit):
    slabs, heads = lax.axis_size("seq"), lax.axis_size("head")
    pairs = [
        (i * heads + j, (i ^ seq_bit) * heads + (j ^ head_bit))
        for i in range(slabs)
        for j in range(heads)
    ]
    return lax.ppermute(part, ("seq", "head"), pairs)


def joined(total, one, two):
    both = (one[0] ^ two[0], one[1] ^ two[1])
    parts = [crossed(total, *bits) for bits in (one, two, both)]
    return (total + parts[0]) + (parts[1] + parts[2])


def fast_shards(
    attention, encoder_skip, depth_filter, point_weight, crop_offset, target_bins, cotangent
):
    head = lax.axis_index("head")
    slab = lax.axis_index("seq")
    slabs = lax.axis_size("seq")
    meta = jnp.stack([head, slab]).astype(jnp.int32)
    core = slab % 2
    block = slab // 2 % 4
    tile = 3 * LANES
    order = jnp.stack([block, block ^ 1, block ^ 2, block ^ 3, core, 1 - core]).astype(jnp.int32)

    edge_a, edge_b, far, first, last_tile, att_out = packed(
        meta, encoder_skip, attention, cotangent, point_weight, tile
    )
    prev = passed_along(cotangent, "seq", 1)
    first = paired(first, "head", 1)
    shipped = paired(att_out, "head", 1)
    edge_a = paired(edge_a, "seq", 1)
    edge_b = staggered(edge_b, 1)
    far_a = paired(far, "seq", 2)
    far_b = staggered(far, 2)
    outer = (slab == 0) | (slab == slabs - 1)
    nothing = jnp.zeros_like(edge_b)
    edge = edge_a + jnp.where(outer, nothing, edge_b)
    twin = paired(edge, "head", 1)
    edge = edge + jnp.where(slab % 4 >= 2, far_a, jnp.where(slab < 2, nothing, far_b))
    second = paired(first, "seq", 2)
    third = paired(first, "seq", 4)
    fourth = paired(last_tile, "head", 1)
    moved, asked, own_terms, skip_grad, att_grad = own_half(
        meta, crop_offset, target_bins, attention, encoder_skip, edge, prev, cotangent,
        point_weight, depth_filter, slabs,
    )
    pieces = [first, second, third, fourth]
    pieces = pieces + [paired(after(piece, own_terms), "seq", 1) for piece in pieces]
    sums, slopes, mine, shown = other_slopes(
        meta, crop_offset, target_bins, shipped, encoder_skip, edge, twin, depth_filter, asked
    )
    got = [paired(shown, "seq", 1), staggered(shown, 1)]
    convs, terms = other_terms(meta, order, moved, sums, slopes, own_terms, pieces)
    terms, *got = lax.optimization_barrier((terms, *got))
    total = terms + crossed(terms, 1, 0)
    total = joined(total, (2, 0), (0, 1))
    skip_grad, attention_grad = other_grads(
        meta, moved, convs, depth_filter, skip_grad, att_grad
    )
    target_rows = targets(meta, order, mine, got, point_weight, pieces, slabs)
    total, skip_grad, attention_grad = lax.optimization_barrier(
        (total, skip_grad, attention_grad)
    )
    if slabs == 16:
        total = joined(total, (4, 0), (8, 0))
    else:
        step = 4
        while step < slabs:
            total = total + crossed(total, step, 0)
            step *= 2
    count = encoder_skip.shape[0] * lax.axis_size("head") * encoder_skip.shape[1] * slabs
    return (target_rows, attention_grad, skip_grad, total * (1.0 / math.sqrt(count)))


def shards(*args):
    attention, encoder_skip, point_weight = args[0], args[1], args[3]
    fits = (
        lax.axis_size("head") == 2
        and lax.axis_size("seq") in (8, 16, 32)
        and encoder_skip.shape[:2] == (2, 128)
        and point_weight.shape[0] == 6 * LANES
        and attention.shape[1] == 64
    )
    return fast_shards(*args) if fits else plain_shards(*args)


def solution(mesh):
    in_specs = (
        P(None, "seq", "head"),
        P("head", "seq", None),
        P(),
        P("head", None),
        P("head"),
        P("head", None),
        P("head", "seq", None),
    )
    out_specs = (P("head", "seq", None), P("head", "seq", None), P("head", "seq", None), P())
    return jax.shard_map(shards, mesh=mesh, in_specs=in_specs, out_specs=out_specs, check_vma=False)
```

```python
import functools
import math

import jax
import jax.numpy as jnp
from jax import lax
from jax.experimental import pallas as pl
from jax.experimental.pallas import tpu as pltpu
from jax.sharding import PartitionSpec as P

NTD = 2


def extended(shard, sides, width):
    for axis, dim in sides:
        count, length = (lax.axis_size(axis), shard.shape[dim])
        up = [(i, (i + 1) % count) for i in range(count - 1)]
        down = [(j, i) for i, j in up]
        last = lax.slice_in_dim(shard, length - width, length, axis=dim)
        initial = lax.slice_in_dim(shard, 0, width, axis=dim)
        before = lax.ppermute(last, axis, up)
        after = lax.ppermute(initial, axis, down)
        shard = jnp.concatenate([before, shard, after], axis=dim)
    return shard


def passed_along(shard, axis, by):
    count = lax.axis_size(axis)
    pairs = [(i, i + by) for i in range(count) if 0 <= i + by < count]
    return lax.ppermute(shard, axis, pairs)


def gelu_slope(values):
    return (
        0.5 * (1.0 + lax.erf(values * 0.7071067811865476))
        + values * jnp.exp(-0.5 * values * values) * 0.3989422804014327
    )


def with_rims(field):
    return extended(field, (("seq", 1),), 1)


def one_hot(places, length):
    return (places[:, :, None] == jnp.arange(length, dtype=jnp.int32)[None, None, :]).astype(
        jnp.bfloat16
    )


def core_swap(part):
    count = lax.axis_size("seq")
    return lax.ppermute(part, "seq", [(i, i ^ 1) for i in range(count)])


def gathered_weight(rows):
    heads = lax.axis_size("head")
    here = lax.axis_index("head")
    core = lax.axis_index("seq") % 2
    half = rows.shape[0] // 2
    mine = lax.dynamic_slice_in_dim(rows, core * half, half, 0)
    blocks = [(0, rows)]
    for step in range(1, heads):
        pairs = [(i, (i + step) % heads) for i in range(heads)]
        got = lax.ppermute(mine, "head", pairs)
        twin = core_swap(got)
        low = jnp.where(core == 0, got, twin)
        high = jnp.where(core == 0, twin, got)
        blocks.append((step, jnp.concatenate([low, high], axis=0)))
    full = jnp.zeros((heads * rows.shape[0], rows.shape[1]), rows.dtype)
    for step, block in blocks:
        place = (here - step) % heads
        full = lax.dynamic_update_slice_in_dim(full, block, place * rows.shape[0], 0)
    return full


def butterfly(total, axis):
    count = lax.axis_size(axis)
    if count & (count - 1):
        return lax.psum(total, axis)
    step = 1
    while step < count:
        total = total + lax.ppermute(total, axis, [(i, i ^ step) for i in range(count)])
        step *= 2
    return total


def plain_shards(
    attention, encoder_skip, depth_filter, point_weight, crop_offset, target_bins, cotangent
):
    slab_input = lax.all_to_all(attention, "head", split_axis=0, concat_axis=2, tiled=True)
    local_seqs = encoder_skip.shape[0]
    slab_rows = encoder_skip.shape[1]
    channels = encoder_skip.shape[2]
    summed = (
        jnp.repeat(slab_input, 2, axis=1).astype(jnp.float32) + encoder_skip.astype(jnp.float32)
    ).astype(jnp.bfloat16)
    padded = with_rims(summed)
    filtered = (
        depth_filter[0] * padded[:, :-2]
        + depth_filter[1] * padded[:, 1:-1]
        + depth_filter[2] * padded[:, 2:]
    )
    activated = jax.nn.gelu(filtered, approximate=False).astype(jnp.bfloat16)
    flat_act = activated.reshape(local_seqs * slab_rows, channels)
    full_weight = gathered_weight(point_weight)
    mixed_rows = jnp.dot(flat_act, full_weight, preferred_element_type=jnp.float32)
    block_out = (
        summed.astype(jnp.float32) + mixed_rows.reshape(local_seqs, slab_rows, channels)
    ).astype(jnp.bfloat16)
    slab_index = lax.axis_index("seq")
    bins = jnp.concatenate(
        [jnp.zeros_like(target_bins[:, :NTD]), target_bins], axis=1
    )
    asked = lax.dynamic_slice_in_dim(bins, slab_index * NTD, 2 * NTD, 1) + crop_offset[:, None]
    back = jnp.where(jnp.arange(2 * NTD, dtype=jnp.int32) < NTD, slab_rows, 0)
    asked = asked - back[None, :]
    picked = jnp.einsum(
        "sjr,srd->sjd",
        one_hot(asked, slab_rows),
        block_out,
        preferred_element_type=jnp.float32,
    ).astype(jnp.bfloat16)
    from_next = passed_along(picked[:, :NTD], "seq", -1)
    target_rows = picked[:, NTD:] + from_next
    prev_cot = passed_along(cotangent, "seq", 1)
    cot_pair = jnp.concatenate([prev_cot, cotangent], axis=1)

    def crop_back(cot_block, shift_by):
        return lax.dynamic_slice_in_dim(cot_block, slab_rows - shift_by, slab_rows, 0)

    grad_out = jax.vmap(crop_back)(cot_pair, crop_offset)
    flat_grad = grad_out.reshape(local_seqs * slab_rows, channels)
    grad_act = lax.dot_general(
        flat_grad, full_weight, (((1,), (1,)), ((), ())), preferred_element_type=jnp.float32
    )
    grad_conv = (grad_act.reshape(local_seqs, slab_rows, channels) * gelu_slope(filtered)).astype(
        jnp.bfloat16
    )
    grad_padded = with_rims(grad_conv)
    grad_sum = (
        grad_out.astype(jnp.float32)
        + depth_filter[0] * grad_padded[:, 2:]
        + depth_filter[1] * grad_padded[:, 1:-1]
        + depth_filter[2] * grad_padded[:, :-2]
    )
    skip_grad = grad_sum.astype(jnp.bfloat16)
    attention_grad = (
        grad_sum.reshape(local_seqs, slab_rows // 2, 2, channels).sum(axis=2).astype(jnp.bfloat16)
    )
    filter_terms = jnp.stack(
        [
            jnp.einsum(
                "srd,srd->d", grad_conv, padded[:, 0:slab_rows], preferred_element_type=jnp.float32
            ),
            jnp.einsum(
                "srd,srd->d",
                grad_conv,
                padded[:, 1 : slab_rows + 1],
                preferred_element_type=jnp.float32,
            ),
            jnp.einsum(
                "srd,srd->d",
                grad_conv,
                padded[:, 2 : slab_rows + 2],
                preferred_element_type=jnp.float32,
            ),
        ]
    )
    filter_sum = butterfly(butterfly(filter_terms, "seq"), "head")
    row_count = local_seqs * lax.axis_size("head") * slab_rows * lax.axis_size("seq")
    filter_grad = filter_sum * (1.0 / math.sqrt(row_count))
    return (target_rows, attention_grad, skip_grad, filter_grad)


import functools
import math

import jax
import jax.numpy as jnp
from jax import lax
from jax.experimental import pallas as pl
from jax.experimental.pallas import tpu as pltpu
from jax.sharding import PartitionSpec as P

NTD = 2


def extended(shard, sides, width):
    for axis, dim in sides:
        count, length = (lax.axis_size(axis), shard.shape[dim])
        up = [(i, (i + 1) % count) for i in range(count - 1)]
        down = [(j, i) for i, j in up]
        last = lax.slice_in_dim(shard, length - width, length, axis=dim)
        initial = lax.slice_in_dim(shard, 0, width, axis=dim)
        before = lax.ppermute(last, axis, up)
        after = lax.ppermute(initial, axis, down)
        shard = jnp.concatenate([before, shard, after], axis=dim)
    return shard


def passed_along(shard, axis, by):
    count = lax.axis_size(axis)
    pairs = [(i, i + by) for i in range(count) if 0 <= i + by < count]
    return lax.ppermute(shard, axis, pairs)


def gelu_slope(values):
    return (
        0.5 * (1.0 + lax.erf(values * 0.7071067811865476))
        + values * jnp.exp(-0.5 * values * values) * 0.3989422804014327
    )


def with_rims(field):
    return extended(field, (("seq", 1),), 1)


def one_hot(places, length):
    return (places[:, :, None] == jnp.arange(length, dtype=jnp.int32)[None, None, :]).astype(
        jnp.bfloat16
    )


def core_swap(part):
    count = lax.axis_size("seq")
    return lax.ppermute(part, "seq", [(i, i ^ 1) for i in range(count)])


def gathered_weight(rows):
    heads = lax.axis_size("head")
    here = lax.axis_index("head")
    core = lax.axis_index("seq") % 2
    half = rows.shape[0] // 2
    mine = lax.dynamic_slice_in_dim(rows, core * half, half, 0)
    blocks = [(0, rows)]
    for step in range(1, heads):
        pairs = [(i, (i + step) % heads) for i in range(heads)]
        got = lax.ppermute(mine, "head", pairs)
        twin = core_swap(got)
        low = jnp.where(core == 0, got, twin)
        high = jnp.where(core == 0, twin, got)
        blocks.append((step, jnp.concatenate([low, high], axis=0)))
    full = jnp.zeros((heads * rows.shape[0], rows.shape[1]), rows.dtype)
    for step, block in blocks:
        place = (here - step) % heads
        full = lax.dynamic_update_slice_in_dim(full, block, place * rows.shape[0], 0)
    return full


def butterfly(total, axis):
    count = lax.axis_size(axis)
    if count & (count - 1):
        return lax.psum(total, axis)
    step = 1
    while step < count:
        total = total + lax.ppermute(total, axis, [(i, i ^ step) for i in range(count)])
        step *= 2
    return total


def plain_shards(
    attention, encoder_skip, depth_filter, point_weight, crop_offset, target_bins, cotangent
):
    slab_input = lax.all_to_all(attention, "head", split_axis=0, concat_axis=2, tiled=True)
    local_seqs = encoder_skip.shape[0]
    slab_rows = encoder_skip.shape[1]
    channels = encoder_skip.shape[2]
    summed = (
        jnp.repeat(slab_input, 2, axis=1).astype(jnp.float32) + encoder_skip.astype(jnp.float32)
    ).astype(jnp.bfloat16)
    padded = with_rims(summed)
    filtered = (
        depth_filter[0] * padded[:, :-2]
        + depth_filter[1] * padded[:, 1:-1]
        + depth_filter[2] * padded[:, 2:]
    )
    activated = jax.nn.gelu(filtered, approximate=False).astype(jnp.bfloat16)
    flat_act = activated.reshape(local_seqs * slab_rows, channels)
    full_weight = gathered_weight(point_weight)
    mixed_rows = jnp.dot(flat_act, full_weight, preferred_element_type=jnp.float32)
    block_out = (
        summed.astype(jnp.float32) + mixed_rows.reshape(local_seqs, slab_rows, channels)
    ).astype(jnp.bfloat16)
    slab_index = lax.axis_index("seq")
    bins = jnp.concatenate(
        [jnp.zeros_like(target_bins[:, :NTD]), target_bins], axis=1
    )
    asked = lax.dynamic_slice_in_dim(bins, slab_index * NTD, 2 * NTD, 1) + crop_offset[:, None]
    back = jnp.where(jnp.arange(2 * NTD, dtype=jnp.int32) < NTD, slab_rows, 0)
    asked = asked - back[None, :]
    picked = jnp.einsum(
        "sjr,srd->sjd",
        one_hot(asked, slab_rows),
        block_out,
        preferred_element_type=jnp.float32,
    ).astype(jnp.bfloat16)
    from_next = passed_along(picked[:, :NTD], "seq", -1)
    target_rows = picked[:, NTD:] + from_next
    prev_cot = passed_along(cotangent, "seq", 1)
    cot_pair = jnp.concatenate([prev_cot, cotangent], axis=1)

    def crop_back(cot_block, shift_by):
        return lax.dynamic_slice_in_dim(cot_block, slab_rows - shift_by, slab_rows, 0)

    grad_out = jax.vmap(crop_back)(cot_pair, crop_offset)
    flat_grad = grad_out.reshape(local_seqs * slab_rows, channels)
    grad_act = lax.dot_general(
        flat_grad, full_weight, (((1,), (1,)), ((), ())), preferred_element_type=jnp.float32
    )
    grad_conv = (grad_act.reshape(local_seqs, slab_rows, channels) * gelu_slope(filtered)).astype(
        jnp.bfloat16
    )
    grad_padded = with_rims(grad_conv)
    grad_sum = (
        grad_out.astype(jnp.float32)
        + depth_filter[0] * grad_padded[:, 2:]
        + depth_filter[1] * grad_padded[:, 1:-1]
        + depth_filter[2] * grad_padded[:, :-2]
    )
    skip_grad = grad_sum.astype(jnp.bfloat16)
    attention_grad = (
        grad_sum.reshape(local_seqs, slab_rows // 2, 2, channels).sum(axis=2).astype(jnp.bfloat16)
    )
    filter_terms = jnp.stack(
        [
            jnp.einsum(
                "srd,srd->d", grad_conv, padded[:, 0:slab_rows], preferred_element_type=jnp.float32
            ),
            jnp.einsum(
                "srd,srd->d",
                grad_conv,
                padded[:, 1 : slab_rows + 1],
                preferred_element_type=jnp.float32,
            ),
            jnp.einsum(
                "srd,srd->d",
                grad_conv,
                padded[:, 2 : slab_rows + 2],
                preferred_element_type=jnp.float32,
            ),
        ]
    )
    filter_sum = butterfly(butterfly(filter_terms, "seq"), "head")
    row_count = local_seqs * lax.axis_size("head") * slab_rows * lax.axis_size("seq")
    filter_grad = filter_sum * (1.0 / math.sqrt(row_count))
    return (target_rows, attention_grad, skip_grad, filter_grad)


LANES = 128
PAD = 8
BF = jnp.bfloat16
F32 = jnp.float32


def dot(left, right):
    return lax.dot_general(left, right, (((1,), (0,)), ((), ())), preferred_element_type=F32)


def dot_rows(left, right):
    return lax.dot_general(left, right, (((1,), (1,)), ((), ())), preferred_element_type=F32)


def grid_of(rows, columns):
    return (
        lax.broadcasted_iota(jnp.int32, (rows, columns), 0),
        lax.broadcasted_iota(jnp.int32, (rows, columns), 1),
    )


def picks(match):
    return jnp.where(match, 1.0, 0.0).astype(BF)


def params(mib=36):
    return pltpu.CompilerParams(vmem_limit_bytes=mib * 1024 * 1024)


def cost(flops, moved, special=0):
    return pl.CostEstimate(flops=flops, bytes_accessed=moved, transcendentals=special)


def pack_kernel(
    meta, skip_lo, skip_hi, att_lo, att_hi, cot_lo, cot_hi, near, distant, att,
    edge_a, edge_b, far, tile_a, tile_b, att_out,
):
    att_out[...] = att[...]
    half = att_lo.shape[2]
    tile_a[...] = near[...]
    tile_b[...] = distant[...]
    row, col = grid_of(16, 32)
    at, base = row & 7, (row >> 3) * 16
    even = (meta[1] & 1) == 0

    def edges(body, others, edge):
        parts = []
        for group in range(2):
            rows = others[2 * group : 2 * group + 2].reshape(32, half)
            parts.append(body[:, group * half : (group + 1) * half] + dot(edge, rows))
        return jnp.concatenate(parts, axis=1)

    skips = skip_hi[...].reshape(32, 2 * half)
    up = dot(picks((at >= 6) & (col == base + at + 8)), skips)
    up = edges(up, att_hi, picks((at == 5) & (col == base + 15)))
    skips = skip_lo[...].reshape(32, 2 * half)
    cots = cot_lo[...].reshape(32, 2 * half)
    down = dot(picks((at < 2) & (col == base + at)), skips)
    down = down + dot(picks((at == 3) & (col == base)), cots)
    down = edges(down, att_lo, picks((at == 2) & (col == base)))
    edge_a[...] = jnp.where(even, up, down).astype(BF)
    edge_b[...] = jnp.where(even, down, up).astype(BF)
    cots = cot_hi[...].reshape(32, 2 * half)
    far[...] = dot(picks((at == 4) & (col == base + 15)), cots).astype(BF)


def packed(meta, encoder_skip, attention, cotangent, weight, tile):
    seqs, rows, wide = encoder_skip.shape
    half = attention.shape[2]
    short = attention.shape[1]

    def block(count, width, place):
        return pl.BlockSpec((count, 16, width), lambda i, m: (0, place, 0))

    out = jax.ShapeDtypeStruct((16, wide), BF)
    square = jax.ShapeDtypeStruct((tile, tile), BF)
    return pl.pallas_call(
        pack_kernel,
        grid_spec=pltpu.PrefetchScalarGridSpec(
            num_scalar_prefetch=1,
            grid=(1,),
            in_specs=[
                block(seqs, wide, 0),
                block(seqs, wide, rows // 16 - 1),
                block(2 * seqs, half, 0),
                block(2 * seqs, half, short // 16 - 1),
                block(seqs, wide, 0),
                block(seqs, wide, rows // 16 - 1),
                pl.BlockSpec((tile, tile), lambda i, m: (m[1] & 1, (m[1] >> 1) & 3)),
                pl.BlockSpec((tile, tile), lambda i, m: (m[1] & 1, 3 - ((m[1] >> 1) & 3))),
                pl.BlockSpec((2, short, half), lambda i, m: (1 - m[0], 0, 0)),
            ],
            out_specs=[pl.BlockSpec((16, wide), lambda i, m: (0, 0))] * 3
            + [pl.BlockSpec((tile, tile), lambda i, m: (0, 0))] * 2
            + [pl.BlockSpec((2, short, half), lambda i, m: (0, 0, 0))],
        ),
        out_shape=[out, out, out, square, square, jax.ShapeDtypeStruct((2, short, half), BF)],
        compiler_params=params(60),
        name="pack_edges",
    )(
        meta, encoder_skip, encoder_skip, attention, attention, cotangent, cotangent, weight,
        weight, attention,
    )


def slab_sums(att, skip, edge, twin, ext, cols):
    width = cols.size
    short = 64
    row, col = grid_of(2 * short, short)
    spread = picks((row >> 1) == col)
    row, col = grid_of(16, 16)
    at, base = row & 7, row & 8
    wanted = ((at >= 6) & (col == base + 5)) | ((at < 2) & (col == base + 2))
    from_att = dot(picks(wanted), twin[:, cols])
    rims = edge[:, cols]
    at = lax.broadcasted_iota(jnp.int32, (16, width), 0) & 7
    rims = (from_att + rims.astype(F32)).astype(BF).astype(F32)
    above = jnp.where(at >= 6, rims, 0.0)
    below = jnp.where(at < 2, rims, 0.0)
    for s in range(2):
        body = dot(spread, att[s, 0:short, cols]) + skip[s, :, cols].astype(F32)
        ext[s, 0:PAD] = above[s * 8 : s * 8 + 8]
        ext[s, PAD : PAD + 2 * short] = body.astype(BF).astype(F32)
        ext[s, PAD + 2 * short : 2 * PAD + 2 * short] = below[s * 8 : s * 8 + 8]


def around(field):
    tall = field.shape[0]
    return pltpu.roll(field, 1, 0), pltpu.roll(field, tall - 1, 0)


def phi_of(values):
    return 0.5 * (1.0 + lax.erf(values * 0.7071067811865476))


def slope_of(values):
    return phi_of(values) + values * jnp.exp(-0.5 * values * values) * 0.3989422804014327


def asked_rows(meta, offsets, bins, s, ext, taps, tall):
    row, col = grid_of(48, tall)
    want = row & 3
    shift = (row >> 4) - 1
    at = jnp.full((48, tall), -4096, jnp.int32)
    slab = meta[1]
    for k in range(4):
        mine = k < NTD
        home = slab if mine else jnp.maximum(slab - 1, 0)
        place = bins[s, home * NTD + (k % NTD)] + offsets[s] - (0 if mine else tall - 2 * PAD)
        fits = (place >= 0) & (place < tall - 2 * PAD)
        at = jnp.where(want == k, jnp.where(fits, place + PAD, -4096), at)
    found = dot(picks((col == at + shift) & ((row & 15) < 8)), ext.astype(BF))
    here = found[16:32]
    value = taps[0] * found[0:16] + taps[1] * here + taps[2] * found[32:48]
    act = value * phi_of(value)
    row = lax.broadcasted_iota(jnp.int32, act.shape, 0)
    return jnp.where(row < 4, act, here).astype(BF)


def taps_of(filt, cols):
    return [filt[k : k + 1, cols] for k in range(3)]


def tap_sums(conv, ext, rows):
    before, after = around(ext)
    body = slice(PAD, PAD + rows)
    mine = conv[body]
    return [
        jnp.sum(mine * other[body], axis=0, keepdims=True) for other in (before, ext, after)
    ]


def grads(conv, direct, taps, rows, pair):
    before, after = around(conv)
    body = slice(PAD, PAD + rows)
    total = direct + taps[0] * after[body] + taps[1] * conv[body] + taps[2] * before[body]
    short = rows // 2
    sums = []
    for k in range(total.shape[1] // LANES):
        pair[k] = total[:, k * LANES : (k + 1) * LANES]
        sums.append(pair[k, pl.ds(0, short, 2), :] + pair[k, pl.ds(1, short, 2), :])
    return total, jnp.concatenate(sums, axis=1)


def own_slope_kernel(meta, offsets, bins, att, skip, edge, filt, asked, sums, slopes, ext):
    half = skip.shape[2]
    tall = ext.shape[1]
    width = ext.shape[2]

    @pl.loop(0, half // width)
    def _(part):
        cols = pl.ds(pl.multiple_of(part * width, width), width)
        slab_sums(att, skip, edge, edge, ext, cols)
        taps = taps_of(filt, cols)
        for s in range(2):
            field = ext[s]
            before, after = around(field)
            slopes[s, :, cols] = slope_of(taps[0] * before + taps[1] * field + taps[2] * after)
            sums[s, :, cols] = field.astype(BF)
            asked[s * 16 : s * 16 + 16, cols] = asked_rows(
                meta, offsets, bins, s, field, taps, tall
            )


def own_slopes(meta, offsets, bins, attention, skip, edge, filt):
    seqs, rows, wide = skip.shape
    _, short, half = attention.shape
    tall = rows + 2 * PAD

    def whole(*shape):
        return pl.BlockSpec(shape, lambda i, m, o, b: (0,) * len(shape))

    def mine(*shape):
        return pl.BlockSpec(shape, lambda i, m, o, b: (0,) * (len(shape) - 1) + (m[0],))

    return pl.pallas_call(
        own_slope_kernel,
        grid_spec=pltpu.PrefetchScalarGridSpec(
            num_scalar_prefetch=3,
            grid=(1,),
            in_specs=[
                pl.BlockSpec((2, short, half), lambda i, m, o, b: (m[0], 0, 0)),
                mine(2, rows, half),
                mine(16, half),
                mine(3, half),
            ],
            out_specs=[whole(32, half), whole(2, tall, half), whole(2, tall, half)],
            scratch_shapes=[pltpu.VMEM((2, tall, 256), F32)],
        ),
        out_shape=[
            jax.ShapeDtypeStruct((32, half), BF),
            jax.ShapeDtypeStruct((2, tall, half), BF),
            jax.ShapeDtypeStruct((2, tall, half), F32),
        ],
        compiler_params=params(),
        cost_estimate=cost(3 * 10**9, 10**6),
        name="own_slopes",
    )(meta, offsets, bins, attention, skip, edge, filt)


def own_kernel(
    slabs, meta, offsets, sums, slopes, rims, prev_far, cot_far, weight_far, filt,
    moved, terms, skip_grad, att_grad, pair, prev, cot, weight, sems,
):
    copies = [
        pltpu.make_async_copy(prev_far, prev, sems.at[0]),
        pltpu.make_async_copy(cot_far, cot, sems.at[1]),
        pltpu.make_async_copy(weight_far, weight, sems.at[2]),
    ]
    for copy in copies:
        copy.start()
    half = sums.shape[2]
    tall = sums.shape[1]
    rows = tall - 2 * PAD
    wide = cot.shape[2]
    row, col = grid_of(tall, rows)
    last = meta[1] == slabs - 1
    copies[0].wait()
    copies[1].wait()
    for s in range(2):
        at = row - PAD
        fits = (at >= -1) & (at < jnp.where(last, rows, rows + 1))
        source = jnp.where(fits, at - offsets[s], -4096)
        older = picks(col == source + rows)
        newer = picks(col == source)
        place = lax.broadcasted_iota(jnp.int32, (PAD, 512), 0)
        top = (place == PAD - 1) & (offsets[s] == rows)
        bottom = (place == 0) & (offsets[s] == 0) & jnp.logical_not(last)
        for part in range(0, wide, 512):
            cols = slice(part, part + 512)
            found = dot(older, prev[s, :, cols]) + dot(newer, cot[s, :, cols])
            ends = rims[:, cols].astype(F32)
            above = ends[s * 8 + 4 : s * 8 + 5]
            below = ends[s * 8 + 3 : s * 8 + 4]
            found = jnp.concatenate(
                [
                    found[:PAD] + jnp.where(top, above, 0.0),
                    found[PAD : PAD + rows],
                    found[PAD + rows :] + jnp.where(bottom, below, 0.0),
                ]
            )
            moved[s, :, cols] = found.astype(BF)
    copies[2].wait()
    width = 2 * LANES
    first = meta[0] * half

    @pl.loop(0, half // width)
    def _(part):
        begin = pl.multiple_of(part * width, width)
        cols = pl.ds(begin, width)
        taps = taps_of(filt, cols)
        piece = weight[pl.ds(begin, width), :]
        total_terms = [0.0, 0.0, 0.0]
        there = pl.ds(pl.multiple_of(first + begin, width), width)
        for s in range(2):
            conv = (dot_rows(moved[s], piece) * slopes[s, :, cols]).astype(BF).astype(F32)
            got = tap_sums(conv, sums[s, :, cols].astype(F32), rows)
            total_terms = [a + b for a, b in zip(total_terms, got)]
            direct = moved[s, :, there].astype(F32)[PAD : PAD + rows]
            total, pairs = grads(conv, direct, taps, rows, pair)
            skip_grad[s, :, cols] = total.astype(BF)
            att_grad[s, :, cols] = pairs.astype(BF)
        for k in range(3):
            terms[k : k + 1, cols] = total_terms[k]


def own_half(meta, offsets, sums, slopes, edge, prev, cot, weight, filt, slabs):
    seqs, rows, wide = cot.shape
    _, tall, half = sums.shape
    short = rows // 2

    def whole(*shape):
        return pl.BlockSpec(shape, lambda i, m, o: (0,) * len(shape))

    def mine(*shape):
        return pl.BlockSpec(shape, lambda i, m, o: (0,) * (len(shape) - 1) + (m[0],))

    anywhere = pl.BlockSpec(memory_space=pl.ANY)
    return pl.pallas_call(
        functools.partial(own_kernel, slabs),
        grid_spec=pltpu.PrefetchScalarGridSpec(
            num_scalar_prefetch=2,
            grid=(1,),
            in_specs=[
                whole(2, tall, half),
                whole(2, tall, half),
                whole(16, wide),
                anywhere,
                anywhere,
                anywhere,
                mine(3, half),
            ],
            out_specs=[
                whole(2, tall, wide),
                whole(3, half),
                mine(2, rows, half),
                mine(2, short, half),
            ],
            scratch_shapes=[
                pltpu.VMEM((2, rows, LANES), F32),
                pltpu.VMEM((2, rows, wide), BF),
                pltpu.VMEM((2, rows, wide), BF),
                pltpu.VMEM((half, wide), BF),
                pltpu.SemaphoreType.DMA((3,)),
            ],
        ),
        out_shape=[
            jax.ShapeDtypeStruct((2, tall, wide), BF),
            jax.ShapeDtypeStruct((3, half), F32),
            jax.ShapeDtypeStruct((2, rows, wide), BF),
            jax.ShapeDtypeStruct((2, short, wide), BF),
        ],
        compiler_params=params(),
        cost_estimate=cost(1, 1),
        name="own_half",
    )(meta, offsets, sums, slopes, edge, prev, cot, weight, filt)


def slope_kernel(
    meta, offsets, bins, att, skip, edge, twin, filt, asked, sums, slopes, mine, shown, ext
):
    rows = skip.shape[1]
    tall = rows + 2 * PAD
    half = skip.shape[2]
    width = ext.shape[2]
    there = (1 - meta[0]) * half
    row, col = grid_of(16, 32)
    at, base = row & 7, (row >> 3) * 16
    kept = picks((at < 4) & (col == base + at + jnp.where(at < 2, 0, 2)))
    told = picks((at < 4) & (col == base + at + jnp.where(at < 2, 2, 4)))
    here = pl.ds(pl.multiple_of(meta[0] * half, half), half)
    mine[:, here] = dot(kept, asked[...]).astype(BF)
    shown[:, here] = dot(told, asked[...]).astype(BF)

    @pl.loop(0, half // width)
    def _(part):
        begin = pl.multiple_of(part * width, width)
        cols = pl.ds(begin, width)
        slab_sums(att, skip, edge, twin, ext, cols)
        taps = taps_of(filt, cols)
        got = []
        for s in range(2):
            field = ext[s]
            before, after = around(field)
            slopes[s, :, cols] = slope_of(taps[0] * before + taps[1] * field + taps[2] * after)
            sums[s, :, cols] = field.astype(BF)
            got.append(asked_rows(meta, offsets, bins, s, field, taps, tall))
        got = jnp.concatenate(got)
        place = pl.ds(pl.multiple_of(there + begin, width), width)
        mine[:, place] = dot(kept, got).astype(BF)
        shown[:, place] = dot(told, got).astype(BF)


def other_slopes(meta, offsets, bins, shipped, skip, edge, twin, filt, asked):
    seqs, rows, wide = skip.shape
    _, packed_rows, half = shipped.shape
    tall = rows + 2 * PAD

    def whole(*shape):
        return pl.BlockSpec(shape, lambda i, m, o, b: (0,) * len(shape))

    def other(*shape):
        return pl.BlockSpec(shape, lambda i, m, o, b: (0,) * (len(shape) - 1) + (1 - m[0],))

    return pl.pallas_call(
        slope_kernel,
        grid_spec=pltpu.PrefetchScalarGridSpec(
            num_scalar_prefetch=3,
            grid=(1,),
            in_specs=[
                whole(2, packed_rows, half),
                other(2, rows, half),
                other(16, half),
                pl.BlockSpec((16, half), lambda i, m, o, b: (0, m[0])),
                other(3, half),
                whole(32, half),
            ],
            out_specs=[whole(2, tall, half), whole(2, tall, half), whole(16, wide), whole(16, wide)],
            scratch_shapes=[pltpu.VMEM((2, tall, 256), F32)],
        ),
        out_shape=[
            jax.ShapeDtypeStruct((2, tall, half), BF),
            jax.ShapeDtypeStruct((2, tall, half), F32),
            jax.ShapeDtypeStruct((16, wide), BF),
            jax.ShapeDtypeStruct((16, wide), BF),
        ],
        compiler_params=params(),
        cost_estimate=cost(3 * 10**9, 10**6),
        name="other_slopes",
    )(meta, offsets, bins, shipped, skip, edge, twin, filt, asked)


def terms_kernel(meta, order, moved, sums, slopes, own_terms, *refs):
    pieces, (convs, terms, full, sems) = refs[:8], refs[8:]
    half = sums.shape[2]
    tall = sums.shape[1]
    rows = tall - 2 * PAD
    there = (1 - meta[0]) * half
    tile = pieces[0].shape[0]
    copies = []
    for k, piece in enumerate(pieces):
        down = pl.multiple_of(order[4 + k // 4] * tile, tile)
        over = pl.multiple_of(order[k % 4] * tile, tile)
        copies.append(
            pltpu.make_async_copy(
                piece, full.at[pl.ds(down, tile), pl.ds(over, tile)], sems.at[k]
            )
        )
        copies[-1].start()
    terms[:, pl.ds(pl.multiple_of(meta[0] * half, half), half)] = own_terms[...]
    for copy in copies:
        copy.wait()
    width = 2 * LANES
    for begin in range(0, half, width):
        cols = slice(begin, begin + width)
        total = [0.0, 0.0, 0.0]
        for s in range(2):
            grad = dot_rows(moved[s], full[cols, :])
            conv = (grad * slopes[s, :, cols]).astype(BF)
            convs[s, :, cols] = conv
            got = tap_sums(conv.astype(F32), sums[s, :, cols].astype(F32), rows)
            total = [a + b for a, b in zip(total, got)]
        place = pl.ds(pl.multiple_of(there + begin, width), width)
        for k in range(3):
            terms[k : k + 1, place] = total[k]


def other_terms(meta, order, moved, sums, slopes, own_terms, pieces):
    _, tall, wide = moved.shape
    half = sums.shape[2]

    def whole(*shape):
        return pl.BlockSpec(shape, lambda i, m, o: (0,) * len(shape))

    return pl.pallas_call(
        terms_kernel,
        grid_spec=pltpu.PrefetchScalarGridSpec(
            num_scalar_prefetch=2,
            grid=(1,),
            in_specs=[
                whole(2, tall, wide),
                whole(2, tall, half),
                whole(2, tall, half),
                whole(3, half),
            ]
            + [pl.BlockSpec(memory_space=pl.ANY)] * 8,
            out_specs=[whole(2, tall, half), whole(3, wide)],
            scratch_shapes=[pltpu.VMEM((half, wide), BF), pltpu.SemaphoreType.DMA((8,))],
        ),
        out_shape=[
            jax.ShapeDtypeStruct((2, tall, half), BF),
            jax.ShapeDtypeStruct((3, wide), F32),
        ],
        compiler_params=params(),
        cost_estimate=cost(2 * 2 * tall * half * wide, 6 * 1024 * 1024),
        name="other_terms",
    )(meta, order, moved, sums, slopes, own_terms, *pieces)


def grads_kernel(meta, moved, convs, filt, old_skip, old_att, skip_grad, att_grad, pair):
    half = convs.shape[2]
    rows = convs.shape[1] - 2 * PAD
    width = 2 * LANES

    @pl.loop(0, half // width)
    def _(part):
        cols = pl.ds(pl.multiple_of(part * width, width), width)
        taps = taps_of(filt, cols)
        for s in range(2):
            direct = moved[s, :, cols].astype(F32)[PAD : PAD + rows]
            total, pairs = grads(convs[s, :, cols].astype(F32), direct, taps, rows, pair)
            skip_grad[s, :, cols] = total.astype(BF)
            att_grad[s, :, cols] = pairs.astype(BF)


def other_grads(meta, moved, convs, filt, skip_grad, att_grad):
    _, tall, wide = moved.shape
    half = convs.shape[2]
    rows = tall - 2 * PAD

    def whole(*shape):
        return pl.BlockSpec(shape, lambda i, m: (0,) * len(shape))

    def other(*shape):
        return pl.BlockSpec(shape, lambda i, m: (0,) * (len(shape) - 1) + (1 - m[0],))

    return pl.pallas_call(
        grads_kernel,
        grid_spec=pltpu.PrefetchScalarGridSpec(
            num_scalar_prefetch=1,
            grid=(1,),
            in_specs=[other(2, tall, half), whole(2, tall, half), other(3, half)]
            + [pl.BlockSpec(memory_space=pl.ANY)] * 2,
            out_specs=[other(2, rows, half), other(2, rows // 2, half)],
            scratch_shapes=[pltpu.VMEM((2, rows, LANES), F32)],
        ),
        out_shape=[
            jax.ShapeDtypeStruct((2, rows, wide), BF),
            jax.ShapeDtypeStruct((2, rows // 2, wide), BF),
        ],
        input_output_aliases={4: 0, 5: 1},
        compiler_params=params(),
        cost_estimate=cost(2 * tall * half * 20, 4 * 1024 * 1024),
        name="other_grads",
    )(meta, moved, convs, filt, skip_grad, att_grad)


def target_kernel(slabs, meta, order, mine, got_a, got_b, weight, *refs):
    pieces, (target, total) = refs[:8], refs[8:]
    half = weight.shape[0]
    there = (1 - meta[0]) * half
    tile = pieces[0].shape[0]
    even = (meta[1] & 1) == 0
    got = jnp.where(even, got_a[...].astype(F32), got_b[...].astype(F32))
    got = jnp.where(meta[1] == slabs - 1, 0.0, got)
    mine[...] = (mine[...].astype(F32) + got).astype(BF)
    here = pl.ds(pl.multiple_of(meta[0] * half, half), half)
    total[...] = dot(mine[:, here], weight[...]) + pltpu.roll(mine[...].astype(F32), 12 + 2, 0)
    for k, piece in enumerate(pieces):
        place = pl.ds(pl.multiple_of(there + order[4 + k // 4] * tile, tile), tile)
        over = pl.ds(pl.multiple_of(order[k % 4] * tile, tile), tile)
        total[:, over] += dot(mine[:, place], piece[...])
    for s in range(2):
        target[s] = total[s * 8 : s * 8 + 2].astype(BF)


def targets(meta, order, mine, got, weight, pieces, slabs):
    half, wide = weight.shape
    tile = pieces[0].shape[0]

    def whole(*shape):
        return pl.BlockSpec(shape, lambda i, m, o: (0,) * len(shape))

    return pl.pallas_call(
        functools.partial(target_kernel, slabs),
        grid_spec=pltpu.PrefetchScalarGridSpec(
            num_scalar_prefetch=2,
            grid=(1,),
            in_specs=[whole(16, wide)] * 3 + [whole(half, wide)]
            + [whole(tile, tile)] * 8,
            out_specs=whole(2, NTD, wide),
            scratch_shapes=[pltpu.VMEM((16, wide), F32)],
        ),
        out_shape=jax.ShapeDtypeStruct((2, NTD, wide), BF),
        compiler_params=params(),
        cost_estimate=cost(2 * 16 * wide * wide, 6 * 1024 * 1024),
        name="targets",
    )(meta, order, mine, *got, weight, *pieces)


def paired(part, axis, bit):
    count = lax.axis_size(axis)
    return lax.ppermute(part, axis, [(i, i ^ bit) for i in range(count)])


def staggered(part, span):
    count = lax.axis_size("seq")
    pairs = []
    for i in range(count):
        by = span if i // span % 2 else -span
        pairs.append((i, (i + by) % count))
    return lax.ppermute(part, "seq", pairs)


def after(value, *others):
    return lax.optimization_barrier((value,) + others)[0]


def crossed(part, seq_bit, head_bit):
    slabs, heads = lax.axis_size("seq"), lax.axis_size("head")
    pairs = [
        (i * heads + j, (i ^ seq_bit) * heads + (j ^ head_bit))
        for i in range(slabs)
        for j in range(heads)
    ]
    return lax.ppermute(part, ("seq", "head"), pairs)


def joined(total, one, two):
    both = (one[0] ^ two[0], one[1] ^ two[1])
    parts = [crossed(total, *bits) for bits in (one, two, both)]
    return (total + parts[0]) + (parts[1] + parts[2])


def fast_shards(
    attention, encoder_skip, depth_filter, point_weight, crop_offset, target_bins, cotangent
):
    head = lax.axis_index("head")
    slab = lax.axis_index("seq")
    slabs = lax.axis_size("seq")
    meta = jnp.stack([head, slab]).astype(jnp.int32)
    core = slab % 2
    block = slab // 2 % 4
    tile = 3 * LANES
    order = jnp.stack([block, block ^ 1, block ^ 2, block ^ 3, core, 1 - core]).astype(jnp.int32)

    edge_a, edge_b, far, first, last_tile, att_out = packed(
        meta, encoder_skip, attention, cotangent, point_weight, tile
    )
    first = paired(first, "head", 1)
    shipped = paired(att_out, "head", 1)
    edge_a = paired(edge_a, "seq", 1)
    edge_b = staggered(edge_b, 1)
    far_a = paired(far, "seq", 2)
    far_b = staggered(far, 2)
    prev = passed_along(after(cotangent, edge_a, edge_b, far_a, far_b), "seq", 1)
    outer = (slab == 0) | (slab == slabs - 1)
    nothing = jnp.zeros_like(edge_b)
    edge = edge_a + jnp.where(outer, nothing, edge_b)
    twin = paired(edge, "head", 1)
    edge = edge + jnp.where(slab % 4 >= 2, far_a, jnp.where(slab < 2, nothing, far_b))
    second = paired(first, "seq", 2)
    third = paired(first, "seq", 4)
    fourth = paired(last_tile, "head", 1)
    asked, own_sums, own_slope = own_slopes(
        meta, crop_offset, target_bins, attention, encoder_skip, edge, depth_filter
    )
    sums, slopes, mine, shown = other_slopes(
        meta, crop_offset, target_bins, shipped, encoder_skip, edge, twin, depth_filter, asked
    )
    got = [paired(shown, "seq", 1), staggered(shown, 1)]
    moved, own_terms, skip_grad, att_grad = own_half(
        after(meta, shown), crop_offset, own_sums, own_slope, edge, prev, cotangent, point_weight, depth_filter,
        slabs,
    )
    pieces = [first, second, third, fourth]
    pieces = pieces + [paired(after(piece, own_terms), "seq", 1) for piece in pieces]
    convs, terms = other_terms(meta, order, moved, sums, slopes, own_terms, pieces)
    terms, *got = lax.optimization_barrier((terms, *got))
    total = terms + crossed(terms, 1, 0)
    total = joined(total, (2, 0), (0, 1))
    skip_grad, attention_grad = other_grads(
        meta, moved, convs, depth_filter, skip_grad, att_grad
    )
    target_rows = targets(meta, order, mine, got, point_weight, pieces, slabs)
    total, skip_grad, attention_grad = lax.optimization_barrier(
        (total, skip_grad, attention_grad)
    )
    if slabs == 16:
        total = joined(total, (4, 0), (8, 0))
    else:
        step = 4
        while step < slabs:
            total = total + crossed(total, step, 0)
            step *= 2
    count = encoder_skip.shape[0] * lax.axis_size("head") * encoder_skip.shape[1] * slabs
    return (target_rows, attention_grad, skip_grad, total * (1.0 / math.sqrt(count)))


def shards(*args):
    attention, encoder_skip, point_weight = args[0], args[1], args[3]
    fits = (
        lax.axis_size("head") == 2
        and lax.axis_size("seq") in (8, 16, 32)
        and encoder_skip.shape[:2] == (2, 128)
        and point_weight.shape[0] == 6 * LANES
        and attention.shape[1] == 64
    )
    return fast_shards(*args) if fits else plain_shards(*args)


def solution(mesh):
    in_specs = (
        P(None, "seq", "head"),
        P("head", "seq", None),
        P(),
        P("head", None),
        P("head"),
        P("head", None),
        P("head", "seq", None),
    )
    out_specs = (P("head", "seq", None), P("head", "seq", None), P("head", "seq", None), P())
    return jax.shard_map(shards, mesh=mesh, in_specs=in_specs, out_specs=out_specs, check_vma=False)
def solution(mesh):
    in_specs = (
        P(None, "seq", "head"),
        P("head", "seq", None),
        P(),
        P("head", None),
        P("head"),
        P("head", None),
        P("head", "seq", None),
    )
    out_specs = (P("head", "seq", None), P("head", "seq", None), P("head", "seq", None), P())
    return jax.shard_map(shards, mesh=mesh, in_specs=in_specs, out_specs=out_specs, check_vma=False)
```

```python
import functools
import math

import jax
import jax.numpy as jnp
from jax import lax
from jax.experimental import pallas as pl
from jax.experimental.pallas import tpu as pltpu
from jax.sharding import PartitionSpec as P

NTD = 2


def extended(shard, sides, width):
    for axis, dim in sides:
        count, length = (lax.axis_size(axis), shard.shape[dim])
        up = [(i, (i + 1) % count) for i in range(count - 1)]
        down = [(j, i) for i, j in up]
        last = lax.slice_in_dim(shard, length - width, length, axis=dim)
        initial = lax.slice_in_dim(shard, 0, width, axis=dim)
        before = lax.ppermute(last, axis, up)
        after = lax.ppermute(initial, axis, down)
        shard = jnp.concatenate([before, shard, after], axis=dim)
    return shard


def passed_along(shard, axis, by):
    count = lax.axis_size(axis)
    pairs = [(i, i + by) for i in range(count) if 0 <= i + by < count]
    return lax.ppermute(shard, axis, pairs)


def gelu_slope(values):
    return (
        0.5 * (1.0 + lax.erf(values * 0.7071067811865476))
        + values * jnp.exp(-0.5 * values * values) * 0.3989422804014327
    )


def with_rims(field):
    return extended(field, (("seq", 1),), 1)


def one_hot(places, length):
    return (places[:, :, None] == jnp.arange(length, dtype=jnp.int32)[None, None, :]).astype(
        jnp.bfloat16
    )


def core_swap(part):
    count = lax.axis_size("seq")
    return lax.ppermute(part, "seq", [(i, i ^ 1) for i in range(count)])


def gathered_weight(rows):
    heads = lax.axis_size("head")
    here = lax.axis_index("head")
    core = lax.axis_index("seq") % 2
    half = rows.shape[0] // 2
    mine = lax.dynamic_slice_in_dim(rows, core * half, half, 0)
    blocks = [(0, rows)]
    for step in range(1, heads):
        pairs = [(i, (i + step) % heads) for i in range(heads)]
        got = lax.ppermute(mine, "head", pairs)
        twin = core_swap(got)
        low = jnp.where(core == 0, got, twin)
        high = jnp.where(core == 0, twin, got)
        blocks.append((step, jnp.concatenate([low, high], axis=0)))
    full = jnp.zeros((heads * rows.shape[0], rows.shape[1]), rows.dtype)
    for step, block in blocks:
        place = (here - step) % heads
        full = lax.dynamic_update_slice_in_dim(full, block, place * rows.shape[0], 0)
    return full


def butterfly(total, axis):
    count = lax.axis_size(axis)
    if count & (count - 1):
        return lax.psum(total, axis)
    step = 1
    while step < count:
        total = total + lax.ppermute(total, axis, [(i, i ^ step) for i in range(count)])
        step *= 2
    return total


def plain_shards(
    attention, encoder_skip, depth_filter, point_weight, crop_offset, target_bins, cotangent
):
    slab_input = lax.all_to_all(attention, "head", split_axis=0, concat_axis=2, tiled=True)
    local_seqs = encoder_skip.shape[0]
    slab_rows = encoder_skip.shape[1]
    channels = encoder_skip.shape[2]
    summed = (
        jnp.repeat(slab_input, 2, axis=1).astype(jnp.float32) + encoder_skip.astype(jnp.float32)
    ).astype(jnp.bfloat16)
    padded = with_rims(summed)
    filtered = (
        depth_filter[0] * padded[:, :-2]
        + depth_filter[1] * padded[:, 1:-1]
        + depth_filter[2] * padded[:, 2:]
    )
    activated = jax.nn.gelu(filtered, approximate=False).astype(jnp.bfloat16)
    flat_act = activated.reshape(local_seqs * slab_rows, channels)
    full_weight = gathered_weight(point_weight)
    mixed_rows = jnp.dot(flat_act, full_weight, preferred_element_type=jnp.float32)
    block_out = (
        summed.astype(jnp.float32) + mixed_rows.reshape(local_seqs, slab_rows, channels)
    ).astype(jnp.bfloat16)
    slab_index = lax.axis_index("seq")
    bins = jnp.concatenate(
        [jnp.zeros_like(target_bins[:, :NTD]), target_bins], axis=1
    )
    asked = lax.dynamic_slice_in_dim(bins, slab_index * NTD, 2 * NTD, 1) + crop_offset[:, None]
    back = jnp.where(jnp.arange(2 * NTD, dtype=jnp.int32) < NTD, slab_rows, 0)
    asked = asked - back[None, :]
    picked = jnp.einsum(
        "sjr,srd->sjd",
        one_hot(asked, slab_rows),
        block_out,
        preferred_element_type=jnp.float32,
    ).astype(jnp.bfloat16)
    from_next = passed_along(picked[:, :NTD], "seq", -1)
    target_rows = picked[:, NTD:] + from_next
    prev_cot = passed_along(cotangent, "seq", 1)
    cot_pair = jnp.concatenate([prev_cot, cotangent], axis=1)

    def crop_back(cot_block, shift_by):
        return lax.dynamic_slice_in_dim(cot_block, slab_rows - shift_by, slab_rows, 0)

    grad_out = jax.vmap(crop_back)(cot_pair, crop_offset)
    flat_grad = grad_out.reshape(local_seqs * slab_rows, channels)
    grad_act = lax.dot_general(
        flat_grad, full_weight, (((1,), (1,)), ((), ())), preferred_element_type=jnp.float32
    )
    grad_conv = (grad_act.reshape(local_seqs, slab_rows, channels) * gelu_slope(filtered)).astype(
        jnp.bfloat16
    )
    grad_padded = with_rims(grad_conv)
    grad_sum = (
        grad_out.astype(jnp.float32)
        + depth_filter[0] * grad_padded[:, 2:]
        + depth_filter[1] * grad_padded[:, 1:-1]
        + depth_filter[2] * grad_padded[:, :-2]
    )
    skip_grad = grad_sum.astype(jnp.bfloat16)
    attention_grad = (
        grad_sum.reshape(local_seqs, slab_rows // 2, 2, channels).sum(axis=2).astype(jnp.bfloat16)
    )
    filter_terms = jnp.stack(
        [
            jnp.einsum(
                "srd,srd->d", grad_conv, padded[:, 0:slab_rows], preferred_element_type=jnp.float32
            ),
            jnp.einsum(
                "srd,srd->d",
                grad_conv,
                padded[:, 1 : slab_rows + 1],
                preferred_element_type=jnp.float32,
            ),
            jnp.einsum(
                "srd,srd->d",
                grad_conv,
                padded[:, 2 : slab_rows + 2],
                preferred_element_type=jnp.float32,
            ),
        ]
    )
    filter_sum = butterfly(butterfly(filter_terms, "seq"), "head")
    row_count = local_seqs * lax.axis_size("head") * slab_rows * lax.axis_size("seq")
    filter_grad = filter_sum * (1.0 / math.sqrt(row_count))
    return (target_rows, attention_grad, skip_grad, filter_grad)


import functools
import math

import jax
import jax.numpy as jnp
from jax import lax
from jax.experimental import pallas as pl
from jax.experimental.pallas import tpu as pltpu
from jax.sharding import PartitionSpec as P

NTD = 2


def extended(shard, sides, width):
    for axis, dim in sides:
        count, length = (lax.axis_size(axis), shard.shape[dim])
        up = [(i, (i + 1) % count) for i in range(count - 1)]
        down = [(j, i) for i, j in up]
        last = lax.slice_in_dim(shard, length - width, length, axis=dim)
        initial = lax.slice_in_dim(shard, 0, width, axis=dim)
        before = lax.ppermute(last, axis, up)
        after = lax.ppermute(initial, axis, down)
        shard = jnp.concatenate([before, shard, after], axis=dim)
    return shard


def passed_along(shard, axis, by):
    count = lax.axis_size(axis)
    pairs = [(i, i + by) for i in range(count) if 0 <= i + by < count]
    return lax.ppermute(shard, axis, pairs)


def gelu_slope(values):
    return (
        0.5 * (1.0 + lax.erf(values * 0.7071067811865476))
        + values * jnp.exp(-0.5 * values * values) * 0.3989422804014327
    )


def with_rims(field):
    return extended(field, (("seq", 1),), 1)


def one_hot(places, length):
    return (places[:, :, None] == jnp.arange(length, dtype=jnp.int32)[None, None, :]).astype(
        jnp.bfloat16
    )


def core_swap(part):
    count = lax.axis_size("seq")
    return lax.ppermute(part, "seq", [(i, i ^ 1) for i in range(count)])


def gathered_weight(rows):
    heads = lax.axis_size("head")
    here = lax.axis_index("head")
    core = lax.axis_index("seq") % 2
    half = rows.shape[0] // 2
    mine = lax.dynamic_slice_in_dim(rows, core * half, half, 0)
    blocks = [(0, rows)]
    for step in range(1, heads):
        pairs = [(i, (i + step) % heads) for i in range(heads)]
        got = lax.ppermute(mine, "head", pairs)
        twin = core_swap(got)
        low = jnp.where(core == 0, got, twin)
        high = jnp.where(core == 0, twin, got)
        blocks.append((step, jnp.concatenate([low, high], axis=0)))
    full = jnp.zeros((heads * rows.shape[0], rows.shape[1]), rows.dtype)
    for step, block in blocks:
        place = (here - step) % heads
        full = lax.dynamic_update_slice_in_dim(full, block, place * rows.shape[0], 0)
    return full


def butterfly(total, axis):
    count = lax.axis_size(axis)
    if count & (count - 1):
        return lax.psum(total, axis)
    step = 1
    while step < count:
        total = total + lax.ppermute(total, axis, [(i, i ^ step) for i in range(count)])
        step *= 2
    return total


def plain_shards(
    attention, encoder_skip, depth_filter, point_weight, crop_offset, target_bins, cotangent
):
    slab_input = lax.all_to_all(attention, "head", split_axis=0, concat_axis=2, tiled=True)
    local_seqs = encoder_skip.shape[0]
    slab_rows = encoder_skip.shape[1]
    channels = encoder_skip.shape[2]
    summed = (
        jnp.repeat(slab_input, 2, axis=1).astype(jnp.float32) + encoder_skip.astype(jnp.float32)
    ).astype(jnp.bfloat16)
    padded = with_rims(summed)
    filtered = (
        depth_filter[0] * padded[:, :-2]
        + depth_filter[1] * padded[:, 1:-1]
        + depth_filter[2] * padded[:, 2:]
    )
    activated = jax.nn.gelu(filtered, approximate=False).astype(jnp.bfloat16)
    flat_act = activated.reshape(local_seqs * slab_rows, channels)
    full_weight = gathered_weight(point_weight)
    mixed_rows = jnp.dot(flat_act, full_weight, preferred_element_type=jnp.float32)
    block_out = (
        summed.astype(jnp.float32) + mixed_rows.reshape(local_seqs, slab_rows, channels)
    ).astype(jnp.bfloat16)
    slab_index = lax.axis_index("seq")
    bins = jnp.concatenate(
        [jnp.zeros_like(target_bins[:, :NTD]), target_bins], axis=1
    )
    asked = lax.dynamic_slice_in_dim(bins, slab_index * NTD, 2 * NTD, 1) + crop_offset[:, None]
    back = jnp.where(jnp.arange(2 * NTD, dtype=jnp.int32) < NTD, slab_rows, 0)
    asked = asked - back[None, :]
    picked = jnp.einsum(
        "sjr,srd->sjd",
        one_hot(asked, slab_rows),
        block_out,
        preferred_element_type=jnp.float32,
    ).astype(jnp.bfloat16)
    from_next = passed_along(picked[:, :NTD], "seq", -1)
    target_rows = picked[:, NTD:] + from_next
    prev_cot = passed_along(cotangent, "seq", 1)
    cot_pair = jnp.concatenate([prev_cot, cotangent], axis=1)

    def crop_back(cot_block, shift_by):
        return lax.dynamic_slice_in_dim(cot_block, slab_rows - shift_by, slab_rows, 0)

    grad_out = jax.vmap(crop_back)(cot_pair, crop_offset)
    flat_grad = grad_out.reshape(local_seqs * slab_rows, channels)
    grad_act = lax.dot_general(
        flat_grad, full_weight, (((1,), (1,)), ((), ())), preferred_element_type=jnp.float32
    )
    grad_conv = (grad_act.reshape(local_seqs, slab_rows, channels) * gelu_slope(filtered)).astype(
        jnp.bfloat16
    )
    grad_padded = with_rims(grad_conv)
    grad_sum = (
        grad_out.astype(jnp.float32)
        + depth_filter[0] * grad_padded[:, 2:]
        + depth_filter[1] * grad_padded[:, 1:-1]
        + depth_filter[2] * grad_padded[:, :-2]
    )
    skip_grad = grad_sum.astype(jnp.bfloat16)
    attention_grad = (
        grad_sum.reshape(local_seqs, slab_rows // 2, 2, channels).sum(axis=2).astype(jnp.bfloat16)
    )
    filter_terms = jnp.stack(
        [
            jnp.einsum(
                "srd,srd->d", grad_conv, padded[:, 0:slab_rows], preferred_element_type=jnp.float32
            ),
            jnp.einsum(
                "srd,srd->d",
                grad_conv,
                padded[:, 1 : slab_rows + 1],
                preferred_element_type=jnp.float32,
            ),
            jnp.einsum(
                "srd,srd->d",
                grad_conv,
                padded[:, 2 : slab_rows + 2],
                preferred_element_type=jnp.float32,
            ),
        ]
    )
    filter_sum = butterfly(butterfly(filter_terms, "seq"), "head")
    row_count = local_seqs * lax.axis_size("head") * slab_rows * lax.axis_size("seq")
    filter_grad = filter_sum * (1.0 / math.sqrt(row_count))
    return (target_rows, attention_grad, skip_grad, filter_grad)


LANES = 128
PAD = 8
BF = jnp.bfloat16
F32 = jnp.float32


def dot(left, right):
    return lax.dot_general(left, right, (((1,), (0,)), ((), ())), preferred_element_type=F32)


def dot_rows(left, right):
    return lax.dot_general(left, right, (((1,), (1,)), ((), ())), preferred_element_type=F32)


def grid_of(rows, columns):
    return (
        lax.broadcasted_iota(jnp.int32, (rows, columns), 0),
        lax.broadcasted_iota(jnp.int32, (rows, columns), 1),
    )


def picks(match):
    return jnp.where(match, 1.0, 0.0).astype(BF)


def params(mib=20):
    return pltpu.CompilerParams(vmem_limit_bytes=mib * 1024 * 1024)


def cost(flops, moved, special=0):
    return pl.CostEstimate(flops=flops, bytes_accessed=moved, transcendentals=special)


def pack_kernel(
    meta, skip_lo, skip_hi, att_lo, att_hi, cot_lo, cot_hi, near, distant, att,
    edge_a, edge_b, far, tile_a, tile_b, att_out,
):
    att_out[...] = att[...]
    tile_a[...] = near[...]
    tile_b[...] = distant[...]
    wide = cot_lo.shape[2]
    at = lax.broadcasted_iota(jnp.int32, (8, wide), 0)
    even = (meta[1] & 1) == 0
    ups, downs, ends = [], [], []
    for s in range(2):
        feats = [jnp.concatenate([part[s], part[2 + s]], axis=1) for part in (att_hi, att_lo)]
        high, low = feats[0].astype(F32)[8:], feats[1].astype(F32)[:8]
        up = jnp.where(at >= 6, skip_hi[s].astype(F32)[8:], 0.0)
        ups.append(jnp.where(at == 5, pltpu.roll(high, 6, 0), up))
        down = jnp.where(at < 2, skip_lo[s].astype(F32)[:8], 0.0)
        down = jnp.where(at == 2, pltpu.roll(low, 2, 0), down)
        downs.append(jnp.where(at == 3, pltpu.roll(cot_lo[s].astype(F32)[:8], 3, 0), down))
        last = pltpu.roll(cot_hi[s].astype(F32)[8:], 5, 0)
        ends.append(jnp.where(at == 4, last, 0.0))
    up, down = jnp.concatenate(ups), jnp.concatenate(downs)
    edge_a[...] = jnp.where(even, up, down).astype(BF)
    edge_b[...] = jnp.where(even, down, up).astype(BF)
    far[...] = jnp.concatenate(ends).astype(BF)


def packed(meta, encoder_skip, attention, cotangent, weight, tile):
    seqs, rows, wide = encoder_skip.shape
    half = attention.shape[2]
    short = attention.shape[1]

    def block(count, width, place):
        return pl.BlockSpec((count, 16, width), lambda i, m: (0, place, 0))

    out = jax.ShapeDtypeStruct((16, wide), BF)
    square = jax.ShapeDtypeStruct((tile, tile), BF)
    return pl.pallas_call(
        pack_kernel,
        grid_spec=pltpu.PrefetchScalarGridSpec(
            num_scalar_prefetch=1,
            grid=(1,),
            in_specs=[
                block(seqs, wide, 0),
                block(seqs, wide, rows // 16 - 1),
                block(2 * seqs, half, 0),
                block(2 * seqs, half, short // 16 - 1),
                block(seqs, wide, 0),
                block(seqs, wide, rows // 16 - 1),
                pl.BlockSpec((tile, tile), lambda i, m: (m[1] & 1, (m[1] >> 1) & 3)),
                pl.BlockSpec((tile, tile), lambda i, m: (m[1] & 1, 3 - ((m[1] >> 1) & 3))),
                pl.BlockSpec((2, short, half), lambda i, m: (1 - m[0], 0, 0)),
            ],
            out_specs=[pl.BlockSpec((16, wide), lambda i, m: (0, 0))] * 3
            + [pl.BlockSpec((tile, tile), lambda i, m: (0, 0))] * 2
            + [pl.BlockSpec((2, short, half), lambda i, m: (0, 0, 0))],
        ),
        out_shape=[out, out, out, square, square, jax.ShapeDtypeStruct((2, short, half), BF)],
        compiler_params=params(60),
        name="pack_edges",
    )(
        meta, encoder_skip, encoder_skip, attention, attention, cotangent, cotangent, weight,
        weight, attention,
    )


def slab_sums(att, skip, edge, twin, ext, cols):
    width = cols.size
    short = 64
    row, col = grid_of(2 * short, short)
    spread = picks((row >> 1) == col)
    row, col = grid_of(16, 16)
    at, base = row & 7, row & 8
    wanted = ((at >= 6) & (col == base + 5)) | ((at < 2) & (col == base + 2))
    from_att = dot(picks(wanted), twin[:, cols])
    rims = edge[:, cols]
    at = lax.broadcasted_iota(jnp.int32, (16, width), 0) & 7
    rims = (from_att + rims.astype(F32)).astype(BF).astype(F32)
    above = jnp.where(at >= 6, rims, 0.0)
    below = jnp.where(at < 2, rims, 0.0)
    for s in range(2):
        body = dot(spread, att[s, 0:short, cols]) + skip[s, :, cols].astype(F32)
        ext[s, 0:PAD] = above[s * 8 : s * 8 + 8]
        ext[s, PAD : PAD + 2 * short] = body.astype(BF).astype(F32)
        ext[s, PAD + 2 * short : 2 * PAD + 2 * short] = below[s * 8 : s * 8 + 8]


def around(field):
    tall = field.shape[0]
    return pltpu.roll(field, 1, 0), pltpu.roll(field, tall - 1, 0)


def phi_of(values):
    return 0.5 * (1.0 + lax.erf(values * 0.7071067811865476))


def slope_of(values):
    return phi_of(values) + values * jnp.exp(-0.5 * values * values) * 0.3989422804014327


def asked_rows(meta, offsets, bins, s, ext, taps, tall):
    row, col = grid_of(48, tall)
    want = row & 3
    shift = (row >> 4) - 1
    at = jnp.full((48, tall), -4096, jnp.int32)
    slab = meta[1]
    for k in range(4):
        mine = k < NTD
        home = slab if mine else jnp.maximum(slab - 1, 0)
        place = bins[s, home * NTD + (k % NTD)] + offsets[s] - (0 if mine else tall - 2 * PAD)
        fits = (place >= 0) & (place < tall - 2 * PAD)
        at = jnp.where(want == k, jnp.where(fits, place + PAD, -4096), at)
    found = dot(picks((col == at + shift) & ((row & 15) < 8)), ext.astype(BF))
    here = found[16:32]
    value = taps[0] * found[0:16] + taps[1] * here + taps[2] * found[32:48]
    act = value * phi_of(value)
    row = lax.broadcasted_iota(jnp.int32, act.shape, 0)
    return jnp.where(row < 4, act, here).astype(BF)


def taps_of(filt, cols):
    return [filt[k : k + 1, cols] for k in range(3)]


def tap_sums(conv, ext, rows):
    before, after = around(ext)
    body = slice(PAD, PAD + rows)
    mine = conv[body]
    return [
        jnp.sum(mine * other[body], axis=0, keepdims=True) for other in (before, ext, after)
    ]


def grads(conv, direct, taps, rows, pair):
    before, after = around(conv)
    body = slice(PAD, PAD + rows)
    total = direct + taps[0] * after[body] + taps[1] * conv[body] + taps[2] * before[body]
    short = rows // 2
    sums = []
    for k in range(total.shape[1] // LANES):
        pair[k] = total[:, k * LANES : (k + 1) * LANES]
        sums.append(pair[k, pl.ds(0, short, 2), :] + pair[k, pl.ds(1, short, 2), :])
    return total, jnp.concatenate(sums, axis=1)


def own_slope_kernel(meta, offsets, bins, att, skip, edge, filt, asked, sums, slopes, ext):
    half = skip.shape[2]
    tall = ext.shape[1]
    width = ext.shape[2]

    @pl.loop(0, half // width)
    def _(part):
        cols = pl.ds(pl.multiple_of(part * width, width), width)
        slab_sums(att, skip, edge, edge, ext, cols)
        taps = taps_of(filt, cols)
        for s in range(2):
            field = ext[s]
            before, after = around(field)
            slopes[s, :, cols] = slope_of(taps[0] * before + taps[1] * field + taps[2] * after)
            sums[s, :, cols] = field.astype(BF)
            asked[s * 16 : s * 16 + 16, cols] = asked_rows(
                meta, offsets, bins, s, field, taps, tall
            )


def own_slopes(meta, offsets, bins, attention, skip, edge, filt):
    seqs, rows, wide = skip.shape
    _, short, half = attention.shape
    tall = rows + 2 * PAD

    def whole(*shape):
        return pl.BlockSpec(shape, lambda i, m, o, b: (0,) * len(shape))

    def mine(*shape):
        return pl.BlockSpec(shape, lambda i, m, o, b: (0,) * (len(shape) - 1) + (m[0],))

    return pl.pallas_call(
        own_slope_kernel,
        grid_spec=pltpu.PrefetchScalarGridSpec(
            num_scalar_prefetch=3,
            grid=(1,),
            in_specs=[
                pl.BlockSpec((2, short, half), lambda i, m, o, b: (m[0], 0, 0)),
                mine(2, rows, half),
                mine(16, half),
                mine(3, half),
            ],
            out_specs=[whole(32, half), whole(2, tall, half), whole(2, tall, half)],
            scratch_shapes=[pltpu.VMEM((2, tall, 256), F32)],
        ),
        out_shape=[
            jax.ShapeDtypeStruct((32, half), BF),
            jax.ShapeDtypeStruct((2, tall, half), BF),
            jax.ShapeDtypeStruct((2, tall, half), F32),
        ],
        compiler_params=params(),
        cost_estimate=cost(3 * 10**9, 10**6),
        name="own_slopes",
    )(meta, offsets, bins, attention, skip, edge, filt)


def own_kernel(
    slabs, meta, offsets, sums, slopes, rims, prev_far, cot_far, weight_far, filt,
    moved, terms, skip_grad, att_grad, pair, prev, cot, weight, sems,
):
    copies = [
        pltpu.make_async_copy(prev_far, prev, sems.at[0]),
        pltpu.make_async_copy(cot_far, cot, sems.at[1]),
        pltpu.make_async_copy(weight_far, weight, sems.at[2]),
    ]
    for copy in copies:
        copy.start()
    half = sums.shape[2]
    tall = sums.shape[1]
    rows = tall - 2 * PAD
    wide = cot.shape[2]
    row, col = grid_of(tall, rows)
    last = meta[1] == slabs - 1
    copies[0].wait()
    copies[1].wait()
    for s in range(2):
        at = row - PAD
        fits = (at >= -1) & (at < jnp.where(last, rows, rows + 1))
        source = jnp.where(fits, at - offsets[s], -4096)
        older = picks(col == source + rows)
        newer = picks(col == source)
        place = lax.broadcasted_iota(jnp.int32, (PAD, 512), 0)
        top = (place == PAD - 1) & (offsets[s] == rows)
        bottom = (place == 0) & (offsets[s] == 0) & jnp.logical_not(last)
        for part in range(0, wide, 512):
            cols = slice(part, part + 512)
            found = dot(older, prev[s, :, cols]) + dot(newer, cot[s, :, cols])
            ends = rims[:, cols].astype(F32)
            above = ends[s * 8 + 4 : s * 8 + 5]
            below = ends[s * 8 + 3 : s * 8 + 4]
            found = jnp.concatenate(
                [
                    found[:PAD] + jnp.where(top, above, 0.0),
                    found[PAD : PAD + rows],
                    found[PAD + rows :] + jnp.where(bottom, below, 0.0),
                ]
            )
            moved[s, :, cols] = found.astype(BF)
    copies[2].wait()
    width = 2 * LANES
    first = meta[0] * half

    @pl.loop(0, half // width)
    def _(part):
        begin = pl.multiple_of(part * width, width)
        cols = pl.ds(begin, width)
        taps = taps_of(filt, cols)
        piece = weight[pl.ds(begin, width), :]
        total_terms = [0.0, 0.0, 0.0]
        there = pl.ds(pl.multiple_of(first + begin, width), width)
        for s in range(2):
            conv = (dot_rows(moved[s], piece) * slopes[s, :, cols]).astype(BF).astype(F32)
            got = tap_sums(conv, sums[s, :, cols].astype(F32), rows)
            total_terms = [a + b for a, b in zip(total_terms, got)]
            direct = moved[s, :, there].astype(F32)[PAD : PAD + rows]
            total, pairs = grads(conv, direct, taps, rows, pair)
            skip_grad[s, :, cols] = total.astype(BF)
            att_grad[s, :, cols] = pairs.astype(BF)
        for k in range(3):
            terms[k : k + 1, cols] = total_terms[k]


def own_half(meta, offsets, sums, slopes, edge, prev, cot, weight, filt, slabs):
    seqs, rows, wide = cot.shape
    _, tall, half = sums.shape
    short = rows // 2

    def whole(*shape):
        return pl.BlockSpec(shape, lambda i, m, o: (0,) * len(shape))

    def mine(*shape):
        return pl.BlockSpec(shape, lambda i, m, o: (0,) * (len(shape) - 1) + (m[0],))

    anywhere = pl.BlockSpec(memory_space=pl.ANY)
    return pl.pallas_call(
        functools.partial(own_kernel, slabs),
        grid_spec=pltpu.PrefetchScalarGridSpec(
            num_scalar_prefetch=2,
            grid=(1,),
            in_specs=[
                whole(2, tall, half),
                whole(2, tall, half),
                whole(16, wide),
                anywhere,
                anywhere,
                anywhere,
                mine(3, half),
            ],
            out_specs=[
                whole(2, tall, wide),
                whole(3, half),
                mine(2, rows, half),
                mine(2, short, half),
            ],
            scratch_shapes=[
                pltpu.VMEM((2, rows, LANES), F32),
                pltpu.VMEM((2, rows, wide), BF),
                pltpu.VMEM((2, rows, wide), BF),
                pltpu.VMEM((half, wide), BF),
                pltpu.SemaphoreType.DMA((3,)),
            ],
        ),
        out_shape=[
            jax.ShapeDtypeStruct((2, tall, wide), BF),
            jax.ShapeDtypeStruct((3, half), F32),
            jax.ShapeDtypeStruct((2, rows, wide), BF),
            jax.ShapeDtypeStruct((2, short, wide), BF),
        ],
        compiler_params=params(),
        cost_estimate=cost(1, 1),
        name="own_half",
    )(meta, offsets, sums, slopes, edge, prev, cot, weight, filt)


def slope_kernel(
    meta, offsets, bins, att, skip, edge, twin, filt, asked, sums, slopes, mine, shown, ext
):
    rows = skip.shape[1]
    tall = rows + 2 * PAD
    half = skip.shape[2]
    width = ext.shape[2]
    there = (1 - meta[0]) * half
    row, col = grid_of(16, 32)
    at, base = row & 7, (row >> 3) * 16
    kept = picks((at < 4) & (col == base + at + jnp.where(at < 2, 0, 2)))
    told = picks((at < 4) & (col == base + at + jnp.where(at < 2, 2, 4)))
    here = pl.ds(pl.multiple_of(meta[0] * half, half), half)
    mine[:, here] = dot(kept, asked[...]).astype(BF)
    shown[:, here] = dot(told, asked[...]).astype(BF)

    @pl.loop(0, half // width)
    def _(part):
        begin = pl.multiple_of(part * width, width)
        cols = pl.ds(begin, width)
        slab_sums(att, skip, edge, twin, ext, cols)
        taps = taps_of(filt, cols)
        got = []
        for s in range(2):
            field = ext[s]
            before, after = around(field)
            slopes[s, :, cols] = slope_of(taps[0] * before + taps[1] * field + taps[2] * after)
            sums[s, :, cols] = field.astype(BF)
            got.append(asked_rows(meta, offsets, bins, s, field, taps, tall))
        got = jnp.concatenate(got)
        place = pl.ds(pl.multiple_of(there + begin, width), width)
        mine[:, place] = dot(kept, got).astype(BF)
        shown[:, place] = dot(told, got).astype(BF)


def other_slopes(meta, offsets, bins, shipped, skip, edge, twin, filt, asked):
    seqs, rows, wide = skip.shape
    _, packed_rows, half = shipped.shape
    tall = rows + 2 * PAD

    def whole(*shape):
        return pl.BlockSpec(shape, lambda i, m, o, b: (0,) * len(shape))

    def other(*shape):
        return pl.BlockSpec(shape, lambda i, m, o, b: (0,) * (len(shape) - 1) + (1 - m[0],))

    return pl.pallas_call(
        slope_kernel,
        grid_spec=pltpu.PrefetchScalarGridSpec(
            num_scalar_prefetch=3,
            grid=(1,),
            in_specs=[
                whole(2, packed_rows, half),
                other(2, rows, half),
                other(16, half),
                pl.BlockSpec((16, half), lambda i, m, o, b: (0, m[0])),
                other(3, half),
                whole(32, half),
            ],
            out_specs=[whole(2, tall, half), whole(2, tall, half), whole(16, wide), whole(16, wide)],
            scratch_shapes=[pltpu.VMEM((2, tall, 256), F32)],
        ),
        out_shape=[
            jax.ShapeDtypeStruct((2, tall, half), BF),
            jax.ShapeDtypeStruct((2, tall, half), F32),
            jax.ShapeDtypeStruct((16, wide), BF),
            jax.ShapeDtypeStruct((16, wide), BF),
        ],
        compiler_params=params(),
        cost_estimate=cost(3 * 10**9, 10**6),
        name="other_slopes",
    )(meta, offsets, bins, shipped, skip, edge, twin, filt, asked)


def terms_kernel(meta, order, moved, sums, slopes, own_terms, *refs):
    pieces, (convs, terms, full, sems) = refs[:8], refs[8:]
    half = sums.shape[2]
    tall = sums.shape[1]
    rows = tall - 2 * PAD
    there = (1 - meta[0]) * half
    tile = pieces[0].shape[0]
    copies = []
    for k, piece in enumerate(pieces):
        down = pl.multiple_of(order[4 + k // 4] * tile, tile)
        over = pl.multiple_of(order[k % 4] * tile, tile)
        copies.append(
            pltpu.make_async_copy(
                piece, full.at[pl.ds(down, tile), pl.ds(over, tile)], sems.at[k]
            )
        )
        copies[-1].start()
    terms[:, pl.ds(pl.multiple_of(meta[0] * half, half), half)] = own_terms[...]
    for copy in copies:
        copy.wait()
    width = 2 * LANES
    for begin in range(0, half, width):
        cols = slice(begin, begin + width)
        total = [0.0, 0.0, 0.0]
        for s in range(2):
            grad = dot_rows(moved[s], full[cols, :])
            conv = (grad * slopes[s, :, cols]).astype(BF)
            convs[s, :, cols] = conv
            got = tap_sums(conv.astype(F32), sums[s, :, cols].astype(F32), rows)
            total = [a + b for a, b in zip(total, got)]
        place = pl.ds(pl.multiple_of(there + begin, width), width)
        for k in range(3):
            terms[k : k + 1, place] = total[k]


def other_terms(meta, order, moved, sums, slopes, own_terms, pieces):
    _, tall, wide = moved.shape
    half = sums.shape[2]

    def whole(*shape):
        return pl.BlockSpec(shape, lambda i, m, o: (0,) * len(shape))

    return pl.pallas_call(
        terms_kernel,
        grid_spec=pltpu.PrefetchScalarGridSpec(
            num_scalar_prefetch=2,
            grid=(1,),
            in_specs=[
                whole(2, tall, wide),
                whole(2, tall, half),
                whole(2, tall, half),
                whole(3, half),
            ]
            + [pl.BlockSpec(memory_space=pl.ANY)] * 8,
            out_specs=[whole(2, tall, half), whole(3, wide)],
            scratch_shapes=[pltpu.VMEM((half, wide), BF), pltpu.SemaphoreType.DMA((8,))],
        ),
        out_shape=[
            jax.ShapeDtypeStruct((2, tall, half), BF),
            jax.ShapeDtypeStruct((3, wide), F32),
        ],
        compiler_params=params(),
        cost_estimate=cost(2 * 2 * tall * half * wide, 6 * 1024 * 1024),
        name="other_terms",
    )(meta, order, moved, sums, slopes, own_terms, *pieces)


def grads_kernel(meta, moved, convs, filt, old_skip, old_att, skip_grad, att_grad, pair):
    half = convs.shape[2]
    rows = convs.shape[1] - 2 * PAD
    width = 2 * LANES

    @pl.loop(0, half // width)
    def _(part):
        cols = pl.ds(pl.multiple_of(part * width, width), width)
        taps = taps_of(filt, cols)
        for s in range(2):
            direct = moved[s, :, cols].astype(F32)[PAD : PAD + rows]
            total, pairs = grads(convs[s, :, cols].astype(F32), direct, taps, rows, pair)
            skip_grad[s, :, cols] = total.astype(BF)
            att_grad[s, :, cols] = pairs.astype(BF)


def other_grads(meta, moved, convs, filt, skip_grad, att_grad):
    _, tall, wide = moved.shape
    half = convs.shape[2]
    rows = tall - 2 * PAD

    def whole(*shape):
        return pl.BlockSpec(shape, lambda i, m: (0,) * len(shape))

    def other(*shape):
        return pl.BlockSpec(shape, lambda i, m: (0,) * (len(shape) - 1) + (1 - m[0],))

    return pl.pallas_call(
        grads_kernel,
        grid_spec=pltpu.PrefetchScalarGridSpec(
            num_scalar_prefetch=1,
            grid=(1,),
            in_specs=[other(2, tall, half), whole(2, tall, half), other(3, half)]
            + [pl.BlockSpec(memory_space=pl.ANY)] * 2,
            out_specs=[other(2, rows, half), other(2, rows // 2, half)],
            scratch_shapes=[pltpu.VMEM((2, rows, LANES), F32)],
        ),
        out_shape=[
            jax.ShapeDtypeStruct((2, rows, wide), BF),
            jax.ShapeDtypeStruct((2, rows // 2, wide), BF),
        ],
        input_output_aliases={4: 0, 5: 1},
        compiler_params=params(),
        cost_estimate=cost(2 * tall * half * 20, 4 * 1024 * 1024),
        name="other_grads",
    )(meta, moved, convs, filt, skip_grad, att_grad)


def target_kernel(slabs, meta, order, mine, got_a, got_b, weight, *refs):
    pieces, (target, total) = refs[:8], refs[8:]
    half = weight.shape[0]
    there = (1 - meta[0]) * half
    tile = pieces[0].shape[0]
    even = (meta[1] & 1) == 0
    got = jnp.where(even, got_a[...].astype(F32), got_b[...].astype(F32))
    got = jnp.where(meta[1] == slabs - 1, 0.0, got)
    mine[...] = (mine[...].astype(F32) + got).astype(BF)
    here = pl.ds(pl.multiple_of(meta[0] * half, half), half)
    total[...] = dot(mine[:, here], weight[...]) + pltpu.roll(mine[...].astype(F32), 12 + 2, 0)
    for k, piece in enumerate(pieces):
        place = pl.ds(pl.multiple_of(there + order[4 + k // 4] * tile, tile), tile)
        over = pl.ds(pl.multiple_of(order[k % 4] * tile, tile), tile)
        total[:, over] += dot(mine[:, place], piece[...])
    for s in range(2):
        target[s] = total[s * 8 : s * 8 + 2].astype(BF)


def targets(meta, order, mine, got, weight, pieces, slabs):
    half, wide = weight.shape
    tile = pieces[0].shape[0]

    def whole(*shape):
        return pl.BlockSpec(shape, lambda i, m, o: (0,) * len(shape))

    return pl.pallas_call(
        functools.partial(target_kernel, slabs),
        grid_spec=pltpu.PrefetchScalarGridSpec(
            num_scalar_prefetch=2,
            grid=(1,),
            in_specs=[whole(16, wide)] * 3 + [whole(half, wide)]
            + [whole(tile, tile)] * 8,
            out_specs=whole(2, NTD, wide),
            scratch_shapes=[pltpu.VMEM((16, wide), F32)],
        ),
        out_shape=jax.ShapeDtypeStruct((2, NTD, wide), BF),
        compiler_params=params(),
        cost_estimate=cost(2 * 16 * wide * wide, 6 * 1024 * 1024),
        name="targets",
    )(meta, order, mine, *got, weight, *pieces)


def paired(part, axis, bit):
    count = lax.axis_size(axis)
    return lax.ppermute(part, axis, [(i, i ^ bit) for i in range(count)])


def staggered(part, span):
    count = lax.axis_size("seq")
    pairs = []
    for i in range(count):
        by = span if i // span % 2 else -span
        pairs.append((i, (i + by) % count))
    return lax.ppermute(part, "seq", pairs)


def after(value, *others):
    return lax.optimization_barrier((value,) + others)[0]


def crossed(part, seq_bit, head_bit):
    slabs, heads = lax.axis_size("seq"), lax.axis_size("head")
    pairs = [
        (i * heads + j, (i ^ seq_bit) * heads + (j ^ head_bit))
        for i in range(slabs)
        for j in range(heads)
    ]
    return lax.ppermute(part, ("seq", "head"), pairs)


def joined(total, one, two):
    both = (one[0] ^ two[0], one[1] ^ two[1])
    parts = [crossed(total, *bits) for bits in (one, two, both)]
    return (total + parts[0]) + (parts[1] + parts[2])


def fast_shards(
    attention, encoder_skip, depth_filter, point_weight, crop_offset, target_bins, cotangent
):
    head = lax.axis_index("head")
    slab = lax.axis_index("seq")
    slabs = lax.axis_size("seq")
    meta = jnp.stack([head, slab]).astype(jnp.int32)
    core = slab % 2
    block = slab // 2 % 4
    tile = 3 * LANES
    order = jnp.stack([block, block ^ 1, block ^ 2, block ^ 3, core, 1 - core]).astype(jnp.int32)

    edge_a, edge_b, far, first, last_tile, att_out = packed(
        meta, encoder_skip, attention, cotangent, point_weight, tile
    )
    first = paired(first, "head", 1)
    shipped = paired(att_out, "head", 1)
    edge_a = paired(edge_a, "seq", 1)
    edge_b = staggered(edge_b, 1)
    far_a = paired(far, "seq", 2)
    far_b = staggered(far, 2)
    prev = passed_along(after(cotangent, edge_b), "seq", 1)
    outer = (slab == 0) | (slab == slabs - 1)
    nothing = jnp.zeros_like(edge_b)
    edge = edge_a + jnp.where(outer, nothing, edge_b)
    twin = paired(edge, "head", 1)
    edge = edge + jnp.where(slab % 4 >= 2, far_a, jnp.where(slab < 2, nothing, far_b))
    second = paired(first, "seq", 2)
    third = paired(first, "seq", 4)
    fourth = paired(last_tile, "head", 1)
    asked, own_sums, own_slope = own_slopes(
        meta, crop_offset, target_bins, attention, encoder_skip, edge, depth_filter
    )
    sums, slopes, mine, shown = other_slopes(
        meta, crop_offset, target_bins, shipped, encoder_skip, edge, twin, depth_filter, asked
    )
    got = [paired(shown, "seq", 1), staggered(shown, 1)]
    moved, own_terms, skip_grad, att_grad = own_half(
        after(meta, shown), crop_offset, own_sums, own_slope, edge, prev, cotangent, point_weight, depth_filter,
        slabs,
    )
    pieces = [first, second, third, fourth]
    pieces = pieces + [paired(after(piece, own_terms), "seq", 1) for piece in pieces]
    convs, terms = other_terms(meta, order, moved, sums, slopes, own_terms, pieces)
    terms, *got = lax.optimization_barrier((terms, *got))
    total = terms + crossed(terms, 1, 0)
    total = joined(total, (2, 0), (0, 1))
    skip_grad, attention_grad = other_grads(
        meta, moved, convs, depth_filter, skip_grad, att_grad
    )
    target_rows = targets(meta, order, mine, got, point_weight, pieces, slabs)
    total, skip_grad, attention_grad = lax.optimization_barrier(
        (total, skip_grad, attention_grad)
    )
    if slabs == 16:
        total = joined(total, (4, 0), (8, 0))
    else:
        step = 4
        while step < slabs:
            total = total + crossed(total, step, 0)
            step *= 2
    count = encoder_skip.shape[0] * lax.axis_size("head") * encoder_skip.shape[1] * slabs
    return (target_rows, attention_grad, skip_grad, total * (1.0 / math.sqrt(count)))


def shards(*args):
    attention, encoder_skip, point_weight = args[0], args[1], args[3]
    fits = (
        lax.axis_size("head") == 2
        and lax.axis_size("seq") in (8, 16, 32)
        and encoder_skip.shape[:2] == (2, 128)
        and point_weight.shape[0] == 6 * LANES
        and attention.shape[1] == 64
    )
    return fast_shards(*args) if fits else plain_shards(*args)


def solution(mesh):
    in_specs = (
        P(None, "seq", "head"),
        P("head", "seq", None),
        P(),
        P("head", None),
        P("head"),
        P("head", None),
        P("head", "seq", None),
    )
    out_specs = (P("head", "seq", None), P("head", "seq", None), P("head", "seq", None), P())
    return jax.shard_map(shards, mesh=mesh, in_specs=in_specs, out_specs=out_specs, check_vma=False)
def solution(mesh):
    in_specs = (
        P(None, "seq", "head"),
        P("head", "seq", None),
        P(),
        P("head", None),
        P("head"),
        P("head", None),
        P("head", "seq", None),
    )
    out_specs = (P("head", "seq", None), P("head", "seq", None), P("head", "seq", None), P())
    return jax.shard_map(shards, mesh=mesh, in_specs=in_specs, out_specs=out_specs, check_vma=False)
```

```python
import functools
import math

import jax
import jax.numpy as jnp
from jax import lax
from jax.experimental import pallas as pl
from jax.experimental.pallas import tpu as pltpu
from jax.sharding import PartitionSpec as P

NTD = 2


def extended(shard, sides, width):
    for axis, dim in sides:
        count, length = (lax.axis_size(axis), shard.shape[dim])
        up = [(i, (i + 1) % count) for i in range(count - 1)]
        down = [(j, i) for i, j in up]
        last = lax.slice_in_dim(shard, length - width, length, axis=dim)
        initial = lax.slice_in_dim(shard, 0, width, axis=dim)
        before = lax.ppermute(last, axis, up)
        after = lax.ppermute(initial, axis, down)
        shard = jnp.concatenate([before, shard, after], axis=dim)
    return shard


def passed_along(shard, axis, by):
    count = lax.axis_size(axis)
    pairs = [(i, i + by) for i in range(count) if 0 <= i + by < count]
    return lax.ppermute(shard, axis, pairs)


def gelu_slope(values):
    return (
        0.5 * (1.0 + lax.erf(values * 0.7071067811865476))
        + values * jnp.exp(-0.5 * values * values) * 0.3989422804014327
    )


def with_rims(field):
    return extended(field, (("seq", 1),), 1)


def one_hot(places, length):
    return (places[:, :, None] == jnp.arange(length, dtype=jnp.int32)[None, None, :]).astype(
        jnp.bfloat16
    )


def core_swap(part):
    count = lax.axis_size("seq")
    return lax.ppermute(part, "seq", [(i, i ^ 1) for i in range(count)])


def gathered_weight(rows):
    heads = lax.axis_size("head")
    here = lax.axis_index("head")
    core = lax.axis_index("seq") % 2
    half = rows.shape[0] // 2
    mine = lax.dynamic_slice_in_dim(rows, core * half, half, 0)
    blocks = [(0, rows)]
    for step in range(1, heads):
        pairs = [(i, (i + step) % heads) for i in range(heads)]
        got = lax.ppermute(mine, "head", pairs)
        twin = core_swap(got)
        low = jnp.where(core == 0, got, twin)
        high = jnp.where(core == 0, twin, got)
        blocks.append((step, jnp.concatenate([low, high], axis=0)))
    full = jnp.zeros((heads * rows.shape[0], rows.shape[1]), rows.dtype)
    for step, block in blocks:
        place = (here - step) % heads
        full = lax.dynamic_update_slice_in_dim(full, block, place * rows.shape[0], 0)
    return full


def butterfly(total, axis):
    count = lax.axis_size(axis)
    if count & (count - 1):
        return lax.psum(total, axis)
    step = 1
    while step < count:
        total = total + lax.ppermute(total, axis, [(i, i ^ step) for i in range(count)])
        step *= 2
    return total


def plain_shards(
    attention, encoder_skip, depth_filter, point_weight, crop_offset, target_bins, cotangent
):
    slab_input = lax.all_to_all(attention, "head", split_axis=0, concat_axis=2, tiled=True)
    local_seqs = encoder_skip.shape[0]
    slab_rows = encoder_skip.shape[1]
    channels = encoder_skip.shape[2]
    summed = (
        jnp.repeat(slab_input, 2, axis=1).astype(jnp.float32) + encoder_skip.astype(jnp.float32)
    ).astype(jnp.bfloat16)
    padded = with_rims(summed)
    filtered = (
        depth_filter[0] * padded[:, :-2]
        + depth_filter[1] * padded[:, 1:-1]
        + depth_filter[2] * padded[:, 2:]
    )
    activated = jax.nn.gelu(filtered, approximate=False).astype(jnp.bfloat16)
    flat_act = activated.reshape(local_seqs * slab_rows, channels)
    full_weight = gathered_weight(point_weight)
    mixed_rows = jnp.dot(flat_act, full_weight, preferred_element_type=jnp.float32)
    block_out = (
        summed.astype(jnp.float32) + mixed_rows.reshape(local_seqs, slab_rows, channels)
    ).astype(jnp.bfloat16)
    slab_index = lax.axis_index("seq")
    bins = jnp.concatenate(
        [jnp.zeros_like(target_bins[:, :NTD]), target_bins], axis=1
    )
    asked = lax.dynamic_slice_in_dim(bins, slab_index * NTD, 2 * NTD, 1) + crop_offset[:, None]
    back = jnp.where(jnp.arange(2 * NTD, dtype=jnp.int32) < NTD, slab_rows, 0)
    asked = asked - back[None, :]
    picked = jnp.einsum(
        "sjr,srd->sjd",
        one_hot(asked, slab_rows),
        block_out,
        preferred_element_type=jnp.float32,
    ).astype(jnp.bfloat16)
    from_next = passed_along(picked[:, :NTD], "seq", -1)
    target_rows = picked[:, NTD:] + from_next
    prev_cot = passed_along(cotangent, "seq", 1)
    cot_pair = jnp.concatenate([prev_cot, cotangent], axis=1)

    def crop_back(cot_block, shift_by):
        return lax.dynamic_slice_in_dim(cot_block, slab_rows - shift_by, slab_rows, 0)

    grad_out = jax.vmap(crop_back)(cot_pair, crop_offset)
    flat_grad = grad_out.reshape(local_seqs * slab_rows, channels)
    grad_act = lax.dot_general(
        flat_grad, full_weight, (((1,), (1,)), ((), ())), preferred_element_type=jnp.float32
    )
    grad_conv = (grad_act.reshape(local_seqs, slab_rows, channels) * gelu_slope(filtered)).astype(
        jnp.bfloat16
    )
    grad_padded = with_rims(grad_conv)
    grad_sum = (
        grad_out.astype(jnp.float32)
        + depth_filter[0] * grad_padded[:, 2:]
        + depth_filter[1] * grad_padded[:, 1:-1]
        + depth_filter[2] * grad_padded[:, :-2]
    )
    skip_grad = grad_sum.astype(jnp.bfloat16)
    attention_grad = (
        grad_sum.reshape(local_seqs, slab_rows // 2, 2, channels).sum(axis=2).astype(jnp.bfloat16)
    )
    filter_terms = jnp.stack(
        [
            jnp.einsum(
                "srd,srd->d", grad_conv, padded[:, 0:slab_rows], preferred_element_type=jnp.float32
            ),
            jnp.einsum(
                "srd,srd->d",
                grad_conv,
                padded[:, 1 : slab_rows + 1],
                preferred_element_type=jnp.float32,
            ),
            jnp.einsum(
                "srd,srd->d",
                grad_conv,
                padded[:, 2 : slab_rows + 2],
                preferred_element_type=jnp.float32,
            ),
        ]
    )
    filter_sum = butterfly(butterfly(filter_terms, "seq"), "head")
    row_count = local_seqs * lax.axis_size("head") * slab_rows * lax.axis_size("seq")
    filter_grad = filter_sum * (1.0 / math.sqrt(row_count))
    return (target_rows, attention_grad, skip_grad, filter_grad)


import functools
import math

import jax
import jax.numpy as jnp
from jax import lax
from jax.experimental import pallas as pl
from jax.experimental.pallas import tpu as pltpu
from jax.sharding import PartitionSpec as P

NTD = 2


def extended(shard, sides, width):
    for axis, dim in sides:
        count, length = (lax.axis_size(axis), shard.shape[dim])
        up = [(i, (i + 1) % count) for i in range(count - 1)]
        down = [(j, i) for i, j in up]
        last = lax.slice_in_dim(shard, length - width, length, axis=dim)
        initial = lax.slice_in_dim(shard, 0, width, axis=dim)
        before = lax.ppermute(last, axis, up)
        after = lax.ppermute(initial, axis, down)
        shard = jnp.concatenate([before, shard, after], axis=dim)
    return shard


def passed_along(shard, axis, by):
    count = lax.axis_size(axis)
    pairs = [(i, i + by) for i in range(count) if 0 <= i + by < count]
    return lax.ppermute(shard, axis, pairs)


def gelu_slope(values):
    return (
        0.5 * (1.0 + lax.erf(values * 0.7071067811865476))
        + values * jnp.exp(-0.5 * values * values) * 0.3989422804014327
    )


def with_rims(field):
    return extended(field, (("seq", 1),), 1)


def one_hot(places, length):
    return (places[:, :, None] == jnp.arange(length, dtype=jnp.int32)[None, None, :]).astype(
        jnp.bfloat16
    )


def core_swap(part):
    count = lax.axis_size("seq")
    return lax.ppermute(part, "seq", [(i, i ^ 1) for i in range(count)])


def gathered_weight(rows):
    heads = lax.axis_size("head")
    here = lax.axis_index("head")
    core = lax.axis_index("seq") % 2
    half = rows.shape[0] // 2
    mine = lax.dynamic_slice_in_dim(rows, core * half, half, 0)
    blocks = [(0, rows)]
    for step in range(1, heads):
        pairs = [(i, (i + step) % heads) for i in range(heads)]
        got = lax.ppermute(mine, "head", pairs)
        twin = core_swap(got)
        low = jnp.where(core == 0, got, twin)
        high = jnp.where(core == 0, twin, got)
        blocks.append((step, jnp.concatenate([low, high], axis=0)))
    full = jnp.zeros((heads * rows.shape[0], rows.shape[1]), rows.dtype)
    for step, block in blocks:
        place = (here - step) % heads
        full = lax.dynamic_update_slice_in_dim(full, block, place * rows.shape[0], 0)
    return full


def butterfly(total, axis):
    count = lax.axis_size(axis)
    if count & (count - 1):
        return lax.psum(total, axis)
    step = 1
    while step < count:
        total = total + lax.ppermute(total, axis, [(i, i ^ step) for i in range(count)])
        step *= 2
    return total


def plain_shards(
    attention, encoder_skip, depth_filter, point_weight, crop_offset, target_bins, cotangent
):
    slab_input = lax.all_to_all(attention, "head", split_axis=0, concat_axis=2, tiled=True)
    local_seqs = encoder_skip.shape[0]
    slab_rows = encoder_skip.shape[1]
    channels = encoder_skip.shape[2]
    summed = (
        jnp.repeat(slab_input, 2, axis=1).astype(jnp.float32) + encoder_skip.astype(jnp.float32)
    ).astype(jnp.bfloat16)
    padded = with_rims(summed)
    filtered = (
        depth_filter[0] * padded[:, :-2]
        + depth_filter[1] * padded[:, 1:-1]
        + depth_filter[2] * padded[:, 2:]
    )
    activated = jax.nn.gelu(filtered, approximate=False).astype(jnp.bfloat16)
    flat_act = activated.reshape(local_seqs * slab_rows, channels)
    full_weight = gathered_weight(point_weight)
    mixed_rows = jnp.dot(flat_act, full_weight, preferred_element_type=jnp.float32)
    block_out = (
        summed.astype(jnp.float32) + mixed_rows.reshape(local_seqs, slab_rows, channels)
    ).astype(jnp.bfloat16)
    slab_index = lax.axis_index("seq")
    bins = jnp.concatenate(
        [jnp.zeros_like(target_bins[:, :NTD]), target_bins], axis=1
    )
    asked = lax.dynamic_slice_in_dim(bins, slab_index * NTD, 2 * NTD, 1) + crop_offset[:, None]
    back = jnp.where(jnp.arange(2 * NTD, dtype=jnp.int32) < NTD, slab_rows, 0)
    asked = asked - back[None, :]
    picked = jnp.einsum(
        "sjr,srd->sjd",
        one_hot(asked, slab_rows),
        block_out,
        preferred_element_type=jnp.float32,
    ).astype(jnp.bfloat16)
    from_next = passed_along(picked[:, :NTD], "seq", -1)
    target_rows = picked[:, NTD:] + from_next
    prev_cot = passed_along(cotangent, "seq", 1)
    cot_pair = jnp.concatenate([prev_cot, cotangent], axis=1)

    def crop_back(cot_block, shift_by):
        return lax.dynamic_slice_in_dim(cot_block, slab_rows - shift_by, slab_rows, 0)

    grad_out = jax.vmap(crop_back)(cot_pair, crop_offset)
    flat_grad = grad_out.reshape(local_seqs * slab_rows, channels)
    grad_act = lax.dot_general(
        flat_grad, full_weight, (((1,), (1,)), ((), ())), preferred_element_type=jnp.float32
    )
    grad_conv = (grad_act.reshape(local_seqs, slab_rows, channels) * gelu_slope(filtered)).astype(
        jnp.bfloat16
    )
    grad_padded = with_rims(grad_conv)
    grad_sum = (
        grad_out.astype(jnp.float32)
        + depth_filter[0] * grad_padded[:, 2:]
        + depth_filter[1] * grad_padded[:, 1:-1]
        + depth_filter[2] * grad_padded[:, :-2]
    )
    skip_grad = grad_sum.astype(jnp.bfloat16)
    attention_grad = (
        grad_sum.reshape(local_seqs, slab_rows // 2, 2, channels).sum(axis=2).astype(jnp.bfloat16)
    )
    filter_terms = jnp.stack(
        [
            jnp.einsum(
                "srd,srd->d", grad_conv, padded[:, 0:slab_rows], preferred_element_type=jnp.float32
            ),
            jnp.einsum(
                "srd,srd->d",
                grad_conv,
                padded[:, 1 : slab_rows + 1],
                preferred_element_type=jnp.float32,
            ),
            jnp.einsum(
                "srd,srd->d",
                grad_conv,
                padded[:, 2 : slab_rows + 2],
                preferred_element_type=jnp.float32,
            ),
        ]
    )
    filter_sum = butterfly(butterfly(filter_terms, "seq"), "head")
    row_count = local_seqs * lax.axis_size("head") * slab_rows * lax.axis_size("seq")
    filter_grad = filter_sum * (1.0 / math.sqrt(row_count))
    return (target_rows, attention_grad, skip_grad, filter_grad)


LANES = 128
PAD = 8
BF = jnp.bfloat16
F32 = jnp.float32


def dot(left, right):
    return lax.dot_general(left, right, (((1,), (0,)), ((), ())), preferred_element_type=F32)


def dot_rows(left, right):
    return lax.dot_general(left, right, (((1,), (1,)), ((), ())), preferred_element_type=F32)


def grid_of(rows, columns):
    return (
        lax.broadcasted_iota(jnp.int32, (rows, columns), 0),
        lax.broadcasted_iota(jnp.int32, (rows, columns), 1),
    )


def picks(match):
    return jnp.where(match, 1.0, 0.0).astype(BF)


def params(mib=20):
    return pltpu.CompilerParams(vmem_limit_bytes=mib * 1024 * 1024)


def cost(flops, moved, special=0):
    return pl.CostEstimate(flops=flops, bytes_accessed=moved, transcendentals=special)


def pack_kernel(
    meta, skip_lo, skip_hi, att_lo, att_hi, cot_lo, cot_hi, near, distant, att,
    edge_a, edge_b, far, tile_a, tile_b, att_out,
):
    att_out[...] = att[...]
    tile_a[...] = near[...]
    tile_b[...] = distant[...]
    wide = cot_lo.shape[2]
    at = lax.broadcasted_iota(jnp.int32, (8, wide), 0)
    even = (meta[1] & 1) == 0
    ups, downs, ends = [], [], []
    for s in range(2):
        feats = [jnp.concatenate([part[s], part[2 + s]], axis=1) for part in (att_hi, att_lo)]
        high, low = feats[0].astype(F32)[8:], feats[1].astype(F32)[:8]
        up = jnp.where(at >= 6, skip_hi[s].astype(F32)[8:], 0.0)
        ups.append(jnp.where(at == 5, pltpu.roll(high, 6, 0), up))
        down = jnp.where(at < 2, skip_lo[s].astype(F32)[:8], 0.0)
        down = jnp.where(at == 2, pltpu.roll(low, 2, 0), down)
        downs.append(jnp.where(at == 3, pltpu.roll(cot_lo[s].astype(F32)[:8], 3, 0), down))
        last = pltpu.roll(cot_hi[s].astype(F32)[8:], 5, 0)
        ends.append(jnp.where(at == 4, last, 0.0))
    up, down = jnp.concatenate(ups), jnp.concatenate(downs)
    edge_a[...] = jnp.where(even, up, down).astype(BF)
    edge_b[...] = jnp.where(even, down, up).astype(BF)
    far[...] = jnp.concatenate(ends).astype(BF)


def packed(meta, encoder_skip, attention, cotangent, weight, tile):
    seqs, rows, wide = encoder_skip.shape
    half = attention.shape[2]
    short = attention.shape[1]

    def block(count, width, place):
        return pl.BlockSpec((count, 16, width), lambda i, m: (0, place, 0))

    out = jax.ShapeDtypeStruct((16, wide), BF)
    square = jax.ShapeDtypeStruct((tile, tile), BF)
    return pl.pallas_call(
        pack_kernel,
        grid_spec=pltpu.PrefetchScalarGridSpec(
            num_scalar_prefetch=1,
            grid=(1,),
            in_specs=[
                block(seqs, wide, 0),
                block(seqs, wide, rows // 16 - 1),
                block(2 * seqs, half, 0),
                block(2 * seqs, half, short // 16 - 1),
                block(seqs, wide, 0),
                block(seqs, wide, rows // 16 - 1),
                pl.BlockSpec((tile, tile), lambda i, m: (m[1] & 1, (m[1] >> 1) & 3)),
                pl.BlockSpec((tile, tile), lambda i, m: (m[1] & 1, 3 - ((m[1] >> 1) & 3))),
                pl.BlockSpec((2, short, half), lambda i, m: (1 - m[0], 0, 0)),
            ],
            out_specs=[pl.BlockSpec((16, wide), lambda i, m: (0, 0))] * 3
            + [pl.BlockSpec((tile, tile), lambda i, m: (0, 0))] * 2
            + [pl.BlockSpec((2, short, half), lambda i, m: (0, 0, 0))],
        ),
        out_shape=[out, out, out, square, square, jax.ShapeDtypeStruct((2, short, half), BF)],
        compiler_params=params(60),
        name="pack_edges",
    )(
        meta, encoder_skip, encoder_skip, attention, attention, cotangent, cotangent, weight,
        weight, attention,
    )


def slab_sums(att, skip, edge, twin, ext, cols):
    width = cols.size
    short = 64
    row, col = grid_of(2 * short, short)
    spread = picks((row >> 1) == col)
    row, col = grid_of(16, 16)
    at, base = row & 7, row & 8
    wanted = ((at >= 6) & (col == base + 5)) | ((at < 2) & (col == base + 2))
    from_att = dot(picks(wanted), twin[:, cols])
    rims = edge[:, cols]
    at = lax.broadcasted_iota(jnp.int32, (16, width), 0) & 7
    rims = (from_att + rims.astype(F32)).astype(BF).astype(F32)
    above = jnp.where(at >= 6, rims, 0.0)
    below = jnp.where(at < 2, rims, 0.0)
    for s in range(2):
        body = dot(spread, att[s, 0:short, cols]) + skip[s, :, cols].astype(F32)
        ext[s, 0:PAD] = above[s * 8 : s * 8 + 8]
        ext[s, PAD : PAD + 2 * short] = body.astype(BF).astype(F32)
        ext[s, PAD + 2 * short : 2 * PAD + 2 * short] = below[s * 8 : s * 8 + 8]


def around(field):
    tall = field.shape[0]
    return pltpu.roll(field, 1, 0), pltpu.roll(field, tall - 1, 0)


def phi_of(values):
    return 0.5 * (1.0 + lax.erf(values * 0.7071067811865476))


def slope_of(values):
    return phi_of(values) + values * jnp.exp(-0.5 * values * values) * 0.3989422804014327


def asked_rows(meta, offsets, bins, s, ext, taps, tall):
    row, col = grid_of(48, tall)
    want = row & 3
    shift = (row >> 4) - 1
    at = jnp.full((48, tall), -4096, jnp.int32)
    slab = meta[1]
    for k in range(4):
        mine = k < NTD
        home = slab if mine else jnp.maximum(slab - 1, 0)
        place = bins[s, home * NTD + (k % NTD)] + offsets[s] - (0 if mine else tall - 2 * PAD)
        fits = (place >= 0) & (place < tall - 2 * PAD)
        at = jnp.where(want == k, jnp.where(fits, place + PAD, -4096), at)
    found = dot(picks((col == at + shift) & ((row & 15) < 8)), ext.astype(BF))
    here = found[16:32]
    value = taps[0] * found[0:16] + taps[1] * here + taps[2] * found[32:48]
    act = value * phi_of(value)
    row = lax.broadcasted_iota(jnp.int32, act.shape, 0)
    return jnp.where(row < 4, act, here).astype(BF)


def taps_of(filt, cols):
    return [filt[k : k + 1, cols] for k in range(3)]


def tap_sums(conv, ext, rows):
    before, after = around(ext)
    body = slice(PAD, PAD + rows)
    mine = conv[body]
    return [
        jnp.sum(mine * other[body], axis=0, keepdims=True) for other in (before, ext, after)
    ]


def grads(conv, direct, taps, rows, pair):
    before, after = around(conv)
    body = slice(PAD, PAD + rows)
    total = direct + taps[0] * after[body] + taps[1] * conv[body] + taps[2] * before[body]
    short = rows // 2
    sums = []
    for k in range(total.shape[1] // LANES):
        pair[k] = total[:, k * LANES : (k + 1) * LANES]
        sums.append(pair[k, pl.ds(0, short, 2), :] + pair[k, pl.ds(1, short, 2), :])
    return total, jnp.concatenate(sums, axis=1)


def own_slope_kernel(meta, offsets, bins, att, skip, edge, filt, asked, sums, slopes, ext):
    half = skip.shape[2]
    tall = ext.shape[1]
    width = ext.shape[2]

    @pl.loop(0, half // width)
    def _(part):
        cols = pl.ds(pl.multiple_of(part * width, width), width)
        slab_sums(att, skip, edge, edge, ext, cols)
        taps = taps_of(filt, cols)
        for s in range(2):
            field = ext[s]
            before, after = around(field)
            slopes[s, :, cols] = slope_of(taps[0] * before + taps[1] * field + taps[2] * after)
            sums[s, :, cols] = field.astype(BF)
            asked[s * 16 : s * 16 + 16, cols] = asked_rows(
                meta, offsets, bins, s, field, taps, tall
            )


def own_slopes(meta, offsets, bins, attention, skip, edge, filt):
    seqs, rows, wide = skip.shape
    _, short, half = attention.shape
    tall = rows + 2 * PAD

    def whole(*shape):
        return pl.BlockSpec(shape, lambda i, m, o, b: (0,) * len(shape))

    def mine(*shape):
        return pl.BlockSpec(shape, lambda i, m, o, b: (0,) * (len(shape) - 1) + (m[0],))

    return pl.pallas_call(
        own_slope_kernel,
        grid_spec=pltpu.PrefetchScalarGridSpec(
            num_scalar_prefetch=3,
            grid=(1,),
            in_specs=[
                pl.BlockSpec((2, short, half), lambda i, m, o, b: (m[0], 0, 0)),
                mine(2, rows, half),
                mine(16, half),
                mine(3, half),
            ],
            out_specs=[whole(32, half), whole(2, tall, half), whole(2, tall, half)],
            scratch_shapes=[pltpu.VMEM((2, tall, 256), F32)],
        ),
        out_shape=[
            jax.ShapeDtypeStruct((32, half), BF),
            jax.ShapeDtypeStruct((2, tall, half), BF),
            jax.ShapeDtypeStruct((2, tall, half), F32),
        ],
        compiler_params=params(),
        cost_estimate=cost(3 * 10**9, 10**6),
        name="own_slopes",
    )(meta, offsets, bins, attention, skip, edge, filt)


def own_kernel(
    slabs, meta, offsets, sums, slopes, rims, prev_far, cot_far, weight_far, filt,
    moved, terms, skip_grad, att_grad, pair, prev, cot, weight, sems,
):
    copies = [
        pltpu.make_async_copy(prev_far, prev, sems.at[0]),
        pltpu.make_async_copy(cot_far, cot, sems.at[1]),
        pltpu.make_async_copy(weight_far, weight, sems.at[2]),
    ]
    for copy in copies:
        copy.start()
    half = sums.shape[2]
    tall = sums.shape[1]
    rows = tall - 2 * PAD
    wide = cot.shape[2]
    row, col = grid_of(tall, rows)
    last = meta[1] == slabs - 1
    copies[0].wait()
    copies[1].wait()
    for s in range(2):
        at = row - PAD
        fits = (at >= -1) & (at < jnp.where(last, rows, rows + 1))
        source = jnp.where(fits, at - offsets[s], -4096)
        older = picks(col == source + rows)
        newer = picks(col == source)
        place = lax.broadcasted_iota(jnp.int32, (PAD, 512), 0)
        top = (place == PAD - 1) & (offsets[s] == rows)
        bottom = (place == 0) & (offsets[s] == 0) & jnp.logical_not(last)
        for part in range(0, wide, 512):
            cols = slice(part, part + 512)
            found = dot(older, prev[s, :, cols]) + dot(newer, cot[s, :, cols])
            ends = rims[:, cols].astype(F32)
            above = ends[s * 8 + 4 : s * 8 + 5]
            below = ends[s * 8 + 3 : s * 8 + 4]
            found = jnp.concatenate(
                [
                    found[:PAD] + jnp.where(top, above, 0.0),
                    found[PAD : PAD + rows],
                    found[PAD + rows :] + jnp.where(bottom, below, 0.0),
                ]
            )
            moved[s, :, cols] = found.astype(BF)
    copies[2].wait()
    width = 2 * LANES
    first = meta[0] * half

    @pl.loop(0, half // width)
    def _(part):
        begin = pl.multiple_of(part * width, width)
        cols = pl.ds(begin, width)
        taps = taps_of(filt, cols)
        piece = weight[pl.ds(begin, width), :]
        total_terms = [0.0, 0.0, 0.0]
        there = pl.ds(pl.multiple_of(first + begin, width), width)
        for s in range(2):
            conv = (dot_rows(moved[s], piece) * slopes[s, :, cols]).astype(BF).astype(F32)
            got = tap_sums(conv, sums[s, :, cols].astype(F32), rows)
            total_terms = [a + b for a, b in zip(total_terms, got)]
            direct = moved[s, :, there].astype(F32)[PAD : PAD + rows]
            total, pairs = grads(conv, direct, taps, rows, pair)
            skip_grad[s, :, cols] = total.astype(BF)
            att_grad[s, :, cols] = pairs.astype(BF)
        for k in range(3):
            terms[k : k + 1, cols] = total_terms[k]


def own_half(meta, offsets, sums, slopes, edge, prev, cot, weight, filt, slabs):
    seqs, rows, wide = cot.shape
    _, tall, half = sums.shape
    short = rows // 2

    def whole(*shape):
        return pl.BlockSpec(shape, lambda i, m, o: (0,) * len(shape))

    def mine(*shape):
        return pl.BlockSpec(shape, lambda i, m, o: (0,) * (len(shape) - 1) + (m[0],))

    anywhere = pl.BlockSpec(memory_space=pl.ANY)
    return pl.pallas_call(
        functools.partial(own_kernel, slabs),
        grid_spec=pltpu.PrefetchScalarGridSpec(
            num_scalar_prefetch=2,
            grid=(1,),
            in_specs=[
                whole(2, tall, half),
                whole(2, tall, half),
                whole(16, wide),
                anywhere,
                anywhere,
                anywhere,
                mine(3, half),
            ],
            out_specs=[
                whole(2, tall, wide),
                whole(3, half),
                mine(2, rows, half),
                mine(2, short, half),
            ],
            scratch_shapes=[
                pltpu.VMEM((2, rows, LANES), F32),
                pltpu.VMEM((2, rows, wide), BF),
                pltpu.VMEM((2, rows, wide), BF),
                pltpu.VMEM((half, wide), BF),
                pltpu.SemaphoreType.DMA((3,)),
            ],
        ),
        out_shape=[
            jax.ShapeDtypeStruct((2, tall, wide), BF),
            jax.ShapeDtypeStruct((3, half), F32),
            jax.ShapeDtypeStruct((2, rows, wide), BF),
            jax.ShapeDtypeStruct((2, short, wide), BF),
        ],
        compiler_params=params(),
        cost_estimate=cost(1, 1),
        name="own_half",
    )(meta, offsets, sums, slopes, edge, prev, cot, weight, filt)


def slope_kernel(
    meta, offsets, bins, att, skip, edge, twin, filt, asked, sums, slopes, mine, shown, ext
):
    rows = skip.shape[1]
    tall = rows + 2 * PAD
    half = skip.shape[2]
    width = ext.shape[2]
    there = (1 - meta[0]) * half
    row, col = grid_of(16, 32)
    at, base = row & 7, (row >> 3) * 16
    kept = picks((at < 4) & (col == base + at + jnp.where(at < 2, 0, 2)))
    told = picks((at < 4) & (col == base + at + jnp.where(at < 2, 2, 4)))
    here = pl.ds(pl.multiple_of(meta[0] * half, half), half)
    mine[:, here] = dot(kept, asked[...]).astype(BF)
    shown[:, here] = dot(told, asked[...]).astype(BF)

    @pl.loop(0, half // width)
    def _(part):
        begin = pl.multiple_of(part * width, width)
        cols = pl.ds(begin, width)
        slab_sums(att, skip, edge, twin, ext, cols)
        taps = taps_of(filt, cols)
        got = []
        for s in range(2):
            field = ext[s]
            before, after = around(field)
            slopes[s, :, cols] = slope_of(taps[0] * before + taps[1] * field + taps[2] * after)
            sums[s, :, cols] = field.astype(BF)
            got.append(asked_rows(meta, offsets, bins, s, field, taps, tall))
        got = jnp.concatenate(got)
        place = pl.ds(pl.multiple_of(there + begin, width), width)
        mine[:, place] = dot(kept, got).astype(BF)
        shown[:, place] = dot(told, got).astype(BF)


def other_slopes(meta, offsets, bins, shipped, skip, edge, twin, filt, asked):
    seqs, rows, wide = skip.shape
    _, packed_rows, half = shipped.shape
    tall = rows + 2 * PAD

    def whole(*shape):
        return pl.BlockSpec(shape, lambda i, m, o, b: (0,) * len(shape))

    def other(*shape):
        return pl.BlockSpec(shape, lambda i, m, o, b: (0,) * (len(shape) - 1) + (1 - m[0],))

    return pl.pallas_call(
        slope_kernel,
        grid_spec=pltpu.PrefetchScalarGridSpec(
            num_scalar_prefetch=3,
            grid=(1,),
            in_specs=[
                whole(2, packed_rows, half),
                other(2, rows, half),
                other(16, half),
                pl.BlockSpec((16, half), lambda i, m, o, b: (0, m[0])),
                other(3, half),
                whole(32, half),
            ],
            out_specs=[whole(2, tall, half), whole(2, tall, half), whole(16, wide), whole(16, wide)],
            scratch_shapes=[pltpu.VMEM((2, tall, 256), F32)],
        ),
        out_shape=[
            jax.ShapeDtypeStruct((2, tall, half), BF),
            jax.ShapeDtypeStruct((2, tall, half), F32),
            jax.ShapeDtypeStruct((16, wide), BF),
            jax.ShapeDtypeStruct((16, wide), BF),
        ],
        compiler_params=params(),
        cost_estimate=cost(3 * 10**9, 10**6),
        name="other_slopes",
    )(meta, offsets, bins, shipped, skip, edge, twin, filt, asked)


def spots(meta, tile):
    core, block = meta[1] & 1, (meta[1] >> 1) & 3
    return [
        (pl.multiple_of(row * tile, tile), pl.multiple_of((block ^ k) * tile, tile))
        for row in (core, 1 - core)
        for k in range(4)
    ]


def terms_kernel(meta, moved, sums, slopes, own_terms, *refs):
    pieces, (convs, terms, full, sems) = refs[:8], refs[8:]
    half = sums.shape[2]
    tall = sums.shape[1]
    rows = tall - 2 * PAD
    there = (1 - meta[0]) * half
    tile = pieces[0].shape[0]
    copies = []
    for k, (down, over) in enumerate(spots(meta, tile)):
        copies.append(
            pltpu.make_async_copy(
                pieces[k], full.at[pl.ds(down, tile), pl.ds(over, tile)], sems.at[k]
            )
        )
        copies[-1].start()
    terms[:, pl.ds(pl.multiple_of(meta[0] * half, half), half)] = own_terms[...]
    for copy in copies:
        copy.wait()
    width = 2 * LANES
    for begin in range(0, half, width):
        cols = slice(begin, begin + width)
        total = [0.0, 0.0, 0.0]
        for s in range(2):
            grad = dot_rows(moved[s], full[cols, :])
            conv = (grad * slopes[s, :, cols]).astype(BF)
            convs[s, :, cols] = conv
            got = tap_sums(conv.astype(F32), sums[s, :, cols].astype(F32), rows)
            total = [a + b for a, b in zip(total, got)]
        place = pl.ds(pl.multiple_of(there + begin, width), width)
        for k in range(3):
            terms[k : k + 1, place] = total[k]


def other_terms(meta, moved, sums, slopes, own_terms, pieces):
    _, tall, wide = moved.shape
    half = sums.shape[2]

    def whole(*shape):
        return pl.BlockSpec(shape, lambda i, m: (0,) * len(shape))

    return pl.pallas_call(
        terms_kernel,
        grid_spec=pltpu.PrefetchScalarGridSpec(
            num_scalar_prefetch=1,
            grid=(1,),
            in_specs=[
                whole(2, tall, wide),
                whole(2, tall, half),
                whole(2, tall, half),
                whole(3, half),
            ]
            + [pl.BlockSpec(memory_space=pl.ANY)] * 8,
            out_specs=[whole(2, tall, half), whole(3, wide)],
            scratch_shapes=[pltpu.VMEM((half, wide), BF), pltpu.SemaphoreType.DMA((8,))],
        ),
        out_shape=[
            jax.ShapeDtypeStruct((2, tall, half), BF),
            jax.ShapeDtypeStruct((3, wide), F32),
        ],
        compiler_params=params(),
        cost_estimate=cost(2 * 2 * tall * half * wide, 6 * 1024 * 1024),
        name="other_terms",
    )(meta, moved, sums, slopes, own_terms, *pieces)


def grads_kernel(meta, moved, convs, filt, old_skip, old_att, skip_grad, att_grad, pair):
    half = convs.shape[2]
    rows = convs.shape[1] - 2 * PAD
    width = 2 * LANES

    @pl.loop(0, half // width)
    def _(part):
        cols = pl.ds(pl.multiple_of(part * width, width), width)
        taps = taps_of(filt, cols)
        for s in range(2):
            direct = moved[s, :, cols].astype(F32)[PAD : PAD + rows]
            total, pairs = grads(convs[s, :, cols].astype(F32), direct, taps, rows, pair)
            skip_grad[s, :, cols] = total.astype(BF)
            att_grad[s, :, cols] = pairs.astype(BF)


def other_grads(meta, moved, convs, filt, skip_grad, att_grad):
    _, tall, wide = moved.shape
    half = convs.shape[2]
    rows = tall - 2 * PAD

    def whole(*shape):
        return pl.BlockSpec(shape, lambda i, m: (0,) * len(shape))

    def other(*shape):
        return pl.BlockSpec(shape, lambda i, m: (0,) * (len(shape) - 1) + (1 - m[0],))

    return pl.pallas_call(
        grads_kernel,
        grid_spec=pltpu.PrefetchScalarGridSpec(
            num_scalar_prefetch=1,
            grid=(1,),
            in_specs=[other(2, tall, half), whole(2, tall, half), other(3, half)]
            + [pl.BlockSpec(memory_space=pl.ANY)] * 2,
            out_specs=[other(2, rows, half), other(2, rows // 2, half)],
            scratch_shapes=[pltpu.VMEM((2, rows, LANES), F32)],
        ),
        out_shape=[
            jax.ShapeDtypeStruct((2, rows, wide), BF),
            jax.ShapeDtypeStruct((2, rows // 2, wide), BF),
        ],
        input_output_aliases={4: 0, 5: 1},
        compiler_params=params(),
        cost_estimate=cost(2 * tall * half * 20, 4 * 1024 * 1024),
        name="other_grads",
    )(meta, moved, convs, filt, skip_grad, att_grad)


def target_kernel(slabs, meta, mine, got_a, got_b, weight, *refs):
    pieces, (target, total) = refs[:8], refs[8:]
    half = weight.shape[0]
    there = (1 - meta[0]) * half
    tile = pieces[0].shape[0]
    even = (meta[1] & 1) == 0
    got = jnp.where(even, got_a[...].astype(F32), got_b[...].astype(F32))
    got = jnp.where(meta[1] == slabs - 1, 0.0, got)
    mine[...] = (mine[...].astype(F32) + got).astype(BF)
    here = pl.ds(pl.multiple_of(meta[0] * half, half), half)
    total[...] = dot(mine[:, here], weight[...]) + pltpu.roll(mine[...].astype(F32), 12 + 2, 0)
    for k, (down, over) in enumerate(spots(meta, tile)):
        place = pl.ds(pl.multiple_of(there + down, tile), tile)
        total[:, pl.ds(over, tile)] += dot(mine[:, place], pieces[k][...])
    for s in range(2):
        target[s] = total[s * 8 : s * 8 + 2].astype(BF)


def targets(meta, mine, got, weight, pieces, slabs):
    half, wide = weight.shape
    tile = pieces[0].shape[0]

    def whole(*shape):
        return pl.BlockSpec(shape, lambda i, m: (0,) * len(shape))

    return pl.pallas_call(
        functools.partial(target_kernel, slabs),
        grid_spec=pltpu.PrefetchScalarGridSpec(
            num_scalar_prefetch=1,
            grid=(1,),
            in_specs=[whole(16, wide)] * 3 + [whole(half, wide)]
            + [whole(tile, tile)] * 8,
            out_specs=whole(2, NTD, wide),
            scratch_shapes=[pltpu.VMEM((16, wide), F32)],
        ),
        out_shape=jax.ShapeDtypeStruct((2, NTD, wide), BF),
        compiler_params=params(),
        cost_estimate=cost(2 * 16 * wide * wide, 6 * 1024 * 1024),
        name="targets",
    )(meta, mine, *got, weight, *pieces)


def paired(part, axis, bit):
    count = lax.axis_size(axis)
    return lax.ppermute(part, axis, [(i, i ^ bit) for i in range(count)])


def staggered(part, span):
    count = lax.axis_size("seq")
    pairs = []
    for i in range(count):
        by = span if i // span % 2 else -span
        pairs.append((i, (i + by) % count))
    return lax.ppermute(part, "seq", pairs)


def after(value, *others):
    return lax.optimization_barrier((value,) + others)[0]


def crossed(part, seq_bit, head_bit):
    slabs, heads = lax.axis_size("seq"), lax.axis_size("head")
    pairs = [
        (i * heads + j, (i ^ seq_bit) * heads + (j ^ head_bit))
        for i in range(slabs)
        for j in range(heads)
    ]
    return lax.ppermute(part, ("seq", "head"), pairs)


def joined(total, one, two):
    both = (one[0] ^ two[0], one[1] ^ two[1])
    parts = [crossed(total, *bits) for bits in (one, two, both)]
    return (total + parts[0]) + (parts[1] + parts[2])


def fast_shards(
    attention, encoder_skip, depth_filter, point_weight, crop_offset, target_bins, cotangent
):
    head = lax.axis_index("head")
    slab = lax.axis_index("seq")
    slabs = lax.axis_size("seq")
    meta = jnp.stack([head, slab]).astype(jnp.int32)
    tile = 3 * LANES

    edge_a, edge_b, far, first, last_tile, att_out = packed(
        meta, encoder_skip, attention, cotangent, point_weight, tile
    )
    first = paired(first, "head", 1)
    shipped = paired(att_out, "head", 1)
    edge_a = paired(edge_a, "seq", 1)
    edge_b = staggered(edge_b, 1)
    far_a = paired(far, "seq", 2)
    far_b = staggered(far, 2)
    prev = passed_along(after(cotangent, edge_b), "seq", 1)
    outer = (slab == 0) | (slab == slabs - 1)
    nothing = jnp.zeros_like(edge_b)
    edge = edge_a + jnp.where(outer, nothing, edge_b)
    twin = paired(edge, "head", 1)
    edge = edge + jnp.where(slab % 4 >= 2, far_a, jnp.where(slab < 2, nothing, far_b))
    second = paired(first, "seq", 2)
    third = paired(first, "seq", 4)
    fourth = paired(last_tile, "head", 1)
    asked, own_sums, own_slope = own_slopes(
        meta, crop_offset, target_bins, attention, encoder_skip, edge, depth_filter
    )
    sums, slopes, mine, shown = other_slopes(
        meta, crop_offset, target_bins, shipped, encoder_skip, edge, twin, depth_filter, asked
    )
    got = [paired(shown, "seq", 1), staggered(shown, 1)]
    moved, own_terms, skip_grad, att_grad = own_half(
        after(meta, shown), crop_offset, own_sums, own_slope, edge, prev, cotangent, point_weight, depth_filter,
        slabs,
    )
    pieces = [first, second, third, fourth]
    pieces = pieces + [paired(after(piece, own_terms), "seq", 1) for piece in pieces]
    convs, terms = other_terms(meta, moved, sums, slopes, own_terms, pieces)
    terms, *got = lax.optimization_barrier((terms, *got))
    total = terms + crossed(terms, 1, 0)
    total = joined(total, (2, 0), (0, 1))
    skip_grad, attention_grad = other_grads(
        meta, moved, convs, depth_filter, skip_grad, att_grad
    )
    target_rows = targets(meta, mine, got, point_weight, pieces, slabs)
    total, skip_grad, attention_grad = lax.optimization_barrier(
        (total, skip_grad, attention_grad)
    )
    if slabs == 16:
        total = joined(total, (4, 0), (8, 0))
    else:
        step = 4
        while step < slabs:
            total = total + crossed(total, step, 0)
            step *= 2
    count = encoder_skip.shape[0] * lax.axis_size("head") * encoder_skip.shape[1] * slabs
    return (target_rows, attention_grad, skip_grad, total * (1.0 / math.sqrt(count)))


def shards(*args):
    attention, encoder_skip, point_weight = args[0], args[1], args[3]
    fits = (
        lax.axis_size("head") == 2
        and lax.axis_size("seq") in (8, 16, 32)
        and encoder_skip.shape[:2] == (2, 128)
        and point_weight.shape[0] == 6 * LANES
        and attention.shape[1] == 64
    )
    return fast_shards(*args) if fits else plain_shards(*args)


def solution(mesh):
    in_specs = (
        P(None, "seq", "head"),
        P("head", "seq", None),
        P(),
        P("head", None),
        P("head"),
        P("head", None),
        P("head", "seq", None),
    )
    out_specs = (P("head", "seq", None), P("head", "seq", None), P("head", "seq", None), P())
    return jax.shard_map(shards, mesh=mesh, in_specs=in_specs, out_specs=out_specs, check_vma=False)
def solution(mesh):
    in_specs = (
        P(None, "seq", "head"),
        P("head", "seq", None),
        P(),
        P("head", None),
        P("head"),
        P("head", None),
        P("head", "seq", None),
    )
    out_specs = (P("head", "seq", None), P("head", "seq", None), P("head", "seq", None), P())
    return jax.shard_map(shards, mesh=mesh, in_specs=in_specs, out_specs=out_specs, check_vma=False)
```

```python
import functools
import math

import jax
import jax.numpy as jnp
from jax import lax
from jax.experimental import pallas as pl
from jax.experimental.pallas import tpu as pltpu
from jax.sharding import PartitionSpec as P

NTD = 2


def extended(shard, sides, width):
    for axis, dim in sides:
        count, length = (lax.axis_size(axis), shard.shape[dim])
        up = [(i, (i + 1) % count) for i in range(count - 1)]
        down = [(j, i) for i, j in up]
        last = lax.slice_in_dim(shard, length - width, length, axis=dim)
        initial = lax.slice_in_dim(shard, 0, width, axis=dim)
        before = lax.ppermute(last, axis, up)
        after = lax.ppermute(initial, axis, down)
        shard = jnp.concatenate([before, shard, after], axis=dim)
    return shard


def passed_along(shard, axis, by):
    count = lax.axis_size(axis)
    pairs = [(i, i + by) for i in range(count) if 0 <= i + by < count]
    return lax.ppermute(shard, axis, pairs)


def gelu_slope(values):
    return (
        0.5 * (1.0 + lax.erf(values * 0.7071067811865476))
        + values * jnp.exp(-0.5 * values * values) * 0.3989422804014327
    )


def with_rims(field):
    return extended(field, (("seq", 1),), 1)


def one_hot(places, length):
    return (places[:, :, None] == jnp.arange(length, dtype=jnp.int32)[None, None, :]).astype(
        jnp.bfloat16
    )


def core_swap(part):
    count = lax.axis_size("seq")
    return lax.ppermute(part, "seq", [(i, i ^ 1) for i in range(count)])


def gathered_weight(rows):
    heads = lax.axis_size("head")
    here = lax.axis_index("head")
    core = lax.axis_index("seq") % 2
    half = rows.shape[0] // 2
    mine = lax.dynamic_slice_in_dim(rows, core * half, half, 0)
    blocks = [(0, rows)]
    for step in range(1, heads):
        pairs = [(i, (i + step) % heads) for i in range(heads)]
        got = lax.ppermute(mine, "head", pairs)
        twin = core_swap(got)
        low = jnp.where(core == 0, got, twin)
        high = jnp.where(core == 0, twin, got)
        blocks.append((step, jnp.concatenate([low, high], axis=0)))
    full = jnp.zeros((heads * rows.shape[0], rows.shape[1]), rows.dtype)
    for step, block in blocks:
        place = (here - step) % heads
        full = lax.dynamic_update_slice_in_dim(full, block, place * rows.shape[0], 0)
    return full


def butterfly(total, axis):
    count = lax.axis_size(axis)
    if count & (count - 1):
        return lax.psum(total, axis)
    step = 1
    while step < count:
        total = total + lax.ppermute(total, axis, [(i, i ^ step) for i in range(count)])
        step *= 2
    return total


def plain_shards(
    attention, encoder_skip, depth_filter, point_weight, crop_offset, target_bins, cotangent
):
    slab_input = lax.all_to_all(attention, "head", split_axis=0, concat_axis=2, tiled=True)
    local_seqs = encoder_skip.shape[0]
    slab_rows = encoder_skip.shape[1]
    channels = encoder_skip.shape[2]
    summed = (
        jnp.repeat(slab_input, 2, axis=1).astype(jnp.float32) + encoder_skip.astype(jnp.float32)
    ).astype(jnp.bfloat16)
    padded = with_rims(summed)
    filtered = (
        depth_filter[0] * padded[:, :-2]
        + depth_filter[1] * padded[:, 1:-1]
        + depth_filter[2] * padded[:, 2:]
    )
    activated = jax.nn.gelu(filtered, approximate=False).astype(jnp.bfloat16)
    flat_act = activated.reshape(local_seqs * slab_rows, channels)
    full_weight = gathered_weight(point_weight)
    mixed_rows = jnp.dot(flat_act, full_weight, preferred_element_type=jnp.float32)
    block_out = (
        summed.astype(jnp.float32) + mixed_rows.reshape(local_seqs, slab_rows, channels)
    ).astype(jnp.bfloat16)
    slab_index = lax.axis_index("seq")
    bins = jnp.concatenate(
        [jnp.zeros_like(target_bins[:, :NTD]), target_bins], axis=1
    )
    asked = lax.dynamic_slice_in_dim(bins, slab_index * NTD, 2 * NTD, 1) + crop_offset[:, None]
    back = jnp.where(jnp.arange(2 * NTD, dtype=jnp.int32) < NTD, slab_rows, 0)
    asked = asked - back[None, :]
    picked = jnp.einsum(
        "sjr,srd->sjd",
        one_hot(asked, slab_rows),
        block_out,
        preferred_element_type=jnp.float32,
    ).astype(jnp.bfloat16)
    from_next = passed_along(picked[:, :NTD], "seq", -1)
    target_rows = picked[:, NTD:] + from_next
    prev_cot = passed_along(cotangent, "seq", 1)
    cot_pair = jnp.concatenate([prev_cot, cotangent], axis=1)

    def crop_back(cot_block, shift_by):
        return lax.dynamic_slice_in_dim(cot_block, slab_rows - shift_by, slab_rows, 0)

    grad_out = jax.vmap(crop_back)(cot_pair, crop_offset)
    flat_grad = grad_out.reshape(local_seqs * slab_rows, channels)
    grad_act = lax.dot_general(
        flat_grad, full_weight, (((1,), (1,)), ((), ())), preferred_element_type=jnp.float32
    )
    grad_conv = (grad_act.reshape(local_seqs, slab_rows, channels) * gelu_slope(filtered)).astype(
        jnp.bfloat16
    )
    grad_padded = with_rims(grad_conv)
    grad_sum = (
        grad_out.astype(jnp.float32)
        + depth_filter[0] * grad_padded[:, 2:]
        + depth_filter[1] * grad_padded[:, 1:-1]
        + depth_filter[2] * grad_padded[:, :-2]
    )
    skip_grad = grad_sum.astype(jnp.bfloat16)
    attention_grad = (
        grad_sum.reshape(local_seqs, slab_rows // 2, 2, channels).sum(axis=2).astype(jnp.bfloat16)
    )
    filter_terms = jnp.stack(
        [
            jnp.einsum(
                "srd,srd->d", grad_conv, padded[:, 0:slab_rows], preferred_element_type=jnp.float32
            ),
            jnp.einsum(
                "srd,srd->d",
                grad_conv,
                padded[:, 1 : slab_rows + 1],
                preferred_element_type=jnp.float32,
            ),
            jnp.einsum(
                "srd,srd->d",
                grad_conv,
                padded[:, 2 : slab_rows + 2],
                preferred_element_type=jnp.float32,
            ),
        ]
    )
    filter_sum = butterfly(butterfly(filter_terms, "seq"), "head")
    row_count = local_seqs * lax.axis_size("head") * slab_rows * lax.axis_size("seq")
    filter_grad = filter_sum * (1.0 / math.sqrt(row_count))
    return (target_rows, attention_grad, skip_grad, filter_grad)


import functools
import math

import jax
import jax.numpy as jnp
from jax import lax
from jax.experimental import pallas as pl
from jax.experimental.pallas import tpu as pltpu
from jax.sharding import PartitionSpec as P

NTD = 2


def extended(shard, sides, width):
    for axis, dim in sides:
        count, length = (lax.axis_size(axis), shard.shape[dim])
        up = [(i, (i + 1) % count) for i in range(count - 1)]
        down = [(j, i) for i, j in up]
        last = lax.slice_in_dim(shard, length - width, length, axis=dim)
        initial = lax.slice_in_dim(shard, 0, width, axis=dim)
        before = lax.ppermute(last, axis, up)
        after = lax.ppermute(initial, axis, down)
        shard = jnp.concatenate([before, shard, after], axis=dim)
    return shard


def passed_along(shard, axis, by):
    count = lax.axis_size(axis)
    pairs = [(i, i + by) for i in range(count) if 0 <= i + by < count]
    return lax.ppermute(shard, axis, pairs)


def gelu_slope(values):
    return (
        0.5 * (1.0 + lax.erf(values * 0.7071067811865476))
        + values * jnp.exp(-0.5 * values * values) * 0.3989422804014327
    )


def with_rims(field):
    return extended(field, (("seq", 1),), 1)


def one_hot(places, length):
    return (places[:, :, None] == jnp.arange(length, dtype=jnp.int32)[None, None, :]).astype(
        jnp.bfloat16
    )


def core_swap(part):
    count = lax.axis_size("seq")
    return lax.ppermute(part, "seq", [(i, i ^ 1) for i in range(count)])


def gathered_weight(rows):
    heads = lax.axis_size("head")
    here = lax.axis_index("head")
    core = lax.axis_index("seq") % 2
    half = rows.shape[0] // 2
    mine = lax.dynamic_slice_in_dim(rows, core * half, half, 0)
    blocks = [(0, rows)]
    for step in range(1, heads):
        pairs = [(i, (i + step) % heads) for i in range(heads)]
        got = lax.ppermute(mine, "head", pairs)
        twin = core_swap(got)
        low = jnp.where(core == 0, got, twin)
        high = jnp.where(core == 0, twin, got)
        blocks.append((step, jnp.concatenate([low, high], axis=0)))
    full = jnp.zeros((heads * rows.shape[0], rows.shape[1]), rows.dtype)
    for step, block in blocks:
        place = (here - step) % heads
        full = lax.dynamic_update_slice_in_dim(full, block, place * rows.shape[0], 0)
    return full


def butterfly(total, axis):
    count = lax.axis_size(axis)
    if count & (count - 1):
        return lax.psum(total, axis)
    step = 1
    while step < count:
        total = total + lax.ppermute(total, axis, [(i, i ^ step) for i in range(count)])
        step *= 2
    return total


def plain_shards(
    attention, encoder_skip, depth_filter, point_weight, crop_offset, target_bins, cotangent
):
    slab_input = lax.all_to_all(attention, "head", split_axis=0, concat_axis=2, tiled=True)
    local_seqs = encoder_skip.shape[0]
    slab_rows = encoder_skip.shape[1]
    channels = encoder_skip.shape[2]
    summed = (
        jnp.repeat(slab_input, 2, axis=1).astype(jnp.float32) + encoder_skip.astype(jnp.float32)
    ).astype(jnp.bfloat16)
    padded = with_rims(summed)
    filtered = (
        depth_filter[0] * padded[:, :-2]
        + depth_filter[1] * padded[:, 1:-1]
        + depth_filter[2] * padded[:, 2:]
    )
    activated = jax.nn.gelu(filtered, approximate=False).astype(jnp.bfloat16)
    flat_act = activated.reshape(local_seqs * slab_rows, channels)
    full_weight = gathered_weight(point_weight)
    mixed_rows = jnp.dot(flat_act, full_weight, preferred_element_type=jnp.float32)
    block_out = (
        summed.astype(jnp.float32) + mixed_rows.reshape(local_seqs, slab_rows, channels)
    ).astype(jnp.bfloat16)
    slab_index = lax.axis_index("seq")
    bins = jnp.concatenate(
        [jnp.zeros_like(target_bins[:, :NTD]), target_bins], axis=1
    )
    asked = lax.dynamic_slice_in_dim(bins, slab_index * NTD, 2 * NTD, 1) + crop_offset[:, None]
    back = jnp.where(jnp.arange(2 * NTD, dtype=jnp.int32) < NTD, slab_rows, 0)
    asked = asked - back[None, :]
    picked = jnp.einsum(
        "sjr,srd->sjd",
        one_hot(asked, slab_rows),
        block_out,
        preferred_element_type=jnp.float32,
    ).astype(jnp.bfloat16)
    from_next = passed_along(picked[:, :NTD], "seq", -1)
    target_rows = picked[:, NTD:] + from_next
    prev_cot = passed_along(cotangent, "seq", 1)
    cot_pair = jnp.concatenate([prev_cot, cotangent], axis=1)

    def crop_back(cot_block, shift_by):
        return lax.dynamic_slice_in_dim(cot_block, slab_rows - shift_by, slab_rows, 0)

    grad_out = jax.vmap(crop_back)(cot_pair, crop_offset)
    flat_grad = grad_out.reshape(local_seqs * slab_rows, channels)
    grad_act = lax.dot_general(
        flat_grad, full_weight, (((1,), (1,)), ((), ())), preferred_element_type=jnp.float32
    )
    grad_conv = (grad_act.reshape(local_seqs, slab_rows, channels) * gelu_slope(filtered)).astype(
        jnp.bfloat16
    )
    grad_padded = with_rims(grad_conv)
    grad_sum = (
        grad_out.astype(jnp.float32)
        + depth_filter[0] * grad_padded[:, 2:]
        + depth_filter[1] * grad_padded[:, 1:-1]
        + depth_filter[2] * grad_padded[:, :-2]
    )
    skip_grad = grad_sum.astype(jnp.bfloat16)
    attention_grad = (
        grad_sum.reshape(local_seqs, slab_rows // 2, 2, channels).sum(axis=2).astype(jnp.bfloat16)
    )
    filter_terms = jnp.stack(
        [
            jnp.einsum(
                "srd,srd->d", grad_conv, padded[:, 0:slab_rows], preferred_element_type=jnp.float32
            ),
            jnp.einsum(
                "srd,srd->d",
                grad_conv,
                padded[:, 1 : slab_rows + 1],
                preferred_element_type=jnp.float32,
            ),
            jnp.einsum(
                "srd,srd->d",
                grad_conv,
                padded[:, 2 : slab_rows + 2],
                preferred_element_type=jnp.float32,
            ),
        ]
    )
    filter_sum = butterfly(butterfly(filter_terms, "seq"), "head")
    row_count = local_seqs * lax.axis_size("head") * slab_rows * lax.axis_size("seq")
    filter_grad = filter_sum * (1.0 / math.sqrt(row_count))
    return (target_rows, attention_grad, skip_grad, filter_grad)


LANES = 128
PAD = 8
BF = jnp.bfloat16
F32 = jnp.float32


def dot(left, right):
    return lax.dot_general(left, right, (((1,), (0,)), ((), ())), preferred_element_type=F32)


def dot_rows(left, right):
    return lax.dot_general(left, right, (((1,), (1,)), ((), ())), preferred_element_type=F32)


def grid_of(rows, columns):
    return (
        lax.broadcasted_iota(jnp.int32, (rows, columns), 0),
        lax.broadcasted_iota(jnp.int32, (rows, columns), 1),
    )


def picks(match):
    return jnp.where(match, 1.0, 0.0).astype(BF)


def params(mib=20):
    return pltpu.CompilerParams(vmem_limit_bytes=mib * 1024 * 1024)


def cost(flops, moved, special=0):
    return pl.CostEstimate(flops=flops, bytes_accessed=moved, transcendentals=special)


def pack_kernel(
    meta, skip_lo, skip_hi, att_lo, att_hi, cot_lo, cot_hi, near, distant, att,
    edge_a, edge_b, far, tile_a, tile_b, att_out,
):
    att_out[...] = att[...]
    tile_a[...] = near[...]
    tile_b[...] = distant[...]
    wide = cot_lo.shape[2]
    at = lax.broadcasted_iota(jnp.int32, (8, wide), 0)
    even = (meta[1] & 1) == 0
    ups, downs, ends = [], [], []
    for s in range(2):
        feats = [jnp.concatenate([part[s], part[2 + s]], axis=1) for part in (att_hi, att_lo)]
        high, low = feats[0].astype(F32)[8:], feats[1].astype(F32)[:8]
        up = jnp.where(at >= 6, skip_hi[s].astype(F32)[8:], 0.0)
        ups.append(jnp.where(at == 5, pltpu.roll(high, 6, 0), up))
        down = jnp.where(at < 2, skip_lo[s].astype(F32)[:8], 0.0)
        down = jnp.where(at == 2, pltpu.roll(low, 2, 0), down)
        downs.append(jnp.where(at == 3, pltpu.roll(cot_lo[s].astype(F32)[:8], 3, 0), down))
        last = pltpu.roll(cot_hi[s].astype(F32)[8:], 5, 0)
        ends.append(jnp.where(at == 4, last, 0.0))
    up, down = jnp.concatenate(ups), jnp.concatenate(downs)
    edge_a[...] = jnp.where(even, up, down).astype(BF)
    edge_b[...] = jnp.where(even, down, up).astype(BF)
    far[...] = jnp.concatenate(ends).astype(BF)


def packed(meta, encoder_skip, attention, cotangent, weight, tile):
    seqs, rows, wide = encoder_skip.shape
    half = attention.shape[2]
    short = attention.shape[1]

    def block(count, width, place):
        return pl.BlockSpec((count, 16, width), lambda i, m: (0, place, 0))

    out = jax.ShapeDtypeStruct((16, wide), BF)
    square = jax.ShapeDtypeStruct((tile, tile), BF)
    return pl.pallas_call(
        pack_kernel,
        grid_spec=pltpu.PrefetchScalarGridSpec(
            num_scalar_prefetch=1,
            grid=(1,),
            in_specs=[
                block(seqs, wide, 0),
                block(seqs, wide, rows // 16 - 1),
                block(2 * seqs, half, 0),
                block(2 * seqs, half, short // 16 - 1),
                block(seqs, wide, 0),
                block(seqs, wide, rows // 16 - 1),
                pl.BlockSpec((tile, tile), lambda i, m: (m[1] & 1, (m[1] >> 1) & 3)),
                pl.BlockSpec((tile, tile), lambda i, m: (m[1] & 1, 3 - ((m[1] >> 1) & 3))),
                pl.BlockSpec((2, short, half), lambda i, m: (1 - m[0], 0, 0)),
            ],
            out_specs=[pl.BlockSpec((16, wide), lambda i, m: (0, 0))] * 3
            + [pl.BlockSpec((tile, tile), lambda i, m: (0, 0))] * 2
            + [pl.BlockSpec((2, short, half), lambda i, m: (0, 0, 0))],
        ),
        out_shape=[out, out, out, square, square, jax.ShapeDtypeStruct((2, short, half), BF)],
        compiler_params=params(60),
        name="pack_edges",
    )(
        meta, encoder_skip, encoder_skip, attention, attention, cotangent, cotangent, weight,
        weight, attention,
    )


def slab_sums(att, skip, edge, twin, ext, cols):
    width = cols.size
    short = 64
    row, col = grid_of(2 * short, short)
    spread = picks((row >> 1) == col)
    row, col = grid_of(16, 16)
    at, base = row & 7, row & 8
    wanted = ((at >= 6) & (col == base + 5)) | ((at < 2) & (col == base + 2))
    from_att = dot(picks(wanted), twin[:, cols])
    rims = edge[:, cols]
    at = lax.broadcasted_iota(jnp.int32, (16, width), 0) & 7
    rims = (from_att + rims.astype(F32)).astype(BF).astype(F32)
    above = jnp.where(at >= 6, rims, 0.0)
    below = jnp.where(at < 2, rims, 0.0)
    for s in range(2):
        body = dot(spread, att[s, 0:short, cols]) + skip[s, :, cols].astype(F32)
        ext[s, 0:PAD] = above[s * 8 : s * 8 + 8]
        ext[s, PAD : PAD + 2 * short] = body.astype(BF).astype(F32)
        ext[s, PAD + 2 * short : 2 * PAD + 2 * short] = below[s * 8 : s * 8 + 8]


def around(field):
    tall = field.shape[0]
    return pltpu.roll(field, 1, 0), pltpu.roll(field, tall - 1, 0)


def phi_of(values):
    return 0.5 * (1.0 + lax.erf(values * 0.7071067811865476))


def slope_of(values):
    return phi_of(values) + values * jnp.exp(-0.5 * values * values) * 0.3989422804014327


def asked_rows(meta, offsets, bins, s, ext, taps, tall):
    row, col = grid_of(48, tall)
    want = row & 3
    shift = (row >> 4) - 1
    at = jnp.full((48, tall), -4096, jnp.int32)
    slab = meta[1]
    for k in range(4):
        mine = k < NTD
        home = slab if mine else jnp.maximum(slab - 1, 0)
        place = bins[s, home * NTD + (k % NTD)] + offsets[s] - (0 if mine else tall - 2 * PAD)
        fits = (place >= 0) & (place < tall - 2 * PAD)
        at = jnp.where(want == k, jnp.where(fits, place + PAD, -4096), at)
    found = dot(picks((col == at + shift) & ((row & 15) < 8)), ext.astype(BF))
    here = found[16:32]
    value = taps[0] * found[0:16] + taps[1] * here + taps[2] * found[32:48]
    act = value * phi_of(value)
    row = lax.broadcasted_iota(jnp.int32, act.shape, 0)
    return jnp.where(row < 4, act, here).astype(BF)


def taps_of(filt, cols):
    return [filt[k : k + 1, cols] for k in range(3)]


def tap_sums(conv, ext, rows):
    before, after = around(ext)
    body = slice(PAD, PAD + rows)
    mine = conv[body]
    return [
        jnp.sum(mine * other[body], axis=0, keepdims=True) for other in (before, ext, after)
    ]


def grads(conv, direct, taps, rows, pair):
    before, after = around(conv)
    body = slice(PAD, PAD + rows)
    total = direct + taps[0] * after[body] + taps[1] * conv[body] + taps[2] * before[body]
    short = rows // 2
    sums = []
    for k in range(total.shape[1] // LANES):
        pair[k] = total[:, k * LANES : (k + 1) * LANES]
        sums.append(pair[k, pl.ds(0, short, 2), :] + pair[k, pl.ds(1, short, 2), :])
    return total, jnp.concatenate(sums, axis=1)


def own_slope_kernel(meta, offsets, bins, att, skip, edge, filt, asked, sums, slopes, ext):
    half = skip.shape[2]
    tall = ext.shape[1]
    width = ext.shape[2]

    @pl.loop(0, half // width)
    def _(part):
        cols = pl.ds(pl.multiple_of(part * width, width), width)
        slab_sums(att, skip, edge, edge, ext, cols)
        taps = taps_of(filt, cols)
        for s in range(2):
            field = ext[s]
            before, after = around(field)
            slopes[s, :, cols] = slope_of(taps[0] * before + taps[1] * field + taps[2] * after)
            sums[s, :, cols] = field.astype(BF)
            asked[s * 16 : s * 16 + 16, cols] = asked_rows(
                meta, offsets, bins, s, field, taps, tall
            )


def own_slopes(meta, offsets, bins, attention, skip, edge, filt):
    seqs, rows, wide = skip.shape
    _, short, half = attention.shape
    tall = rows + 2 * PAD

    def whole(*shape):
        return pl.BlockSpec(shape, lambda i, m, o, b: (0,) * len(shape))

    def mine(*shape):
        return pl.BlockSpec(shape, lambda i, m, o, b: (0,) * (len(shape) - 1) + (m[0],))

    return pl.pallas_call(
        own_slope_kernel,
        grid_spec=pltpu.PrefetchScalarGridSpec(
            num_scalar_prefetch=3,
            grid=(1,),
            in_specs=[
                pl.BlockSpec((2, short, half), lambda i, m, o, b: (m[0], 0, 0)),
                mine(2, rows, half),
                mine(16, half),
                mine(3, half),
            ],
            out_specs=[whole(32, half), whole(2, tall, half), whole(2, tall, half)],
            scratch_shapes=[pltpu.VMEM((2, tall, 256), F32)],
        ),
        out_shape=[
            jax.ShapeDtypeStruct((32, half), BF),
            jax.ShapeDtypeStruct((2, tall, half), BF),
            jax.ShapeDtypeStruct((2, tall, half), F32),
        ],
        compiler_params=params(),
        cost_estimate=cost(3 * 10**9, 10**6),
        name="own_slopes",
    )(meta, offsets, bins, attention, skip, edge, filt)


def own_kernel(
    slabs, meta, offsets, sums, slopes, rims, prev_far, cot_far, weight_far, filt,
    moved, terms, skip_grad, att_grad, pair, prev, cot, weight, sems,
):
    copies = [
        pltpu.make_async_copy(prev_far, prev, sems.at[0]),
        pltpu.make_async_copy(cot_far, cot, sems.at[1]),
        pltpu.make_async_copy(weight_far, weight, sems.at[2]),
    ]
    for copy in copies:
        copy.start()
    half = sums.shape[2]
    tall = sums.shape[1]
    rows = tall - 2 * PAD
    wide = cot.shape[2]
    row, col = grid_of(tall, rows)
    last = meta[1] == slabs - 1
    copies[0].wait()
    copies[1].wait()
    for s in range(2):
        at = row - PAD
        fits = (at >= -1) & (at < jnp.where(last, rows, rows + 1))
        source = jnp.where(fits, at - offsets[s], -4096)
        older = picks(col == source + rows)
        newer = picks(col == source)
        place = lax.broadcasted_iota(jnp.int32, (PAD, 512), 0)
        top = (place == PAD - 1) & (offsets[s] == rows)
        bottom = (place == 0) & (offsets[s] == 0) & jnp.logical_not(last)
        for part in range(0, wide, 512):
            cols = slice(part, part + 512)
            found = dot(older, prev[s, :, cols]) + dot(newer, cot[s, :, cols])
            ends = rims[:, cols].astype(F32)
            above = ends[s * 8 + 4 : s * 8 + 5]
            below = ends[s * 8 + 3 : s * 8 + 4]
            found = jnp.concatenate(
                [
                    found[:PAD] + jnp.where(top, above, 0.0),
                    found[PAD : PAD + rows],
                    found[PAD + rows :] + jnp.where(bottom, below, 0.0),
                ]
            )
            moved[s, :, cols] = found.astype(BF)
    copies[2].wait()
    width = 2 * LANES
    first = meta[0] * half

    @pl.loop(0, half // width)
    def _(part):
        begin = pl.multiple_of(part * width, width)
        cols = pl.ds(begin, width)
        taps = taps_of(filt, cols)
        piece = weight[pl.ds(begin, width), :]
        total_terms = [0.0, 0.0, 0.0]
        there = pl.ds(pl.multiple_of(first + begin, width), width)
        for s in range(2):
            conv = (dot_rows(moved[s], piece) * slopes[s, :, cols]).astype(BF).astype(F32)
            got = tap_sums(conv, sums[s, :, cols].astype(F32), rows)
            total_terms = [a + b for a, b in zip(total_terms, got)]
            direct = moved[s, :, there].astype(F32)[PAD : PAD + rows]
            total, pairs = grads(conv, direct, taps, rows, pair)
            skip_grad[s, :, cols] = total.astype(BF)
            att_grad[s, :, cols] = pairs.astype(BF)
        for k in range(3):
            terms[k : k + 1, cols] = total_terms[k]


def own_half(meta, offsets, sums, slopes, edge, prev, cot, weight, filt, slabs):
    seqs, rows, wide = cot.shape
    _, tall, half = sums.shape
    short = rows // 2

    def whole(*shape):
        return pl.BlockSpec(shape, lambda i, m, o: (0,) * len(shape))

    def mine(*shape):
        return pl.BlockSpec(shape, lambda i, m, o: (0,) * (len(shape) - 1) + (m[0],))

    anywhere = pl.BlockSpec(memory_space=pl.ANY)
    return pl.pallas_call(
        functools.partial(own_kernel, slabs),
        grid_spec=pltpu.PrefetchScalarGridSpec(
            num_scalar_prefetch=2,
            grid=(1,),
            in_specs=[
                whole(2, tall, half),
                whole(2, tall, half),
                whole(16, wide),
                anywhere,
                anywhere,
                anywhere,
                mine(3, half),
            ],
            out_specs=[
                whole(2, tall, wide),
                whole(3, half),
                mine(2, rows, half),
                mine(2, short, half),
            ],
            scratch_shapes=[
                pltpu.VMEM((2, rows, LANES), F32),
                pltpu.VMEM((2, rows, wide), BF),
                pltpu.VMEM((2, rows, wide), BF),
                pltpu.VMEM((half, wide), BF),
                pltpu.SemaphoreType.DMA((3,)),
            ],
        ),
        out_shape=[
            jax.ShapeDtypeStruct((2, tall, wide), BF),
            jax.ShapeDtypeStruct((3, half), F32),
            jax.ShapeDtypeStruct((2, rows, wide), BF),
            jax.ShapeDtypeStruct((2, short, wide), BF),
        ],
        compiler_params=params(),
        cost_estimate=cost(1, 1),
        name="own_half",
    )(meta, offsets, sums, slopes, edge, prev, cot, weight, filt)


def slope_kernel(
    meta, offsets, bins, att, skip, edge, twin, filt, asked, sums, slopes, mine, shown, ext
):
    rows = skip.shape[1]
    tall = rows + 2 * PAD
    half = skip.shape[2]
    width = ext.shape[2]
    there = (1 - meta[0]) * half
    row, col = grid_of(16, 32)
    at, base = row & 7, (row >> 3) * 16
    kept = picks((at < 4) & (col == base + at + jnp.where(at < 2, 0, 2)))
    told = picks((at < 4) & (col == base + at + jnp.where(at < 2, 2, 4)))
    here = pl.ds(pl.multiple_of(meta[0] * half, half), half)
    mine[:, here] = dot(kept, asked[...]).astype(BF)
    shown[:, here] = dot(told, asked[...]).astype(BF)

    @pl.loop(0, half // width)
    def _(part):
        begin = pl.multiple_of(part * width, width)
        cols = pl.ds(begin, width)
        slab_sums(att, skip, edge, twin, ext, cols)
        taps = taps_of(filt, cols)
        got = []
        for s in range(2):
            field = ext[s]
            before, after = around(field)
            slopes[s, :, cols] = slope_of(taps[0] * before + taps[1] * field + taps[2] * after)
            sums[s, :, cols] = field.astype(BF)
            got.append(asked_rows(meta, offsets, bins, s, field, taps, tall))
        got = jnp.concatenate(got)
        place = pl.ds(pl.multiple_of(there + begin, width), width)
        mine[:, place] = dot(kept, got).astype(BF)
        shown[:, place] = dot(told, got).astype(BF)


def other_slopes(meta, offsets, bins, shipped, skip, edge, twin, filt, asked):
    seqs, rows, wide = skip.shape
    _, packed_rows, half = shipped.shape
    tall = rows + 2 * PAD

    def whole(*shape):
        return pl.BlockSpec(shape, lambda i, m, o, b: (0,) * len(shape))

    def other(*shape):
        return pl.BlockSpec(shape, lambda i, m, o, b: (0,) * (len(shape) - 1) + (1 - m[0],))

    return pl.pallas_call(
        slope_kernel,
        grid_spec=pltpu.PrefetchScalarGridSpec(
            num_scalar_prefetch=3,
            grid=(1,),
            in_specs=[
                whole(2, packed_rows, half),
                other(2, rows, half),
                other(16, half),
                pl.BlockSpec((16, half), lambda i, m, o, b: (0, m[0])),
                other(3, half),
                whole(32, half),
            ],
            out_specs=[whole(2, tall, half), whole(2, tall, half), whole(16, wide), whole(16, wide)],
            scratch_shapes=[pltpu.VMEM((2, tall, 256), F32)],
        ),
        out_shape=[
            jax.ShapeDtypeStruct((2, tall, half), BF),
            jax.ShapeDtypeStruct((2, tall, half), F32),
            jax.ShapeDtypeStruct((16, wide), BF),
            jax.ShapeDtypeStruct((16, wide), BF),
        ],
        compiler_params=params(),
        cost_estimate=cost(3 * 10**9, 10**6),
        name="other_slopes",
    )(meta, offsets, bins, shipped, skip, edge, twin, filt, asked)


def spots(meta, tile):
    core, block = meta[1] & 1, (meta[1] >> 1) & 3
    return [
        (pl.multiple_of(row * tile, tile), pl.multiple_of((block ^ k) * tile, tile))
        for row in (core, 1 - core)
        for k in range(4)
    ]


def terms_kernel(meta, moved, sums, slopes, own_terms, *refs):
    pieces, (convs, terms, full, sems) = refs[:8], refs[8:]
    half = sums.shape[2]
    tall = sums.shape[1]
    rows = tall - 2 * PAD
    there = (1 - meta[0]) * half
    tile = pieces[0].shape[0]
    copies = []
    for k, (down, over) in enumerate(spots(meta, tile)):
        copies.append(
            pltpu.make_async_copy(
                pieces[k], full.at[pl.ds(down, tile), pl.ds(over, tile)], sems.at[k]
            )
        )
        copies[-1].start()
    terms[:, pl.ds(pl.multiple_of(meta[0] * half, half), half)] = own_terms[...]
    for copy in copies:
        copy.wait()
    width = 2 * LANES
    for begin in range(0, half, width):
        cols = slice(begin, begin + width)
        total = [0.0, 0.0, 0.0]
        for s in range(2):
            grad = dot_rows(moved[s], full[cols, :])
            conv = (grad * slopes[s, :, cols]).astype(BF)
            convs[s, :, cols] = conv
            got = tap_sums(conv.astype(F32), sums[s, :, cols].astype(F32), rows)
            total = [a + b for a, b in zip(total, got)]
        place = pl.ds(pl.multiple_of(there + begin, width), width)
        for k in range(3):
            terms[k : k + 1, place] = total[k]


def other_terms(meta, moved, sums, slopes, own_terms, pieces):
    _, tall, wide = moved.shape
    half = sums.shape[2]

    def whole(*shape):
        return pl.BlockSpec(shape, lambda i, m: (0,) * len(shape))

    return pl.pallas_call(
        terms_kernel,
        grid_spec=pltpu.PrefetchScalarGridSpec(
            num_scalar_prefetch=1,
            grid=(1,),
            in_specs=[
                whole(2, tall, wide),
                whole(2, tall, half),
                whole(2, tall, half),
                whole(3, half),
            ]
            + [pl.BlockSpec(memory_space=pl.ANY)] * 8,
            out_specs=[whole(2, tall, half), whole(3, wide)],
            scratch_shapes=[pltpu.VMEM((half, wide), BF), pltpu.SemaphoreType.DMA((8,))],
        ),
        out_shape=[
            jax.ShapeDtypeStruct((2, tall, half), BF),
            jax.ShapeDtypeStruct((3, wide), F32),
        ],
        compiler_params=params(),
        cost_estimate=cost(2 * 2 * tall * half * wide, 6 * 1024 * 1024),
        name="other_terms",
    )(meta, moved, sums, slopes, own_terms, *pieces)


def grads_kernel(meta, moved, convs, filt, old_skip, old_att, skip_grad, att_grad, pair):
    half = convs.shape[2]
    rows = convs.shape[1] - 2 * PAD
    width = 2 * LANES

    @pl.loop(0, half // width)
    def _(part):
        cols = pl.ds(pl.multiple_of(part * width, width), width)
        taps = taps_of(filt, cols)
        for s in range(2):
            direct = moved[s, :, cols].astype(F32)[PAD : PAD + rows]
            total, pairs = grads(convs[s, :, cols].astype(F32), direct, taps, rows, pair)
            skip_grad[s, :, cols] = total.astype(BF)
            att_grad[s, :, cols] = pairs.astype(BF)


def other_grads(meta, moved, convs, filt, skip_grad, att_grad):
    _, tall, wide = moved.shape
    half = convs.shape[2]
    rows = tall - 2 * PAD

    def whole(*shape):
        return pl.BlockSpec(shape, lambda i, m: (0,) * len(shape))

    def other(*shape):
        return pl.BlockSpec(shape, lambda i, m: (0,) * (len(shape) - 1) + (1 - m[0],))

    return pl.pallas_call(
        grads_kernel,
        grid_spec=pltpu.PrefetchScalarGridSpec(
            num_scalar_prefetch=1,
            grid=(1,),
            in_specs=[other(2, tall, half), whole(2, tall, half), other(3, half)]
            + [pl.BlockSpec(memory_space=pl.ANY)] * 2,
            out_specs=[other(2, rows, half), other(2, rows // 2, half)],
            scratch_shapes=[pltpu.VMEM((2, rows, LANES), F32)],
        ),
        out_shape=[
            jax.ShapeDtypeStruct((2, rows, wide), BF),
            jax.ShapeDtypeStruct((2, rows // 2, wide), BF),
        ],
        input_output_aliases={4: 0, 5: 1},
        compiler_params=params(),
        cost_estimate=cost(2 * tall * half * 20, 4 * 1024 * 1024),
        name="other_grads",
    )(meta, moved, convs, filt, skip_grad, att_grad)


def target_kernel(slabs, meta, mine, got_a, got_b, weight, *refs):
    pieces, (target, total) = refs[:8], refs[8:]
    half = weight.shape[0]
    there = (1 - meta[0]) * half
    tile = pieces[0].shape[0]
    even = (meta[1] & 1) == 0
    got = jnp.where(even, got_a[...].astype(F32), got_b[...].astype(F32))
    got = jnp.where(meta[1] == slabs - 1, 0.0, got)
    mine[...] = (mine[...].astype(F32) + got).astype(BF)
    here = pl.ds(pl.multiple_of(meta[0] * half, half), half)
    total[...] = dot(mine[:, here], weight[...]) + pltpu.roll(mine[...].astype(F32), 12 + 2, 0)
    for k, (down, over) in enumerate(spots(meta, tile)):
        place = pl.ds(pl.multiple_of(there + down, tile), tile)
        total[:, pl.ds(over, tile)] += dot(mine[:, place], pieces[k][...])
    for s in range(2):
        target[s] = total[s * 8 : s * 8 + 2].astype(BF)


def targets(meta, mine, got, weight, pieces, slabs):
    half, wide = weight.shape
    tile = pieces[0].shape[0]

    def whole(*shape):
        return pl.BlockSpec(shape, lambda i, m: (0,) * len(shape))

    return pl.pallas_call(
        functools.partial(target_kernel, slabs),
        grid_spec=pltpu.PrefetchScalarGridSpec(
            num_scalar_prefetch=1,
            grid=(1,),
            in_specs=[whole(16, wide)] * 3 + [whole(half, wide)]
            + [whole(tile, tile)] * 8,
            out_specs=whole(2, NTD, wide),
            scratch_shapes=[pltpu.VMEM((16, wide), F32)],
        ),
        out_shape=jax.ShapeDtypeStruct((2, NTD, wide), BF),
        compiler_params=params(),
        cost_estimate=cost(2 * 16 * wide * wide, 6 * 1024 * 1024),
        name="targets",
    )(meta, mine, *got, weight, *pieces)


def paired(part, axis, bit):
    count = lax.axis_size(axis)
    return lax.ppermute(part, axis, [(i, i ^ bit) for i in range(count)])


def staggered(part, span):
    count = lax.axis_size("seq")
    pairs = []
    for i in range(count):
        by = span if i // span % 2 else -span
        pairs.append((i, (i + by) % count))
    return lax.ppermute(part, "seq", pairs)


def after(value, *others):
    return lax.optimization_barrier((value,) + others)[0]


def crossed(part, seq_bit, head_bit):
    slabs, heads = lax.axis_size("seq"), lax.axis_size("head")
    pairs = [
        (i * heads + j, (i ^ seq_bit) * heads + (j ^ head_bit))
        for i in range(slabs)
        for j in range(heads)
    ]
    return lax.ppermute(part, ("seq", "head"), pairs)


def joined(total, one, two):
    both = (one[0] ^ two[0], one[1] ^ two[1])
    parts = [crossed(total, *bits) for bits in (one, two, both)]
    return (total + parts[0]) + (parts[1] + parts[2])


def fast_shards(
    attention, encoder_skip, depth_filter, point_weight, crop_offset, target_bins, cotangent
):
    head = lax.axis_index("head")
    slab = lax.axis_index("seq")
    slabs = lax.axis_size("seq")
    meta = jnp.stack([head, slab]).astype(jnp.int32)
    tile = 3 * LANES

    edge_a, edge_b, far, first, last_tile, att_out = packed(
        meta, encoder_skip, attention, cotangent, point_weight, tile
    )
    first = paired(first, "head", 1)
    shipped = paired(att_out, "head", 1)
    edge_a = paired(edge_a, "seq", 1)
    edge_b = staggered(edge_b, 1)
    far_a = paired(far, "seq", 2)
    far_b = staggered(far, 2)
    prev = passed_along(after(cotangent, edge_b), "seq", 1)
    outer = (slab == 0) | (slab == slabs - 1)
    nothing = jnp.zeros_like(edge_b)
    edge = edge_a + jnp.where(outer, nothing, edge_b)
    twin = paired(edge, "head", 1)
    edge = edge + jnp.where(slab % 4 >= 2, far_a, jnp.where(slab < 2, nothing, far_b))
    asked, own_sums, own_slope = own_slopes(
        meta, crop_offset, target_bins, attention, encoder_skip, edge, depth_filter
    )
    second = paired(first, "seq", 2)
    third = paired(first, "seq", 4)
    fourth = paired(last_tile, "head", 1)
    moved, own_terms, skip_grad, att_grad = own_half(
        meta, crop_offset, own_sums, own_slope, edge, prev, cotangent, point_weight, depth_filter,
        slabs,
    )
    sums, slopes, mine, shown = other_slopes(
        after(meta, own_terms), crop_offset, target_bins, shipped, encoder_skip, edge, twin, depth_filter, asked
    )
    got = [paired(shown, "seq", 1), staggered(shown, 1)]
    pieces = [first, second, third, fourth]
    ties = [own_terms] * 3 + [shown]
    pieces = pieces + [paired(after(*both), "seq", 1) for both in zip(pieces, ties)]
    convs, terms = other_terms(meta, moved, sums, slopes, own_terms, pieces)
    terms, *got = lax.optimization_barrier((terms, *got))
    total = terms + crossed(terms, 1, 0)
    total = joined(total, (2, 0), (0, 1))
    skip_grad, attention_grad = other_grads(
        meta, moved, convs, depth_filter, skip_grad, att_grad
    )
    target_rows = targets(meta, mine, got, point_weight, pieces, slabs)
    total, skip_grad, attention_grad = lax.optimization_barrier(
        (total, skip_grad, attention_grad)
    )
    if slabs == 16:
        total = joined(total, (4, 0), (8, 0))
    else:
        step = 4
        while step < slabs:
            total = total + crossed(total, step, 0)
            step *= 2
    count = encoder_skip.shape[0] * lax.axis_size("head") * encoder_skip.shape[1] * slabs
    return (target_rows, attention_grad, skip_grad, total * (1.0 / math.sqrt(count)))


def shards(*args):
    attention, encoder_skip, point_weight = args[0], args[1], args[3]
    fits = (
        lax.axis_size("head") == 2
        and lax.axis_size("seq") in (8, 16, 32)
        and encoder_skip.shape[:2] == (2, 128)
        and point_weight.shape[0] == 6 * LANES
        and attention.shape[1] == 64
    )
    return fast_shards(*args) if fits else plain_shards(*args)


def solution(mesh):
    in_specs = (
        P(None, "seq", "head"),
        P("head", "seq", None),
        P(),
        P("head", None),
        P("head"),
        P("head", None),
        P("head", "seq", None),
    )
    out_specs = (P("head", "seq", None), P("head", "seq", None), P("head", "seq", None), P())
    return jax.shard_map(shards, mesh=mesh, in_specs=in_specs, out_specs=out_specs, check_vma=False)
def solution(mesh):
    in_specs = (
        P(None, "seq", "head"),
        P("head", "seq", None),
        P(),
        P("head", None),
        P("head"),
        P("head", None),
        P("head", "seq", None),
    )
    out_specs = (P("head", "seq", None), P("head", "seq", None), P("head", "seq", None), P())
    return jax.shard_map(shards, mesh=mesh, in_specs=in_specs, out_specs=out_specs, check_vma=False)
```

```python
import functools
import math

import jax
import jax.numpy as jnp
from jax import lax
from jax.experimental import pallas as pl
from jax.experimental.pallas import tpu as pltpu
from jax.sharding import PartitionSpec as P

NTD = 2


def extended(shard, sides, width):
    for axis, dim in sides:
        count, length = (lax.axis_size(axis), shard.shape[dim])
        up = [(i, (i + 1) % count) for i in range(count - 1)]
        down = [(j, i) for i, j in up]
        last = lax.slice_in_dim(shard, length - width, length, axis=dim)
        initial = lax.slice_in_dim(shard, 0, width, axis=dim)
        before = lax.ppermute(last, axis, up)
        after = lax.ppermute(initial, axis, down)
        shard = jnp.concatenate([before, shard, after], axis=dim)
    return shard


def passed_along(shard, axis, by):
    count = lax.axis_size(axis)
    pairs = [(i, i + by) for i in range(count) if 0 <= i + by < count]
    return lax.ppermute(shard, axis, pairs)


def gelu_slope(values):
    return (
        0.5 * (1.0 + lax.erf(values * 0.7071067811865476))
        + values * jnp.exp(-0.5 * values * values) * 0.3989422804014327
    )


def with_rims(field):
    return extended(field, (("seq", 1),), 1)


def one_hot(places, length):
    return (places[:, :, None] == jnp.arange(length, dtype=jnp.int32)[None, None, :]).astype(
        jnp.bfloat16
    )


def core_swap(part):
    count = lax.axis_size("seq")
    return lax.ppermute(part, "seq", [(i, i ^ 1) for i in range(count)])


def gathered_weight(rows):
    heads = lax.axis_size("head")
    here = lax.axis_index("head")
    core = lax.axis_index("seq") % 2
    half = rows.shape[0] // 2
    mine = lax.dynamic_slice_in_dim(rows, core * half, half, 0)
    blocks = [(0, rows)]
    for step in range(1, heads):
        pairs = [(i, (i + step) % heads) for i in range(heads)]
        got = lax.ppermute(mine, "head", pairs)
        twin = core_swap(got)
        low = jnp.where(core == 0, got, twin)
        high = jnp.where(core == 0, twin, got)
        blocks.append((step, jnp.concatenate([low, high], axis=0)))
    full = jnp.zeros((heads * rows.shape[0], rows.shape[1]), rows.dtype)
    for step, block in blocks:
        place = (here - step) % heads
        full = lax.dynamic_update_slice_in_dim(full, block, place * rows.shape[0], 0)
    return full


def butterfly(total, axis):
    count = lax.axis_size(axis)
    if count & (count - 1):
        return lax.psum(total, axis)
    step = 1
    while step < count:
        total = total + lax.ppermute(total, axis, [(i, i ^ step) for i in range(count)])
        step *= 2
    return total


def plain_shards(
    attention, encoder_skip, depth_filter, point_weight, crop_offset, target_bins, cotangent
):
    slab_input = lax.all_to_all(attention, "head", split_axis=0, concat_axis=2, tiled=True)
    local_seqs = encoder_skip.shape[0]
    slab_rows = encoder_skip.shape[1]
    channels = encoder_skip.shape[2]
    summed = (
        jnp.repeat(slab_input, 2, axis=1).astype(jnp.float32) + encoder_skip.astype(jnp.float32)
    ).astype(jnp.bfloat16)
    padded = with_rims(summed)
    filtered = (
        depth_filter[0] * padded[:, :-2]
        + depth_filter[1] * padded[:, 1:-1]
        + depth_filter[2] * padded[:, 2:]
    )
    activated = jax.nn.gelu(filtered, approximate=False).astype(jnp.bfloat16)
    flat_act = activated.reshape(local_seqs * slab_rows, channels)
    full_weight = gathered_weight(point_weight)
    mixed_rows = jnp.dot(flat_act, full_weight, preferred_element_type=jnp.float32)
    block_out = (
        summed.astype(jnp.float32) + mixed_rows.reshape(local_seqs, slab_rows, channels)
    ).astype(jnp.bfloat16)
    slab_index = lax.axis_index("seq")
    bins = jnp.concatenate(
        [jnp.zeros_like(target_bins[:, :NTD]), target_bins], axis=1
    )
    asked = lax.dynamic_slice_in_dim(bins, slab_index * NTD, 2 * NTD, 1) + crop_offset[:, None]
    back = jnp.where(jnp.arange(2 * NTD, dtype=jnp.int32) < NTD, slab_rows, 0)
    asked = asked - back[None, :]
    picked = jnp.einsum(
        "sjr,srd->sjd",
        one_hot(asked, slab_rows),
        block_out,
        preferred_element_type=jnp.float32,
    ).astype(jnp.bfloat16)
    from_next = passed_along(picked[:, :NTD], "seq", -1)
    target_rows = picked[:, NTD:] + from_next
    prev_cot = passed_along(cotangent, "seq", 1)
    cot_pair = jnp.concatenate([prev_cot, cotangent], axis=1)

    def crop_back(cot_block, shift_by):
        return lax.dynamic_slice_in_dim(cot_block, slab_rows - shift_by, slab_rows, 0)

    grad_out = jax.vmap(crop_back)(cot_pair, crop_offset)
    flat_grad = grad_out.reshape(local_seqs * slab_rows, channels)
    grad_act = lax.dot_general(
        flat_grad, full_weight, (((1,), (1,)), ((), ())), preferred_element_type=jnp.float32
    )
    grad_conv = (grad_act.reshape(local_seqs, slab_rows, channels) * gelu_slope(filtered)).astype(
        jnp.bfloat16
    )
    grad_padded = with_rims(grad_conv)
    grad_sum = (
        grad_out.astype(jnp.float32)
        + depth_filter[0] * grad_padded[:, 2:]
        + depth_filter[1] * grad_padded[:, 1:-1]
        + depth_filter[2] * grad_padded[:, :-2]
    )
    skip_grad = grad_sum.astype(jnp.bfloat16)
    attention_grad = (
        grad_sum.reshape(local_seqs, slab_rows // 2, 2, channels).sum(axis=2).astype(jnp.bfloat16)
    )
    filter_terms = jnp.stack(
        [
            jnp.einsum(
                "srd,srd->d", grad_conv, padded[:, 0:slab_rows], preferred_element_type=jnp.float32
            ),
            jnp.einsum(
                "srd,srd->d",
                grad_conv,
                padded[:, 1 : slab_rows + 1],
                preferred_element_type=jnp.float32,
            ),
            jnp.einsum(
                "srd,srd->d",
                grad_conv,
                padded[:, 2 : slab_rows + 2],
                preferred_element_type=jnp.float32,
            ),
        ]
    )
    filter_sum = butterfly(butterfly(filter_terms, "seq"), "head")
    row_count = local_seqs * lax.axis_size("head") * slab_rows * lax.axis_size("seq")
    filter_grad = filter_sum * (1.0 / math.sqrt(row_count))
    return (target_rows, attention_grad, skip_grad, filter_grad)


import functools
import math

import jax
import jax.numpy as jnp
from jax import lax
from jax.experimental import pallas as pl
from jax.experimental.pallas import tpu as pltpu
from jax.sharding import PartitionSpec as P

NTD = 2


def extended(shard, sides, width):
    for axis, dim in sides:
        count, length = (lax.axis_size(axis), shard.shape[dim])
        up = [(i, (i + 1) % count) for i in range(count - 1)]
        down = [(j, i) for i, j in up]
        last = lax.slice_in_dim(shard, length - width, length, axis=dim)
        initial = lax.slice_in_dim(shard, 0, width, axis=dim)
        before = lax.ppermute(last, axis, up)
        after = lax.ppermute(initial, axis, down)
        shard = jnp.concatenate([before, shard, after], axis=dim)
    return shard


def passed_along(shard, axis, by):
    count = lax.axis_size(axis)
    pairs = [(i, i + by) for i in range(count) if 0 <= i + by < count]
    return lax.ppermute(shard, axis, pairs)


def gelu_slope(values):
    return (
        0.5 * (1.0 + lax.erf(values * 0.7071067811865476))
        + values * jnp.exp(-0.5 * values * values) * 0.3989422804014327
    )


def with_rims(field):
    return extended(field, (("seq", 1),), 1)


def one_hot(places, length):
    return (places[:, :, None] == jnp.arange(length, dtype=jnp.int32)[None, None, :]).astype(
        jnp.bfloat16
    )


def core_swap(part):
    count = lax.axis_size("seq")
    return lax.ppermute(part, "seq", [(i, i ^ 1) for i in range(count)])


def gathered_weight(rows):
    heads = lax.axis_size("head")
    here = lax.axis_index("head")
    core = lax.axis_index("seq") % 2
    half = rows.shape[0] // 2
    mine = lax.dynamic_slice_in_dim(rows, core * half, half, 0)
    blocks = [(0, rows)]
    for step in range(1, heads):
        pairs = [(i, (i + step) % heads) for i in range(heads)]
        got = lax.ppermute(mine, "head", pairs)
        twin = core_swap(got)
        low = jnp.where(core == 0, got, twin)
        high = jnp.where(core == 0, twin, got)
        blocks.append((step, jnp.concatenate([low, high], axis=0)))
    full = jnp.zeros((heads * rows.shape[0], rows.shape[1]), rows.dtype)
    for step, block in blocks:
        place = (here - step) % heads
        full = lax.dynamic_update_slice_in_dim(full, block, place * rows.shape[0], 0)
    return full


def butterfly(total, axis):
    count = lax.axis_size(axis)
    if count & (count - 1):
        return lax.psum(total, axis)
    step = 1
    while step < count:
        total = total + lax.ppermute(total, axis, [(i, i ^ step) for i in range(count)])
        step *= 2
    return total


def plain_shards(
    attention, encoder_skip, depth_filter, point_weight, crop_offset, target_bins, cotangent
):
    slab_input = lax.all_to_all(attention, "head", split_axis=0, concat_axis=2, tiled=True)
    local_seqs = encoder_skip.shape[0]
    slab_rows = encoder_skip.shape[1]
    channels = encoder_skip.shape[2]
    summed = (
        jnp.repeat(slab_input, 2, axis=1).astype(jnp.float32) + encoder_skip.astype(jnp.float32)
    ).astype(jnp.bfloat16)
    padded = with_rims(summed)
    filtered = (
        depth_filter[0] * padded[:, :-2]
        + depth_filter[1] * padded[:, 1:-1]
        + depth_filter[2] * padded[:, 2:]
    )
    activated = jax.nn.gelu(filtered, approximate=False).astype(jnp.bfloat16)
    flat_act = activated.reshape(local_seqs * slab_rows, channels)
    full_weight = gathered_weight(point_weight)
    mixed_rows = jnp.dot(flat_act, full_weight, preferred_element_type=jnp.float32)
    block_out = (
        summed.astype(jnp.float32) + mixed_rows.reshape(local_seqs, slab_rows, channels)
    ).astype(jnp.bfloat16)
    slab_index = lax.axis_index("seq")
    bins = jnp.concatenate(
        [jnp.zeros_like(target_bins[:, :NTD]), target_bins], axis=1
    )
    asked = lax.dynamic_slice_in_dim(bins, slab_index * NTD, 2 * NTD, 1) + crop_offset[:, None]
    back = jnp.where(jnp.arange(2 * NTD, dtype=jnp.int32) < NTD, slab_rows, 0)
    asked = asked - back[None, :]
    picked = jnp.einsum(
        "sjr,srd->sjd",
        one_hot(asked, slab_rows),
        block_out,
        preferred_element_type=jnp.float32,
    ).astype(jnp.bfloat16)
    from_next = passed_along(picked[:, :NTD], "seq", -1)
    target_rows = picked[:, NTD:] + from_next
    prev_cot = passed_along(cotangent, "seq", 1)
    cot_pair = jnp.concatenate([prev_cot, cotangent], axis=1)

    def crop_back(cot_block, shift_by):
        return lax.dynamic_slice_in_dim(cot_block, slab_rows - shift_by, slab_rows, 0)

    grad_out = jax.vmap(crop_back)(cot_pair, crop_offset)
    flat_grad = grad_out.reshape(local_seqs * slab_rows, channels)
    grad_act = lax.dot_general(
        flat_grad, full_weight, (((1,), (1,)), ((), ())), preferred_element_type=jnp.float32
    )
    grad_conv = (grad_act.reshape(local_seqs, slab_rows, channels) * gelu_slope(filtered)).astype(
        jnp.bfloat16
    )
    grad_padded = with_rims(grad_conv)
    grad_sum = (
        grad_out.astype(jnp.float32)
        + depth_filter[0] * grad_padded[:, 2:]
        + depth_filter[1] * grad_padded[:, 1:-1]
        + depth_filter[2] * grad_padded[:, :-2]
    )
    skip_grad = grad_sum.astype(jnp.bfloat16)
    attention_grad = (
        grad_sum.reshape(local_seqs, slab_rows // 2, 2, channels).sum(axis=2).astype(jnp.bfloat16)
    )
    filter_terms = jnp.stack(
        [
            jnp.einsum(
                "srd,srd->d", grad_conv, padded[:, 0:slab_rows], preferred_element_type=jnp.float32
            ),
            jnp.einsum(
                "srd,srd->d",
                grad_conv,
                padded[:, 1 : slab_rows + 1],
                preferred_element_type=jnp.float32,
            ),
            jnp.einsum(
                "srd,srd->d",
                grad_conv,
                padded[:, 2 : slab_rows + 2],
                preferred_element_type=jnp.float32,
            ),
        ]
    )
    filter_sum = butterfly(butterfly(filter_terms, "seq"), "head")
    row_count = local_seqs * lax.axis_size("head") * slab_rows * lax.axis_size("seq")
    filter_grad = filter_sum * (1.0 / math.sqrt(row_count))
    return (target_rows, attention_grad, skip_grad, filter_grad)


LANES = 128
PAD = 8
BF = jnp.bfloat16
F32 = jnp.float32


def dot(left, right):
    return lax.dot_general(left, right, (((1,), (0,)), ((), ())), preferred_element_type=F32)


def dot_rows(left, right):
    return lax.dot_general(left, right, (((1,), (1,)), ((), ())), preferred_element_type=F32)


def grid_of(rows, columns):
    return (
        lax.broadcasted_iota(jnp.int32, (rows, columns), 0),
        lax.broadcasted_iota(jnp.int32, (rows, columns), 1),
    )


def picks(match):
    return jnp.where(match, 1.0, 0.0).astype(BF)


def params(mib=20):
    return pltpu.CompilerParams(vmem_limit_bytes=mib * 1024 * 1024)


def cost(flops, moved, special=0):
    return pl.CostEstimate(flops=flops, bytes_accessed=moved, transcendentals=special)


def pack_kernel(
    skip, attention, cotangent, weight, edge_a, edge_b, far, tile_a, tile_b, att_out,
    skip_lo, skip_hi, att_lo, att_hi, cot_lo, cot_hi, sems,
):
    head, slab = lax.axis_index("head"), lax.axis_index("seq")
    tile = tile_a.shape[0]
    core, block = slab & 1, (slab >> 1) & 3
    down = pl.ds(pl.multiple_of(core * tile, tile), tile)

    def piece(which):
        return weight.at[down, pl.ds(pl.multiple_of(which * tile, tile), tile)]

    edges = []
    for source, lo, hi in (
        (skip, skip_lo, skip_hi), (attention, att_lo, att_hi), (cotangent, cot_lo, cot_hi)
    ):
        rows = source.shape[1]
        for part, begin in ((lo, 0), (hi, rows - 16)):
            edges.append(
                pltpu.make_async_copy(source.at[:, pl.ds(begin, 16)], part, sems.at[len(edges)])
            )
    whole = [
        pltpu.make_async_copy(piece(block), tile_a, sems.at[6]),
        pltpu.make_async_copy(piece(3 - block), tile_b, sems.at[7]),
        pltpu.make_async_copy(attention.at[pl.ds(2 - 2 * head, 2)], att_out, sems.at[8]),
    ]
    for copy in edges + whole:
        copy.start()
    for copy in edges:
        copy.wait()
    wide = cot_lo.shape[2]
    at = lax.broadcasted_iota(jnp.int32, (8, wide), 0)
    even = core == 0
    ups, downs, ends = [], [], []
    for s in range(2):
        feats = [jnp.concatenate([part[s], part[2 + s]], axis=1) for part in (att_hi, att_lo)]
        high, low = feats[0].astype(F32)[8:], feats[1].astype(F32)[:8]
        up = jnp.where(at >= 6, skip_hi[s].astype(F32)[8:], 0.0)
        ups.append(jnp.where(at == 5, pltpu.roll(high, 6, 0), up))
        down = jnp.where(at < 2, skip_lo[s].astype(F32)[:8], 0.0)
        down = jnp.where(at == 2, pltpu.roll(low, 2, 0), down)
        downs.append(jnp.where(at == 3, pltpu.roll(cot_lo[s].astype(F32)[:8], 3, 0), down))
        last = pltpu.roll(cot_hi[s].astype(F32)[8:], 5, 0)
        ends.append(jnp.where(at == 4, last, 0.0))
    up, down = jnp.concatenate(ups), jnp.concatenate(downs)
    edge_a[...] = jnp.where(even, up, down).astype(BF)
    edge_b[...] = jnp.where(even, down, up).astype(BF)
    far[...] = jnp.concatenate(ends).astype(BF)
    for copy in whole:
        copy.wait()


def packed(encoder_skip, attention, cotangent, weight, tile):
    seqs, rows, wide = encoder_skip.shape
    count, short, half = attention.shape
    out = jax.ShapeDtypeStruct((16, wide), BF)
    square = jax.ShapeDtypeStruct((tile, tile), BF)
    anywhere = pl.BlockSpec(memory_space=pl.ANY)
    return pl.pallas_call(
        pack_kernel,
        in_specs=[anywhere] * 4,
        out_specs=[pl.BlockSpec(memory_space=pltpu.VMEM)] * 3 + [anywhere] * 3,
        out_shape=[out, out, out, square, square, jax.ShapeDtypeStruct((2, short, half), BF)],
        scratch_shapes=[
            pltpu.VMEM((seqs, 16, wide), BF),
            pltpu.VMEM((seqs, 16, wide), BF),
            pltpu.VMEM((count, 16, half), BF),
            pltpu.VMEM((count, 16, half), BF),
            pltpu.VMEM((seqs, 16, wide), BF),
            pltpu.VMEM((seqs, 16, wide), BF),
            pltpu.SemaphoreType.DMA((9,)),
        ],
        compiler_params=params(60),
        name="pack_edges",
    )(encoder_skip, attention, cotangent, weight)


def slab_sums(att, skip, edge, twin, ext, cols):
    width = cols.size
    short = 64
    row, col = grid_of(2 * short, short)
    spread = picks((row >> 1) == col)
    row, col = grid_of(16, 16)
    at, base = row & 7, row & 8
    wanted = ((at >= 6) & (col == base + 5)) | ((at < 2) & (col == base + 2))
    from_att = dot(picks(wanted), twin[:, cols])
    rims = edge[:, cols]
    at = lax.broadcasted_iota(jnp.int32, (16, width), 0) & 7
    rims = (from_att + rims.astype(F32)).astype(BF).astype(F32)
    above = jnp.where(at >= 6, rims, 0.0)
    below = jnp.where(at < 2, rims, 0.0)
    for s in range(2):
        body = dot(spread, att[s, 0:short, cols]) + skip[s, :, cols].astype(F32)
        ext[s, 0:PAD] = above[s * 8 : s * 8 + 8]
        ext[s, PAD : PAD + 2 * short] = body.astype(BF).astype(F32)
        ext[s, PAD + 2 * short : 2 * PAD + 2 * short] = below[s * 8 : s * 8 + 8]


def around(field):
    tall = field.shape[0]
    return pltpu.roll(field, 1, 0), pltpu.roll(field, tall - 1, 0)


def phi_of(values):
    return 0.5 * (1.0 + lax.erf(values * 0.7071067811865476))


def slope_of(values):
    return phi_of(values) + values * jnp.exp(-0.5 * values * values) * 0.3989422804014327


def asked_rows(meta, offsets, bins, s, ext, taps, tall):
    row, col = grid_of(48, tall)
    want = row & 3
    shift = (row >> 4) - 1
    at = jnp.full((48, tall), -4096, jnp.int32)
    slab = meta[1]
    for k in range(4):
        mine = k < NTD
        home = slab if mine else jnp.maximum(slab - 1, 0)
        place = bins[s, home * NTD + (k % NTD)] + offsets[s] - (0 if mine else tall - 2 * PAD)
        fits = (place >= 0) & (place < tall - 2 * PAD)
        at = jnp.where(want == k, jnp.where(fits, place + PAD, -4096), at)
    found = dot(picks((col == at + shift) & ((row & 15) < 8)), ext.astype(BF))
    here = found[16:32]
    value = taps[0] * found[0:16] + taps[1] * here + taps[2] * found[32:48]
    act = value * phi_of(value)
    row = lax.broadcasted_iota(jnp.int32, act.shape, 0)
    return jnp.where(row < 4, act, here).astype(BF)


def taps_of(filt, cols):
    return [filt[k : k + 1, cols] for k in range(3)]


def tap_sums(conv, ext, rows):
    before, after = around(ext)
    body = slice(PAD, PAD + rows)
    mine = conv[body]
    return [
        jnp.sum(mine * other[body], axis=0, keepdims=True) for other in (before, ext, after)
    ]


def grads(conv, direct, taps, rows, pair):
    before, after = around(conv)
    body = slice(PAD, PAD + rows)
    total = direct + taps[0] * after[body] + taps[1] * conv[body] + taps[2] * before[body]
    short = rows // 2
    sums = []
    for k in range(total.shape[1] // LANES):
        pair[k] = total[:, k * LANES : (k + 1) * LANES]
        sums.append(pair[k, pl.ds(0, short, 2), :] + pair[k, pl.ds(1, short, 2), :])
    return total, jnp.concatenate(sums, axis=1)


def own_slope_kernel(meta, offsets, bins, att, skip, edge, filt, asked, sums, slopes, ext):
    half = skip.shape[2]
    tall = ext.shape[1]
    width = ext.shape[2]

    @pl.loop(0, half // width)
    def _(part):
        cols = pl.ds(pl.multiple_of(part * width, width), width)
        slab_sums(att, skip, edge, edge, ext, cols)
        taps = taps_of(filt, cols)
        for s in range(2):
            field = ext[s]
            before, after = around(field)
            slopes[s, :, cols] = slope_of(taps[0] * before + taps[1] * field + taps[2] * after)
            sums[s, :, cols] = field.astype(BF)
            asked[s * 16 : s * 16 + 16, cols] = asked_rows(
                meta, offsets, bins, s, field, taps, tall
            )


def own_slopes(meta, offsets, bins, attention, skip, edge, filt):
    seqs, rows, wide = skip.shape
    _, short, half = attention.shape
    tall = rows + 2 * PAD

    def whole(*shape):
        return pl.BlockSpec(shape, lambda i, m, o, b: (0,) * len(shape))

    def mine(*shape):
        return pl.BlockSpec(shape, lambda i, m, o, b: (0,) * (len(shape) - 1) + (m[0],))

    return pl.pallas_call(
        own_slope_kernel,
        grid_spec=pltpu.PrefetchScalarGridSpec(
            num_scalar_prefetch=3,
            grid=(1,),
            in_specs=[
                pl.BlockSpec((2, short, half), lambda i, m, o, b: (m[0], 0, 0)),
                mine(2, rows, half),
                mine(16, half),
                mine(3, half),
            ],
            out_specs=[whole(32, half), whole(2, tall, half), whole(2, tall, half)],
            scratch_shapes=[pltpu.VMEM((2, tall, 256), F32)],
        ),
        out_shape=[
            jax.ShapeDtypeStruct((32, half), BF),
            jax.ShapeDtypeStruct((2, tall, half), BF),
            jax.ShapeDtypeStruct((2, tall, half), F32),
        ],
        compiler_params=params(),
        cost_estimate=cost(3 * 10**9, 10**6),
        name="own_slopes",
    )(meta, offsets, bins, attention, skip, edge, filt)


def own_kernel(
    slabs, meta, offsets, sums, slopes, rims, prev_far, cot_far, weight_far, filt,
    moved, terms, skip_grad, att_grad, pair, prev, cot, weight, sems,
):
    copies = [
        pltpu.make_async_copy(prev_far, prev, sems.at[0]),
        pltpu.make_async_copy(cot_far, cot, sems.at[1]),
        pltpu.make_async_copy(weight_far, weight, sems.at[2]),
    ]
    for copy in copies:
        copy.start()
    half = sums.shape[2]
    tall = sums.shape[1]
    rows = tall - 2 * PAD
    wide = cot.shape[2]
    row, col = grid_of(tall, rows)
    last = meta[1] == slabs - 1
    copies[0].wait()
    copies[1].wait()
    for s in range(2):
        at = row - PAD
        fits = (at >= -1) & (at < jnp.where(last, rows, rows + 1))
        source = jnp.where(fits, at - offsets[s], -4096)
        older = picks(col == source + rows)
        newer = picks(col == source)
        place = lax.broadcasted_iota(jnp.int32, (PAD, 512), 0)
        top = (place == PAD - 1) & (offsets[s] == rows)
        bottom = (place == 0) & (offsets[s] == 0) & jnp.logical_not(last)
        for part in range(0, wide, 512):
            cols = slice(part, part + 512)
            found = dot(older, prev[s, :, cols]) + dot(newer, cot[s, :, cols])
            ends = rims[:, cols].astype(F32)
            above = ends[s * 8 + 4 : s * 8 + 5]
            below = ends[s * 8 + 3 : s * 8 + 4]
            found = jnp.concatenate(
                [
                    found[:PAD] + jnp.where(top, above, 0.0),
                    found[PAD : PAD + rows],
                    found[PAD + rows :] + jnp.where(bottom, below, 0.0),
                ]
            )
            moved[s, :, cols] = found.astype(BF)
    copies[2].wait()
    width = 2 * LANES
    first = meta[0] * half

    @pl.loop(0, half // width)
    def _(part):
        begin = pl.multiple_of(part * width, width)
        cols = pl.ds(begin, width)
        taps = taps_of(filt, cols)
        piece = weight[pl.ds(begin, width), :]
        total_terms = [0.0, 0.0, 0.0]
        there = pl.ds(pl.multiple_of(first + begin, width), width)
        for s in range(2):
            conv = (dot_rows(moved[s], piece) * slopes[s, :, cols]).astype(BF).astype(F32)
            got = tap_sums(conv, sums[s, :, cols].astype(F32), rows)
            total_terms = [a + b for a, b in zip(total_terms, got)]
            direct = moved[s, :, there].astype(F32)[PAD : PAD + rows]
            total, pairs = grads(conv, direct, taps, rows, pair)
            skip_grad[s, :, cols] = total.astype(BF)
            att_grad[s, :, cols] = pairs.astype(BF)
        for k in range(3):
            terms[k : k + 1, cols] = total_terms[k]


def own_half(meta, offsets, sums, slopes, edge, prev, cot, weight, filt, slabs):
    seqs, rows, wide = cot.shape
    _, tall, half = sums.shape
    short = rows // 2

    def whole(*shape):
        return pl.BlockSpec(shape, lambda i, m, o: (0,) * len(shape))

    def mine(*shape):
        return pl.BlockSpec(shape, lambda i, m, o: (0,) * (len(shape) - 1) + (m[0],))

    anywhere = pl.BlockSpec(memory_space=pl.ANY)
    return pl.pallas_call(
        functools.partial(own_kernel, slabs),
        grid_spec=pltpu.PrefetchScalarGridSpec(
            num_scalar_prefetch=2,
            grid=(1,),
            in_specs=[
                whole(2, tall, half),
                whole(2, tall, half),
                whole(16, wide),
                anywhere,
                anywhere,
                anywhere,
                mine(3, half),
            ],
            out_specs=[
                whole(2, tall, wide),
                whole(3, half),
                mine(2, rows, half),
                mine(2, short, half),
            ],
            scratch_shapes=[
                pltpu.VMEM((2, rows, LANES), F32),
                pltpu.VMEM((2, rows, wide), BF),
                pltpu.VMEM((2, rows, wide), BF),
                pltpu.VMEM((half, wide), BF),
                pltpu.SemaphoreType.DMA((3,)),
            ],
        ),
        out_shape=[
            jax.ShapeDtypeStruct((2, tall, wide), BF),
            jax.ShapeDtypeStruct((3, half), F32),
            jax.ShapeDtypeStruct((2, rows, wide), BF),
            jax.ShapeDtypeStruct((2, short, wide), BF),
        ],
        compiler_params=params(),
        cost_estimate=cost(1, 1),
        name="own_half",
    )(meta, offsets, sums, slopes, edge, prev, cot, weight, filt)


def slope_kernel(
    meta, offsets, bins, att, skip, edge, twin, filt, asked, sums, slopes, mine, shown, ext
):
    rows = skip.shape[1]
    tall = rows + 2 * PAD
    half = skip.shape[2]
    width = ext.shape[2]
    there = (1 - meta[0]) * half
    row, col = grid_of(16, 32)
    at, base = row & 7, (row >> 3) * 16
    kept = picks((at < 4) & (col == base + at + jnp.where(at < 2, 0, 2)))
    told = picks((at < 4) & (col == base + at + jnp.where(at < 2, 2, 4)))
    here = pl.ds(pl.multiple_of(meta[0] * half, half), half)
    mine[:, here] = dot(kept, asked[...]).astype(BF)
    shown[:, here] = dot(told, asked[...]).astype(BF)

    @pl.loop(0, half // width)
    def _(part):
        begin = pl.multiple_of(part * width, width)
        cols = pl.ds(begin, width)
        slab_sums(att, skip, edge, twin, ext, cols)
        taps = taps_of(filt, cols)
        got = []
        for s in range(2):
            field = ext[s]
            before, after = around(field)
            slopes[s, :, cols] = slope_of(taps[0] * before + taps[1] * field + taps[2] * after)
            sums[s, :, cols] = field.astype(BF)
            got.append(asked_rows(meta, offsets, bins, s, field, taps, tall))
        got = jnp.concatenate(got)
        place = pl.ds(pl.multiple_of(there + begin, width), width)
        mine[:, place] = dot(kept, got).astype(BF)
        shown[:, place] = dot(told, got).astype(BF)


def other_slopes(meta, offsets, bins, shipped, skip, edge, twin, filt, asked):
    seqs, rows, wide = skip.shape
    _, packed_rows, half = shipped.shape
    tall = rows + 2 * PAD

    def whole(*shape):
        return pl.BlockSpec(shape, lambda i, m, o, b: (0,) * len(shape))

    def other(*shape):
        return pl.BlockSpec(shape, lambda i, m, o, b: (0,) * (len(shape) - 1) + (1 - m[0],))

    return pl.pallas_call(
        slope_kernel,
        grid_spec=pltpu.PrefetchScalarGridSpec(
            num_scalar_prefetch=3,
            grid=(1,),
            in_specs=[
                whole(2, packed_rows, half),
                other(2, rows, half),
                other(16, half),
                pl.BlockSpec((16, half), lambda i, m, o, b: (0, m[0])),
                other(3, half),
                whole(32, half),
            ],
            out_specs=[whole(2, tall, half), whole(2, tall, half), whole(16, wide), whole(16, wide)],
            scratch_shapes=[pltpu.VMEM((2, tall, 256), F32)],
        ),
        out_shape=[
            jax.ShapeDtypeStruct((2, tall, half), BF),
            jax.ShapeDtypeStruct((2, tall, half), F32),
            jax.ShapeDtypeStruct((16, wide), BF),
            jax.ShapeDtypeStruct((16, wide), BF),
        ],
        compiler_params=params(),
        cost_estimate=cost(3 * 10**9, 10**6),
        name="other_slopes",
    )(meta, offsets, bins, shipped, skip, edge, twin, filt, asked)


def spots(meta, tile):
    core, block = meta[1] & 1, (meta[1] >> 1) & 3
    return [
        (pl.multiple_of(row * tile, tile), pl.multiple_of((block ^ k) * tile, tile))
        for row in (core, 1 - core)
        for k in range(4)
    ]


def terms_kernel(meta, moved, sums, slopes, own_terms, *refs):
    pieces, (convs, terms, full, sems) = refs[:8], refs[8:]
    half = sums.shape[2]
    tall = sums.shape[1]
    rows = tall - 2 * PAD
    there = (1 - meta[0]) * half
    tile = pieces[0].shape[0]
    copies = []
    for k, (down, over) in enumerate(spots(meta, tile)):
        copies.append(
            pltpu.make_async_copy(
                pieces[k], full.at[pl.ds(down, tile), pl.ds(over, tile)], sems.at[k]
            )
        )
        copies[-1].start()
    terms[:, pl.ds(pl.multiple_of(meta[0] * half, half), half)] = own_terms[...]
    for copy in copies:
        copy.wait()
    width = 2 * LANES
    for begin in range(0, half, width):
        cols = slice(begin, begin + width)
        total = [0.0, 0.0, 0.0]
        for s in range(2):
            grad = dot_rows(moved[s], full[cols, :])
            conv = (grad * slopes[s, :, cols]).astype(BF)
            convs[s, :, cols] = conv
            got = tap_sums(conv.astype(F32), sums[s, :, cols].astype(F32), rows)
            total = [a + b for a, b in zip(total, got)]
        place = pl.ds(pl.multiple_of(there + begin, width), width)
        for k in range(3):
            terms[k : k + 1, place] = total[k]


def other_terms(meta, moved, sums, slopes, own_terms, pieces):
    _, tall, wide = moved.shape
    half = sums.shape[2]

    def whole(*shape):
        return pl.BlockSpec(shape, lambda i, m: (0,) * len(shape))

    return pl.pallas_call(
        terms_kernel,
        grid_spec=pltpu.PrefetchScalarGridSpec(
            num_scalar_prefetch=1,
            grid=(1,),
            in_specs=[
                whole(2, tall, wide),
                whole(2, tall, half),
                whole(2, tall, half),
                whole(3, half),
            ]
            + [pl.BlockSpec(memory_space=pl.ANY)] * 8,
            out_specs=[whole(2, tall, half), whole(3, wide)],
            scratch_shapes=[pltpu.VMEM((half, wide), BF), pltpu.SemaphoreType.DMA((8,))],
        ),
        out_shape=[
            jax.ShapeDtypeStruct((2, tall, half), BF),
            jax.ShapeDtypeStruct((3, wide), F32),
        ],
        compiler_params=params(),
        cost_estimate=cost(2 * 2 * tall * half * wide, 6 * 1024 * 1024),
        name="other_terms",
    )(meta, moved, sums, slopes, own_terms, *pieces)


def grads_kernel(meta, moved, convs, filt, old_skip, old_att, skip_grad, att_grad, pair):
    half = convs.shape[2]
    rows = convs.shape[1] - 2 * PAD
    width = 2 * LANES

    @pl.loop(0, half // width)
    def _(part):
        cols = pl.ds(pl.multiple_of(part * width, width), width)
        taps = taps_of(filt, cols)
        for s in range(2):
            direct = moved[s, :, cols].astype(F32)[PAD : PAD + rows]
            total, pairs = grads(convs[s, :, cols].astype(F32), direct, taps, rows, pair)
            skip_grad[s, :, cols] = total.astype(BF)
            att_grad[s, :, cols] = pairs.astype(BF)


def other_grads(meta, moved, convs, filt, skip_grad, att_grad):
    _, tall, wide = moved.shape
    half = convs.shape[2]
    rows = tall - 2 * PAD

    def whole(*shape):
        return pl.BlockSpec(shape, lambda i, m: (0,) * len(shape))

    def other(*shape):
        return pl.BlockSpec(shape, lambda i, m: (0,) * (len(shape) - 1) + (1 - m[0],))

    return pl.pallas_call(
        grads_kernel,
        grid_spec=pltpu.PrefetchScalarGridSpec(
            num_scalar_prefetch=1,
            grid=(1,),
            in_specs=[other(2, tall, half), whole(2, tall, half), other(3, half)]
            + [pl.BlockSpec(memory_space=pl.ANY)] * 2,
            out_specs=[other(2, rows, half), other(2, rows // 2, half)],
            scratch_shapes=[pltpu.VMEM((2, rows, LANES), F32)],
        ),
        out_shape=[
            jax.ShapeDtypeStruct((2, rows, wide), BF),
            jax.ShapeDtypeStruct((2, rows // 2, wide), BF),
        ],
        input_output_aliases={4: 0, 5: 1},
        compiler_params=params(),
        cost_estimate=cost(2 * tall * half * 20, 4 * 1024 * 1024),
        name="other_grads",
    )(meta, moved, convs, filt, skip_grad, att_grad)


def target_kernel(slabs, meta, mine, got_a, got_b, weight, *refs):
    pieces, (target, total) = refs[:8], refs[8:]
    half = weight.shape[0]
    there = (1 - meta[0]) * half
    tile = pieces[0].shape[0]
    even = (meta[1] & 1) == 0
    got = jnp.where(even, got_a[...].astype(F32), got_b[...].astype(F32))
    got = jnp.where(meta[1] == slabs - 1, 0.0, got)
    mine[...] = (mine[...].astype(F32) + got).astype(BF)
    here = pl.ds(pl.multiple_of(meta[0] * half, half), half)
    total[...] = dot(mine[:, here], weight[...]) + pltpu.roll(mine[...].astype(F32), 12 + 2, 0)
    for k, (down, over) in enumerate(spots(meta, tile)):
        place = pl.ds(pl.multiple_of(there + down, tile), tile)
        total[:, pl.ds(over, tile)] += dot(mine[:, place], pieces[k][...])
    for s in range(2):
        target[s] = total[s * 8 : s * 8 + 2].astype(BF)


def targets(meta, mine, got, weight, pieces, slabs):
    half, wide = weight.shape
    tile = pieces[0].shape[0]

    def whole(*shape):
        return pl.BlockSpec(shape, lambda i, m: (0,) * len(shape))

    return pl.pallas_call(
        functools.partial(target_kernel, slabs),
        grid_spec=pltpu.PrefetchScalarGridSpec(
            num_scalar_prefetch=1,
            grid=(1,),
            in_specs=[whole(16, wide)] * 3 + [whole(half, wide)]
            + [whole(tile, tile)] * 8,
            out_specs=whole(2, NTD, wide),
            scratch_shapes=[pltpu.VMEM((16, wide), F32)],
        ),
        out_shape=jax.ShapeDtypeStruct((2, NTD, wide), BF),
        compiler_params=params(),
        cost_estimate=cost(2 * 16 * wide * wide, 6 * 1024 * 1024),
        name="targets",
    )(meta, mine, *got, weight, *pieces)


def paired(part, axis, bit):
    count = lax.axis_size(axis)
    return lax.ppermute(part, axis, [(i, i ^ bit) for i in range(count)])


def staggered(part, span):
    count = lax.axis_size("seq")
    pairs = []
    for i in range(count):
        by = span if i // span % 2 else -span
        pairs.append((i, (i + by) % count))
    return lax.ppermute(part, "seq", pairs)


def after(value, *others):
    return lax.optimization_barrier((value,) + others)[0]


def crossed(part, seq_bit, head_bit):
    slabs, heads = lax.axis_size("seq"), lax.axis_size("head")
    pairs = [
        (i * heads + j, (i ^ seq_bit) * heads + (j ^ head_bit))
        for i in range(slabs)
        for j in range(heads)
    ]
    return lax.ppermute(part, ("seq", "head"), pairs)


def joined(total, one, two):
    both = (one[0] ^ two[0], one[1] ^ two[1])
    parts = [crossed(total, *bits) for bits in (one, two, both)]
    return (total + parts[0]) + (parts[1] + parts[2])


def fast_shards(
    attention, encoder_skip, depth_filter, point_weight, crop_offset, target_bins, cotangent
):
    head = lax.axis_index("head")
    slab = lax.axis_index("seq")
    slabs = lax.axis_size("seq")
    meta = jnp.stack([head, slab]).astype(jnp.int32)
    tile = 3 * LANES

    edge_a, edge_b, far, first, last_tile, att_out = packed(
        encoder_skip, attention, cotangent, point_weight, tile
    )
    first = paired(first, "head", 1)
    edge_a = paired(edge_a, "seq", 1)
    edge_b = staggered(edge_b, 1)
    far_a = paired(far, "seq", 2)
    far_b = staggered(far, 2)
    prev = passed_along(after(cotangent, edge_b), "seq", 1)
    outer = (slab == 0) | (slab == slabs - 1)
    nothing = jnp.zeros_like(edge_b)
    edge = edge_a + jnp.where(outer, nothing, edge_b)
    twin = paired(edge, "head", 1)
    shipped = paired(after(att_out, edge), "head", 1)
    edge = edge + jnp.where(slab % 4 >= 2, far_a, jnp.where(slab < 2, nothing, far_b))
    asked, own_sums, own_slope = own_slopes(
        meta, crop_offset, target_bins, attention, encoder_skip, edge, depth_filter
    )
    ready = after(first, asked)
    second = paired(ready, "seq", 2)
    third = paired(ready, "seq", 4)
    fourth = paired(last_tile, "head", 1)
    sums, slopes, mine, shown = other_slopes(
        meta, crop_offset, target_bins, shipped, encoder_skip, edge, twin, depth_filter, asked
    )
    got = [paired(shown, "seq", 1), staggered(shown, 1)]
    moved, own_terms, skip_grad, att_grad = own_half(
        after(meta, shown), crop_offset, own_sums, own_slope, edge, prev, cotangent, point_weight, depth_filter,
        slabs,
    )
    pieces = [first, second, third, fourth]
    pieces = pieces + [paired(after(piece, own_terms), "seq", 1) for piece in pieces]
    convs, terms = other_terms(meta, moved, sums, slopes, own_terms, pieces)
    terms, *got = lax.optimization_barrier((terms, *got))
    total = terms + crossed(terms, 1, 0)
    total = joined(total, (2, 0), (0, 1))
    skip_grad, attention_grad = other_grads(
        meta, moved, convs, depth_filter, skip_grad, att_grad
    )
    target_rows = targets(meta, mine, got, point_weight, pieces, slabs)
    total, skip_grad, attention_grad = lax.optimization_barrier(
        (total, skip_grad, attention_grad)
    )
    if slabs == 16:
        total = joined(total, (4, 0), (8, 0))
    else:
        step = 4
        while step < slabs:
            total = total + crossed(total, step, 0)
            step *= 2
    count = encoder_skip.shape[0] * lax.axis_size("head") * encoder_skip.shape[1] * slabs
    return (target_rows, attention_grad, skip_grad, total * (1.0 / math.sqrt(count)))


def shards(*args):
    attention, encoder_skip, point_weight = args[0], args[1], args[3]
    fits = (
        lax.axis_size("head") == 2
        and lax.axis_size("seq") in (8, 16, 32)
        and encoder_skip.shape[:2] == (2, 128)
        and point_weight.shape[0] == 6 * LANES
        and attention.shape[1] == 64
    )
    return fast_shards(*args) if fits else plain_shards(*args)


def solution(mesh):
    in_specs = (
        P(None, "seq", "head"),
        P("head", "seq", None),
        P(),
        P("head", None),
        P("head"),
        P("head", None),
        P("head", "seq", None),
    )
    out_specs = (P("head", "seq", None), P("head", "seq", None), P("head", "seq", None), P())
    return jax.shard_map(shards, mesh=mesh, in_specs=in_specs, out_specs=out_specs, check_vma=False)
def solution(mesh):
    in_specs = (
        P(None, "seq", "head"),
        P("head", "seq", None),
        P(),
        P("head", None),
        P("head"),
        P("head", None),
        P("head", "seq", None),
    )
    out_specs = (P("head", "seq", None), P("head", "seq", None), P("head", "seq", None), P())
    return jax.shard_map(shards, mesh=mesh, in_specs=in_specs, out_specs=out_specs, check_vma=False)
```

```python
import functools
import math

import jax
import jax.numpy as jnp
from jax import lax
from jax.experimental import pallas as pl
from jax.experimental.pallas import tpu as pltpu
from jax.sharding import PartitionSpec as P

NTD = 2


def extended(shard, sides, width):
    for axis, dim in sides:
        count, length = (lax.axis_size(axis), shard.shape[dim])
        up = [(i, (i + 1) % count) for i in range(count - 1)]
        down = [(j, i) for i, j in up]
        last = lax.slice_in_dim(shard, length - width, length, axis=dim)
        initial = lax.slice_in_dim(shard, 0, width, axis=dim)
        before = lax.ppermute(last, axis, up)
        after = lax.ppermute(initial, axis, down)
        shard = jnp.concatenate([before, shard, after], axis=dim)
    return shard


def passed_along(shard, axis, by):
    count = lax.axis_size(axis)
    pairs = [(i, i + by) for i in range(count) if 0 <= i + by < count]
    return lax.ppermute(shard, axis, pairs)


def gelu_slope(values):
    return (
        0.5 * (1.0 + lax.erf(values * 0.7071067811865476))
        + values * jnp.exp(-0.5 * values * values) * 0.3989422804014327
    )


def with_rims(field):
    return extended(field, (("seq", 1),), 1)


def one_hot(places, length):
    return (places[:, :, None] == jnp.arange(length, dtype=jnp.int32)[None, None, :]).astype(
        jnp.bfloat16
    )


def core_swap(part):
    count = lax.axis_size("seq")
    return lax.ppermute(part, "seq", [(i, i ^ 1) for i in range(count)])


def gathered_weight(rows):
    heads = lax.axis_size("head")
    here = lax.axis_index("head")
    core = lax.axis_index("seq") % 2
    half = rows.shape[0] // 2
    mine = lax.dynamic_slice_in_dim(rows, core * half, half, 0)
    blocks = [(0, rows)]
    for step in range(1, heads):
        pairs = [(i, (i + step) % heads) for i in range(heads)]
        got = lax.ppermute(mine, "head", pairs)
        twin = core_swap(got)
        low = jnp.where(core == 0, got, twin)
        high = jnp.where(core == 0, twin, got)
        blocks.append((step, jnp.concatenate([low, high], axis=0)))
    full = jnp.zeros((heads * rows.shape[0], rows.shape[1]), rows.dtype)
    for step, block in blocks:
        place = (here - step) % heads
        full = lax.dynamic_update_slice_in_dim(full, block, place * rows.shape[0], 0)
    return full


def butterfly(total, axis):
    count = lax.axis_size(axis)
    if count & (count - 1):
        return lax.psum(total, axis)
    step = 1
    while step < count:
        total = total + lax.ppermute(total, axis, [(i, i ^ step) for i in range(count)])
        step *= 2
    return total


def plain_shards(
    attention, encoder_skip, depth_filter, point_weight, crop_offset, target_bins, cotangent
):
    slab_input = lax.all_to_all(attention, "head", split_axis=0, concat_axis=2, tiled=True)
    local_seqs = encoder_skip.shape[0]
    slab_rows = encoder_skip.shape[1]
    channels = encoder_skip.shape[2]
    summed = (
        jnp.repeat(slab_input, 2, axis=1).astype(jnp.float32) + encoder_skip.astype(jnp.float32)
    ).astype(jnp.bfloat16)
    padded = with_rims(summed)
    filtered = (
        depth_filter[0] * padded[:, :-2]
        + depth_filter[1] * padded[:, 1:-1]
        + depth_filter[2] * padded[:, 2:]
    )
    activated = jax.nn.gelu(filtered, approximate=False).astype(jnp.bfloat16)
    flat_act = activated.reshape(local_seqs * slab_rows, channels)
    full_weight = gathered_weight(point_weight)
    mixed_rows = jnp.dot(flat_act, full_weight, preferred_element_type=jnp.float32)
    block_out = (
        summed.astype(jnp.float32) + mixed_rows.reshape(local_seqs, slab_rows, channels)
    ).astype(jnp.bfloat16)
    slab_index = lax.axis_index("seq")
    bins = jnp.concatenate(
        [jnp.zeros_like(target_bins[:, :NTD]), target_bins], axis=1
    )
    asked = lax.dynamic_slice_in_dim(bins, slab_index * NTD, 2 * NTD, 1) + crop_offset[:, None]
    back = jnp.where(jnp.arange(2 * NTD, dtype=jnp.int32) < NTD, slab_rows, 0)
    asked = asked - back[None, :]
    picked = jnp.einsum(
        "sjr,srd->sjd",
        one_hot(asked, slab_rows),
        block_out,
        preferred_element_type=jnp.float32,
    ).astype(jnp.bfloat16)
    from_next = passed_along(picked[:, :NTD], "seq", -1)
    target_rows = picked[:, NTD:] + from_next
    prev_cot = passed_along(cotangent, "seq", 1)
    cot_pair = jnp.concatenate([prev_cot, cotangent], axis=1)

    def crop_back(cot_block, shift_by):
        return lax.dynamic_slice_in_dim(cot_block, slab_rows - shift_by, slab_rows, 0)

    grad_out = jax.vmap(crop_back)(cot_pair, crop_offset)
    flat_grad = grad_out.reshape(local_seqs * slab_rows, channels)
    grad_act = lax.dot_general(
        flat_grad, full_weight, (((1,), (1,)), ((), ())), preferred_element_type=jnp.float32
    )
    grad_conv = (grad_act.reshape(local_seqs, slab_rows, channels) * gelu_slope(filtered)).astype(
        jnp.bfloat16
    )
    grad_padded = with_rims(grad_conv)
    grad_sum = (
        grad_out.astype(jnp.float32)
        + depth_filter[0] * grad_padded[:, 2:]
        + depth_filter[1] * grad_padded[:, 1:-1]
        + depth_filter[2] * grad_padded[:, :-2]
    )
    skip_grad = grad_sum.astype(jnp.bfloat16)
    attention_grad = (
        grad_sum.reshape(local_seqs, slab_rows // 2, 2, channels).sum(axis=2).astype(jnp.bfloat16)
    )
    filter_terms = jnp.stack(
        [
            jnp.einsum(
                "srd,srd->d", grad_conv, padded[:, 0:slab_rows], preferred_element_type=jnp.float32
            ),
            jnp.einsum(
                "srd,srd->d",
                grad_conv,
                padded[:, 1 : slab_rows + 1],
                preferred_element_type=jnp.float32,
            ),
            jnp.einsum(
                "srd,srd->d",
                grad_conv,
                padded[:, 2 : slab_rows + 2],
                preferred_element_type=jnp.float32,
            ),
        ]
    )
    filter_sum = butterfly(butterfly(filter_terms, "seq"), "head")
    row_count = local_seqs * lax.axis_size("head") * slab_rows * lax.axis_size("seq")
    filter_grad = filter_sum * (1.0 / math.sqrt(row_count))
    return (target_rows, attention_grad, skip_grad, filter_grad)


import functools
import math

import jax
import jax.numpy as jnp
from jax import lax
from jax.experimental import pallas as pl
from jax.experimental.pallas import tpu as pltpu
from jax.sharding import PartitionSpec as P

NTD = 2


def extended(shard, sides, width):
    for axis, dim in sides:
        count, length = (lax.axis_size(axis), shard.shape[dim])
        up = [(i, (i + 1) % count) for i in range(count - 1)]
        down = [(j, i) for i, j in up]
        last = lax.slice_in_dim(shard, length - width, length, axis=dim)
        initial = lax.slice_in_dim(shard, 0, width, axis=dim)
        before = lax.ppermute(last, axis, up)
        after = lax.ppermute(initial, axis, down)
        shard = jnp.concatenate([before, shard, after], axis=dim)
    return shard


def passed_along(shard, axis, by):
    count = lax.axis_size(axis)
    pairs = [(i, i + by) for i in range(count) if 0 <= i + by < count]
    return lax.ppermute(shard, axis, pairs)


def gelu_slope(values):
    return (
        0.5 * (1.0 + lax.erf(values * 0.7071067811865476))
        + values * jnp.exp(-0.5 * values * values) * 0.3989422804014327
    )


def with_rims(field):
    return extended(field, (("seq", 1),), 1)


def one_hot(places, length):
    return (places[:, :, None] == jnp.arange(length, dtype=jnp.int32)[None, None, :]).astype(
        jnp.bfloat16
    )


def core_swap(part):
    count = lax.axis_size("seq")
    return lax.ppermute(part, "seq", [(i, i ^ 1) for i in range(count)])


def gathered_weight(rows):
    heads = lax.axis_size("head")
    here = lax.axis_index("head")
    core = lax.axis_index("seq") % 2
    half = rows.shape[0] // 2
    mine = lax.dynamic_slice_in_dim(rows, core * half, half, 0)
    blocks = [(0, rows)]
    for step in range(1, heads):
        pairs = [(i, (i + step) % heads) for i in range(heads)]
        got = lax.ppermute(mine, "head", pairs)
        twin = core_swap(got)
        low = jnp.where(core == 0, got, twin)
        high = jnp.where(core == 0, twin, got)
        blocks.append((step, jnp.concatenate([low, high], axis=0)))
    full = jnp.zeros((heads * rows.shape[0], rows.shape[1]), rows.dtype)
    for step, block in blocks:
        place = (here - step) % heads
        full = lax.dynamic_update_slice_in_dim(full, block, place * rows.shape[0], 0)
    return full


def butterfly(total, axis):
    count = lax.axis_size(axis)
    if count & (count - 1):
        return lax.psum(total, axis)
    step = 1
    while step < count:
        total = total + lax.ppermute(total, axis, [(i, i ^ step) for i in range(count)])
        step *= 2
    return total


def plain_shards(
    attention, encoder_skip, depth_filter, point_weight, crop_offset, target_bins, cotangent
):
    slab_input = lax.all_to_all(attention, "head", split_axis=0, concat_axis=2, tiled=True)
    local_seqs = encoder_skip.shape[0]
    slab_rows = encoder_skip.shape[1]
    channels = encoder_skip.shape[2]
    summed = (
        jnp.repeat(slab_input, 2, axis=1).astype(jnp.float32) + encoder_skip.astype(jnp.float32)
    ).astype(jnp.bfloat16)
    padded = with_rims(summed)
    filtered = (
        depth_filter[0] * padded[:, :-2]
        + depth_filter[1] * padded[:, 1:-1]
        + depth_filter[2] * padded[:, 2:]
    )
    activated = jax.nn.gelu(filtered, approximate=False).astype(jnp.bfloat16)
    flat_act = activated.reshape(local_seqs * slab_rows, channels)
    full_weight = gathered_weight(point_weight)
    mixed_rows = jnp.dot(flat_act, full_weight, preferred_element_type=jnp.float32)
    block_out = (
        summed.astype(jnp.float32) + mixed_rows.reshape(local_seqs, slab_rows, channels)
    ).astype(jnp.bfloat16)
    slab_index = lax.axis_index("seq")
    bins = jnp.concatenate(
        [jnp.zeros_like(target_bins[:, :NTD]), target_bins], axis=1
    )
    asked = lax.dynamic_slice_in_dim(bins, slab_index * NTD, 2 * NTD, 1) + crop_offset[:, None]
    back = jnp.where(jnp.arange(2 * NTD, dtype=jnp.int32) < NTD, slab_rows, 0)
    asked = asked - back[None, :]
    picked = jnp.einsum(
        "sjr,srd->sjd",
        one_hot(asked, slab_rows),
        block_out,
        preferred_element_type=jnp.float32,
    ).astype(jnp.bfloat16)
    from_next = passed_along(picked[:, :NTD], "seq", -1)
    target_rows = picked[:, NTD:] + from_next
    prev_cot = passed_along(cotangent, "seq", 1)
    cot_pair = jnp.concatenate([prev_cot, cotangent], axis=1)

    def crop_back(cot_block, shift_by):
        return lax.dynamic_slice_in_dim(cot_block, slab_rows - shift_by, slab_rows, 0)

    grad_out = jax.vmap(crop_back)(cot_pair, crop_offset)
    flat_grad = grad_out.reshape(local_seqs * slab_rows, channels)
    grad_act = lax.dot_general(
        flat_grad, full_weight, (((1,), (1,)), ((), ())), preferred_element_type=jnp.float32
    )
    grad_conv = (grad_act.reshape(local_seqs, slab_rows, channels) * gelu_slope(filtered)).astype(
        jnp.bfloat16
    )
    grad_padded = with_rims(grad_conv)
    grad_sum = (
        grad_out.astype(jnp.float32)
        + depth_filter[0] * grad_padded[:, 2:]
        + depth_filter[1] * grad_padded[:, 1:-1]
        + depth_filter[2] * grad_padded[:, :-2]
    )
    skip_grad = grad_sum.astype(jnp.bfloat16)
    attention_grad = (
        grad_sum.reshape(local_seqs, slab_rows // 2, 2, channels).sum(axis=2).astype(jnp.bfloat16)
    )
    filter_terms = jnp.stack(
        [
            jnp.einsum(
                "srd,srd->d", grad_conv, padded[:, 0:slab_rows], preferred_element_type=jnp.float32
            ),
            jnp.einsum(
                "srd,srd->d",
                grad_conv,
                padded[:, 1 : slab_rows + 1],
                preferred_element_type=jnp.float32,
            ),
            jnp.einsum(
                "srd,srd->d",
                grad_conv,
                padded[:, 2 : slab_rows + 2],
                preferred_element_type=jnp.float32,
            ),
        ]
    )
    filter_sum = butterfly(butterfly(filter_terms, "seq"), "head")
    row_count = local_seqs * lax.axis_size("head") * slab_rows * lax.axis_size("seq")
    filter_grad = filter_sum * (1.0 / math.sqrt(row_count))
    return (target_rows, attention_grad, skip_grad, filter_grad)


LANES = 128
PAD = 8
BF = jnp.bfloat16
F32 = jnp.float32


def dot(left, right):
    return lax.dot_general(left, right, (((1,), (0,)), ((), ())), preferred_element_type=F32)


def dot_rows(left, right):
    return lax.dot_general(left, right, (((1,), (1,)), ((), ())), preferred_element_type=F32)


def grid_of(rows, columns):
    return (
        lax.broadcasted_iota(jnp.int32, (rows, columns), 0),
        lax.broadcasted_iota(jnp.int32, (rows, columns), 1),
    )


def picks(match):
    return jnp.where(match, 1.0, 0.0).astype(BF)


def params(mib=20):
    return pltpu.CompilerParams(vmem_limit_bytes=mib * 1024 * 1024)


def cost(flops, moved, special=0):
    return pl.CostEstimate(flops=flops, bytes_accessed=moved, transcendentals=special)


def pack_kernel(
    skip, attention, cotangent, weight, edge_a, edge_b, far, tile_a, tile_b, att_out,
    skip_lo, skip_hi, att_lo, att_hi, cot_lo, cot_hi, sems,
):
    head, slab = lax.axis_index("head"), lax.axis_index("seq")
    tile = tile_a.shape[0]
    core, block = slab & 1, (slab >> 1) & 3
    down = pl.ds(pl.multiple_of(core * tile, tile), tile)

    def piece(which):
        return weight.at[down, pl.ds(pl.multiple_of(which * tile, tile), tile)]

    edges = []
    for source, lo, hi in (
        (skip, skip_lo, skip_hi), (attention, att_lo, att_hi), (cotangent, cot_lo, cot_hi)
    ):
        rows = source.shape[1]
        for part, begin in ((lo, 0), (hi, rows - 16)):
            edges.append(
                pltpu.make_async_copy(source.at[:, pl.ds(begin, 16)], part, sems.at[len(edges)])
            )
    whole = [
        pltpu.make_async_copy(piece(block), tile_a, sems.at[6]),
        pltpu.make_async_copy(piece(3 - block), tile_b, sems.at[7]),
        pltpu.make_async_copy(attention.at[pl.ds(2 - 2 * head, 2)], att_out, sems.at[8]),
    ]
    for copy in edges + whole:
        copy.start()
    for copy in edges:
        copy.wait()
    wide = cot_lo.shape[2]
    at = lax.broadcasted_iota(jnp.int32, (8, wide), 0)
    even = core == 0
    ups, downs, ends = [], [], []
    for s in range(2):
        feats = [jnp.concatenate([part[s], part[2 + s]], axis=1) for part in (att_hi, att_lo)]
        high, low = feats[0].astype(F32)[8:], feats[1].astype(F32)[:8]
        up = jnp.where(at >= 6, skip_hi[s].astype(F32)[8:], 0.0)
        ups.append(jnp.where(at == 5, pltpu.roll(high, 6, 0), up))
        down = jnp.where(at < 2, skip_lo[s].astype(F32)[:8], 0.0)
        down = jnp.where(at == 2, pltpu.roll(low, 2, 0), down)
        downs.append(jnp.where(at == 3, pltpu.roll(cot_lo[s].astype(F32)[:8], 3, 0), down))
        last = pltpu.roll(cot_hi[s].astype(F32)[8:], 5, 0)
        ends.append(jnp.where(at == 4, last, 0.0))
    up, down = jnp.concatenate(ups), jnp.concatenate(downs)
    edge_a[...] = jnp.where(even, up, down).astype(BF)
    edge_b[...] = jnp.where(even, down, up).astype(BF)
    far[...] = jnp.concatenate(ends).astype(BF)
    for copy in whole:
        copy.wait()


def packed(encoder_skip, attention, cotangent, weight, tile):
    seqs, rows, wide = encoder_skip.shape
    count, short, half = attention.shape
    out = jax.ShapeDtypeStruct((16, wide), BF)
    square = jax.ShapeDtypeStruct((tile, tile), BF)
    anywhere = pl.BlockSpec(memory_space=pl.ANY)
    flat = pl.BlockSpec((16, wide), lambda i: (0, 0))
    cut = pl.BlockSpec((tile, tile), lambda i: (0, 0))
    return pl.pallas_call(
        pack_kernel,
        grid=(1,),
        in_specs=[anywhere] * 4,
        out_specs=[flat] * 3 + [cut] * 2 + [pl.BlockSpec((2, short, half), lambda i: (0, 0, 0))],
        out_shape=[out, out, out, square, square, jax.ShapeDtypeStruct((2, short, half), BF)],
        scratch_shapes=[
            pltpu.VMEM((seqs, 16, wide), BF),
            pltpu.VMEM((seqs, 16, wide), BF),
            pltpu.VMEM((count, 16, half), BF),
            pltpu.VMEM((count, 16, half), BF),
            pltpu.VMEM((seqs, 16, wide), BF),
            pltpu.VMEM((seqs, 16, wide), BF),
            pltpu.SemaphoreType.DMA((9,)),
        ],
        compiler_params=params(60),
        name="pack_edges",
    )(encoder_skip, attention, cotangent, weight)


def slab_sums(att, skip, edge, twin, ext, cols):
    width = cols.size
    short = 64
    row, col = grid_of(2 * short, short)
    spread = picks((row >> 1) == col)
    row, col = grid_of(16, 16)
    at, base = row & 7, row & 8
    wanted = ((at >= 6) & (col == base + 5)) | ((at < 2) & (col == base + 2))
    from_att = dot(picks(wanted), twin[:, cols])
    rims = edge[:, cols]
    at = lax.broadcasted_iota(jnp.int32, (16, width), 0) & 7
    rims = (from_att + rims.astype(F32)).astype(BF).astype(F32)
    above = jnp.where(at >= 6, rims, 0.0)
    below = jnp.where(at < 2, rims, 0.0)
    for s in range(2):
        body = dot(spread, att[s, 0:short, cols]) + skip[s, :, cols].astype(F32)
        ext[s, 0:PAD] = above[s * 8 : s * 8 + 8]
        ext[s, PAD : PAD + 2 * short] = body.astype(BF).astype(F32)
        ext[s, PAD + 2 * short : 2 * PAD + 2 * short] = below[s * 8 : s * 8 + 8]


def around(field):
    tall = field.shape[0]
    return pltpu.roll(field, 1, 0), pltpu.roll(field, tall - 1, 0)


def phi_of(values):
    return 0.5 * (1.0 + lax.erf(values * 0.7071067811865476))


def slope_of(values):
    return phi_of(values) + values * jnp.exp(-0.5 * values * values) * 0.3989422804014327


def asked_rows(meta, offsets, bins, s, ext, taps, tall):
    row, col = grid_of(48, tall)
    want = row & 3
    shift = (row >> 4) - 1
    at = jnp.full((48, tall), -4096, jnp.int32)
    slab = meta[1]
    for k in range(4):
        mine = k < NTD
        home = slab if mine else jnp.maximum(slab - 1, 0)
        place = bins[s, home * NTD + (k % NTD)] + offsets[s] - (0 if mine else tall - 2 * PAD)
        fits = (place >= 0) & (place < tall - 2 * PAD)
        at = jnp.where(want == k, jnp.where(fits, place + PAD, -4096), at)
    found = dot(picks((col == at + shift) & ((row & 15) < 8)), ext.astype(BF))
    here = found[16:32]
    value = taps[0] * found[0:16] + taps[1] * here + taps[2] * found[32:48]
    act = value * phi_of(value)
    row = lax.broadcasted_iota(jnp.int32, act.shape, 0)
    return jnp.where(row < 4, act, here).astype(BF)


def taps_of(filt, cols):
    return [filt[k : k + 1, cols] for k in range(3)]


def tap_sums(conv, ext, rows):
    before, after = around(ext)
    body = slice(PAD, PAD + rows)
    mine = conv[body]
    return [
        jnp.sum(mine * other[body], axis=0, keepdims=True) for other in (before, ext, after)
    ]


def grads(conv, direct, taps, rows, pair):
    before, after = around(conv)
    body = slice(PAD, PAD + rows)
    total = direct + taps[0] * after[body] + taps[1] * conv[body] + taps[2] * before[body]
    short = rows // 2
    sums = []
    for k in range(total.shape[1] // LANES):
        pair[k] = total[:, k * LANES : (k + 1) * LANES]
        sums.append(pair[k, pl.ds(0, short, 2), :] + pair[k, pl.ds(1, short, 2), :])
    return total, jnp.concatenate(sums, axis=1)


def own_slope_kernel(meta, offsets, bins, att, skip, edge, filt, asked, sums, slopes, ext):
    half = skip.shape[2]
    tall = ext.shape[1]
    width = ext.shape[2]

    @pl.loop(0, half // width)
    def _(part):
        cols = pl.ds(pl.multiple_of(part * width, width), width)
        slab_sums(att, skip, edge, edge, ext, cols)
        taps = taps_of(filt, cols)
        for s in range(2):
            field = ext[s]
            before, after = around(field)
            slopes[s, :, cols] = slope_of(taps[0] * before + taps[1] * field + taps[2] * after)
            sums[s, :, cols] = field.astype(BF)
            asked[s * 16 : s * 16 + 16, cols] = asked_rows(
                meta, offsets, bins, s, field, taps, tall
            )


def own_slopes(meta, offsets, bins, attention, skip, edge, filt):
    seqs, rows, wide = skip.shape
    _, short, half = attention.shape
    tall = rows + 2 * PAD

    def whole(*shape):
        return pl.BlockSpec(shape, lambda i, m, o, b: (0,) * len(shape))

    def mine(*shape):
        return pl.BlockSpec(shape, lambda i, m, o, b: (0,) * (len(shape) - 1) + (m[0],))

    return pl.pallas_call(
        own_slope_kernel,
        grid_spec=pltpu.PrefetchScalarGridSpec(
            num_scalar_prefetch=3,
            grid=(1,),
            in_specs=[
                pl.BlockSpec((2, short, half), lambda i, m, o, b: (m[0], 0, 0)),
                mine(2, rows, half),
                mine(16, half),
                mine(3, half),
            ],
            out_specs=[whole(32, half), whole(2, tall, half), whole(2, tall, half)],
            scratch_shapes=[pltpu.VMEM((2, tall, 256), F32)],
        ),
        out_shape=[
            jax.ShapeDtypeStruct((32, half), BF),
            jax.ShapeDtypeStruct((2, tall, half), BF),
            jax.ShapeDtypeStruct((2, tall, half), F32),
        ],
        compiler_params=params(),
        cost_estimate=cost(3 * 10**9, 10**6),
        name="own_slopes",
    )(meta, offsets, bins, attention, skip, edge, filt)


def own_kernel(
    slabs, meta, offsets, sums, slopes, rims, prev_far, cot_far, weight_far, filt,
    moved, terms, skip_grad, att_grad, pair, prev, cot, weight, sems,
):
    copies = [
        pltpu.make_async_copy(prev_far, prev, sems.at[0]),
        pltpu.make_async_copy(cot_far, cot, sems.at[1]),
        pltpu.make_async_copy(weight_far, weight, sems.at[2]),
    ]
    for copy in copies:
        copy.start()
    half = sums.shape[2]
    tall = sums.shape[1]
    rows = tall - 2 * PAD
    wide = cot.shape[2]
    row, col = grid_of(tall, rows)
    last = meta[1] == slabs - 1
    copies[0].wait()
    copies[1].wait()
    for s in range(2):
        at = row - PAD
        fits = (at >= -1) & (at < jnp.where(last, rows, rows + 1))
        source = jnp.where(fits, at - offsets[s], -4096)
        older = picks(col == source + rows)
        newer = picks(col == source)
        place = lax.broadcasted_iota(jnp.int32, (PAD, 512), 0)
        top = (place == PAD - 1) & (offsets[s] == rows)
        bottom = (place == 0) & (offsets[s] == 0) & jnp.logical_not(last)
        for part in range(0, wide, 512):
            cols = slice(part, part + 512)
            found = dot(older, prev[s, :, cols]) + dot(newer, cot[s, :, cols])
            ends = rims[:, cols].astype(F32)
            above = ends[s * 8 + 4 : s * 8 + 5]
            below = ends[s * 8 + 3 : s * 8 + 4]
            found = jnp.concatenate(
                [
                    found[:PAD] + jnp.where(top, above, 0.0),
                    found[PAD : PAD + rows],
                    found[PAD + rows :] + jnp.where(bottom, below, 0.0),
                ]
            )
            moved[s, :, cols] = found.astype(BF)
    copies[2].wait()
    width = 2 * LANES
    first = meta[0] * half

    @pl.loop(0, half // width)
    def _(part):
        begin = pl.multiple_of(part * width, width)
        cols = pl.ds(begin, width)
        taps = taps_of(filt, cols)
        piece = weight[pl.ds(begin, width), :]
        total_terms = [0.0, 0.0, 0.0]
        there = pl.ds(pl.multiple_of(first + begin, width), width)
        for s in range(2):
            conv = (dot_rows(moved[s], piece) * slopes[s, :, cols]).astype(BF).astype(F32)
            got = tap_sums(conv, sums[s, :, cols].astype(F32), rows)
            total_terms = [a + b for a, b in zip(total_terms, got)]
            direct = moved[s, :, there].astype(F32)[PAD : PAD + rows]
            total, pairs = grads(conv, direct, taps, rows, pair)
            skip_grad[s, :, cols] = total.astype(BF)
            att_grad[s, :, cols] = pairs.astype(BF)
        for k in range(3):
            terms[k : k + 1, cols] = total_terms[k]


def own_half(meta, offsets, sums, slopes, edge, prev, cot, weight, filt, slabs):
    seqs, rows, wide = cot.shape
    _, tall, half = sums.shape
    short = rows // 2

    def whole(*shape):
        return pl.BlockSpec(shape, lambda i, m, o: (0,) * len(shape))

    def mine(*shape):
        return pl.BlockSpec(shape, lambda i, m, o: (0,) * (len(shape) - 1) + (m[0],))

    anywhere = pl.BlockSpec(memory_space=pl.ANY)
    return pl.pallas_call(
        functools.partial(own_kernel, slabs),
        grid_spec=pltpu.PrefetchScalarGridSpec(
            num_scalar_prefetch=2,
            grid=(1,),
            in_specs=[
                whole(2, tall, half),
                whole(2, tall, half),
                whole(16, wide),
                anywhere,
                anywhere,
                anywhere,
                mine(3, half),
            ],
            out_specs=[
                whole(2, tall, wide),
                whole(3, half),
                mine(2, rows, half),
                mine(2, short, half),
            ],
            scratch_shapes=[
                pltpu.VMEM((2, rows, LANES), F32),
                pltpu.VMEM((2, rows, wide), BF),
                pltpu.VMEM((2, rows, wide), BF),
                pltpu.VMEM((half, wide), BF),
                pltpu.SemaphoreType.DMA((3,)),
            ],
        ),
        out_shape=[
            jax.ShapeDtypeStruct((2, tall, wide), BF),
            jax.ShapeDtypeStruct((3, half), F32),
            jax.ShapeDtypeStruct((2, rows, wide), BF),
            jax.ShapeDtypeStruct((2, short, wide), BF),
        ],
        compiler_params=params(),
        cost_estimate=cost(1, 1),
        name="own_half",
    )(meta, offsets, sums, slopes, edge, prev, cot, weight, filt)


def slope_kernel(
    meta, offsets, bins, att, skip, edge, twin, filt, asked, sums, slopes, mine, shown, ext
):
    rows = skip.shape[1]
    tall = rows + 2 * PAD
    half = skip.shape[2]
    width = ext.shape[2]
    there = (1 - meta[0]) * half
    row, col = grid_of(16, 32)
    at, base = row & 7, (row >> 3) * 16
    kept = picks((at < 4) & (col == base + at + jnp.where(at < 2, 0, 2)))
    told = picks((at < 4) & (col == base + at + jnp.where(at < 2, 2, 4)))
    here = pl.ds(pl.multiple_of(meta[0] * half, half), half)
    mine[:, here] = dot(kept, asked[...]).astype(BF)
    shown[:, here] = dot(told, asked[...]).astype(BF)

    @pl.loop(0, half // width)
    def _(part):
        begin = pl.multiple_of(part * width, width)
        cols = pl.ds(begin, width)
        slab_sums(att, skip, edge, twin, ext, cols)
        taps = taps_of(filt, cols)
        got = []
        for s in range(2):
            field = ext[s]
            before, after = around(field)
            slopes[s, :, cols] = slope_of(taps[0] * before + taps[1] * field + taps[2] * after)
            sums[s, :, cols] = field.astype(BF)
            got.append(asked_rows(meta, offsets, bins, s, field, taps, tall))
        got = jnp.concatenate(got)
        place = pl.ds(pl.multiple_of(there + begin, width), width)
        mine[:, place] = dot(kept, got).astype(BF)
        shown[:, place] = dot(told, got).astype(BF)


def other_slopes(meta, offsets, bins, shipped, skip, edge, twin, filt, asked):
    seqs, rows, wide = skip.shape
    _, packed_rows, half = shipped.shape
    tall = rows + 2 * PAD

    def whole(*shape):
        return pl.BlockSpec(shape, lambda i, m, o, b: (0,) * len(shape))

    def other(*shape):
        return pl.BlockSpec(shape, lambda i, m, o, b: (0,) * (len(shape) - 1) + (1 - m[0],))

    return pl.pallas_call(
        slope_kernel,
        grid_spec=pltpu.PrefetchScalarGridSpec(
            num_scalar_prefetch=3,
            grid=(1,),
            in_specs=[
                whole(2, packed_rows, half),
                other(2, rows, half),
                other(16, half),
                pl.BlockSpec((16, half), lambda i, m, o, b: (0, m[0])),
                other(3, half),
                whole(32, half),
            ],
            out_specs=[whole(2, tall, half), whole(2, tall, half), whole(16, wide), whole(16, wide)],
            scratch_shapes=[pltpu.VMEM((2, tall, 256), F32)],
        ),
        out_shape=[
            jax.ShapeDtypeStruct((2, tall, half), BF),
            jax.ShapeDtypeStruct((2, tall, half), F32),
            jax.ShapeDtypeStruct((16, wide), BF),
            jax.ShapeDtypeStruct((16, wide), BF),
        ],
        compiler_params=params(),
        cost_estimate=cost(3 * 10**9, 10**6),
        name="other_slopes",
    )(meta, offsets, bins, shipped, skip, edge, twin, filt, asked)


def spots(meta, tile):
    core, block = meta[1] & 1, (meta[1] >> 1) & 3
    return [
        (pl.multiple_of(row * tile, tile), pl.multiple_of((block ^ k) * tile, tile))
        for row in (core, 1 - core)
        for k in range(4)
    ]


def terms_kernel(meta, moved, sums, slopes, own_terms, *refs):
    pieces, (convs, terms, full, sems) = refs[:8], refs[8:]
    half = sums.shape[2]
    tall = sums.shape[1]
    rows = tall - 2 * PAD
    there = (1 - meta[0]) * half
    tile = pieces[0].shape[0]
    copies = []
    for k, (down, over) in enumerate(spots(meta, tile)):
        copies.append(
            pltpu.make_async_copy(
                pieces[k], full.at[pl.ds(down, tile), pl.ds(over, tile)], sems.at[k]
            )
        )
        copies[-1].start()
    terms[:, pl.ds(pl.multiple_of(meta[0] * half, half), half)] = own_terms[...]
    for copy in copies:
        copy.wait()
    width = 2 * LANES
    for begin in range(0, half, width):
        cols = slice(begin, begin + width)
        total = [0.0, 0.0, 0.0]
        for s in range(2):
            grad = dot_rows(moved[s], full[cols, :])
            conv = (grad * slopes[s, :, cols]).astype(BF)
            convs[s, :, cols] = conv
            got = tap_sums(conv.astype(F32), sums[s, :, cols].astype(F32), rows)
            total = [a + b for a, b in zip(total, got)]
        place = pl.ds(pl.multiple_of(there + begin, width), width)
        for k in range(3):
            terms[k : k + 1, place] = total[k]


def other_terms(meta, moved, sums, slopes, own_terms, pieces):
    _, tall, wide = moved.shape
    half = sums.shape[2]

    def whole(*shape):
        return pl.BlockSpec(shape, lambda i, m: (0,) * len(shape))

    return pl.pallas_call(
        terms_kernel,
        grid_spec=pltpu.PrefetchScalarGridSpec(
            num_scalar_prefetch=1,
            grid=(1,),
            in_specs=[
                whole(2, tall, wide),
                whole(2, tall, half),
                whole(2, tall, half),
                whole(3, half),
            ]
            + [pl.BlockSpec(memory_space=pl.ANY)] * 8,
            out_specs=[whole(2, tall, half), whole(3, wide)],
            scratch_shapes=[pltpu.VMEM((half, wide), BF), pltpu.SemaphoreType.DMA((8,))],
        ),
        out_shape=[
            jax.ShapeDtypeStruct((2, tall, half), BF),
            jax.ShapeDtypeStruct((3, wide), F32),
        ],
        compiler_params=params(),
        cost_estimate=cost(2 * 2 * tall * half * wide, 6 * 1024 * 1024),
        name="other_terms",
    )(meta, moved, sums, slopes, own_terms, *pieces)


def grads_kernel(meta, moved, convs, filt, old_skip, old_att, skip_grad, att_grad, pair):
    half = convs.shape[2]
    rows = convs.shape[1] - 2 * PAD
    width = 2 * LANES

    @pl.loop(0, half // width)
    def _(part):
        cols = pl.ds(pl.multiple_of(part * width, width), width)
        taps = taps_of(filt, cols)
        for s in range(2):
            direct = moved[s, :, cols].astype(F32)[PAD : PAD + rows]
            total, pairs = grads(convs[s, :, cols].astype(F32), direct, taps, rows, pair)
            skip_grad[s, :, cols] = total.astype(BF)
            att_grad[s, :, cols] = pairs.astype(BF)


def other_grads(meta, moved, convs, filt, skip_grad, att_grad):
    _, tall, wide = moved.shape
    half = convs.shape[2]
    rows = tall - 2 * PAD

    def whole(*shape):
        return pl.BlockSpec(shape, lambda i, m: (0,) * len(shape))

    def other(*shape):
        return pl.BlockSpec(shape, lambda i, m: (0,) * (len(shape) - 1) + (1 - m[0],))

    return pl.pallas_call(
        grads_kernel,
        grid_spec=pltpu.PrefetchScalarGridSpec(
            num_scalar_prefetch=1,
            grid=(1,),
            in_specs=[other(2, tall, half), whole(2, tall, half), other(3, half)]
            + [pl.BlockSpec(memory_space=pl.ANY)] * 2,
            out_specs=[other(2, rows, half), other(2, rows // 2, half)],
            scratch_shapes=[pltpu.VMEM((2, rows, LANES), F32)],
        ),
        out_shape=[
            jax.ShapeDtypeStruct((2, rows, wide), BF),
            jax.ShapeDtypeStruct((2, rows // 2, wide), BF),
        ],
        input_output_aliases={4: 0, 5: 1},
        compiler_params=params(),
        cost_estimate=cost(2 * tall * half * 20, 4 * 1024 * 1024),
        name="other_grads",
    )(meta, moved, convs, filt, skip_grad, att_grad)


def target_kernel(slabs, meta, mine, got_a, got_b, weight, *refs):
    pieces, (target, total) = refs[:8], refs[8:]
    half = weight.shape[0]
    there = (1 - meta[0]) * half
    tile = pieces[0].shape[0]
    even = (meta[1] & 1) == 0
    got = jnp.where(even, got_a[...].astype(F32), got_b[...].astype(F32))
    got = jnp.where(meta[1] == slabs - 1, 0.0, got)
    mine[...] = (mine[...].astype(F32) + got).astype(BF)
    here = pl.ds(pl.multiple_of(meta[0] * half, half), half)
    total[...] = dot(mine[:, here], weight[...]) + pltpu.roll(mine[...].astype(F32), 12 + 2, 0)
    for k, (down, over) in enumerate(spots(meta, tile)):
        place = pl.ds(pl.multiple_of(there + down, tile), tile)
        total[:, pl.ds(over, tile)] += dot(mine[:, place], pieces[k][...])
    for s in range(2):
        target[s] = total[s * 8 : s * 8 + 2].astype(BF)


def targets(meta, mine, got, weight, pieces, slabs):
    half, wide = weight.shape
    tile = pieces[0].shape[0]

    def whole(*shape):
        return pl.BlockSpec(shape, lambda i, m: (0,) * len(shape))

    return pl.pallas_call(
        functools.partial(target_kernel, slabs),
        grid_spec=pltpu.PrefetchScalarGridSpec(
            num_scalar_prefetch=1,
            grid=(1,),
            in_specs=[whole(16, wide)] * 3 + [whole(half, wide)]
            + [whole(tile, tile)] * 8,
            out_specs=whole(2, NTD, wide),
            scratch_shapes=[pltpu.VMEM((16, wide), F32)],
        ),
        out_shape=jax.ShapeDtypeStruct((2, NTD, wide), BF),
        compiler_params=params(),
        cost_estimate=cost(2 * 16 * wide * wide, 6 * 1024 * 1024),
        name="targets",
    )(meta, mine, *got, weight, *pieces)


def paired(part, axis, bit):
    count = lax.axis_size(axis)
    return lax.ppermute(part, axis, [(i, i ^ bit) for i in range(count)])


def staggered(part, span):
    count = lax.axis_size("seq")
    pairs = []
    for i in range(count):
        by = span if i // span % 2 else -span
        pairs.append((i, (i + by) % count))
    return lax.ppermute(part, "seq", pairs)


def after(value, *others):
    return lax.optimization_barrier((value,) + others)[0]


def crossed(part, seq_bit, head_bit):
    slabs, heads = lax.axis_size("seq"), lax.axis_size("head")
    pairs = [
        (i * heads + j, (i ^ seq_bit) * heads + (j ^ head_bit))
        for i in range(slabs)
        for j in range(heads)
    ]
    return lax.ppermute(part, ("seq", "head"), pairs)


def joined(total, one, two):
    both = (one[0] ^ two[0], one[1] ^ two[1])
    parts = [crossed(total, *bits) for bits in (one, two, both)]
    return (total + parts[0]) + (parts[1] + parts[2])


def fast_shards(
    attention, encoder_skip, depth_filter, point_weight, crop_offset, target_bins, cotangent
):
    head = lax.axis_index("head")
    slab = lax.axis_index("seq")
    slabs = lax.axis_size("seq")
    meta = jnp.stack([head, slab]).astype(jnp.int32)
    tile = 3 * LANES

    edge_a, edge_b, far, first, last_tile, att_out = packed(
        encoder_skip, attention, cotangent, point_weight, tile
    )
    first = paired(first, "head", 1)
    edge_a = paired(edge_a, "seq", 1)
    edge_b = staggered(edge_b, 1)
    far_a = paired(far, "seq", 2)
    far_b = staggered(far, 2)
    prev = passed_along(after(cotangent, edge_a), "seq", 1)
    outer = (slab == 0) | (slab == slabs - 1)
    nothing = jnp.zeros_like(edge_b)
    edge = edge_a + jnp.where(outer, nothing, edge_b)
    twin = paired(edge, "head", 1)
    shipped = paired(after(att_out, edge), "head", 1)
    edge = edge + jnp.where(slab % 4 >= 2, far_a, jnp.where(slab < 2, nothing, far_b))
    asked, own_sums, own_slope = own_slopes(
        meta, crop_offset, target_bins, attention, encoder_skip, edge, depth_filter
    )
    ready = after(first, asked)
    second = paired(ready, "seq", 2)
    third = paired(ready, "seq", 4)
    fourth = paired(last_tile, "head", 1)
    sums, slopes, mine, shown = other_slopes(
        meta, crop_offset, target_bins, shipped, encoder_skip, edge, twin, depth_filter, asked
    )
    got = [paired(shown, "seq", 1), staggered(shown, 1)]
    moved, own_terms, skip_grad, att_grad = own_half(
        after(meta, shown), crop_offset, own_sums, own_slope, edge, prev, cotangent, point_weight, depth_filter,
        slabs,
    )
    pieces = [first, second, third, fourth]
    pieces = pieces + [paired(after(piece, own_terms), "seq", 1) for piece in pieces]
    convs, terms = other_terms(meta, moved, sums, slopes, own_terms, pieces)
    terms, *got = lax.optimization_barrier((terms, *got))
    total = terms + crossed(terms, 1, 0)
    total = joined(total, (2, 0), (0, 1))
    skip_grad, attention_grad = other_grads(
        meta, moved, convs, depth_filter, skip_grad, att_grad
    )
    target_rows = targets(meta, mine, got, point_weight, pieces, slabs)
    total, skip_grad, attention_grad = lax.optimization_barrier(
        (total, skip_grad, attention_grad)
    )
    if slabs == 16:
        total = joined(total, (4, 0), (8, 0))
    else:
        step = 4
        while step < slabs:
            total = total + crossed(total, step, 0)
            step *= 2
    count = encoder_skip.shape[0] * lax.axis_size("head") * encoder_skip.shape[1] * slabs
    return (target_rows, attention_grad, skip_grad, total * (1.0 / math.sqrt(count)))


def shards(*args):
    attention, encoder_skip, point_weight = args[0], args[1], args[3]
    fits = (
        lax.axis_size("head") == 2
        and lax.axis_size("seq") in (8, 16, 32)
        and encoder_skip.shape[:2] == (2, 128)
        and point_weight.shape[0] == 6 * LANES
        and attention.shape[1] == 64
    )
    return fast_shards(*args) if fits else plain_shards(*args)


def solution(mesh):
    in_specs = (
        P(None, "seq", "head"),
        P("head", "seq", None),
        P(),
        P("head", None),
        P("head"),
        P("head", None),
        P("head", "seq", None),
    )
    out_specs = (P("head", "seq", None), P("head", "seq", None), P("head", "seq", None), P())
    return jax.shard_map(shards, mesh=mesh, in_specs=in_specs, out_specs=out_specs, check_vma=False)
def solution(mesh):
    in_specs = (
        P(None, "seq", "head"),
        P("head", "seq", None),
        P(),
        P("head", None),
        P("head"),
        P("head", None),
        P("head", "seq", None),
    )
    out_specs = (P("head", "seq", None), P("head", "seq", None), P("head", "seq", None), P())
    return jax.shard_map(shards, mesh=mesh, in_specs=in_specs, out_specs=out_specs, check_vma=False)
```

```python
import functools
import math

import jax
import jax.numpy as jnp
from jax import lax
from jax.experimental import pallas as pl
from jax.experimental.pallas import tpu as pltpu
from jax.sharding import PartitionSpec as P

NTD = 2


def extended(shard, sides, width):
    for axis, dim in sides:
        count, length = (lax.axis_size(axis), shard.shape[dim])
        up = [(i, (i + 1) % count) for i in range(count - 1)]
        down = [(j, i) for i, j in up]
        last = lax.slice_in_dim(shard, length - width, length, axis=dim)
        initial = lax.slice_in_dim(shard, 0, width, axis=dim)
        before = lax.ppermute(last, axis, up)
        after = lax.ppermute(initial, axis, down)
        shard = jnp.concatenate([before, shard, after], axis=dim)
    return shard


def passed_along(shard, axis, by):
    count = lax.axis_size(axis)
    pairs = [(i, i + by) for i in range(count) if 0 <= i + by < count]
    return lax.ppermute(shard, axis, pairs)


def gelu_slope(values):
    return (
        0.5 * (1.0 + lax.erf(values * 0.7071067811865476))
        + values * jnp.exp(-0.5 * values * values) * 0.3989422804014327
    )


def with_rims(field):
    return extended(field, (("seq", 1),), 1)


def one_hot(places, length):
    return (places[:, :, None] == jnp.arange(length, dtype=jnp.int32)[None, None, :]).astype(
        jnp.bfloat16
    )


def core_swap(part):
    count = lax.axis_size("seq")
    return lax.ppermute(part, "seq", [(i, i ^ 1) for i in range(count)])


def gathered_weight(rows):
    heads = lax.axis_size("head")
    here = lax.axis_index("head")
    core = lax.axis_index("seq") % 2
    half = rows.shape[0] // 2
    mine = lax.dynamic_slice_in_dim(rows, core * half, half, 0)
    blocks = [(0, rows)]
    for step in range(1, heads):
        pairs = [(i, (i + step) % heads) for i in range(heads)]
        got = lax.ppermute(mine, "head", pairs)
        twin = core_swap(got)
        low = jnp.where(core == 0, got, twin)
        high = jnp.where(core == 0, twin, got)
        blocks.append((step, jnp.concatenate([low, high], axis=0)))
    full = jnp.zeros((heads * rows.shape[0], rows.shape[1]), rows.dtype)
    for step, block in blocks:
        place = (here - step) % heads
        full = lax.dynamic_update_slice_in_dim(full, block, place * rows.shape[0], 0)
    return full


def butterfly(total, axis):
    count = lax.axis_size(axis)
    if count & (count - 1):
        return lax.psum(total, axis)
    step = 1
    while step < count:
        total = total + lax.ppermute(total, axis, [(i, i ^ step) for i in range(count)])
        step *= 2
    return total


def plain_shards(
    attention, encoder_skip, depth_filter, point_weight, crop_offset, target_bins, cotangent
):
    slab_input = lax.all_to_all(attention, "head", split_axis=0, concat_axis=2, tiled=True)
    local_seqs = encoder_skip.shape[0]
    slab_rows = encoder_skip.shape[1]
    channels = encoder_skip.shape[2]
    summed = (
        jnp.repeat(slab_input, 2, axis=1).astype(jnp.float32) + encoder_skip.astype(jnp.float32)
    ).astype(jnp.bfloat16)
    padded = with_rims(summed)
    filtered = (
        depth_filter[0] * padded[:, :-2]
        + depth_filter[1] * padded[:, 1:-1]
        + depth_filter[2] * padded[:, 2:]
    )
    activated = jax.nn.gelu(filtered, approximate=False).astype(jnp.bfloat16)
    flat_act = activated.reshape(local_seqs * slab_rows, channels)
    full_weight = gathered_weight(point_weight)
    mixed_rows = jnp.dot(flat_act, full_weight, preferred_element_type=jnp.float32)
    block_out = (
        summed.astype(jnp.float32) + mixed_rows.reshape(local_seqs, slab_rows, channels)
    ).astype(jnp.bfloat16)
    slab_index = lax.axis_index("seq")
    bins = jnp.concatenate(
        [jnp.zeros_like(target_bins[:, :NTD]), target_bins], axis=1
    )
    asked = lax.dynamic_slice_in_dim(bins, slab_index * NTD, 2 * NTD, 1) + crop_offset[:, None]
    back = jnp.where(jnp.arange(2 * NTD, dtype=jnp.int32) < NTD, slab_rows, 0)
    asked = asked - back[None, :]
    picked = jnp.einsum(
        "sjr,srd->sjd",
        one_hot(asked, slab_rows),
        block_out,
        preferred_element_type=jnp.float32,
    ).astype(jnp.bfloat16)
    from_next = passed_along(picked[:, :NTD], "seq", -1)
    target_rows = picked[:, NTD:] + from_next
    prev_cot = passed_along(cotangent, "seq", 1)
    cot_pair = jnp.concatenate([prev_cot, cotangent], axis=1)

    def crop_back(cot_block, shift_by):
        return lax.dynamic_slice_in_dim(cot_block, slab_rows - shift_by, slab_rows, 0)

    grad_out = jax.vmap(crop_back)(cot_pair, crop_offset)
    flat_grad = grad_out.reshape(local_seqs * slab_rows, channels)
    grad_act = lax.dot_general(
        flat_grad, full_weight, (((1,), (1,)), ((), ())), preferred_element_type=jnp.float32
    )
    grad_conv = (grad_act.reshape(local_seqs, slab_rows, channels) * gelu_slope(filtered)).astype(
        jnp.bfloat16
    )
    grad_padded = with_rims(grad_conv)
    grad_sum = (
        grad_out.astype(jnp.float32)
        + depth_filter[0] * grad_padded[:, 2:]
        + depth_filter[1] * grad_padded[:, 1:-1]
        + depth_filter[2] * grad_padded[:, :-2]
    )
    skip_grad = grad_sum.astype(jnp.bfloat16)
    attention_grad = (
        grad_sum.reshape(local_seqs, slab_rows // 2, 2, channels).sum(axis=2).astype(jnp.bfloat16)
    )
    filter_terms = jnp.stack(
        [
            jnp.einsum(
                "srd,srd->d", grad_conv, padded[:, 0:slab_rows], preferred_element_type=jnp.float32
            ),
            jnp.einsum(
                "srd,srd->d",
                grad_conv,
                padded[:, 1 : slab_rows + 1],
                preferred_element_type=jnp.float32,
            ),
            jnp.einsum(
                "srd,srd->d",
                grad_conv,
                padded[:, 2 : slab_rows + 2],
                preferred_element_type=jnp.float32,
            ),
        ]
    )
    filter_sum = butterfly(butterfly(filter_terms, "seq"), "head")
    row_count = local_seqs * lax.axis_size("head") * slab_rows * lax.axis_size("seq")
    filter_grad = filter_sum * (1.0 / math.sqrt(row_count))
    return (target_rows, attention_grad, skip_grad, filter_grad)


import functools
import math

import jax
import jax.numpy as jnp
from jax import lax
from jax.experimental import pallas as pl
from jax.experimental.pallas import tpu as pltpu
from jax.sharding import PartitionSpec as P

NTD = 2


def extended(shard, sides, width):
    for axis, dim in sides:
        count, length = (lax.axis_size(axis), shard.shape[dim])
        up = [(i, (i + 1) % count) for i in range(count - 1)]
        down = [(j, i) for i, j in up]
        last = lax.slice_in_dim(shard, length - width, length, axis=dim)
        initial = lax.slice_in_dim(shard, 0, width, axis=dim)
        before = lax.ppermute(last, axis, up)
        after = lax.ppermute(initial, axis, down)
        shard = jnp.concatenate([before, shard, after], axis=dim)
    return shard


def passed_along(shard, axis, by):
    count = lax.axis_size(axis)
    pairs = [(i, i + by) for i in range(count) if 0 <= i + by < count]
    return lax.ppermute(shard, axis, pairs)


def gelu_slope(values):
    return (
        0.5 * (1.0 + lax.erf(values * 0.7071067811865476))
        + values * jnp.exp(-0.5 * values * values) * 0.3989422804014327
    )


def with_rims(field):
    return extended(field, (("seq", 1),), 1)


def one_hot(places, length):
    return (places[:, :, None] == jnp.arange(length, dtype=jnp.int32)[None, None, :]).astype(
        jnp.bfloat16
    )


def core_swap(part):
    count = lax.axis_size("seq")
    return lax.ppermute(part, "seq", [(i, i ^ 1) for i in range(count)])


def gathered_weight(rows):
    heads = lax.axis_size("head")
    here = lax.axis_index("head")
    core = lax.axis_index("seq") % 2
    half = rows.shape[0] // 2
    mine = lax.dynamic_slice_in_dim(rows, core * half, half, 0)
    blocks = [(0, rows)]
    for step in range(1, heads):
        pairs = [(i, (i + step) % heads) for i in range(heads)]
        got = lax.ppermute(mine, "head", pairs)
        twin = core_swap(got)
        low = jnp.where(core == 0, got, twin)
        high = jnp.where(core == 0, twin, got)
        blocks.append((step, jnp.concatenate([low, high], axis=0)))
    full = jnp.zeros((heads * rows.shape[0], rows.shape[1]), rows.dtype)
    for step, block in blocks:
        place = (here - step) % heads
        full = lax.dynamic_update_slice_in_dim(full, block, place * rows.shape[0], 0)
    return full


def butterfly(total, axis):
    count = lax.axis_size(axis)
    if count & (count - 1):
        return lax.psum(total, axis)
    step = 1
    while step < count:
        total = total + lax.ppermute(total, axis, [(i, i ^ step) for i in range(count)])
        step *= 2
    return total


def plain_shards(
    attention, encoder_skip, depth_filter, point_weight, crop_offset, target_bins, cotangent
):
    slab_input = lax.all_to_all(attention, "head", split_axis=0, concat_axis=2, tiled=True)
    local_seqs = encoder_skip.shape[0]
    slab_rows = encoder_skip.shape[1]
    channels = encoder_skip.shape[2]
    summed = (
        jnp.repeat(slab_input, 2, axis=1).astype(jnp.float32) + encoder_skip.astype(jnp.float32)
    ).astype(jnp.bfloat16)
    padded = with_rims(summed)
    filtered = (
        depth_filter[0] * padded[:, :-2]
        + depth_filter[1] * padded[:, 1:-1]
        + depth_filter[2] * padded[:, 2:]
    )
    activated = jax.nn.gelu(filtered, approximate=False).astype(jnp.bfloat16)
    flat_act = activated.reshape(local_seqs * slab_rows, channels)
    full_weight = gathered_weight(point_weight)
    mixed_rows = jnp.dot(flat_act, full_weight, preferred_element_type=jnp.float32)
    block_out = (
        summed.astype(jnp.float32) + mixed_rows.reshape(local_seqs, slab_rows, channels)
    ).astype(jnp.bfloat16)
    slab_index = lax.axis_index("seq")
    bins = jnp.concatenate(
        [jnp.zeros_like(target_bins[:, :NTD]), target_bins], axis=1
    )
    asked = lax.dynamic_slice_in_dim(bins, slab_index * NTD, 2 * NTD, 1) + crop_offset[:, None]
    back = jnp.where(jnp.arange(2 * NTD, dtype=jnp.int32) < NTD, slab_rows, 0)
    asked = asked - back[None, :]
    picked = jnp.einsum(
        "sjr,srd->sjd",
        one_hot(asked, slab_rows),
        block_out,
        preferred_element_type=jnp.float32,
    ).astype(jnp.bfloat16)
    from_next = passed_along(picked[:, :NTD], "seq", -1)
    target_rows = picked[:, NTD:] + from_next
    prev_cot = passed_along(cotangent, "seq", 1)
    cot_pair = jnp.concatenate([prev_cot, cotangent], axis=1)

    def crop_back(cot_block, shift_by):
        return lax.dynamic_slice_in_dim(cot_block, slab_rows - shift_by, slab_rows, 0)

    grad_out = jax.vmap(crop_back)(cot_pair, crop_offset)
    flat_grad = grad_out.reshape(local_seqs * slab_rows, channels)
    grad_act = lax.dot_general(
        flat_grad, full_weight, (((1,), (1,)), ((), ())), preferred_element_type=jnp.float32
    )
    grad_conv = (grad_act.reshape(local_seqs, slab_rows, channels) * gelu_slope(filtered)).astype(
        jnp.bfloat16
    )
    grad_padded = with_rims(grad_conv)
    grad_sum = (
        grad_out.astype(jnp.float32)
        + depth_filter[0] * grad_padded[:, 2:]
        + depth_filter[1] * grad_padded[:, 1:-1]
        + depth_filter[2] * grad_padded[:, :-2]
    )
    skip_grad = grad_sum.astype(jnp.bfloat16)
    attention_grad = (
        grad_sum.reshape(local_seqs, slab_rows // 2, 2, channels).sum(axis=2).astype(jnp.bfloat16)
    )
    filter_terms = jnp.stack(
        [
            jnp.einsum(
                "srd,srd->d", grad_conv, padded[:, 0:slab_rows], preferred_element_type=jnp.float32
            ),
            jnp.einsum(
                "srd,srd->d",
                grad_conv,
                padded[:, 1 : slab_rows + 1],
                preferred_element_type=jnp.float32,
            ),
            jnp.einsum(
                "srd,srd->d",
                grad_conv,
                padded[:, 2 : slab_rows + 2],
                preferred_element_type=jnp.float32,
            ),
        ]
    )
    filter_sum = butterfly(butterfly(filter_terms, "seq"), "head")
    row_count = local_seqs * lax.axis_size("head") * slab_rows * lax.axis_size("seq")
    filter_grad = filter_sum * (1.0 / math.sqrt(row_count))
    return (target_rows, attention_grad, skip_grad, filter_grad)


import functools
import math

import jax
import jax.numpy as jnp
from jax import lax
from jax.experimental import pallas as pl
from jax.experimental.pallas import tpu as pltpu
from jax.sharding import PartitionSpec as P

NTD = 2


def extended(shard, sides, width):
    for axis, dim in sides:
        count, length = (lax.axis_size(axis), shard.shape[dim])
        up = [(i, (i + 1) % count) for i in range(count - 1)]
        down = [(j, i) for i, j in up]
        last = lax.slice_in_dim(shard, length - width, length, axis=dim)
        initial = lax.slice_in_dim(shard, 0, width, axis=dim)
        before = lax.ppermute(last, axis, up)
        after = lax.ppermute(initial, axis, down)
        shard = jnp.concatenate([before, shard, after], axis=dim)
    return shard


def passed_along(shard, axis, by):
    count = lax.axis_size(axis)
    pairs = [(i, i + by) for i in range(count) if 0 <= i + by < count]
    return lax.ppermute(shard, axis, pairs)


def gelu_slope(values):
    return (
        0.5 * (1.0 + lax.erf(values * 0.7071067811865476))
        + values * jnp.exp(-0.5 * values * values) * 0.3989422804014327
    )


def with_rims(field):
    return extended(field, (("seq", 1),), 1)


def one_hot(places, length):
    return (places[:, :, None] == jnp.arange(length, dtype=jnp.int32)[None, None, :]).astype(
        jnp.bfloat16
    )


def core_swap(part):
    count = lax.axis_size("seq")
    return lax.ppermute(part, "seq", [(i, i ^ 1) for i in range(count)])


def gathered_weight(rows):
    heads = lax.axis_size("head")
    here = lax.axis_index("head")
    core = lax.axis_index("seq") % 2
    half = rows.shape[0] // 2
    mine = lax.dynamic_slice_in_dim(rows, core * half, half, 0)
    blocks = [(0, rows)]
    for step in range(1, heads):
        pairs = [(i, (i + step) % heads) for i in range(heads)]
        got = lax.ppermute(mine, "head", pairs)
        twin = core_swap(got)
        low = jnp.where(core == 0, got, twin)
        high = jnp.where(core == 0, twin, got)
        blocks.append((step, jnp.concatenate([low, high], axis=0)))
    full = jnp.zeros((heads * rows.shape[0], rows.shape[1]), rows.dtype)
    for step, block in blocks:
        place = (here - step) % heads
        full = lax.dynamic_update_slice_in_dim(full, block, place * rows.shape[0], 0)
    return full


def butterfly(total, axis):
    count = lax.axis_size(axis)
    if count & (count - 1):
        return lax.psum(total, axis)
    step = 1
    while step < count:
        total = total + lax.ppermute(total, axis, [(i, i ^ step) for i in range(count)])
        step *= 2
    return total


def plain_shards(
    attention, encoder_skip, depth_filter, point_weight, crop_offset, target_bins, cotangent
):
    slab_input = lax.all_to_all(attention, "head", split_axis=0, concat_axis=2, tiled=True)
    local_seqs = encoder_skip.shape[0]
    slab_rows = encoder_skip.shape[1]
    channels = encoder_skip.shape[2]
    summed = (
        jnp.repeat(slab_input, 2, axis=1).astype(jnp.float32) + encoder_skip.astype(jnp.float32)
    ).astype(jnp.bfloat16)
    padded = with_rims(summed)
    filtered = (
        depth_filter[0] * padded[:, :-2]
        + depth_filter[1] * padded[:, 1:-1]
        + depth_filter[2] * padded[:, 2:]
    )
    activated = jax.nn.gelu(filtered, approximate=False).astype(jnp.bfloat16)
    flat_act = activated.reshape(local_seqs * slab_rows, channels)
    full_weight = gathered_weight(point_weight)
    mixed_rows = jnp.dot(flat_act, full_weight, preferred_element_type=jnp.float32)
    block_out = (
        summed.astype(jnp.float32) + mixed_rows.reshape(local_seqs, slab_rows, channels)
    ).astype(jnp.bfloat16)
    slab_index = lax.axis_index("seq")
    bins = jnp.concatenate(
        [jnp.zeros_like(target_bins[:, :NTD]), target_bins], axis=1
    )
    asked = lax.dynamic_slice_in_dim(bins, slab_index * NTD, 2 * NTD, 1) + crop_offset[:, None]
    back = jnp.where(jnp.arange(2 * NTD, dtype=jnp.int32) < NTD, slab_rows, 0)
    asked = asked - back[None, :]
    picked = jnp.einsum(
        "sjr,srd->sjd",
        one_hot(asked, slab_rows),
        block_out,
        preferred_element_type=jnp.float32,
    ).astype(jnp.bfloat16)
    from_next = passed_along(picked[:, :NTD], "seq", -1)
    target_rows = picked[:, NTD:] + from_next
    prev_cot = passed_along(cotangent, "seq", 1)
    cot_pair = jnp.concatenate([prev_cot, cotangent], axis=1)

    def crop_back(cot_block, shift_by):
        return lax.dynamic_slice_in_dim(cot_block, slab_rows - shift_by, slab_rows, 0)

    grad_out = jax.vmap(crop_back)(cot_pair, crop_offset)
    flat_grad = grad_out.reshape(local_seqs * slab_rows, channels)
    grad_act = lax.dot_general(
        flat_grad, full_weight, (((1,), (1,)), ((), ())), preferred_element_type=jnp.float32
    )
    grad_conv = (grad_act.reshape(local_seqs, slab_rows, channels) * gelu_slope(filtered)).astype(
        jnp.bfloat16
    )
    grad_padded = with_rims(grad_conv)
    grad_sum = (
        grad_out.astype(jnp.float32)
        + depth_filter[0] * grad_padded[:, 2:]
        + depth_filter[1] * grad_padded[:, 1:-1]
        + depth_filter[2] * grad_padded[:, :-2]
    )
    skip_grad = grad_sum.astype(jnp.bfloat16)
    attention_grad = (
        grad_sum.reshape(local_seqs, slab_rows // 2, 2, channels).sum(axis=2).astype(jnp.bfloat16)
    )
    filter_terms = jnp.stack(
        [
            jnp.einsum(
                "srd,srd->d", grad_conv, padded[:, 0:slab_rows], preferred_element_type=jnp.float32
            ),
            jnp.einsum(
                "srd,srd->d",
                grad_conv,
                padded[:, 1 : slab_rows + 1],
                preferred_element_type=jnp.float32,
            ),
            jnp.einsum(
                "srd,srd->d",
                grad_conv,
                padded[:, 2 : slab_rows + 2],
                preferred_element_type=jnp.float32,
            ),
        ]
    )
    filter_sum = butterfly(butterfly(filter_terms, "seq"), "head")
    row_count = local_seqs * lax.axis_size("head") * slab_rows * lax.axis_size("seq")
    filter_grad = filter_sum * (1.0 / math.sqrt(row_count))
    return (target_rows, attention_grad, skip_grad, filter_grad)


LANES = 128
PAD = 8
BF = jnp.bfloat16
F32 = jnp.float32


def dot(left, right):
    return lax.dot_general(left, right, (((1,), (0,)), ((), ())), preferred_element_type=F32)


def dot_rows(left, right):
    return lax.dot_general(left, right, (((1,), (1,)), ((), ())), preferred_element_type=F32)


def grid_of(rows, columns):
    return (
        lax.broadcasted_iota(jnp.int32, (rows, columns), 0),
        lax.broadcasted_iota(jnp.int32, (rows, columns), 1),
    )


def picks(match):
    return jnp.where(match, 1.0, 0.0).astype(BF)


def params(mib=20):
    return pltpu.CompilerParams(vmem_limit_bytes=mib * 1024 * 1024)


def cost(flops, moved, special=0):
    return pl.CostEstimate(flops=flops, bytes_accessed=moved, transcendentals=special)


def pack_kernel(
    skip, attention, cotangent, weight, edge_a, edge_b, far, tile_a, tile_b, att_out,
    skip_lo, skip_hi, att_lo, att_hi, cot_lo, cot_hi, sems,
):
    head, slab = lax.axis_index("head"), lax.axis_index("seq")
    tile = tile_a.shape[0]
    core, block = slab & 1, (slab >> 1) & 3
    down = pl.ds(pl.multiple_of(core * tile, tile), tile)

    def piece(which):
        return weight.at[down, pl.ds(pl.multiple_of(which * tile, tile), tile)]

    edges = []
    for source, lo, hi in (
        (skip, skip_lo, skip_hi), (attention, att_lo, att_hi), (cotangent, cot_lo, cot_hi)
    ):
        rows = source.shape[1]
        for part, begin in ((lo, 0), (hi, rows - 16)):
            edges.append(
                pltpu.make_async_copy(source.at[:, pl.ds(begin, 16)], part, sems.at[len(edges)])
            )
    whole = [
        pltpu.make_async_copy(piece(block), tile_a, sems.at[6]),
        pltpu.make_async_copy(piece(3 - block), tile_b, sems.at[7]),
        pltpu.make_async_copy(attention.at[pl.ds(2 - 2 * head, 2)], att_out, sems.at[8]),
    ]
    for copy in edges + whole:
        copy.start()
    for copy in edges:
        copy.wait()
    wide = cot_lo.shape[2]
    at = lax.broadcasted_iota(jnp.int32, (8, wide), 0)
    even = core == 0
    ups, downs, ends = [], [], []
    for s in range(2):
        feats = [jnp.concatenate([part[s], part[2 + s]], axis=1) for part in (att_hi, att_lo)]
        high, low = feats[0].astype(F32)[8:], feats[1].astype(F32)[:8]
        up = jnp.where(at >= 6, skip_hi[s].astype(F32)[8:], 0.0)
        ups.append(jnp.where(at == 5, pltpu.roll(high, 6, 0), up))
        down = jnp.where(at < 2, skip_lo[s].astype(F32)[:8], 0.0)
        down = jnp.where(at == 2, pltpu.roll(low, 2, 0), down)
        downs.append(jnp.where(at == 3, pltpu.roll(cot_lo[s].astype(F32)[:8], 3, 0), down))
        last = pltpu.roll(cot_hi[s].astype(F32)[8:], 5, 0)
        ends.append(jnp.where(at == 4, last, 0.0))
    up, down = jnp.concatenate(ups), jnp.concatenate(downs)
    edge_a[...] = jnp.where(even, up, down).astype(BF)
    edge_b[...] = jnp.where(even, down, up).astype(BF)
    far[...] = jnp.concatenate(ends).astype(BF)
    for copy in whole:
        copy.wait()


def packed(encoder_skip, attention, cotangent, weight, tile):
    seqs, rows, wide = encoder_skip.shape
    count, short, half = attention.shape
    out = jax.ShapeDtypeStruct((16, wide), BF)
    square = jax.ShapeDtypeStruct((tile, tile), BF)
    anywhere = pl.BlockSpec(memory_space=pl.ANY)
    flat = pl.BlockSpec((16, wide), lambda i: (0, 0))
    cut = pl.BlockSpec((tile, tile), lambda i: (0, 0))
    return pl.pallas_call(
        pack_kernel,
        grid=(1,),
        in_specs=[anywhere] * 4,
        out_specs=[flat] * 3 + [cut] * 2 + [pl.BlockSpec((2, short, half), lambda i: (0, 0, 0))],
        out_shape=[out, out, out, square, square, jax.ShapeDtypeStruct((2, short, half), BF)],
        scratch_shapes=[
            pltpu.VMEM((seqs, 16, wide), BF),
            pltpu.VMEM((seqs, 16, wide), BF),
            pltpu.VMEM((count, 16, half), BF),
            pltpu.VMEM((count, 16, half), BF),
            pltpu.VMEM((seqs, 16, wide), BF),
            pltpu.VMEM((seqs, 16, wide), BF),
            pltpu.SemaphoreType.DMA((9,)),
        ],
        compiler_params=params(60),
        name="pack_edges",
    )(encoder_skip, attention, cotangent, weight)


def slab_sums(att, skip, edge, twin, ext, cols):
    width = cols.size
    short = 64
    row, col = grid_of(2 * short, short)
    spread = picks((row >> 1) == col)
    row, col = grid_of(16, 16)
    at, base = row & 7, row & 8
    wanted = ((at >= 6) & (col == base + 5)) | ((at < 2) & (col == base + 2))
    from_att = dot(picks(wanted), twin[:, cols])
    rims = edge[:, cols]
    at = lax.broadcasted_iota(jnp.int32, (16, width), 0) & 7
    rims = (from_att + rims.astype(F32)).astype(BF).astype(F32)
    above = jnp.where(at >= 6, rims, 0.0)
    below = jnp.where(at < 2, rims, 0.0)
    for s in range(2):
        body = dot(spread, att[s, 0:short, cols]) + skip[s, :, cols].astype(F32)
        ext[s, 0:PAD] = above[s * 8 : s * 8 + 8]
        ext[s, PAD : PAD + 2 * short] = body.astype(BF).astype(F32)
        ext[s, PAD + 2 * short : 2 * PAD + 2 * short] = below[s * 8 : s * 8 + 8]


def around(field):
    tall = field.shape[0]
    return pltpu.roll(field, 1, 0), pltpu.roll(field, tall - 1, 0)


def phi_of(values):
    return 0.5 * (1.0 + lax.erf(values * 0.7071067811865476))


def slope_of(values):
    return phi_of(values) + values * jnp.exp(-0.5 * values * values) * 0.3989422804014327


def asked_rows(meta, offsets, bins, s, ext, taps, tall):
    row, col = grid_of(48, tall)
    want = row & 3
    shift = (row >> 4) - 1
    at = jnp.full((48, tall), -4096, jnp.int32)
    slab = meta[1]
    for k in range(4):
        mine = k < NTD
        home = slab if mine else jnp.maximum(slab - 1, 0)
        place = bins[s, home * NTD + (k % NTD)] + offsets[s] - (0 if mine else tall - 2 * PAD)
        fits = (place >= 0) & (place < tall - 2 * PAD)
        at = jnp.where(want == k, jnp.where(fits, place + PAD, -4096), at)
    found = dot(picks((col == at + shift) & ((row & 15) < 8)), ext.astype(BF))
    here = found[16:32]
    value = taps[0] * found[0:16] + taps[1] * here + taps[2] * found[32:48]
    act = value * phi_of(value)
    row = lax.broadcasted_iota(jnp.int32, act.shape, 0)
    return jnp.where(row < 4, act, here).astype(BF)


def taps_of(filt, cols):
    return [filt[k : k + 1, cols] for k in range(3)]


def tap_sums(conv, ext, rows):
    before, after = around(ext)
    body = slice(PAD, PAD + rows)
    mine = conv[body]
    return [
        jnp.sum(mine * other[body], axis=0, keepdims=True) for other in (before, ext, after)
    ]


def grads(conv, direct, taps, rows, pair):
    before, after = around(conv)
    body = slice(PAD, PAD + rows)
    total = direct + taps[0] * after[body] + taps[1] * conv[body] + taps[2] * before[body]
    short = rows // 2
    sums = []
    for k in range(total.shape[1] // LANES):
        pair[k] = total[:, k * LANES : (k + 1) * LANES]
        sums.append(pair[k, pl.ds(0, short, 2), :] + pair[k, pl.ds(1, short, 2), :])
    return total, jnp.concatenate(sums, axis=1)


def own_slope_kernel(meta, offsets, bins, att, skip, edge, filt, asked, sums, slopes, ext):
    half = skip.shape[2]
    tall = ext.shape[1]
    width = ext.shape[2]

    @pl.loop(0, half // width)
    def _(part):
        cols = pl.ds(pl.multiple_of(part * width, width), width)
        slab_sums(att, skip, edge, edge, ext, cols)
        taps = taps_of(filt, cols)
        for s in range(2):
            field = ext[s]
            before, after = around(field)
            slopes[s, :, cols] = slope_of(taps[0] * before + taps[1] * field + taps[2] * after)
            sums[s, :, cols] = field.astype(BF)
            asked[s * 16 : s * 16 + 16, cols] = asked_rows(
                meta, offsets, bins, s, field, taps, tall
            )


def own_slopes(meta, offsets, bins, attention, skip, edge, filt):
    seqs, rows, wide = skip.shape
    _, short, half = attention.shape
    tall = rows + 2 * PAD

    def whole(*shape):
        return pl.BlockSpec(shape, lambda i, m, o, b: (0,) * len(shape))

    def mine(*shape):
        return pl.BlockSpec(shape, lambda i, m, o, b: (0,) * (len(shape) - 1) + (m[0],))

    return pl.pallas_call(
        own_slope_kernel,
        grid_spec=pltpu.PrefetchScalarGridSpec(
            num_scalar_prefetch=3,
            grid=(1,),
            in_specs=[
                pl.BlockSpec((2, short, half), lambda i, m, o, b: (m[0], 0, 0)),
                mine(2, rows, half),
                mine(16, half),
                mine(3, half),
            ],
            out_specs=[whole(32, half), whole(2, tall, half), whole(2, tall, half)],
            scratch_shapes=[pltpu.VMEM((2, tall, 256), F32)],
        ),
        out_shape=[
            jax.ShapeDtypeStruct((32, half), BF),
            jax.ShapeDtypeStruct((2, tall, half), BF),
            jax.ShapeDtypeStruct((2, tall, half), F32),
        ],
        compiler_params=params(),
        cost_estimate=cost(3 * 10**9, 10**6),
        name="own_slopes",
    )(meta, offsets, bins, attention, skip, edge, filt)


def own_kernel(
    slabs, meta, offsets, sums, slopes, rims, prev_far, cot_far, weight_far, filt,
    moved, terms, skip_grad, att_grad, pair, prev, cot, weight, sems,
):
    copies = [
        pltpu.make_async_copy(prev_far, prev, sems.at[0]),
        pltpu.make_async_copy(cot_far, cot, sems.at[1]),
        pltpu.make_async_copy(weight_far, weight, sems.at[2]),
    ]
    for copy in copies:
        copy.start()
    half = sums.shape[2]
    tall = sums.shape[1]
    rows = tall - 2 * PAD
    wide = cot.shape[2]
    row, col = grid_of(tall, rows)
    last = meta[1] == slabs - 1
    copies[0].wait()
    copies[1].wait()
    for s in range(2):
        at = row - PAD
        fits = (at >= -1) & (at < jnp.where(last, rows, rows + 1))
        source = jnp.where(fits, at - offsets[s], -4096)
        older = picks(col == source + rows)
        newer = picks(col == source)
        place = lax.broadcasted_iota(jnp.int32, (PAD, 512), 0)
        top = (place == PAD - 1) & (offsets[s] == rows)
        bottom = (place == 0) & (offsets[s] == 0) & jnp.logical_not(last)
        for part in range(0, wide, 512):
            cols = slice(part, part + 512)
            found = dot(older, prev[s, :, cols]) + dot(newer, cot[s, :, cols])
            ends = rims[:, cols].astype(F32)
            above = ends[s * 8 + 4 : s * 8 + 5]
            below = ends[s * 8 + 3 : s * 8 + 4]
            found = jnp.concatenate(
                [
                    found[:PAD] + jnp.where(top, above, 0.0),
                    found[PAD : PAD + rows],
                    found[PAD + rows :] + jnp.where(bottom, below, 0.0),
                ]
            )
            moved[s, :, cols] = found.astype(BF)
    copies[2].wait()
    width = 2 * LANES
    first = meta[0] * half

    @pl.loop(0, half // width)
    def _(part):
        begin = pl.multiple_of(part * width, width)
        cols = pl.ds(begin, width)
        taps = taps_of(filt, cols)
        piece = weight[pl.ds(begin, width), :]
        total_terms = [0.0, 0.0, 0.0]
        there = pl.ds(pl.multiple_of(first + begin, width), width)
        for s in range(2):
            conv = (dot_rows(moved[s], piece) * slopes[s, :, cols]).astype(BF).astype(F32)
            got = tap_sums(conv, sums[s, :, cols].astype(F32), rows)
            total_terms = [a + b for a, b in zip(total_terms, got)]
            direct = moved[s, :, there].astype(F32)[PAD : PAD + rows]
            total, pairs = grads(conv, direct, taps, rows, pair)
            skip_grad[s, :, cols] = total.astype(BF)
            att_grad[s, :, cols] = pairs.astype(BF)
        for k in range(3):
            terms[k : k + 1, cols] = total_terms[k]


def own_half(meta, offsets, sums, slopes, edge, prev, cot, weight, filt, slabs):
    seqs, rows, wide = cot.shape
    _, tall, half = sums.shape
    short = rows // 2

    def whole(*shape):
        return pl.BlockSpec(shape, lambda i, m, o: (0,) * len(shape))

    def mine(*shape):
        return pl.BlockSpec(shape, lambda i, m, o: (0,) * (len(shape) - 1) + (m[0],))

    anywhere = pl.BlockSpec(memory_space=pl.ANY)
    return pl.pallas_call(
        functools.partial(own_kernel, slabs),
        grid_spec=pltpu.PrefetchScalarGridSpec(
            num_scalar_prefetch=2,
            grid=(1,),
            in_specs=[
                whole(2, tall, half),
                whole(2, tall, half),
                whole(16, wide),
                anywhere,
                anywhere,
                anywhere,
                mine(3, half),
            ],
            out_specs=[
                whole(2, tall, wide),
                whole(3, half),
                mine(2, rows, half),
                mine(2, short, half),
            ],
            scratch_shapes=[
                pltpu.VMEM((2, rows, LANES), F32),
                pltpu.VMEM((2, rows, wide), BF),
                pltpu.VMEM((2, rows, wide), BF),
                pltpu.VMEM((half, wide), BF),
                pltpu.SemaphoreType.DMA((3,)),
            ],
        ),
        out_shape=[
            jax.ShapeDtypeStruct((2, tall, wide), BF),
            jax.ShapeDtypeStruct((3, half), F32),
            jax.ShapeDtypeStruct((2, rows, wide), BF),
            jax.ShapeDtypeStruct((2, short, wide), BF),
        ],
        compiler_params=params(),
        cost_estimate=cost(1, 1),
        name="own_half",
    )(meta, offsets, sums, slopes, edge, prev, cot, weight, filt)


def slope_kernel(
    meta, offsets, bins, att, skip, edge, twin, filt, asked, sums, slopes, mine, shown, ext
):
    rows = skip.shape[1]
    tall = rows + 2 * PAD
    half = skip.shape[2]
    width = ext.shape[2]
    there = (1 - meta[0]) * half
    row, col = grid_of(16, 32)
    at, base = row & 7, (row >> 3) * 16
    kept = picks((at < 4) & (col == base + at + jnp.where(at < 2, 0, 2)))
    told = picks((at < 4) & (col == base + at + jnp.where(at < 2, 2, 4)))
    here = pl.ds(pl.multiple_of(meta[0] * half, half), half)
    mine[:, here] = dot(kept, asked[...]).astype(BF)
    shown[:, here] = dot(told, asked[...]).astype(BF)

    @pl.loop(0, half // width)
    def _(part):
        begin = pl.multiple_of(part * width, width)
        cols = pl.ds(begin, width)
        slab_sums(att, skip, edge, twin, ext, cols)
        taps = taps_of(filt, cols)
        got = []
        for s in range(2):
            field = ext[s]
            before, after = around(field)
            slopes[s, :, cols] = slope_of(taps[0] * before + taps[1] * field + taps[2] * after)
            sums[s, :, cols] = field.astype(BF)
            got.append(asked_rows(meta, offsets, bins, s, field, taps, tall))
        got = jnp.concatenate(got)
        place = pl.ds(pl.multiple_of(there + begin, width), width)
        mine[:, place] = dot(kept, got).astype(BF)
        shown[:, place] = dot(told, got).astype(BF)


def other_slopes(meta, offsets, bins, shipped, skip, edge, twin, filt, asked):
    seqs, rows, wide = skip.shape
    _, packed_rows, half = shipped.shape
    tall = rows + 2 * PAD

    def whole(*shape):
        return pl.BlockSpec(shape, lambda i, m, o, b: (0,) * len(shape))

    def other(*shape):
        return pl.BlockSpec(shape, lambda i, m, o, b: (0,) * (len(shape) - 1) + (1 - m[0],))

    return pl.pallas_call(
        slope_kernel,
        grid_spec=pltpu.PrefetchScalarGridSpec(
            num_scalar_prefetch=3,
            grid=(1,),
            in_specs=[
                whole(2, packed_rows, half),
                other(2, rows, half),
                other(16, half),
                pl.BlockSpec((16, half), lambda i, m, o, b: (0, m[0])),
                other(3, half),
                whole(32, half),
            ],
            out_specs=[whole(2, tall, half), whole(2, tall, half), whole(16, wide), whole(16, wide)],
            scratch_shapes=[pltpu.VMEM((2, tall, 256), F32)],
        ),
        out_shape=[
            jax.ShapeDtypeStruct((2, tall, half), BF),
            jax.ShapeDtypeStruct((2, tall, half), F32),
            jax.ShapeDtypeStruct((16, wide), BF),
            jax.ShapeDtypeStruct((16, wide), BF),
        ],
        compiler_params=params(),
        cost_estimate=cost(3 * 10**9, 10**6),
        name="other_slopes",
    )(meta, offsets, bins, shipped, skip, edge, twin, filt, asked)


def spots(meta, tile):
    core, block = meta[1] & 1, (meta[1] >> 1) & 3
    return [
        (pl.multiple_of(row * tile, tile), pl.multiple_of((block ^ k) * tile, tile))
        for row in (core, 1 - core)
        for k in range(4)
    ]


def terms_kernel(meta, moved, sums, slopes, own_terms, *refs):
    pieces, (convs, terms, full, sems) = refs[:8], refs[8:]
    half = sums.shape[2]
    tall = sums.shape[1]
    rows = tall - 2 * PAD
    there = (1 - meta[0]) * half
    tile = pieces[0].shape[0]
    copies = []
    for k, (down, over) in enumerate(spots(meta, tile)):
        copies.append(
            pltpu.make_async_copy(
                pieces[k], full.at[pl.ds(down, tile), pl.ds(over, tile)], sems.at[k]
            )
        )
        copies[-1].start()
    terms[:, pl.ds(pl.multiple_of(meta[0] * half, half), half)] = own_terms[...]
    for copy in copies:
        copy.wait()
    width = 2 * LANES
    for begin in range(0, half, width):
        cols = slice(begin, begin + width)
        total = [0.0, 0.0, 0.0]
        for s in range(2):
            grad = dot_rows(moved[s], full[cols, :])
            conv = (grad * slopes[s, :, cols]).astype(BF)
            convs[s, :, cols] = conv
            got = tap_sums(conv.astype(F32), sums[s, :, cols].astype(F32), rows)
            total = [a + b for a, b in zip(total, got)]
        place = pl.ds(pl.multiple_of(there + begin, width), width)
        for k in range(3):
            terms[k : k + 1, place] = total[k]


def other_terms(meta, moved, sums, slopes, own_terms, pieces):
    _, tall, wide = moved.shape
    half = sums.shape[2]

    def whole(*shape):
        return pl.BlockSpec(shape, lambda i, m: (0,) * len(shape))

    return pl.pallas_call(
        terms_kernel,
        grid_spec=pltpu.PrefetchScalarGridSpec(
            num_scalar_prefetch=1,
            grid=(1,),
            in_specs=[
                whole(2, tall, wide),
                whole(2, tall, half),
                whole(2, tall, half),
                whole(3, half),
            ]
            + [pl.BlockSpec(memory_space=pl.ANY)] * 8,
            out_specs=[whole(2, tall, half), whole(3, wide)],
            scratch_shapes=[pltpu.VMEM((half, wide), BF), pltpu.SemaphoreType.DMA((8,))],
        ),
        out_shape=[
            jax.ShapeDtypeStruct((2, tall, half), BF),
            jax.ShapeDtypeStruct((3, wide), F32),
        ],
        compiler_params=params(),
        cost_estimate=cost(2 * 2 * tall * half * wide, 6 * 1024 * 1024),
        name="other_terms",
    )(meta, moved, sums, slopes, own_terms, *pieces)


def grads_kernel(meta, moved, convs, filt, old_skip, old_att, skip_grad, att_grad, pair):
    half = convs.shape[2]
    rows = convs.shape[1] - 2 * PAD
    width = 2 * LANES

    @pl.loop(0, half // width)
    def _(part):
        cols = pl.ds(pl.multiple_of(part * width, width), width)
        taps = taps_of(filt, cols)
        for s in range(2):
            direct = moved[s, :, cols].astype(F32)[PAD : PAD + rows]
            total, pairs = grads(convs[s, :, cols].astype(F32), direct, taps, rows, pair)
            skip_grad[s, :, cols] = total.astype(BF)
            att_grad[s, :, cols] = pairs.astype(BF)


def other_grads(meta, moved, convs, filt, skip_grad, att_grad):
    _, tall, wide = moved.shape
    half = convs.shape[2]
    rows = tall - 2 * PAD

    def whole(*shape):
        return pl.BlockSpec(shape, lambda i, m: (0,) * len(shape))

    def other(*shape):
        return pl.BlockSpec(shape, lambda i, m: (0,) * (len(shape) - 1) + (1 - m[0],))

    return pl.pallas_call(
        grads_kernel,
        grid_spec=pltpu.PrefetchScalarGridSpec(
            num_scalar_prefetch=1,
            grid=(1,),
            in_specs=[other(2, tall, half), whole(2, tall, half), other(3, half)]
            + [pl.BlockSpec(memory_space=pl.ANY)] * 2,
            out_specs=[other(2, rows, half), other(2, rows // 2, half)],
            scratch_shapes=[pltpu.VMEM((2, rows, LANES), F32)],
        ),
        out_shape=[
            jax.ShapeDtypeStruct((2, rows, wide), BF),
            jax.ShapeDtypeStruct((2, rows // 2, wide), BF),
        ],
        input_output_aliases={4: 0, 5: 1},
        compiler_params=params(),
        cost_estimate=cost(2 * tall * half * 20, 4 * 1024 * 1024),
        name="other_grads",
    )(meta, moved, convs, filt, skip_grad, att_grad)


def target_kernel(slabs, meta, mine, got_a, got_b, weight, *refs):
    pieces, (target, total) = refs[:8], refs[8:]
    half = weight.shape[0]
    there = (1 - meta[0]) * half
    tile = pieces[0].shape[0]
    even = (meta[1] & 1) == 0
    got = jnp.where(even, got_a[...].astype(F32), got_b[...].astype(F32))
    got = jnp.where(meta[1] == slabs - 1, 0.0, got)
    mine[...] = (mine[...].astype(F32) + got).astype(BF)
    here = pl.ds(pl.multiple_of(meta[0] * half, half), half)
    total[...] = dot(mine[:, here], weight[...]) + pltpu.roll(mine[...].astype(F32), 12 + 2, 0)
    for k, (down, over) in enumerate(spots(meta, tile)):
        place = pl.ds(pl.multiple_of(there + down, tile), tile)
        total[:, pl.ds(over, tile)] += dot(mine[:, place], pieces[k][...])
    for s in range(2):
        target[s] = total[s * 8 : s * 8 + 2].astype(BF)


def targets(meta, mine, got, weight, pieces, slabs):
    half, wide = weight.shape
    tile = pieces[0].shape[0]

    def whole(*shape):
        return pl.BlockSpec(shape, lambda i, m: (0,) * len(shape))

    return pl.pallas_call(
        functools.partial(target_kernel, slabs),
        grid_spec=pltpu.PrefetchScalarGridSpec(
            num_scalar_prefetch=1,
            grid=(1,),
            in_specs=[whole(16, wide)] * 3 + [whole(half, wide)]
            + [whole(tile, tile)] * 8,
            out_specs=whole(2, NTD, wide),
            scratch_shapes=[pltpu.VMEM((16, wide), F32)],
        ),
        out_shape=jax.ShapeDtypeStruct((2, NTD, wide), BF),
        compiler_params=params(),
        cost_estimate=cost(2 * 16 * wide * wide, 6 * 1024 * 1024),
        name="targets",
    )(meta, mine, *got, weight, *pieces)


def paired(part, axis, bit):
    count = lax.axis_size(axis)
    return lax.ppermute(part, axis, [(i, i ^ bit) for i in range(count)])


def staggered(part, span):
    count = lax.axis_size("seq")
    pairs = []
    for i in range(count):
        by = span if i // span % 2 else -span
        pairs.append((i, (i + by) % count))
    return lax.ppermute(part, "seq", pairs)


def after(value, *others):
    return lax.optimization_barrier((value,) + others)[0]


def crossed(part, seq_bit, head_bit):
    slabs, heads = lax.axis_size("seq"), lax.axis_size("head")
    pairs = [
        (i * heads + j, (i ^ seq_bit) * heads + (j ^ head_bit))
        for i in range(slabs)
        for j in range(heads)
    ]
    return lax.ppermute(part, ("seq", "head"), pairs)


def joined(total, one, two):
    both = (one[0] ^ two[0], one[1] ^ two[1])
    parts = [crossed(total, *bits) for bits in (one, two, both)]
    return (total + parts[0]) + (parts[1] + parts[2])


def fast_shards(
    attention, encoder_skip, depth_filter, point_weight, crop_offset, target_bins, cotangent
):
    head = lax.axis_index("head")
    slab = lax.axis_index("seq")
    slabs = lax.axis_size("seq")
    meta = jnp.stack([head, slab]).astype(jnp.int32)
    tile = 3 * LANES

    edge_a, edge_b, far, first, last_tile, att_out = packed(
        encoder_skip, attention, cotangent, point_weight, tile
    )
    first = paired(first, "head", 1)
    edge_a = paired(edge_a, "seq", 1)
    edge_b = staggered(edge_b, 1)
    far_a = paired(far, "seq", 2)
    far_b = staggered(far, 2)
    prev = passed_along(after(cotangent, edge_a), "seq", 1)
    outer = (slab == 0) | (slab == slabs - 1)
    nothing = jnp.zeros_like(edge_b)
    edge = edge_a + jnp.where(outer, nothing, edge_b)
    twin = paired(edge, "head", 1)
    shipped = paired(after(att_out, edge), "head", 1)
    edge = edge + jnp.where(slab % 4 >= 2, far_a, jnp.where(slab < 2, nothing, far_b))
    asked, own_sums, own_slope = own_slopes(
        meta, crop_offset, target_bins, attention, encoder_skip, edge, depth_filter
    )
    ready = after(first, asked)
    second = paired(ready, "seq", 2)
    third = paired(ready, "seq", 4)
    fourth = paired(after(last_tile, asked), "head", 1)
    sums, slopes, mine, shown = other_slopes(
        meta, crop_offset, target_bins, shipped, encoder_skip, edge, twin, depth_filter, asked
    )
    got = [paired(shown, "seq", 1), staggered(shown, 1)]
    moved, own_terms, skip_grad, att_grad = own_half(
        after(meta, shown), crop_offset, own_sums, own_slope, edge, prev, cotangent, point_weight, depth_filter,
        slabs,
    )
    pieces = [first, second, third, fourth]
    ties = [own_terms, own_terms, own_terms, own_terms]
    pieces = pieces + [paired(after(*both), "seq", 1) for both in zip(pieces, ties)]
    convs, terms = other_terms(meta, moved, sums, slopes, own_terms, pieces)
    total = terms + crossed(terms, 1, 0)
    total = joined(total, (2, 0), (0, 1))
    skip_grad, attention_grad = other_grads(
        meta, moved, convs, depth_filter, skip_grad, att_grad
    )
    target_rows = targets(meta, mine, got, point_weight, pieces, slabs)
    total, skip_grad, attention_grad = lax.optimization_barrier(
        (total, skip_grad, attention_grad)
    )
    if slabs == 16:
        total = joined(total, (4, 0), (8, 0))
    else:
        step = 4
        while step < slabs:
            total = total + crossed(total, step, 0)
            step *= 2
    count = encoder_skip.shape[0] * lax.axis_size("head") * encoder_skip.shape[1] * slabs
    return (target_rows, attention_grad, skip_grad, total * (1.0 / math.sqrt(count)))


def shards(*args):
    attention, encoder_skip, point_weight = args[0], args[1], args[3]
    fits = (
        lax.axis_size("head") == 2
        and lax.axis_size("seq") in (8, 16, 32)
        and encoder_skip.shape[:2] == (2, 128)
        and point_weight.shape[0] == 6 * LANES
        and attention.shape[1] == 64
    )
    return fast_shards(*args) if fits else plain_shards(*args)


def solution(mesh):
    in_specs = (
        P(None, "seq", "head"),
        P("head", "seq", None),
        P(),
        P("head", None),
        P("head"),
        P("head", None),
        P("head", "seq", None),
    )
    out_specs = (P("head", "seq", None), P("head", "seq", None), P("head", "seq", None), P())
    return jax.shard_map(shards, mesh=mesh, in_specs=in_specs, out_specs=out_specs, check_vma=False)
def solution(mesh):
    in_specs = (
        P(None, "seq", "head"),
        P("head", "seq", None),
        P(),
        P("head", None),
        P("head"),
        P("head", None),
        P("head", "seq", None),
    )
    out_specs = (P("head", "seq", None), P("head", "seq", None), P("head", "seq", None), P())
    return jax.shard_map(shards, mesh=mesh, in_specs=in_specs, out_specs=out_specs, check_vma=False)
def solution(mesh):
    in_specs = (
        P(None, "seq", "head"),
        P("head", "seq", None),
        P(),
        P("head", None),
        P("head"),
        P("head", None),
        P("head", "seq", None),
    )
    out_specs = (P("head", "seq", None), P("head", "seq", None), P("head", "seq", None), P())
    return jax.shard_map(shards, mesh=mesh, in_specs=in_specs, out_specs=out_specs, check_vma=False)
```
